32 devices in a mesh: gx: 8 (over z, y), gy: 4 (over x, core).
Axes of the slice: x: 2, y: 2, z: 4, core: 2. Of those that a mesh axis runs over, the one named last changes fastest.
Arguments:
- phi: float32 [256, 128, 1024], P('gx', 'gy'), may hold values from -6 to 6
- kappa: float32 [256, 128, 1024], P('gx', 'gy'), may hold values from 0.02 to 0.12
- stiffness: float32 [512, 2048], P('gx', 'gy'), may hold values from 0.5 to 4
- face_cell: int32 [8, 4, 32, 128], P('gx', 'gy'), may hold values from 0 to 131071
- load_dof: int32 [8, 4, 32, 128], P('gx', 'gy'), may hold values from 0 to 32767
- displacement: float32 [512, 2048], P('gx', 'gy'), may hold values from -6 to 6
- v_hist: float32 [40, 512, 2048], P(None, 'gx', 'gy'), may hold values from -100 to 100
- w_hist: float32 [40, 512, 2048], P(None, 'gx', 'gy'), may hold values from -100 to 100
- r_prev: float32 [512, 2048], P('gx', 'gy'), may hold values from -6 to 6
- w_prev: float32 [512, 2048], P('gx', 'gy'), may hold values from -6 to 6
Outputs:
- phi_out: float32 [256, 128, 1024], P('gx', 'gy')
- x_next: float32 [512, 2048], P('gx', 'gy')
The draws below stay inside these ranges and needn't reach their ends.
All inputs are finite; a program needn't handle non-finite values.
Results may differ from the reference program's by a relative error of at most 0.0003.
Values sent between devices are 32-bit elements; how exact they have to be, the bound alone decides.
No kernel may reach another device: no remote copies, remote signals or barrier semaphores. Data moves between devices by JAX's collectives and lax.ppermute only.
A program may use at most 128 MiB of HBM per device.

```python
import math
import jax
import jax.numpy as jnp
from jax import lax

CX = 32
CY = 32
CZ = 1024
SX = 64
SY = 512
BLK = 128
NSUB = 4
SWEEPS = 3
HIST = 40
NX = 256
NY = 128
SNX = 512
SNY = 2048
N_GX = 8
N_GY = 4


def shared_basis(key, top_scale):
    fields = jax.random.normal(jax.random.fold_in(key, 101), (6, SNX, SNY), jnp.float32)
    mixing = jax.random.normal(jax.random.fold_in(key, 102), (HIST, 6), jnp.float32) * (1.0 / math.sqrt(6.0))
    spread = jax.random.uniform(jax.random.fold_in(key, 103), (HIST,), jnp.float32)
    scales = jnp.exp(spread * math.log(top_scale))
    return (fields, mixing, scales)


def combine(fields, mixing, scales, jitter):
    summed = jitter
    for member in range(6):
        summed = summed + mixing[:, member][:, None, None] * fields[member][None]
    return jnp.clip(summed * scales[:, None, None], -100.0, 100.0)


def draw_displacement(key, part):
    fields, mixing, scales = shared_basis(key, 10.0)
    key = jax.random.fold_in(key, 3)
    jitter = jax.random.normal(key, (SNX, SNY), jnp.float32)
    result = 0.8 * fields[0] + 0.6 * jitter
    return jnp.clip(result, -6.0, 6.0)


def draw_v_hist(key, part):
    fields, mixing, scales = shared_basis(key, 10.0)
    key = jax.random.fold_in(key, 1)
    jitter = jax.random.normal(key, (HIST, SNX, SNY), jnp.float32) * 0.5
    return combine(fields, mixing, scales, jitter)


def draw_w_hist(key, part):
    fields, mixing, scales = shared_basis(key, 10.0)
    key = jax.random.fold_in(key, 2)
    own_key, noise_key = jax.random.split(key)
    jitter = jax.random.normal(noise_key, (HIST, SNX, SNY), jnp.float32) * 0.5
    own_mix = jax.random.normal(own_key, (HIST, 6), jnp.float32) * (1.0 / math.sqrt(6.0))
    blended = 0.7 * mixing + 0.7 * own_mix
    return combine(fields, blended, scales, jitter)


def plant(drawn, rng, smallest, largest):
    place = [jax.random.randint(jax.random.fold_in(rng, axis), (), 0, length) for axis, length in enumerate(drawn.shape)]
    longest = drawn.shape.index(max(drawn.shape))
    beside = place[:longest] + [(place[longest] + 1) % drawn.shape[longest]] + place[longest + 1:]
    return drawn.at[tuple(place)].set(smallest).at[tuple(beside)].set(largest)


def block_scale(stream_key, extent, cuts, least, top_value):
    gain, own = 1.0, jax.random.fold_in(stream_key, 6)
    for axis_at, blocks in cuts:
        steps = jnp.exp(jax.random.uniform(jax.random.fold_in(own, axis_at), (blocks,), jnp.float32, least / len(cuts), top_value / len(cuts)))
        gain = gain * jnp.repeat(steps, extent[axis_at] // blocks).reshape([-1 if axis == axis_at else 1 for axis in range(len(extent))])
    return gain


def normal_values(stream_key, shape, scale, reach, cuts=(), kind=jnp.bfloat16):
    values = jax.random.normal(stream_key, shape, jnp.float32) * scale
    if len(cuts) > 0:
        values = block_scale(stream_key, shape, cuts, -0.22, 0.18) * values
    return jnp.clip(values, min=-reach, max=reach).astype(kind)


def setup_inputs(seed: int = 0) -> dict:
    seeds = jax.random.split(jax.random.key(seed), 11)
    phi = normal_values(seeds[0], (NX, NY, CZ), 1.0, 6.0, ((0, 8), (1, 4)), jnp.float32)
    kappa = jnp.clip(jnp.exp(math.log(0.12) - 1.7917595 * jax.random.uniform(seeds[1], (NX, NY, CZ), jnp.float32) ** block_scale(seeds[1], (NX, NY, CZ), ((0, 8), (1, 4)), -0.2, 0.2)), 0.02, 0.12)
    stiffness = jnp.clip(jnp.exp(math.log(4.0) - 2.0794415 * jax.random.uniform(seeds[2], (SNX, SNY), jnp.float32) ** block_scale(seeds[2], (SNX, SNY), ((0, 8), (1, 4)), -0.2, 0.2)), 0.5, 4.0)
    face_cell = plant(jax.random.randint(seeds[3], (N_GX, N_GY, N_GX * N_GY, BLK), 0, CX * CY * CZ // 8), jax.random.fold_in(seeds[3], 1), 0, (CX * CY * CZ // 8) - 1).astype(jnp.int32)
    load_dof = plant(jax.random.randint(seeds[4], (N_GX, N_GY, N_GX * N_GY, BLK), 0, SX * SY), jax.random.fold_in(seeds[4], 1), 0, (SX * SY) - 1).astype(jnp.int32)
    displacement = draw_displacement(jax.random.fold_in(seeds[10], 71), 0)
    v_hist = draw_v_hist(jax.random.fold_in(seeds[10], 71), 0)
    w_hist = draw_w_hist(jax.random.fold_in(seeds[10], 71), 0)
    r_prev = normal_values(seeds[8], (SNX, SNY), 1.0, 6.0, ((0, 8), (1, 4)), jnp.float32)
    w_prev = normal_values(seeds[9], (SNX, SNY), 1.0, 6.0, ((0, 8), (1, 4)), jnp.float32)
    return dict(phi=phi, kappa=kappa, stiffness=stiffness, face_cell=face_cell, load_dof=load_dof, displacement=displacement, v_hist=v_hist, w_hist=w_hist, r_prev=r_prev, w_prev=w_prev)


def to_blocks3(field):
    return field.reshape(N_GX, CX, N_GY, CY, CZ).transpose(0, 2, 1, 3, 4).reshape(N_GX * N_GY, CX * CY * CZ)

def from_blocks3(blocks):
    return blocks.reshape(N_GX, N_GY, CX, CY, CZ).transpose(0, 2, 1, 3, 4).reshape(N_GX * CX, N_GY * CY, CZ)

def to_blocks2(field):
    return field.reshape(N_GX, SX, N_GY, SY).transpose(0, 2, 1, 3).reshape(N_GX * N_GY, SX * SY)

def from_blocks2(blocks):
    return blocks.reshape(N_GX, N_GY, SX, SY).transpose(0, 2, 1, 3).reshape(N_GX * SX, N_GY * SY)

def fluid_step(field, kappa):
    padded = jnp.pad(field, 1)
    lap = padded[2:, 1:-1, 1:-1] + padded[:-2, 1:-1, 1:-1] + padded[1:-1, 2:, 1:-1] + padded[1:-1, :-2, 1:-1]
    lap = lap + padded[1:-1, 1:-1, 2:] + padded[1:-1, 1:-1, :-2] - 6.0 * field
    return field + kappa * lap - 0.25 * (field - padded[:-2, 1:-1, 1:-1])

def shell_sweep(resp, force, stiffness):
    padded = jnp.pad(resp, 1)
    beside = padded[2:, 1:-1] + padded[:-2, 1:-1] + padded[1:-1, 2:] + padded[1:-1, :-2]
    diag = 1.0 + 4.0 * stiffness
    applied = diag * resp - stiffness * beside
    return resp + 0.8 * (force - applied) / diag

def reference(phi, kappa, stiffness, face_cell, load_dof, displacement, v_hist, w_hist, r_prev, w_prev):
    count = N_GX * N_GY
    ldof = load_dof.reshape(count, count * BLK).astype(jnp.int32)
    fcell = face_cell.reshape(count, count * BLK).astype(jnp.int32)
    xdev = to_blocks2(displacement)
    sent = jnp.take_along_axis(xdev, ldof, axis=1).reshape(count, count, BLK)
    disp = sent.transpose(1, 0, 2).reshape(count, count * BLK)
    pdev = to_blocks3(phi)
    pdev = jax.vmap(lambda p, i, v: p.at[i].add(0.5 * v))(pdev, fcell, disp)
    field = from_blocks3(pdev)
    for step in range(NSUB):
        field = fluid_step(field, kappa)
    pdev = to_blocks3(field)
    press = jnp.take_along_axis(pdev, fcell, axis=1).reshape(count, count, BLK)
    loads = press.transpose(1, 0, 2).reshape(count, count * BLK)
    fdev = jax.vmap(lambda i, v: jnp.zeros((SX * SY,), jnp.float32).at[i].add(v))(ldof, loads)
    force = from_blocks2(fdev)
    resp = displacement
    for sweep in range(SWEEPS):
        resp = shell_sweep(resp, force, stiffness)
    resid = resp - displacement
    vcols = jnp.concatenate([v_hist[1:], (resid - r_prev)[None]], axis=0).reshape(HIST, -1)
    wcols = jnp.concatenate([w_hist[1:], (resp - w_prev)[None]], axis=0).reshape(HIST, -1)
    gram = jnp.dot(vcols, vcols.T, precision=lax.Precision.HIGHEST)
    proj = jnp.dot(vcols, resid.reshape(-1), precision=lax.Precision.HIGHEST)
    ridge = 0.001 * jnp.trace(gram) / HIST
    factor = jnp.linalg.cholesky(gram + ridge * jnp.eye(HIST, dtype=jnp.float32))
    coef = jax.scipy.linalg.cho_solve((factor, True), -proj)
    update = jnp.dot(coef, wcols, precision=lax.Precision.HIGHEST).reshape(resp.shape)
    return (field, resp + update)
```

```python
import functools

import jax
import jax.numpy as jnp
from jax import lax
from jax.experimental import pallas as pl
from jax.experimental.pallas import tpu as pltpu
from jax.sharding import PartitionSpec as P

NSUB = 4
SWEEPS = 3
HIST = 40
VMEM_BYTES = 56 * 1024 * 1024
F32 = jnp.float32
BF16 = jnp.bfloat16


def params():
    return pltpu.CompilerParams(vmem_limit_bytes=VMEM_BYTES)


def vmem_specs(count):
    return [pl.BlockSpec(memory_space=pltpu.VMEM)] * count


def any_specs(count):
    return [pl.BlockSpec(memory_space=pl.ANY)] * count


def pieces(value, count):
    parts = []
    for _ in range(count):
        part = value.astype(BF16)
        parts.append(part)
        value = value - part.astype(F32)
    return parts


def as_row(block):
    return jnp.concatenate([block[i : i + 1] for i in range(block.shape[0])], axis=1)


def one_hot(keys, rows):
    ids = lax.broadcasted_iota(jnp.int32, (rows, keys.shape[1]), 0)
    return jnp.where(ids == keys, 1.0, 0.0).astype(BF16)


def select_sum(table, lane, group, rows, parts):
    total = table[:rows]
    for part in range(1, parts):
        total = total + table[part * rows : (part + 1) * rows]
    ids = lax.broadcasted_iota(jnp.int32, total.shape, 0)
    return jnp.sum(jnp.where(ids == lane, total, 0.0), axis=0, keepdims=True)


def pick(table_t, index_ref, out_rows, rows, lane_bits, chunk_bits, parts, step=8):
    lanes = 1 << lane_bits
    for base in range(0, index_ref.shape[0], step):
        index = as_row(index_ref[base : base + step, :])
        lane = index & (lanes - 1)
        keys = ((index >> lane_bits) & ((1 << chunk_bits) - 1)) * rows + (
            index >> (lane_bits + chunk_bits)
        )
        hot = one_hot(keys, rows << chunk_bits)
        found = lax.dot_general(
            table_t, hot, (((1,), (0,)), ((), ())), preferred_element_type=F32
        )
        out_rows(base, select_sum(found, lane, step, lanes, parts))


def spread_values(values, lane, lanes, parts):
    ids = lax.broadcasted_iota(jnp.int32, (lanes, lane.shape[1]), 0)
    match = ids == lane
    return jnp.concatenate(
        [jnp.where(match, part.astype(F32), 0.0).astype(BF16) for part in pieces(values, parts)],
        axis=0,
    )


def gather_disp(n_gy, disp_ref, index_ref, out_ref):
    sx, sy = disp_ref.shape
    peers, blk = index_ref.shape
    chunk_bits = (sy // 128).bit_length() - 1
    columns = []
    for q in range(sy // 128):
        columns.append(jnp.transpose(disp_ref[:, q * 128 : (q + 1) * 128]))
    flat = jnp.concatenate(columns, axis=1)
    table_t = jnp.concatenate(pieces(flat, 3), axis=0)

    def write(base, row):
        for i in range(8):
            out_ref[base + i : base + i + 1, 0:blk] = row[:, i * blk : (i + 1) * blk]

    pick(table_t, index_ref, write, sx, 7, chunk_bits, 3)
    own = out_ref[:, 0:blk]
    beside = lax.broadcasted_iota(jnp.int32, own.shape, 0) % n_gy
    out_ref[:, blk : 2 * blk] = jnp.where(
        beside == n_gy - 1, 0.0, pltpu.roll(own, peers - 1, axis=0)
    )
    out_ref[:, 2 * blk : 3 * blk] = jnp.where(beside == 0, 0.0, pltpu.roll(own, 1, axis=0))


def scatter_force_field(cy, cz, disp_ref, cells_ref, out_ref, acc_ref, side_ref):
    planes = out_ref.shape[0]
    peers = disp_ref.shape[0]
    blk = cells_ref.shape[2]
    rows = planes * cy
    chunks = cz // 256
    row_bits = cz.bit_length() - 1
    n_gy = cells_ref.shape[0]
    here = lax.axis_index("gy")
    above = jnp.minimum(here + 1, n_gy - 1)
    below = jnp.maximum(here - 1, 0)
    step = 8

    def accumulate(target, first, keys, height, lane, values):
        hot = one_hot(keys, height)
        added = lax.dot_general(
            hot, spread_values(values, lane, 256, 2), (((1,), (1,)), ((), ())),
            preferred_element_type=F32,
        )
        if first:
            target[...] = added
        else:
            target[...] += added

    for base in range(0, peers, step):
        index = as_row(cells_ref[here, base : base + step, :])
        values = 0.5 * as_row(disp_ref[base : base + step, 0:blk])
        keys = ((index >> 8) & (chunks - 1)) * rows + (index >> row_bits)
        accumulate(acc_ref, base == 0, keys, rows * chunks, index & 255, values)
        for side in range(2):
            index = as_row(cells_ref[above if side == 0 else below, base : base + step, :])
            values = 0.5 * as_row(
                disp_ref[base : base + step, (side + 1) * blk : (side + 2) * blk]
            )
            row = index >> row_bits
            plane = row // cy
            column = row - plane * cy
            inside = column < 4 if side == 0 else column >= cy - 4
            place = column if side == 0 else column - (cy - 8)
            keys = ((index >> 8) & (chunks - 1)) * (planes * 8) + plane * 8 + place
            keys = jnp.where(inside, keys, -1)
            accumulate(
                side_ref, base == 0 and side == 0, keys, planes * 8 * chunks, index & 255, values
            )
    for q in range(chunks):
        part = acc_ref[q * rows : (q + 1) * rows, :]
        out_ref[:, 0:cy, q * 256 : (q + 1) * 256] = (part[:, :256] + part[:, 256:]).reshape(
            planes, cy, 256
        )
        part = side_ref[q * planes * 8 : (q + 1) * planes * 8, :]
        out_ref[:, cy : cy + 8, q * 256 : (q + 1) * 256] = (
            part[:, :256] + part[:, 256:]
        ).reshape(planes, 8, 256)


def gather_press(wet_ref, index_ref, out_ref):
    planes, cy, cz = wet_ref.shape
    peers, blk = index_ref.shape
    rows = planes * cy
    chunks = cz // 256
    columns = []
    for q in range(chunks):
        part = wet_ref[:, :, q * 256 : (q + 1) * 256].reshape(rows, 256)
        columns.append(jnp.transpose(part))
    table_t = jnp.concatenate(pieces(jnp.concatenate(columns, axis=1), 2), axis=0)

    def write(base, row):
        for i in range(8):
            out_ref[base + i : base + i + 1, :] = row[:, i * blk : (i + 1) * blk]

    pick(table_t, index_ref, write, rows, 8, chunks.bit_length() - 1, 2)


def scatter_loads(loads_ref, index_ref, out_ref, acc_ref):
    sx, sy = out_ref.shape
    peers, blk = index_ref.shape
    chunks = sy // 128
    for base in range(0, peers, 8):
        index = as_row(index_ref[base : base + 8, :])
        values = as_row(loads_ref[base : base + 8, :])
        keys = ((index >> 7) & (chunks - 1)) * sx + index // sy
        added = lax.dot_general(
            one_hot(keys, sx * chunks), spread_values(values, index & 127, 128, 3),
            (((1,), (1,)), ((), ())), preferred_element_type=F32,
        )
        if base == 0:
            acc_ref[...] = added
        else:
            acc_ref[...] += added
    for q in range(chunks):
        part = acc_ref[q * sx : (q + 1) * sx, :]
        out_ref[:, q * 128 : (q + 1) * 128] = part[:, :128] + part[:, 128:256] + part[:, 256:]


def pack_edges(phi_lo, kap_lo, phi_hi, kap_hi, low_ref, high_ref):
    first = lax.broadcasted_iota(jnp.int32, phi_lo.shape, 1) < 4
    low_ref[...] = jnp.where(first, phi_lo[...], pltpu.roll(kap_lo[...], 4, axis=1))
    high_ref[...] = jnp.where(first, pltpu.roll(kap_hi[...], 4, axis=1), phi_hi[...])


def packed_edges(phi, kappa):
    cx, cy, cz = phi.shape
    depth = 4
    low = pl.BlockSpec((depth, 8, cz), lambda i: (i, 0, 0))
    high = pl.BlockSpec((depth, 8, cz), lambda i: (i, cy // 8 - 1, 0))
    shape = jax.ShapeDtypeStruct((cx, 8, cz), F32)
    return pl.pallas_call(
        pack_edges,
        grid=(cx // depth,),
        in_specs=[low, low, high, high],
        out_specs=[low, low],
        out_shape=[shape, shape],
        compiler_params=params(),
        name="pack_edges",
    )(phi, kappa, phi, kappa)


def substep(src, kap, dst, plane, advect, cy, cz):
    wide = cy + 8
    chunks = cz // 128
    lane = lax.broadcasted_iota(jnp.int32, (wide, 128), 1)
    first, last = lane == 0, lane == 127

    def take(ref, at, q):
        return ref[at, :, q * 128 : (q + 1) * 128]

    zero = jnp.zeros((wide, 128), F32)
    now = take(src, plane, 0)
    back = pltpu.roll(now, 1, axis=1)
    back_before = zero
    ahead = pltpu.roll(now, 127, axis=1)
    for q in range(chunks):
        if q + 1 < chunks:
            later = take(src, plane, q + 1)
            ahead_later = pltpu.roll(later, 127, axis=1)
        else:
            later, ahead_later = None, zero
        before = take(src, plane - 1, q)
        total = (before + take(src, plane + 1, q)) + (
            pltpu.roll(now, 1, axis=0) + pltpu.roll(now, wide - 1, axis=0)
        )
        total = total + (jnp.where(first, back_before, back) + jnp.where(last, ahead_later, ahead))
        k = take(kap, plane - 1, q)
        dst[plane, :, q * 128 : (q + 1) * 128] = (
            now + advect * (before - now) + k * (total - 6.0 * now)
        )
        if later is not None:
            back_before, back = back, pltpu.roll(later, 1, axis=1)
            now, ahead = later, ahead_later


def fluid(x0, x1, cx, cy, cz, with_wet, *refs):
    planes = x1 - x0 + 8
    names = ["phi", "kappa", "up", "down", "forced"]
    names += ["low", "low_up", "low_down"] if x0 - 4 < 0 else []
    names += ["high"] if x1 + 4 > cx else []
    names += ["wet"] if with_wet else []
    names += ["out"] + ([] if with_wet else ["send"])
    names += ["a", "b", "kap", "upb", "downb", "sems", "out_sems"]
    r = dict(zip(names, refs))
    a, b, kap, upb, downb = r["a"], r["b"], r["kap"], r["upb"], r["downb"]
    sems, out_sems = r["sems"], r["out_sems"]
    is_last = lax.axis_index("gx") == lax.axis_size("gx") - 1
    used = [0]

    def copy(src, dst):
        made = pltpu.make_async_copy(src, dst, sems.at[used[0]])
        used[0] += 1
        made.start()
        return made

    own0, own1 = max(0, x0 - 4), min(cx, x1 + 4)
    groups = []
    if x0 - 4 < 0:
        groups.append((0, 4, [
            copy(r["low"].at[pl.ds(0, 4)], a.at[pl.ds(0, 4), pl.ds(0, cy)]),
            copy(r["low"].at[pl.ds(4, 3)], kap.at[pl.ds(0, 3), pl.ds(0, cy)]),
            copy(r["low_up"], upb.at[pl.ds(0, 4)]),
            copy(r["low_down"], downb.at[pl.ds(0, 4)]),
        ]))
    for start in range(own0, own1, 4):
        i = start - (x0 - 4)
        copies = [
            copy(r["phi"].at[pl.ds(start, 4)], a.at[pl.ds(i, 4), pl.ds(0, cy)]),
            copy(r["up"].at[pl.ds(start, 4)], upb.at[pl.ds(i, 4)]),
            copy(r["down"].at[pl.ds(start, 4)], downb.at[pl.ds(i, 4)]),
        ]
        k0, k1 = max(start, x0 - 3), min(start + 4, x1 + 3)
        copies.append(
            copy(r["kappa"].at[pl.ds(k0, k1 - k0)],
                 kap.at[pl.ds(k0 - (x0 - 3), k1 - k0), pl.ds(0, cy)])
        )
        groups.append((i, i + 4, copies))
    if x1 + 4 > cx:
        i = cx - (x0 - 4)
        groups.append((i, i + 4, [
            copy(r["high"].at[pl.ds(0, 4)], a.at[pl.ds(i, 4)]),
            copy(r["high"].at[pl.ds(4, 3)], kap.at[pl.ds(i - 1, 3)]),
        ]))
    outs = []
    if with_wet:
        made = pltpu.make_async_copy(r["wet"], r["out"].at[pl.ds(0, x0)], out_sems.at[0])
        made.start()
        outs.append(made)

    upper = lax.broadcasted_iota(jnp.int32, (8, cz), 0) < 4

    def assemble(i0, i1):
        for i in range(i0, i1):
            x = x0 - 4 + i
            if x >= cx:
                continue
            up, down = upb[i], downb[i]
            a[i, cy : cy + 8, :] = jnp.where(upper, up, down)
            if 1 <= i < planes - 1:
                kap[i - 1, cy : cy + 8, :] = pltpu.roll(jnp.where(upper, down, up), 4, axis=0)
            if 0 <= x < r["forced"].shape[0]:
                a[i] = a[i] + r["forced"][x]

    def run(src, dst, lo, hi):
        def body(i, carry):
            outside = jnp.logical_and(is_last, i + (x0 - 4) >= cx)
            substep(src, kap, dst, i, jnp.where(outside, 0.0, 0.25), cy, cz)
            return carry

        lax.fori_loop(lo, hi, body, 0)

    done = 1
    sends = []
    for i0, i1, copies in groups:
        for made in copies:
            made.wait()
        assemble(i0, i1)
        if not with_wet and i0 == 4:
            sends = [
                pltpu.make_async_copy(a.at[pl.ds(4, 4)], r["send"].at[pl.ds(0, 4)], out_sems.at[0]),
                pltpu.make_async_copy(kap.at[pl.ds(3, 3)], r["send"].at[pl.ds(4, 3)], out_sems.at[1]),
            ]
            for made in sends:
                made.start()
        ready = i1 - 1
        if ready > done:
            run(a, b, done, ready)
            done = ready
    for made in sends:
        made.wait()
    run(b, a, 2, planes - 2)
    run(a, b, 3, planes - 3)
    for number, start in enumerate(range(4, planes - 4, 4)):
        run(b, a, start, start + 4)
        x = x0 + start - 4
        target = r["out"].at[pl.ds(x if with_wet else x - x0, 4)]
        made = pltpu.make_async_copy(
            a.at[pl.ds(start, 4), pl.ds(0, cy)], target, out_sems.at[number + 2]
        )
        made.start()
        outs.append(made)
    for made in outs:
        made.wait()


def fluid_call(x0, x1, phi, kappa, up, down, forced, low=None, high=None, wet=None):
    cx, cy, cz = phi.shape
    planes = x1 - x0 + 8
    args = [phi, kappa, up, down, forced]
    specs = any_specs(4) + vmem_specs(1)
    if low is not None:
        args += list(low)
        specs += any_specs(3)
    if high is not None:
        args.append(high)
        specs += any_specs(1)
    if wet is not None:
        args.append(wet)
        specs += any_specs(1)
        out_shape = jax.ShapeDtypeStruct((cx, cy, cz), F32)
        out_specs = pl.BlockSpec(memory_space=pl.ANY)
    else:
        out_shape = [
            jax.ShapeDtypeStruct((x1 - x0, cy, cz), F32),
            jax.ShapeDtypeStruct((7, cy + 8, cz), F32),
        ]
        out_specs = any_specs(2)
    cells = planes * (cy + 8) * cz
    return pl.pallas_call(
        functools.partial(fluid, x0, x1, cx, cy, cz, wet is not None),
        in_specs=specs,
        out_specs=out_specs,
        out_shape=out_shape,
        scratch_shapes=[
            pltpu.VMEM((planes, cy + 8, cz), F32),
            pltpu.VMEM((planes, cy + 8, cz), F32),
            pltpu.VMEM((planes - 2, cy + 8, cz), F32),
            pltpu.VMEM((planes, 8, cz), F32),
            pltpu.VMEM((planes, 8, cz), F32),
            pltpu.SemaphoreType.DMA((64,)),
            pltpu.SemaphoreType.DMA((16,)),
        ],
        compiler_params=params(),
        cost_estimate=pl.CostEstimate(
            flops=48 * cells, bytes_accessed=12 * cells, transcendentals=0
        ),
        name="fluid_wet" if wet is None else "fluid_rest",
    )(*args)


def extended(block, sides, width):
    for axis, dim in sides:
        count = lax.axis_size(axis)
        forward = [(i, i + 1) for i in range(count - 1)]
        backward = [(target, source) for source, target in forward]
        low = lax.ppermute(
            lax.slice_in_dim(block, block.shape[dim] - width, None, axis=dim), axis, forward
        )
        high = lax.ppermute(lax.slice_in_dim(block, 0, width, axis=dim), axis, backward)
        block = jnp.concatenate([low, block, high], axis=dim)
    return block


def shifted_pairs(n_gx, n_gy, dx, dy):
    pairs = []
    for gx in range(n_gx):
        for gy in range(n_gy):
            tx, ty = gx + dx, gy + dy
            if 0 <= tx < n_gx and 0 <= ty < n_gy:
                pairs.append((gx * n_gy + gy, tx * n_gy + ty))
    return pairs


def local(phi, kappa, stiffness, face_cell, load_dof, displacement, v_hist, w_hist, r_prev, w_prev):
    n_gx, n_gy = lax.axis_size("gx"), lax.axis_size("gy")
    peers, blk = face_cell.shape[2:]
    cx, cy, cz = phi.shape
    sx, sy = displacement.shape
    wet_planes = cx // 8
    fcell = face_cell.reshape(peers, blk)
    ldof = load_dof.reshape(peers, blk)
    axes = ("gx", "gy")

    def shift(value, dx, dy):
        return lax.ppermute(value, axes, shifted_pairs(n_gx, n_gy, dx, dy))

    low_raw = shift(jnp.concatenate([phi[cx - 4 :], kappa[cx - 3 :]], axis=0), 1, 0)
    low_edge, high_edge = packed_edges(phi, kappa)
    up = shift(low_edge, 0, -1)
    down = shift(high_edge, 0, 1)
    low_up = shift(low_edge[cx - 4 :], 1, -1)
    low_down = shift(high_edge[cx - 4 :], 1, 1)
    cells = lax.all_gather(fcell, "gy", axis=0, tiled=False)

    sent = pl.pallas_call(
        functools.partial(gather_disp, n_gy),
        in_specs=vmem_specs(2),
        out_specs=vmem_specs(1)[0],
        out_shape=jax.ShapeDtypeStruct((peers, 3 * blk), F32),
        compiler_params=params(),
        name="gather_disp",
    )(displacement, ldof)
    disp = lax.all_to_all(sent, axes, split_axis=0, concat_axis=0, tiled=True)
    forced = pl.pallas_call(
        functools.partial(scatter_force_field, cy, cz),
        in_specs=vmem_specs(2),
        out_specs=vmem_specs(1)[0],
        out_shape=jax.ShapeDtypeStruct((wet_planes, cy + 8, cz), F32),
        scratch_shapes=[
            pltpu.VMEM((wet_planes * cy * (cz // 256), 512), F32),
            pltpu.VMEM((wet_planes * 8 * (cz // 256), 512), F32),
        ],
        compiler_params=params(),
        name="scatter_disp",
    )(disp, cells)
    wet, send = fluid_call(
        0, wet_planes, phi, kappa, up, down, forced, low=(low_raw, low_up, low_down)
    )
    press = pl.pallas_call(
        gather_press,
        in_specs=vmem_specs(2),
        out_specs=vmem_specs(1)[0],
        out_shape=jax.ShapeDtypeStruct((peers, blk), F32),
        compiler_params=params(),
        name="gather_press",
    )(wet, fcell)
    loads = lax.all_to_all(press, axes, split_axis=0, concat_axis=0, tiled=True)
    high = shift(send, -1, 0)
    force = pl.pallas_call(
        scatter_loads,
        in_specs=vmem_specs(2),
        out_specs=vmem_specs(1)[0],
        out_shape=jax.ShapeDtypeStruct((sx, sy), F32),
        scratch_shapes=[pltpu.VMEM((sx * (sy // 128), 384), F32)],
        compiler_params=params(),
        name="scatter_loads",
    )(loads, ldof)

    sides = (("gx", 1), ("gy", 2))
    fixed = extended(jnp.stack([displacement, stiffness]), sides, 3)
    moving = extended(force[None], sides, 2)[0]
    resp, stiff = fixed[0], fixed[1]
    for sweep in range(SWEEPS):
        inner = resp[1:-1, 1:-1]
        stiff = stiff[1:-1, 1:-1]
        beside = resp[2:, 1:-1] + resp[:-2, 1:-1] + resp[1:-1, 2:] + resp[1:-1, :-2]
        diag = 1.0 + 4.0 * stiff
        resp = inner + 0.8 * (moving - (diag * inner - stiff * beside)) / diag
        moving = moving[1:-1, 1:-1]
    resid = resp - displacement
    newest = (resid - r_prev).reshape(-1)
    kept = v_hist[1:].reshape(HIST - 1, -1)
    gram_kept = jnp.dot(kept, kept.T, precision=lax.Precision.HIGHEST)
    gram_kept = jnp.pad(gram_kept, ((0, 1), (0, 128 - HIST + 1)))
    gram_kept = jnp.sum(lax.all_gather(gram_kept, axes, axis=0, tiled=False), axis=0)
    vcols = jnp.concatenate([kept, newest[None]], axis=0)
    pair = jnp.stack([newest, resid.reshape(-1)])
    late = jnp.dot(pair, vcols.T, precision=lax.Precision.HIGHEST)
    late = jnp.pad(late, ((0, 0), (0, 128 - HIST))).reshape(1, 256)
    late = lax.all_to_all(
        jnp.broadcast_to(late, (peers, 256)), axes, split_axis=0, concat_axis=0, tiled=True
    )
    late = jnp.sum(late, axis=0)
    border, proj = late[:HIST], late[128 : 128 + HIST]
    gram = gram_kept[:, :HIST]
    unit = jnp.arange(HIST) == HIST - 1
    gram = jnp.where(unit[:, None], border[None, :], jnp.where(unit[None, :], border[:, None], gram))
    ridge = 0.001 * jnp.trace(gram) / HIST
    factor = jnp.linalg.cholesky(gram + ridge * jnp.eye(HIST, dtype=F32))
    coef = jax.scipy.linalg.cho_solve((factor, True), -proj)
    update = jnp.dot(
        coef[: HIST - 1], w_hist[1:].reshape(HIST - 1, -1), precision=lax.Precision.HIGHEST
    ).reshape(sx, sy) + coef[HIST - 1] * (resp - w_prev)
    x_next = resp + update
    field = fluid_call(
        wet_planes, cx, phi, kappa, up, down, forced, high=high, wet=wet
    )
    return (field, x_next)


def solution(mesh):
    in_specs = (
        P("gx", "gy", None),
        P("gx", "gy", None),
        P("gx", "gy"),
        P("gx", "gy", None, None),
        P("gx", "gy", None, None),
        P("gx", "gy"),
        P(None, "gx", "gy"),
        P(None, "gx", "gy"),
        P("gx", "gy"),
        P("gx", "gy"),
    )
    out_specs = (P("gx", "gy", None), P("gx", "gy"))
    return jax.shard_map(local, mesh=mesh, in_specs=in_specs, out_specs=out_specs, check_vma=False)
```

```python
import functools

import jax
import jax.numpy as jnp
from jax import lax
from jax.experimental import pallas as pl
from jax.experimental.pallas import tpu as pltpu
from jax.sharding import PartitionSpec as P

NSUB = 4
SWEEPS = 3
HIST = 40
VMEM_BYTES = 56 * 1024 * 1024
F32 = jnp.float32
BF16 = jnp.bfloat16


def params():
    return pltpu.CompilerParams(vmem_limit_bytes=VMEM_BYTES)


def vmem_specs(count):
    return [pl.BlockSpec(memory_space=pltpu.VMEM)] * count


def any_specs(count):
    return [pl.BlockSpec(memory_space=pl.ANY)] * count


def pieces(value, count):
    parts = []
    for _ in range(count):
        part = value.astype(BF16)
        parts.append(part)
        value = value - part.astype(F32)
    return parts


def as_row(block):
    return jnp.concatenate([block[i : i + 1] for i in range(block.shape[0])], axis=1)


def one_hot(keys, rows):
    ids = lax.broadcasted_iota(jnp.int32, (rows, keys.shape[1]), 0)
    return jnp.where(ids == keys, 1.0, 0.0).astype(BF16)


def select_sum(table, lane, group, rows, parts):
    total = table[:rows]
    for part in range(1, parts):
        total = total + table[part * rows : (part + 1) * rows]
    ids = lax.broadcasted_iota(jnp.int32, total.shape, 0)
    return jnp.sum(jnp.where(ids == lane, total, 0.0), axis=0, keepdims=True)


def pick(table_t, index_ref, out_rows, rows, lane_bits, chunk_bits, parts, step=8):
    lanes = 1 << lane_bits
    for base in range(0, index_ref.shape[0], step):
        index = as_row(index_ref[base : base + step, :])
        lane = index & (lanes - 1)
        keys = ((index >> lane_bits) & ((1 << chunk_bits) - 1)) * rows + (
            index >> (lane_bits + chunk_bits)
        )
        hot = one_hot(keys, rows << chunk_bits)
        found = lax.dot_general(
            table_t, hot, (((1,), (0,)), ((), ())), preferred_element_type=F32
        )
        out_rows(base, select_sum(found, lane, step, lanes, parts))


def spread_values(values, lane, lanes, parts):
    ids = lax.broadcasted_iota(jnp.int32, (lanes, lane.shape[1]), 0)
    match = ids == lane
    return jnp.concatenate(
        [jnp.where(match, part.astype(F32), 0.0).astype(BF16) for part in pieces(values, parts)],
        axis=0,
    )


NEAR = ((0, 0), (1, 0), (-1, 0), (0, 1), (0, -1), (1, 1), (1, -1), (-1, 1), (-1, -1))


def tile_of(ref, plane, number):
    at = (number % 8) * 128
    return ref[plane + number // 8, :, at : at + 128]


def starter(sems):
    used = [0]

    def copy(src, dst):
        made = pltpu.make_async_copy(src, dst, sems.at[used[0]])
        used[0] += 1
        made.start()
        return made

    return copy


def gather_disp(n_gy, disp_ref, index_ref, out_ref, own_ref):
    sx, sy = disp_ref.shape
    peers, blk = index_ref.shape
    chunk_bits = (sy // 128).bit_length() - 1
    columns = []
    for q in range(sy // 128):
        columns.append(jnp.transpose(disp_ref[:, q * 128 : (q + 1) * 128]))
    table_t = jnp.concatenate(pieces(jnp.concatenate(columns, axis=1), 3), axis=0)

    def write(base, row):
        for i in range(8):
            own_ref[base + i : base + i + 1, :] = row[:, i * blk : (i + 1) * blk]

    pick(table_t, index_ref, write, sx, 7, chunk_bits, 3)
    own = own_ref[...]
    beside = lax.broadcasted_iota(jnp.int32, own.shape, 0) % n_gy
    out_ref[:, 0, 0:blk] = own
    out_ref[:, 0, blk : 2 * blk] = jnp.where(
        beside == n_gy - 1, 0.0, pltpu.roll(own, peers - 1, axis=0)
    )
    out_ref[:, 0, 2 * blk : 3 * blk] = jnp.where(beside == 0, 0.0, pltpu.roll(own, 1, axis=0))


def scatter_disp(cx, cy, cz, disp_ref, cells_ref, up_ref, down_ref, out_ref, acc_ref, side_ref, near_ref, sems):
    planes = out_ref.shape[0]
    peers, blk = cells_ref.shape
    rows = planes * cy
    chunks = cz // 256
    row_bits = cz.bit_length() - 1
    step = 8
    extra = near_ref.shape[1]
    copy = starter(sems)
    copies = [
        copy(ref.at[pl.ds(cx, extra)], near_ref.at[side])
        for side, ref in enumerate((up_ref, down_ref))
    ]

    def accumulate(target, first, keys, height, lane, values):
        added = lax.dot_general(
            one_hot(keys, height), spread_values(values, lane, 256, 2),
            (((1,), (1,)), ((), ())), preferred_element_type=F32,
        )
        if first:
            target[...] = added
        else:
            target[...] += added

    for base in range(0, peers, step):
        index = as_row(cells_ref[base : base + step, :])
        values = 0.5 * as_row(disp_ref[base : base + step, 0, 0:blk])
        keys = ((index >> 8) & (chunks - 1)) * rows + (index >> row_bits)
        accumulate(acc_ref, base == 0, keys, rows * chunks, index & 255, values)
    for made in copies:
        made.wait()
    for side in range(2):
        for base in range(0, peers, step):
            index = as_row(tile_of(near_ref.at[side], 0, base // step).astype(jnp.int32))
            values = 0.5 * as_row(
                disp_ref[base : base + step, 0, (side + 1) * blk : (side + 2) * blk]
            )
            row = index >> row_bits
            plane = row // cy
            column = row - plane * cy
            inside = column < 4 if side == 0 else column >= cy - 4
            place = column if side == 0 else column - (cy - 8)
            keys = ((index >> 8) & (chunks - 1)) * (planes * 8) + plane * 8 + place
            keys = jnp.where(inside, keys, -1)
            accumulate(
                side_ref, base == 0 and side == 0, keys, planes * 8 * chunks, index & 255, values
            )
    for q in range(chunks):
        part = acc_ref[q * rows : (q + 1) * rows, :]
        out_ref[:, 0:cy, q * 256 : (q + 1) * 256] = (part[:, :256] + part[:, 256:]).reshape(
            planes, cy, 256
        )
        part = side_ref[q * planes * 8 : (q + 1) * planes * 8, :]
        out_ref[:, cy : cy + 8, q * 256 : (q + 1) * 256] = (
            part[:, :256] + part[:, 256:]
        ).reshape(planes, 8, 256)


def gather_press(n_gx, n_gy, wet_ref, index_ref, gram_ref, out_ref, own_ref):
    planes, cy, cz = wet_ref.shape
    peers, blk = index_ref.shape
    rows = planes * cy
    chunks = cz // 256
    columns = []
    for q in range(chunks):
        part = wet_ref[:, :, q * 256 : (q + 1) * 256].reshape(rows, 256)
        columns.append(jnp.transpose(part))
    table_t = jnp.concatenate(pieces(jnp.concatenate(columns, axis=1), 2), axis=0)

    def write(base, row):
        for i in range(8):
            own_ref[base + i : base + i + 1, :] = row[:, i * blk : (i + 1) * blk]

    pick(table_t, index_ref, write, rows, 8, chunks.bit_length() - 1, 2)
    own = own_ref[...]
    number = lax.broadcasted_iota(jnp.int32, own.shape, 0)
    at_x, at_y = number // n_gy, number % n_gy
    for k, (dx, dy) in enumerate(NEAR):
        ok = (at_x + dx >= 0) & (at_x + dx < n_gx) & (at_y + dy >= 0) & (at_y + dy < n_gy)
        moved = pltpu.roll(own, (-(dx * n_gy + dy)) % peers, axis=0) if k else own
        out_ref[:, 0, k * blk : (k + 1) * blk] = jnp.where(ok, moved, 0.0)
    out_ref[:, 0, len(NEAR) * blk : (len(NEAR) + 1) * blk] = gram_ref[...]


def gram_rows(v_ref, out_ref, v, same, cross, wide, sems):
    hist, sx, sy = v_ref.shape
    tiles = sx // 8
    copy = starter(sems)
    copies = [
        copy(v_ref.at[:, pl.ds(8 * t, 8), :], v.at[t]) for t in range(tiles)
    ]
    for t in range(tiles):
        copies[t].wait()
        high, low = pieces(v[t].reshape(hist * 8, sy), 2)

        def dot(x, y):
            return lax.dot_general(x, y, (((1,), (1,)), ((), ())), preferred_element_type=F32)

        if t == 0:
            same[...] = dot(high, high) + dot(low, low)
            cross[...] = dot(high, low)
        else:
            same[...] += dot(high, high) + dot(low, low)
            cross[...] += dot(high, low)
    size = hist * 8
    row = lax.broadcasted_iota(jnp.int32, (size, size), 0)
    column = lax.broadcasted_iota(jnp.int32, (size, size), 1)
    match = (row & 7) == (column & 7)
    group = (
        lax.broadcasted_iota(jnp.int32, (size, 128), 0) // 8
        == lax.broadcasted_iota(jnp.int32, (size, 128), 1)
    ).astype(F32)

    def reduced(ref):
        part = jnp.sum(jnp.where(match, ref[...], 0.0).reshape(hist, 8, size), axis=1)
        return jnp.dot(part, group, precision=lax.Precision.HIGHEST, preferred_element_type=F32)

    wide[...] = jnp.zeros_like(wide)
    wide[0:hist, :] = reduced(cross)
    turned = jnp.transpose(wide[0:128, :])
    wide[0:128, :] = wide[0:128, :] + turned
    wide[0:hist, :] = wide[0:hist, :] + reduced(same)
    peers = out_ref.shape[0]
    if peers >= hist:
        out_ref[...] = wide[0:peers, :]
    else:
        out_ref[...] = wide[0:peers, :] + pltpu.roll(wide[peers : 2 * peers, :], 64, axis=1)


def shell(recv_ref, index_ref, disp_ref, stiff_ref, prev_ref, v_ref, up_ref, down_ref, low_ref,
          low_up_ref, low_down_ref, high_ref, resp_ref, late_ref, v, packs, acc, rows_acc, cols_acc,
          corner_acc, ext, dots, sems, v_sem):
    sx, sy = disp_ref.shape
    peers, blk = index_ref.shape
    extra = packs.shape[1]
    index_planes = extra - 2
    load_tiles = peers // 8
    chunks = sy // 128
    hist = v_ref.shape[0]
    v_copy = pltpu.make_async_copy(v_ref, v, v_sem.at[0])
    v_copy.start()
    copy = starter(sems)
    top = up_ref.shape[0] - extra
    corner = low_up_ref.shape[0] - extra
    low_planes = low_ref.shape[0] - (-(-extra // 4))
    copies = [
        copy(high_ref.at[pl.ds(0, extra)], packs.at[0]),
        copy(up_ref.at[pl.ds(top, extra)], packs.at[2]),
        copy(down_ref.at[pl.ds(top, extra)], packs.at[3]),
        copy(high_ref.at[pl.ds(extra, extra)], packs.at[4]),
        copy(high_ref.at[pl.ds(2 * extra, extra)], packs.at[5]),
        copy(low_up_ref.at[pl.ds(corner, extra)], packs.at[6]),
        copy(low_down_ref.at[pl.ds(corner, extra)], packs.at[7]),
    ]
    for e in range(extra):
        copies.append(
            copy(low_ref.at[low_planes + e // 4, pl.ds(8 * (e % 4), 8)], packs.at[1, e])
        )

    def accumulate(target, first, keys, height, lane, lanes, values):
        added = lax.dot_general(
            one_hot(keys, height), spread_values(values, lane, lanes, 2),
            (((1,), (1,)), ((), ())), preferred_element_type=F32,
        )
        if first:
            target[...] = added
        else:
            target[...] += added

    def values_of(k, base):
        return as_row(recv_ref[base : base + 8, 0, k * blk : (k + 1) * blk])

    for base in range(0, peers, 8):
        index = as_row(index_ref[base : base + 8, :])
        keys = ((index >> 7) & (chunks - 1)) * sx + index // sy
        accumulate(acc, base == 0, keys, sx * chunks, index & 127, 128, values_of(0, base))
    for made in copies:
        made.wait()
    for k, (dx, dy) in enumerate(NEAR):
        if k == 0:
            continue
        for base in range(0, peers, 8):
            number = load_tiles + base // 8
            index = as_row(tile_of(packs.at[k - 1], 0, number).astype(jnp.int32))
            row = index // sy
            lane = index & (sy - 1)
            if dx == 1:
                row8 = jnp.where(row < 4, row, -1)
            elif dx == -1:
                row8 = jnp.where(row >= sx - 4, row - (sx - 8), -1)
            if dy == 1:
                lane8 = jnp.where(lane < 4, lane, -1)
            elif dy == -1:
                lane8 = jnp.where(lane >= sy - 4, lane - (sy - 8), -1)
            values = values_of(k, base)
            if dy == 0:
                keys = jnp.where(row8 < 0, -1, (lane >> 7) * 8 + row8)
                accumulate(
                    rows_acc, k == 1 and base == 0, keys, 8 * chunks, lane & 127, 128, values
                )
            elif dx == 0:
                accumulate(cols_acc, k == 3 and base == 0, row, sx, lane8, 8, values)
            else:
                accumulate(corner_acc, k == 5 and base == 0, row8, 8, lane8, 8, values)

    ids = lax.broadcasted_iota(jnp.int32, (8, 128), 0)
    lanes = lax.broadcasted_iota(jnp.int32, (8, 128), 1)
    placed = (jnp.where(ids < 4, ids, ids + 120) == lanes).astype(F32)

    def widened(ref):
        both = ref[:, 0:8] + ref[:, 8:16]
        return jnp.dot(both, placed, precision=lax.Precision.HIGHEST, preferred_element_type=F32)

    force, disp, stiff = ext.at[0], ext.at[1], ext.at[2]
    for q in range(chunks):
        at = slice(q * 128, (q + 1) * 128)
        part = acc[q * sx : (q + 1) * sx, :]
        force[0:sx, at] = part[:, 0:128] + part[:, 128:256]
        part = rows_acc[q * 8 : (q + 1) * 8, :]
        force[sx : sx + 8, at] = part[:, 0:128] + part[:, 128:256]
    side = slice(sy, sy + 128)
    force[0:sx, side] = widened(cols_acc)
    force[sx : sx + 8, side] = widened(corner_acc)
    sub = lax.broadcasted_iota(jnp.int32, (8, sy), 0) < 4
    sub1 = lax.broadcasted_iota(jnp.int32, (8, 128), 0) < 4
    lane = lax.broadcasted_iota(jnp.int32, (sx, 128), 1)
    lane1 = lax.broadcasted_iota(jnp.int32, (8, 128), 1)
    for kind, (target, own) in enumerate(((disp, disp_ref), (stiff, stiff_ref))):

        def row_tile(pack, start, size):
            at = kind * sy + start
            return packs[pack, index_planes, :, at : at + size]

        def col_tile(pack):
            return jnp.concatenate(
                [tile_of(packs.at[pack], index_planes + 1, m) for m in range(sx // 8)], axis=0
            )

        target[0:sx, 0:sy] = own[...]
        target[sx : sx + 8, 0:sy] = jnp.where(sub, row_tile(0, 0, sy), row_tile(1, 0, sy))
        ahead, behind = col_tile(2), col_tile(3)
        if kind == 0:
            behind = pltpu.roll(behind, 64, axis=1)
        else:
            ahead = pltpu.roll(ahead, 64, axis=1)
        target[0:sx, side] = jnp.where(lane < 32, ahead, jnp.where(lane >= 96, behind, 0.0))

        def corner_tile(pack_ahead, pack_behind):
            return jnp.where(
                lane1 < 32, row_tile(pack_ahead, 0, 128),
                jnp.where(lane1 >= 96, row_tile(pack_behind, sy - 128, 128), 0.0),
            )

        target[sx : sx + 8, side] = jnp.where(sub1, corner_tile(4, 5), corner_tile(6, 7))

    load = force[...]
    k = stiff[...]
    diag = 1.0 + 4.0 * k
    scale = 0.8 / diag
    resp = disp[...]
    high, wide = sx + 8, sy + 128
    for sweep in range(SWEEPS):
        beside = (pltpu.roll(resp, 1, axis=0) + pltpu.roll(resp, high - 1, axis=0)) + (
            pltpu.roll(resp, 1, axis=1) + pltpu.roll(resp, wide - 1, axis=1)
        )
        resp = resp + scale * (load - (diag * resp - k * beside))
    own = resp[0:sx, 0:sy]
    resp_ref[...] = own
    resid = own - disp_ref[...]
    newest = resid - prev_ref[...]
    dots[...] = jnp.zeros_like(dots)

    def folded(value):
        total = value[0:8]
        for t in range(1, sx // 8):
            total = total + value[8 * t : 8 * t + 8]
        out = total[:, 0:128]
        for q in range(1, chunks):
            out = out + total[:, q * 128 : (q + 1) * 128]
        return jnp.sum(out, axis=0, keepdims=True)

    dots[0:1, :] = folded(newest * newest)
    dots[64:65, :] = folded(resid * newest)
    v_copy.wait()
    for number in range(1, hist):
        column = v[number]
        dots[number : number + 1, :] = folded(column * newest)
        dots[64 + number : 65 + number, :] = folded(column * resid)
    late = lax.dot_general(
        jnp.ones((8, 128), F32), dots[...], (((1,), (1,)), ((), ())),
        precision=lax.Precision.HIGHEST, preferred_element_type=F32,
    )
    gram_at = len(NEAR) * blk
    gram = jnp.sum(recv_ref[:, 0, gram_at : gram_at + 128], axis=0, keepdims=True)
    late_ref[:, 0, 0:128] = jnp.broadcast_to(late[0:1], (peers, 128))
    late_ref[:, 0, 128:256] = jnp.broadcast_to(gram, (peers, 128))


def solve(recv_ref, resp_ref, prev_ref, w_ref, out_ref, w, sems):
    peers = recv_ref.shape[0]
    hist = w_ref.shape[0]
    sx, sy = resp_ref.shape
    w_copy = pltpu.make_async_copy(w_ref, w, sems.at[0])
    w_copy.start()
    late = jnp.sum(recv_ref[:, 0, 0:128], axis=0, keepdims=True)
    rows = recv_ref[:, 0, 128:256]
    if peers >= hist:
        gram = rows[0:hist]
    else:
        gram = jnp.concatenate(
            [rows, pltpu.roll(rows, 64, axis=1)[0 : hist - peers]], axis=0
        )
    row = lax.broadcasted_iota(jnp.int32, (hist, 128), 0)
    lane = lax.broadcasted_iota(jnp.int32, (hist, 128), 1)
    turned = jnp.transpose(jnp.broadcast_to(late, (128, 128)))
    gram = jnp.where(row == 0, jnp.broadcast_to(late, (hist, 128)), gram)
    gram = jnp.where(lane == 0, turned[0:hist], gram)
    gram = jnp.where(lane < hist, gram, 0.0)
    unit = row == lane
    trace = jnp.sum(jnp.where(unit, gram, 0.0), keepdims=True)
    a = gram + jnp.where(unit, 0.001 * trace / hist, 0.0)
    a = jnp.where(lane == 64, -turned[64 : 64 + hist], a)
    for j in range(hist):
        column = jnp.broadcast_to(a[:, j : j + 1], (hist, 128))
        scaled = a[j : j + 1, :] / column[j : j + 1, :]
        a = jnp.where(row == j, scaled, a - column * scaled)
    coef = jnp.broadcast_to(a[:, 64:65], (hist, 128))
    coef = jnp.concatenate([coef] * (sy // 128), axis=1)
    resp = resp_ref[...]
    total = resp + coef[0:1] * (resp - prev_ref[...])
    w_copy.wait()
    for number in range(1, hist):
        total = total + coef[number : number + 1] * w[number]
    out_ref[...] = total


def pack(phi_ref, kappa_ref, disp_ref, stiff_ref, cells_ref, loads_ref, up_ref, down_ref, low_ref,
         low_up_ref, low_down_ref, own_ref, phi_lo, kap_lo, phi_hi, kap_hi, up, down, own,
         in_sems, out_sems):
    cx, cy, cz = phi_ref.shape
    sx, sy = disp_ref.shape
    peers = cells_ref.shape[0]
    extra = own.shape[0]
    copy_in, copy_out = starter(in_sems), starter(out_sems)
    depth = 8
    groups = []
    for x in range(0, cx, depth):
        at = pl.ds(x, depth)
        groups.append([
            copy_in(phi_ref.at[at, pl.ds(0, 8)], phi_lo.at[at]),
            copy_in(kappa_ref.at[at, pl.ds(0, 8)], kap_lo.at[at]),
            copy_in(phi_ref.at[at, pl.ds(cy - 8, 8)], phi_hi.at[at]),
            copy_in(kappa_ref.at[at, pl.ds(cy - 8, 8)], kap_hi.at[at]),
        ])
    outs = [
        copy_out(phi_ref.at[pl.ds(cx - 4, 4)], low_ref.at[pl.ds(0, 4)]),
        copy_out(kappa_ref.at[pl.ds(cx - 3, 3)], low_ref.at[pl.ds(4, 3)]),
    ]
    for n in range(2 * peers // 8):
        source = cells_ref if n < peers // 8 else loads_ref
        base = 8 * (n % (peers // 8))
        own[n // 8, :, (n % 8) * 128 : (n % 8 + 1) * 128] = source[base : base + 8, :].astype(F32)
    if 2 * peers % 64:
        own[2 * peers // 64, :, 2 * peers % 64 * 16 :] = jnp.zeros(
            (8, 1024 - 2 * peers % 64 * 16), F32
        )
    sub = lax.broadcasted_iota(jnp.int32, (8, sy), 0) < 4
    for kind, ref in enumerate((disp_ref, stiff_ref)):
        own[extra - 2, :, kind * sy : (kind + 1) * sy] = jnp.where(
            sub, ref[0:8, :], ref[sx - 8 : sx, :]
        )
    lane = lax.broadcasted_iota(jnp.int32, (sx, 128), 1)
    first, final = slice(0, 128), slice(sy - 128, sy)
    columns = jnp.where(
        lane < 32, disp_ref[:, first],
        jnp.where(
            lane < 64, pltpu.roll(disp_ref[:, final], 64, axis=1),
            jnp.where(lane < 96, pltpu.roll(stiff_ref[:, first], 64, axis=1), stiff_ref[:, final]),
        ),
    )
    for m in range(sx // 8):
        own[extra - 1, :, m * 128 : (m + 1) * 128] = columns[8 * m : 8 * m + 8, :]
    outs += [
        copy_out(own, own_ref),
        copy_out(own, up_ref.at[pl.ds(cx, extra)]),
        copy_out(own, down_ref.at[pl.ds(cx, extra)]),
        copy_out(own, low_up_ref.at[pl.ds(4, extra)]),
        copy_out(own, low_down_ref.at[pl.ds(4, extra)]),
    ]
    for e in range(extra):
        outs.append(copy_out(own.at[e], low_ref.at[7 + e // 4, pl.ds(8 * (e % 4), 8)]))
    upper = lax.broadcasted_iota(jnp.int32, (depth, 8, cz), 1) < 4
    for number, copies in enumerate(groups):
        for made in copies:
            made.wait()
        x = number * depth
        at = slice(x, x + depth)
        up[at] = jnp.where(upper, phi_lo[at], pltpu.roll(kap_lo[at], 4, axis=1))
        down[at] = jnp.where(upper, pltpu.roll(kap_hi[at], 4, axis=1), phi_hi[at])
        at = pl.ds(x, depth)
        outs.append(copy_out(up.at[at], up_ref.at[at]))
        outs.append(copy_out(down.at[at], down_ref.at[at]))
    at = pl.ds(cx - 4, 4)
    outs.append(copy_out(up.at[at], low_up_ref.at[pl.ds(0, 4)]))
    outs.append(copy_out(down.at[at], low_down_ref.at[pl.ds(0, 4)]))
    for made in outs:
        made.wait()


def packed(phi, kappa, displacement, stiffness, cells, loads):
    cx, cy, cz = phi.shape
    peers = cells.shape[0]
    extra = -(-2 * peers // 64) + 2

    def shape(planes, rows=8):
        return jax.ShapeDtypeStruct((planes, rows, cz), F32)

    return pl.pallas_call(
        pack,
        in_specs=any_specs(2) + vmem_specs(4),
        out_specs=any_specs(6),
        out_shape=[
            shape(cx + extra), shape(cx + extra), shape(7 + -(-extra // 4), cy),
            shape(4 + extra), shape(4 + extra), shape(extra),
        ],
        scratch_shapes=[pltpu.VMEM((cx, 8, cz), F32)] * 6
        + [
            pltpu.VMEM((extra, 8, cz), F32),
            pltpu.SemaphoreType.DMA((cx // 2,)),
            pltpu.SemaphoreType.DMA((32,)),
        ],
        compiler_params=params(),
        name="pack",
    )(phi, kappa, displacement, stiffness, cells, loads)


def substep(src, kap, coef, dst, plane, advect, cy, cz):
    wide = cy + 8
    chunks = cz // 128
    lane = lax.broadcasted_iota(jnp.int32, (wide, 128), 1)
    first, last = lane == 0, lane == 127

    def take(ref, at, q):
        return ref[at, :, q * 128 : (q + 1) * 128]

    zero = jnp.zeros((wide, 128), F32)
    now = take(src, plane, 0)
    back, back_before = pltpu.roll(now, 1, axis=1), zero
    ahead = pltpu.roll(now, 127, axis=1)
    for q in range(chunks):
        if q + 1 < chunks:
            later = take(src, plane, q + 1)
            ahead_later = pltpu.roll(later, 127, axis=1)
        else:
            later, ahead_later = None, zero
        before = take(src, plane - 1, q)
        above = jnp.concatenate([now[8:], pltpu.roll(now[:8], 7, axis=0)], axis=0)
        below = jnp.concatenate([pltpu.roll(now[wide - 8 :], 1, axis=0), now[: wide - 8]], axis=0)
        total = (before + take(src, plane + 1, q)) + (above + below)
        total = total + (jnp.where(first, back_before, back) + jnp.where(last, ahead_later, ahead))
        dst[plane, :, q * 128 : (q + 1) * 128] = (
            take(coef, plane, q) * now + advect * before + take(kap, plane, q) * total
        )
        if later is not None:
            back_before, back = back, pltpu.roll(later, 1, axis=1)
            now, ahead = later, ahead_later


def fluid(x0, x1, cx, cy, cz, with_wet, *refs):
    planes = x1 - x0 + 8
    wide = cy + 8
    chunks = cz // 128
    names = ["phi", "kappa", "up", "down", "forced"]
    names += ["low", "low_up", "low_down"] if x0 - 4 < 0 else []
    names += ["high"] if x1 + 4 > cx else []
    names += ["wet"] if with_wet else []
    names += ["out"] + ([] if with_wet else ["send"])
    names += ["nat", "knat", "a", "b", "kap", "coef", "upb", "downb", "sems", "out_sems"]
    r = dict(zip(names, refs))
    nat, knat, a, b, kap, coef = (r[n] for n in ("nat", "knat", "a", "b", "kap", "coef"))
    upb, downb = r["upb"], r["downb"]
    is_last = lax.axis_index("gx") == lax.axis_size("gx") - 1
    copy, copy_out = starter(r["sems"]), starter(r["out_sems"])

    def chunked(src, s0, count, dst, d0, rows, start=copy):
        return [
            start(
                src.at[pl.ds(s0, count), pl.ds(0, rows), pl.ds(q * 128, 128)],
                dst.at[pl.ds(d0, count), q, pl.ds(0, rows)],
            )
            for q in range(chunks)
        ]

    def unchunked(src, s0, count, dst, d0, rows):
        return [
            copy_out(
                src.at[pl.ds(s0, count), q, pl.ds(0, rows)],
                dst.at[pl.ds(d0, count), pl.ds(0, rows), pl.ds(q * 128, 128)],
            )
            for q in range(chunks)
        ]

    outs = []
    groups = []
    if x0 - 4 < 0:
        groups.append((0, 4, True, chunked(r["low"], 0, 4, nat, 0, cy)
                       + chunked(r["low"], 4, 3, knat, 1, cy) + [
            copy(r["low_up"].at[pl.ds(0, 4)], upb.at[pl.ds(0, 4)]),
            copy(r["low_down"].at[pl.ds(0, 4)], downb.at[pl.ds(0, 4)]),
        ]))
    own0, own1 = max(0, x0 - 4), min(cx, x1 + 4)
    start = own0
    while start < own1:
        count = min(8, own1 - start)
        i = start - (x0 - 4)
        groups.append((i, i + count, True, chunked(r["phi"], start, count, nat, i, cy)
                       + chunked(r["kappa"], start, count, knat, i, cy) + [
            copy(r["up"].at[pl.ds(start, count)], upb.at[pl.ds(i, count)]),
            copy(r["down"].at[pl.ds(start, count)], downb.at[pl.ds(i, count)]),
        ]))
        start += count
    if x1 + 4 > cx:
        i = cx - (x0 - 4)
        groups.append((i, i + 4, False, chunked(r["high"], 0, 4, nat, i, wide)
                       + chunked(r["high"], 4, 3, knat, i, wide)))
    if with_wet:
        outs.append(copy_out(r["wet"], r["out"].at[pl.ds(0, x0)]))

    upper = lax.broadcasted_iota(jnp.int32, (8, cz), 0) < 4
    tiles = wide // 8

    def prepare(i, halo, wet):
        if halo:
            up, down = upb[i], downb[i]
            edge = jnp.where(upper, up, down)
            kedge = pltpu.roll(jnp.where(upper, down, up), 4, axis=0)
            for q in range(chunks):
                nat[i, q, cy:wide, :] = edge[:, q * 128 : (q + 1) * 128]
                knat[i, q, cy:wide, :] = kedge[:, q * 128 : (q + 1) * 128]
        for q in range(chunks):
            at = slice(q * 128, (q + 1) * 128)
            if wet:
                nat[i, q] = nat[i, q] + r["forced"][i + (x0 - 4), :, at]
            for j in range(tiles):
                rows = slice(8 * j, 8 * j + 8)
                a[i, rows, at] = nat[i, q, pl.ds(j, 8, stride=tiles), :]
                k = knat[i, q, pl.ds(j, 8, stride=tiles), :]
                kap[i, rows, at] = k
                coef[i, rows, at] = 0.75 - 6.0 * k

    def step(src, dst, i):
        outside = jnp.logical_and(is_last, i + (x0 - 4) >= cx)
        substep(src, kap, coef, dst, i, jnp.where(outside, 0.0, 0.25), cy, cz)

    def loop(lo, hi, *work):
        def body(i, carry):
            for one in work:
                one(i)
            return carry

        if hi > lo:
            lax.fori_loop(lo, hi, body, 0)

    wet_lo, wet_hi = 4 - x0, 4 - x0 + r["forced"].shape[0]
    for i0, i1, halo, copies in groups:
        for made in copies:
            made.wait()
        edges = sorted({i0, i1, min(max(2, i0), i1), min(max(wet_lo, i0), i1), min(max(wet_hi, i0), i1)})
        for lo, hi in zip(edges[:-1], edges[1:]):
            wet = wet_lo <= lo < wet_hi
            work = [lambda i: prepare(i, halo, wet)]
            if lo >= 2:
                work.append(lambda i: step(a, b, i - 1))
            loop(lo, hi, *work)
        if not with_wet and i0 == 4:
            outs += unchunked(nat, 4, 4, r["send"], 0, wide)
            outs += unchunked(knat, 4, 3, r["send"], 4, wide)
    loop(2, planes - 2, lambda i: step(b, a, i))
    loop(3, planes - 3, lambda i: step(a, b, i))

    def finish(i):
        step(b, a, i)
        for q in range(chunks):
            for j in range(tiles):
                rows = slice(8 * j, 8 * j + 8)
                done[i, q, pl.ds(j, 8, stride=tiles), :] = a[i, rows, q * 128 : (q + 1) * 128]

    done = nat if with_wet else knat
    if not with_wet:
        for made in outs:
            made.wait()
        outs = []
    start = 4
    while start < planes - 4:
        count = min(8, planes - 4 - start)
        loop(start, start + count, finish)
        x = x0 + start - 4
        outs += unchunked(done, start, count, r["out"], x if with_wet else x - x0, cy)
        start += count
    for made in outs:
        made.wait()


def fluid_call(x0, x1, phi, kappa, up, down, forced, low=None, high=None, wet=None):
    cx, cy, cz = phi.shape
    planes = x1 - x0 + 8
    args = [phi, kappa, up, down, forced]
    specs = any_specs(4) + vmem_specs(1)
    if low is not None:
        args += list(low)
        specs += any_specs(3)
    if high is not None:
        args.append(high)
        specs += any_specs(1)
    if wet is not None:
        args.append(wet)
        specs += any_specs(1)
        out_shape = jax.ShapeDtypeStruct((cx, cy, cz), F32)
        out_specs = pl.BlockSpec(memory_space=pl.ANY)
    else:
        out_shape = [
            jax.ShapeDtypeStruct((x1 - x0, cy, cz), F32),
            jax.ShapeDtypeStruct((7, cy + 8, cz), F32),
        ]
        out_specs = any_specs(2)
    cells = planes * (cy + 8) * cz
    natural = pltpu.VMEM((planes, cz // 128, cy + 8, 128), F32)
    stored = pltpu.VMEM((planes, cy + 8, cz), F32)
    return pl.pallas_call(
        functools.partial(fluid, x0, x1, cx, cy, cz, wet is not None),
        in_specs=specs,
        out_specs=out_specs,
        out_shape=out_shape,
        scratch_shapes=[natural, natural, stored, stored, stored, stored]
        + [pltpu.VMEM((planes, 8, cz), F32)] * 2
        + [pltpu.SemaphoreType.DMA((128,)), pltpu.SemaphoreType.DMA((64,))],
        compiler_params=params(),
        cost_estimate=pl.CostEstimate(
            flops=48 * cells, bytes_accessed=12 * cells, transcendentals=0
        ),
        name="fluid_wet" if wet is None else "fluid_rest",
    )(*args)


def shifted_pairs(n_gx, n_gy, dx, dy):
    pairs = []
    for gx in range(n_gx):
        for gy in range(n_gy):
            tx, ty = gx + dx, gy + dy
            if 0 <= tx < n_gx and 0 <= ty < n_gy:
                pairs.append((gx * n_gy + gy, tx * n_gy + ty))
    return pairs


def local(phi, kappa, stiffness, face_cell, load_dof, displacement, v_hist, w_hist, r_prev, w_prev):
    n_gx, n_gy = lax.axis_size("gx"), lax.axis_size("gy")
    peers, blk = face_cell.shape[2:]
    cx, cy, cz = phi.shape
    sx, sy = displacement.shape
    hist = v_hist.shape[0]
    wet_planes = cx // 8
    fcell = face_cell.reshape(peers, blk)
    ldof = load_dof.reshape(peers, blk)
    axes = ("gx", "gy")

    def shift(value, dx, dy):
        return lax.ppermute(value, axes, shifted_pairs(n_gx, n_gy, dx, dy))

    def exchange(value):
        return lax.all_to_all(value, axes, split_axis=0, concat_axis=0, tiled=True)

    def call(body, out_shape, scratch, name, specs, *args):
        several = isinstance(out_shape, list)
        return pl.pallas_call(
            body,
            in_specs=specs,
            out_specs=vmem_specs(len(out_shape)) if several else vmem_specs(1)[0],
            out_shape=out_shape,
            scratch_shapes=scratch,
            compiler_params=params(),
            name=name,
        )(*args)

    def f32(*shape):
        return jax.ShapeDtypeStruct(shape, F32)

    up_send, down_send, low_send, low_up_send, low_down_send, own = packed(
        phi, kappa, displacement, stiffness, fcell, ldof
    )
    extra = own.shape[0]
    low = shift(low_send, 1, 0)
    up = shift(up_send, 0, -1)
    down = shift(down_send, 0, 1)
    low_up = shift(low_up_send, 1, -1)
    low_down = shift(low_down_send, 1, 1)
    near = shift(jnp.concatenate([own, up[cx:], down[cx:]], axis=0), -1, 0)

    sent = call(
        functools.partial(gather_disp, n_gy), f32(peers, 1, 3 * blk),
        [pltpu.VMEM((peers, blk), F32)], "gather_disp", vmem_specs(2), displacement, ldof,
    )
    disp = exchange(sent)
    chunks = cz // 256
    forced = call(
        functools.partial(scatter_disp, cx, cy, cz), f32(wet_planes, cy + 8, cz),
        [
            pltpu.VMEM((wet_planes * cy * chunks, 512), F32),
            pltpu.VMEM((wet_planes * 8 * chunks, 512), F32),
            pltpu.VMEM((2, (extra - 2) // 2 + (extra - 2) % 2, 8, cz), F32),
            pltpu.SemaphoreType.DMA((2,)),
        ],
        "scatter_disp", vmem_specs(2) + any_specs(2), disp, fcell, up, down,
    )
    wet, send = fluid_call(
        0, wet_planes, phi, kappa, up, down, forced, low=(low, low_up, low_down)
    )
    size = 8 * hist
    gram = call(
        gram_rows, f32(peers, 128),
        [
            pltpu.VMEM((sx // 8, hist, 8, sy), F32), pltpu.VMEM((size, size), F32),
            pltpu.VMEM((size, size), F32),
            pltpu.VMEM((max(128, peers, 2 * peers if peers < hist else 0), 128), F32),
            pltpu.SemaphoreType.DMA((sx // 8,)),
        ],
        "gram_rows", any_specs(1), v_hist,
    )
    press = call(
        functools.partial(gather_press, n_gx, n_gy), f32(peers, 1, (len(NEAR) + 1) * blk),
        [pltpu.VMEM((peers, blk), F32)], "gather_press", vmem_specs(3), wet, fcell, gram,
    )
    loads = exchange(press)
    high = shift(send, -1, 0)
    resp, late = call(
        shell, [f32(sx, sy), f32(peers, 1, 256)],
        [
            pltpu.VMEM((hist, sx, sy), F32),
            pltpu.VMEM((8, extra, 8, cz), F32),
            pltpu.VMEM((sx * (sy // 128), 256), F32),
            pltpu.VMEM((8 * (sy // 128), 256), F32),
            pltpu.VMEM((sx, 16), F32),
            pltpu.VMEM((8, 16), F32),
            pltpu.VMEM((3, sx + 8, sy + 128), F32),
            pltpu.VMEM((128, 128), F32),
            pltpu.SemaphoreType.DMA((7 + extra,)),
            pltpu.SemaphoreType.DMA((1,)),
        ],
        "shell", vmem_specs(5) + any_specs(7),
        loads, ldof, displacement, stiffness, r_prev, v_hist, up, down, low, low_up, low_down, near,
    )
    x_next = call(
        solve, f32(sx, sy),
        [pltpu.VMEM((hist, sx, sy), F32), pltpu.SemaphoreType.DMA((1,))],
        "solve", vmem_specs(3) + any_specs(1), exchange(late), resp, w_prev, w_hist,
    )
    field = fluid_call(wet_planes, cx, phi, kappa, up, down, forced, high=high, wet=wet)
    return (field, x_next)


def solution(mesh):
    in_specs = (
        P("gx", "gy", None),
        P("gx", "gy", None),
        P("gx", "gy"),
        P("gx", "gy", None, None),
        P("gx", "gy", None, None),
        P("gx", "gy"),
        P(None, "gx", "gy"),
        P(None, "gx", "gy"),
        P("gx", "gy"),
        P("gx", "gy"),
    )
    out_specs = (P("gx", "gy", None), P("gx", "gy"))
    return jax.shard_map(local, mesh=mesh, in_specs=in_specs, out_specs=out_specs, check_vma=False)
```

```python
import functools

import jax
import jax.numpy as jnp
from jax import lax
from jax.experimental import pallas as pl
from jax.experimental.pallas import tpu as pltpu
from jax.sharding import PartitionSpec as P

NSUB = 4
SWEEPS = 3
HIST = 40
VMEM_BYTES = 56 * 1024 * 1024
F32 = jnp.float32
BF16 = jnp.bfloat16


def params():
    return pltpu.CompilerParams(vmem_limit_bytes=VMEM_BYTES)


def vmem_specs(count):
    return [pl.BlockSpec(memory_space=pltpu.VMEM)] * count


def hbm_specs(count):
    return [pl.BlockSpec(memory_space=pltpu.HBM)] * count


def pieces(value, count):
    parts = []
    for _ in range(count):
        part = value.astype(BF16)
        parts.append(part)
        value = value - part.astype(F32)
    return parts


def as_row(block):
    return jnp.concatenate([block[i : i + 1] for i in range(block.shape[0])], axis=1)


def one_hot(keys, rows):
    ids = lax.broadcasted_iota(jnp.int32, (rows, keys.shape[1]), 0)
    return jnp.where(ids == keys, 1.0, 0.0).astype(BF16)


def select_sum(table, lane, group, rows, parts):
    total = table[:rows]
    for part in range(1, parts):
        total = total + table[part * rows : (part + 1) * rows]
    ids = lax.broadcasted_iota(jnp.int32, total.shape, 0)
    return jnp.sum(jnp.where(ids == lane, total, 0.0), axis=0, keepdims=True)


def pick(table_t, index_ref, out_rows, rows, lane_bits, chunk_bits, parts, step=8):
    lanes = 1 << lane_bits
    for base in range(0, index_ref.shape[0], step):
        index = as_row(index_ref[base : base + step, :])
        lane = index & (lanes - 1)
        keys = ((index >> lane_bits) & ((1 << chunk_bits) - 1)) * rows + (
            index >> (lane_bits + chunk_bits)
        )
        hot = one_hot(keys, rows << chunk_bits)
        found = lax.dot_general(
            table_t, hot, (((1,), (0,)), ((), ())), preferred_element_type=F32
        )
        out_rows(base, select_sum(found, lane, step, lanes, parts))


def spread_values(values, lane, lanes, parts):
    ids = lax.broadcasted_iota(jnp.int32, (lanes, lane.shape[1]), 0)
    match = ids == lane
    return jnp.concatenate(
        [jnp.where(match, part.astype(F32), 0.0).astype(BF16) for part in pieces(values, parts)],
        axis=0,
    )


NEAR = ((0, 0), (1, 0), (-1, 0), (0, 1), (0, -1), (1, 1), (1, -1), (-1, 1), (-1, -1))


def tile_of(ref, plane, number):
    at = (number % 8) * 128
    return ref[plane + number // 8, :, at : at + 128]


def starter(sems):
    used = [0]

    def copy(src, dst):
        made = pltpu.make_async_copy(src, dst, sems.at[used[0]])
        used[0] += 1
        made.start()
        return made

    return copy


def gather_disp(n_gy, disp_ref, index_ref, out_ref, own_ref):
    sx, sy = disp_ref.shape
    peers, blk = index_ref.shape
    chunk_bits = (sy // 128).bit_length() - 1
    columns = []
    for q in range(sy // 128):
        columns.append(jnp.transpose(disp_ref[:, q * 128 : (q + 1) * 128]))
    table_t = jnp.concatenate(pieces(jnp.concatenate(columns, axis=1), 3), axis=0)

    def write(base, row):
        for i in range(8):
            own_ref[base + i : base + i + 1, :] = row[:, i * blk : (i + 1) * blk]

    pick(table_t, index_ref, write, sx, 7, chunk_bits, 3)
    own = own_ref[...]
    beside = lax.broadcasted_iota(jnp.int32, own.shape, 0) % n_gy
    out_ref[:, 0, 0:blk] = own
    out_ref[:, 0, blk : 2 * blk] = jnp.where(
        beside == n_gy - 1, 0.0, pltpu.roll(own, peers - 1, axis=0)
    )
    out_ref[:, 0, 2 * blk : 3 * blk] = jnp.where(beside == 0, 0.0, pltpu.roll(own, 1, axis=0))


def scatter_disp(cx, cy, cz, disp_ref, cells_ref, up_ref, down_ref, out_ref, acc_ref, side_ref, near_ref, sems):
    planes = out_ref.shape[0]
    peers, blk = cells_ref.shape
    rows = planes * cy
    chunks = cz // 128
    row_bits = cz.bit_length() - 1
    step = 8
    extra = near_ref.shape[1]
    copy = starter(sems)
    copies = [
        copy(ref.at[pl.ds(cx, extra)], near_ref.at[side])
        for side, ref in enumerate((up_ref, down_ref))
    ]

    def accumulate(target, first, left, right):
        added = lax.dot_general(
            left, right, (((1,), (1,)), ((), ())), preferred_element_type=F32
        )
        if first:
            target[...] = added
        else:
            target[...] += added

    for base in range(0, peers, step):
        index = as_row(cells_ref[base : base + step, :])
        values = 0.5 * as_row(disp_ref[base : base + step, 0, 0:blk])
        keys = ((index >> 7) & (chunks - 1)) * rows + (index >> row_bits)
        accumulate(
            acc_ref, base == 0, one_hot(keys, rows * chunks),
            spread_values(values, index & 127, 128, 2),
        )
    for made in copies:
        made.wait()
    for base in range(0, peers, step):
        for side in range(2):
            index = as_row(tile_of(near_ref.at[side], 0, base // step).astype(jnp.int32))
            values = 0.5 * as_row(
                disp_ref[base : base + step, 0, (side + 1) * blk : (side + 2) * blk]
            )
            row = index >> row_bits
            plane = row // cy
            column = row - plane * cy
            inside = column < 4 if side == 0 else column >= cy - 4
            place = column if side == 0 else column - (cy - 8)
            keys = ((index >> 8) & (chunks // 2 - 1)) * (planes * 8) + plane * 8 + place
            keys = jnp.where(inside, keys, -1)
            accumulate(
                side_ref, base == 0 and side == 0, spread_values(values, index & 255, 256, 2),
                one_hot(keys, planes * 4 * chunks),
            )
    for q in range(chunks):
        part = acc_ref[q * rows : (q + 1) * rows, :]
        out_ref[:, 0:cy, q * 128 : (q + 1) * 128] = (part[:, :128] + part[:, 128:]).reshape(
            planes, cy, 128
        )
    both = jnp.transpose(side_ref[0:256, :] + side_ref[256:512, :])
    for q in range(chunks // 2):
        part = both[q * planes * 8 : (q + 1) * planes * 8, :]
        out_ref[:, cy : cy + 8, q * 256 : (q + 1) * 256] = part.reshape(planes, 8, 256)


def gather_press(n_gx, n_gy, wet_ref, index_ref, gram_ref, after_ref, out_ref, own_ref):
    planes, cy, cz = wet_ref.shape
    peers, blk = index_ref.shape
    rows = planes * cy
    chunks = cz // 256
    columns = []
    for q in range(chunks):
        part = wet_ref[:, :, q * 256 : (q + 1) * 256].reshape(rows, 256)
        columns.append(jnp.transpose(part))
    table_t = jnp.concatenate(pieces(jnp.concatenate(columns, axis=1), 2), axis=0)

    def write(base, row):
        for i in range(8):
            own_ref[base + i : base + i + 1, :] = row[:, i * blk : (i + 1) * blk]

    pick(table_t, index_ref, write, rows, 8, chunks.bit_length() - 1, 2)
    own = own_ref[...]
    number = lax.broadcasted_iota(jnp.int32, own.shape, 0)
    at_x, at_y = number // n_gy, number % n_gy
    for k, (dx, dy) in enumerate(NEAR):
        ok = (at_x + dx >= 0) & (at_x + dx < n_gx) & (at_y + dy >= 0) & (at_y + dy < n_gy)
        moved = pltpu.roll(own, (-(dx * n_gy + dy)) % peers, axis=0) if k else own
        out_ref[:, 0, k * blk : (k + 1) * blk] = jnp.where(ok, moved, 0.0)
    out_ref[:, 0, len(NEAR) * blk : (len(NEAR) + 1) * blk] = gram_ref[...]


def gram_rows(v_ref, out_ref, v, same, cross, wide, sems):
    hist, sx, sy = v_ref.shape
    tiles = sx // 8
    copy = starter(sems)
    copies = [
        copy(v_ref.at[:, pl.ds(8 * t, 8), :], v.at[t]) for t in range(tiles)
    ]
    for t in range(tiles):
        copies[t].wait()
        high, low = pieces(v[t].reshape(hist * 8, sy), 2)

        def dot(x, y):
            return lax.dot_general(x, y, (((1,), (1,)), ((), ())), preferred_element_type=F32)

        if t == 0:
            same[...] = dot(high, high) + dot(low, low)
            cross[...] = dot(high, low)
        else:
            same[...] += dot(high, high) + dot(low, low)
            cross[...] += dot(high, low)
    size = hist * 8
    row = lax.broadcasted_iota(jnp.int32, (size, size), 0)
    column = lax.broadcasted_iota(jnp.int32, (size, size), 1)
    match = (row & 7) == (column & 7)
    group = (
        lax.broadcasted_iota(jnp.int32, (size, 128), 0) // 8
        == lax.broadcasted_iota(jnp.int32, (size, 128), 1)
    ).astype(F32)

    def reduced(ref):
        part = jnp.sum(jnp.where(match, ref[...], 0.0).reshape(hist, 8, size), axis=1)
        return jnp.dot(part, group, precision=lax.Precision.HIGHEST, preferred_element_type=F32)

    wide[...] = jnp.zeros_like(wide)
    wide[0:hist, :] = reduced(cross)
    turned = jnp.transpose(wide[0:128, :])
    wide[0:128, :] = wide[0:128, :] + turned
    wide[0:hist, :] = wide[0:hist, :] + reduced(same)
    peers = out_ref.shape[0]
    if peers >= hist:
        out_ref[...] = wide[0:peers, :]
    else:
        out_ref[...] = wide[0:peers, :] + pltpu.roll(wide[peers : 2 * peers, :], 64, axis=1)


def shell(recv_ref, index_ref, disp_ref, stiff_ref, prev_ref, v_ref, up_ref, down_ref, low_ref,
          low_up_ref, low_down_ref, high_ref, resp_ref, late_ref, v, packs, acc, rows_acc, cols_acc,
          corner_acc, ext, dots, sems, v_sem):
    sx, sy = disp_ref.shape
    peers, blk = index_ref.shape
    extra = packs.shape[1]
    index_planes = extra - 2
    load_tiles = peers // 8
    chunks = sy // 128
    hist = v_ref.shape[0]
    v_copy = pltpu.make_async_copy(v_ref, v, v_sem.at[0])
    v_copy.start()
    copy = starter(sems)
    top = up_ref.shape[0] - extra
    corner = low_up_ref.shape[0] - extra
    low_planes = low_ref.shape[0] - (-(-extra // 4))
    copies = [
        copy(high_ref.at[pl.ds(0, extra)], packs.at[0]),
        copy(up_ref.at[pl.ds(top, extra)], packs.at[2]),
        copy(down_ref.at[pl.ds(top, extra)], packs.at[3]),
        copy(high_ref.at[pl.ds(extra, extra)], packs.at[4]),
        copy(high_ref.at[pl.ds(2 * extra, extra)], packs.at[5]),
        copy(low_up_ref.at[pl.ds(corner, extra)], packs.at[6]),
        copy(low_down_ref.at[pl.ds(corner, extra)], packs.at[7]),
    ]
    for e in range(extra):
        copies.append(
            copy(low_ref.at[low_planes + e // 4, pl.ds(8 * (e % 4), 8)], packs.at[1, e])
        )

    def accumulate(target, first, keys, height, lane, lanes, values):
        added = lax.dot_general(
            one_hot(keys, height), spread_values(values, lane, lanes, 2),
            (((1,), (1,)), ((), ())), preferred_element_type=F32,
        )
        if first:
            target[...] = added
        else:
            target[...] += added

    def values_of(k, base):
        return as_row(recv_ref[base : base + 8, 0, k * blk : (k + 1) * blk])

    for base in range(0, peers, 8):
        index = as_row(index_ref[base : base + 8, :])
        keys = ((index >> 7) & (chunks - 1)) * sx + index // sy
        accumulate(acc, base == 0, keys, sx * chunks, index & 127, 128, values_of(0, base))
    for made in copies:
        made.wait()
    for k, (dx, dy) in enumerate(NEAR):
        if k == 0:
            continue
        for base in range(0, peers, 8):
            number = load_tiles + base // 8
            index = as_row(tile_of(packs.at[k - 1], 0, number).astype(jnp.int32))
            row = index // sy
            lane = index & (sy - 1)
            if dx == 1:
                row8 = jnp.where(row < 4, row, -1)
            elif dx == -1:
                row8 = jnp.where(row >= sx - 4, row - (sx - 8), -1)
            if dy == 1:
                lane8 = jnp.where(lane < 4, lane, -1)
            elif dy == -1:
                lane8 = jnp.where(lane >= sy - 4, lane - (sy - 8), -1)
            values = values_of(k, base)
            if dy == 0:
                keys = jnp.where(row8 < 0, -1, (lane >> 7) * 8 + row8)
                accumulate(
                    rows_acc, k == 1 and base == 0, keys, 8 * chunks, lane & 127, 128, values
                )
            elif dx == 0:
                accumulate(cols_acc, k == 3 and base == 0, row, sx, lane8, 8, values)
            else:
                accumulate(corner_acc, k == 5 and base == 0, row8, 8, lane8, 8, values)

    ids = lax.broadcasted_iota(jnp.int32, (8, 128), 0)
    lanes = lax.broadcasted_iota(jnp.int32, (8, 128), 1)
    placed = (jnp.where(ids < 4, ids, ids + 120) == lanes).astype(F32)

    def widened(ref):
        both = ref[:, 0:8] + ref[:, 8:16]
        return jnp.dot(both, placed, precision=lax.Precision.HIGHEST, preferred_element_type=F32)

    force, disp, stiff = ext.at[0], ext.at[1], ext.at[2]
    for q in range(chunks):
        at = slice(q * 128, (q + 1) * 128)
        part = acc[q * sx : (q + 1) * sx, :]
        force[0:sx, at] = part[:, 0:128] + part[:, 128:256]
        part = rows_acc[q * 8 : (q + 1) * 8, :]
        force[sx : sx + 8, at] = part[:, 0:128] + part[:, 128:256]
    side = slice(sy, sy + 128)
    force[0:sx, side] = widened(cols_acc)
    force[sx : sx + 8, side] = widened(corner_acc)
    sub = lax.broadcasted_iota(jnp.int32, (8, sy), 0) < 4
    sub1 = lax.broadcasted_iota(jnp.int32, (8, 128), 0) < 4
    lane = lax.broadcasted_iota(jnp.int32, (sx, 128), 1)
    lane1 = lax.broadcasted_iota(jnp.int32, (8, 128), 1)
    for kind, (target, own) in enumerate(((disp, disp_ref), (stiff, stiff_ref))):

        def row_tile(pack, start, size):
            at = kind * sy + start
            return packs[pack, index_planes, :, at : at + size]

        def col_tile(pack):
            return jnp.concatenate(
                [tile_of(packs.at[pack], index_planes + 1, m) for m in range(sx // 8)], axis=0
            )

        target[0:sx, 0:sy] = own[...]
        target[sx : sx + 8, 0:sy] = jnp.where(sub, row_tile(0, 0, sy), row_tile(1, 0, sy))
        ahead, behind = col_tile(2), col_tile(3)
        if kind == 0:
            behind = pltpu.roll(behind, 64, axis=1)
        else:
            ahead = pltpu.roll(ahead, 64, axis=1)
        target[0:sx, side] = jnp.where(lane < 32, ahead, jnp.where(lane >= 96, behind, 0.0))

        def corner_tile(pack_ahead, pack_behind):
            return jnp.where(
                lane1 < 32, row_tile(pack_ahead, 0, 128),
                jnp.where(lane1 >= 96, row_tile(pack_behind, sy - 128, 128), 0.0),
            )

        target[sx : sx + 8, side] = jnp.where(sub1, corner_tile(4, 5), corner_tile(6, 7))

    load = force[...]
    k = stiff[...]
    diag = 1.0 + 4.0 * k
    scale = 0.8 / diag
    resp = disp[...]
    high, wide = sx + 8, sy + 128
    for sweep in range(SWEEPS):
        beside = (pltpu.roll(resp, 1, axis=0) + pltpu.roll(resp, high - 1, axis=0)) + (
            pltpu.roll(resp, 1, axis=1) + pltpu.roll(resp, wide - 1, axis=1)
        )
        resp = resp + scale * (load - (diag * resp - k * beside))
    own = resp[0:sx, 0:sy]
    resp_ref[...] = own
    resid = own - disp_ref[...]
    newest = resid - prev_ref[...]
    dots[...] = jnp.zeros_like(dots)

    def folded(value):
        total = value[0:8]
        for t in range(1, sx // 8):
            total = total + value[8 * t : 8 * t + 8]
        out = total[:, 0:128]
        for q in range(1, chunks):
            out = out + total[:, q * 128 : (q + 1) * 128]
        return jnp.sum(out, axis=0, keepdims=True)

    dots[0:1, :] = folded(newest * newest)
    dots[64:65, :] = folded(resid * newest)
    v_copy.wait()
    for number in range(1, hist):
        column = v[number]
        dots[number : number + 1, :] = folded(column * newest)
        dots[64 + number : 65 + number, :] = folded(column * resid)
    late = lax.dot_general(
        jnp.ones((8, 128), F32), dots[...], (((1,), (1,)), ((), ())),
        precision=lax.Precision.HIGHEST, preferred_element_type=F32,
    )
    gram_at = len(NEAR) * blk
    gram = jnp.sum(recv_ref[:, 0, gram_at : gram_at + 128], axis=0, keepdims=True)
    late_ref[:, 0, 0:128] = jnp.broadcast_to(late[0:1], (peers, 128))
    late_ref[:, 0, 128:256] = jnp.broadcast_to(gram, (peers, 128))


def solve(recv_ref, resp_ref, prev_ref, w_ref, out_ref, w, sems):
    peers = recv_ref.shape[0]
    hist = w_ref.shape[0]
    sx, sy = resp_ref.shape
    w_copy = pltpu.make_async_copy(w_ref, w, sems.at[0])
    w_copy.start()
    late = jnp.sum(recv_ref[:, 0, 0:128], axis=0, keepdims=True)
    rows = recv_ref[:, 0, 128:256]
    if peers >= hist:
        gram = rows[0:hist]
    else:
        gram = jnp.concatenate(
            [rows, pltpu.roll(rows, 64, axis=1)[0 : hist - peers]], axis=0
        )
    row = lax.broadcasted_iota(jnp.int32, (hist, 128), 0)
    lane = lax.broadcasted_iota(jnp.int32, (hist, 128), 1)
    turned = jnp.transpose(jnp.broadcast_to(late, (128, 128)))
    gram = jnp.where(row == 0, jnp.broadcast_to(late, (hist, 128)), gram)
    gram = jnp.where(lane == 0, turned[0:hist], gram)
    gram = jnp.where(lane < hist, gram, 0.0)
    unit = row == lane
    trace = jnp.sum(jnp.where(unit, gram, 0.0), keepdims=True)
    a = gram + jnp.where(unit, 0.001 * trace / hist, 0.0)
    a = jnp.where(lane == 64, -turned[64 : 64 + hist], a)
    for j in range(hist):
        column = jnp.broadcast_to(a[:, j : j + 1], (hist, 128))
        scaled = a[j : j + 1, :] / column[j : j + 1, :]
        a = jnp.where(row == j, scaled, a - column * scaled)
    coef = jnp.broadcast_to(a[:, 64:65], (hist, 128))
    coef = jnp.concatenate([coef] * (sy // 128), axis=1)
    resp = resp_ref[...]
    total = resp + coef[0:1] * (resp - prev_ref[...])
    w_copy.wait()
    for number in range(1, hist):
        total = total + coef[number : number + 1] * w[number]
    out_ref[...] = total


def pack(phi_ref, kappa_ref, after_ref, disp_ref, stiff_ref, cells_ref, loads_ref, up_ref, down_ref, low_ref,
         low_up_ref, low_down_ref, own_ref, phi_lo, kap_lo, phi_hi, kap_hi, up, down, own, last,
         in_sems, out_sems):
    cx, cy, cz = phi_ref.shape
    sx, sy = disp_ref.shape
    peers = cells_ref.shape[0]
    extra = own.shape[0]
    copy_in, copy_out = starter(in_sems), starter(out_sems)
    depth = 8
    lows = [
        copy_in(phi_ref.at[pl.ds(cx - 4, 4)], last.at[pl.ds(0, 4)]),
        copy_in(kappa_ref.at[pl.ds(cx - 3, 3)], last.at[pl.ds(4, 3)]),
    ]
    groups = []
    for x in range(0, cx, depth):
        at = pl.ds(x, depth)
        groups.append([
            copy_in(phi_ref.at[at, pl.ds(0, 8)], phi_lo.at[at]),
            copy_in(kappa_ref.at[at, pl.ds(0, 8)], kap_lo.at[at]),
            copy_in(phi_ref.at[at, pl.ds(cy - 8, 8)], phi_hi.at[at]),
            copy_in(kappa_ref.at[at, pl.ds(cy - 8, 8)], kap_hi.at[at]),
        ])
    outs = []
    for n in range(2 * peers // 8):
        source = cells_ref if n < peers // 8 else loads_ref
        base = 8 * (n % (peers // 8))
        own[n // 8, :, (n % 8) * 128 : (n % 8 + 1) * 128] = source[base : base + 8, :].astype(F32)
    if 2 * peers % 64:
        own[2 * peers // 64, :, 2 * peers % 64 * 16 :] = jnp.zeros(
            (8, 1024 - 2 * peers % 64 * 16), F32
        )
    sub = lax.broadcasted_iota(jnp.int32, (8, sy), 0) < 4
    for kind, ref in enumerate((disp_ref, stiff_ref)):
        own[extra - 2, :, kind * sy : (kind + 1) * sy] = jnp.where(
            sub, ref[0:8, :], ref[sx - 8 : sx, :]
        )
    lane = lax.broadcasted_iota(jnp.int32, (sx, 128), 1)
    first, final = slice(0, 128), slice(sy - 128, sy)
    columns = jnp.where(
        lane < 32, disp_ref[:, first],
        jnp.where(
            lane < 64, pltpu.roll(disp_ref[:, final], 64, axis=1),
            jnp.where(lane < 96, pltpu.roll(stiff_ref[:, first], 64, axis=1), stiff_ref[:, final]),
        ),
    )
    for m in range(sx // 8):
        own[extra - 1, :, m * 128 : (m + 1) * 128] = columns[8 * m : 8 * m + 8, :]
    outs += [
        copy_out(own, own_ref),
        copy_out(own, up_ref.at[pl.ds(cx, extra)]),
        copy_out(own, down_ref.at[pl.ds(cx, extra)]),
        copy_out(own, low_up_ref.at[pl.ds(4, extra)]),
        copy_out(own, low_down_ref.at[pl.ds(4, extra)]),
    ]
    for e in range(extra):
        outs.append(copy_out(own.at[e], low_ref.at[7 + e // 4, pl.ds(8 * (e % 4), 8)]))
    for made in lows:
        made.wait()
    outs.append(copy_out(last, low_ref.at[pl.ds(0, 7)]))
    upper = lax.broadcasted_iota(jnp.int32, (depth, 8, cz), 1) < 4
    for number, copies in enumerate(groups):
        for made in copies:
            made.wait()
        x = number * depth
        at = slice(x, x + depth)
        up[at] = jnp.where(upper, phi_lo[at], pltpu.roll(kap_lo[at], 4, axis=1))
        down[at] = jnp.where(upper, pltpu.roll(kap_hi[at], 4, axis=1), phi_hi[at])
        at = pl.ds(x, depth)
        outs.append(copy_out(up.at[at], up_ref.at[at]))
        outs.append(copy_out(down.at[at], down_ref.at[at]))
    at = pl.ds(cx - 4, 4)
    outs.append(copy_out(up.at[at], low_up_ref.at[pl.ds(0, 4)]))
    outs.append(copy_out(down.at[at], low_down_ref.at[pl.ds(0, 4)]))
    for made in outs:
        made.wait()


def packed(phi, kappa, after, displacement, stiffness, cells, loads):
    cx, cy, cz = phi.shape
    peers = cells.shape[0]
    extra = -(-2 * peers // 64) + 2

    def shape(planes, rows=8):
        return jax.ShapeDtypeStruct((planes, rows, cz), F32)

    return pl.pallas_call(
        pack,
        in_specs=hbm_specs(3) + vmem_specs(4),
        out_specs=hbm_specs(6),
        out_shape=[
            shape(cx + extra), shape(cx + extra), shape(7 + -(-extra // 4), cy),
            shape(4 + extra), shape(4 + extra), shape(extra),
        ],
        scratch_shapes=[pltpu.VMEM((cx, 8, cz), F32)] * 6
        + [
            pltpu.VMEM((extra, 8, cz), F32),
            pltpu.VMEM((7, cy, cz), F32),
            pltpu.SemaphoreType.DMA((cx // 2 + 2,)),
            pltpu.SemaphoreType.DMA((32,)),
        ],
        compiler_params=params(),
        name="pack",
    )(phi, kappa, after, displacement, stiffness, cells, loads)


def substep(src, kap, dst, plane, advect, cy, cz):
    wide = cy + 8
    chunks = cz // 128
    lane = lax.broadcasted_iota(jnp.int32, (wide, 128), 1)
    first, last = lane == 0, lane == 127

    def take(ref, at, q):
        return ref[at, :, q * 128 : (q + 1) * 128]

    for q in range(chunks):
        now = take(src, plane, q)
        left = take(src, plane, q - 1) if q else 0.0
        right = take(src, plane, q + 1) if q + 1 < chunks else 0.0
        total = pltpu.roll(jnp.where(last, left, now), 1, axis=1) + pltpu.roll(
            jnp.where(first, right, now), 127, axis=1
        )
        total = total + (pltpu.roll(now, 1, axis=0) + pltpu.roll(now, wide - 1, axis=0))
        before = take(src, plane - 1, q)
        total = total + (before + take(src, plane + 1, q))
        dst[plane, :, q * 128 : (q + 1) * 128] = (
            now + advect * (before - now) + take(kap, plane - 1, q) * (total - 6.0 * now)
        )


def fluid(x0, x1, cx, cy, cz, kind, *refs):
    planes = x1 - x0 + 8
    names = ["phi", "kappa", "up", "down"]
    names += {"wet": ["forced", "low", "low_up", "low_down"], "middle": ["forced", "wet"],
              "end": ["high", "whole"]}[kind]
    names += {"wet": ["out", "send"]}.get(kind, ["out"])
    names += ["a", "b", "kap", "upb", "downb", "sems", "out_sems"]
    r = dict(zip(names, refs))
    a, b, kap, upb, downb = r["a"], r["b"], r["kap"], r["upb"], r["downb"]
    is_last = lax.axis_index("gx") == lax.axis_size("gx") - 1
    copy, copy_out = starter(r["sems"]), starter(r["out_sems"])

    own0, own1 = max(0, x0 - 4), min(cx, x1 + 4)
    groups = []
    if kind == "wet":
        groups.append((0, 4, [
            copy(r["low"].at[pl.ds(0, 4)], a.at[pl.ds(0, 4), pl.ds(0, cy)]),
            copy(r["low"].at[pl.ds(4, 3)], kap.at[pl.ds(0, 3), pl.ds(0, cy)]),
            copy(r["low_up"].at[pl.ds(0, 4)], upb.at[pl.ds(0, 4)]),
            copy(r["low_down"].at[pl.ds(0, 4)], downb.at[pl.ds(0, 4)]),
        ]))
    for start in range(own0, own1, 4):
        i = start - (x0 - 4)
        k0, k1 = max(start, x0 - 3), min(start + 4, x1 + 3)
        groups.append((i, i + 4, [
            copy(r["phi"].at[pl.ds(start, 4)], a.at[pl.ds(i, 4), pl.ds(0, cy)]),
            copy(r["up"].at[pl.ds(start, 4)], upb.at[pl.ds(i, 4)]),
            copy(r["down"].at[pl.ds(start, 4)], downb.at[pl.ds(i, 4)]),
            copy(r["kappa"].at[pl.ds(k0, k1 - k0)],
                 kap.at[pl.ds(k0 - (x0 - 3), k1 - k0), pl.ds(0, cy)]),
        ]))
    if kind == "end":
        i = cx - (x0 - 4)
        groups.append((i, i + 4, [
            copy(r["high"].at[pl.ds(0, 4)], a.at[pl.ds(i, 4)]),
            copy(r["high"].at[pl.ds(4, 3)], kap.at[pl.ds(i - 1, 3)]),
        ]))
    outs = []
    if kind == "middle":
        outs.append(copy_out(r["wet"], r["out"].at[pl.ds(0, x0)]))

    upper = lax.broadcasted_iota(jnp.int32, (8, cz), 0) < 4

    def assemble(i0, i1):
        for i in range(i0, i1):
            x = x0 - 4 + i
            if x >= cx:
                continue
            up, down = upb[i], downb[i]
            a[i, cy : cy + 8, :] = jnp.where(upper, up, down)
            if 1 <= i < planes - 1:
                kap[i - 1, cy : cy + 8, :] = pltpu.roll(jnp.where(upper, down, up), 4, axis=0)
            if "forced" in r and 0 <= x < r["forced"].shape[0]:
                a[i] = a[i] + r["forced"][x]

    def run(src, dst, lo, hi):
        def body(i, carry):
            advect = 0.25
            if kind == "end":
                outside = jnp.logical_and(is_last, i + (x0 - 4) >= cx)
                advect = jnp.where(outside, 0.0, 0.25)
            substep(src, kap, dst, i, advect, cy, cz)
            return carry

        lax.fori_loop(lo, hi, body, 0)

    done = 1
    for i0, i1, copies in groups:
        for made in copies:
            made.wait()
        assemble(i0, i1)
        if kind == "wet" and i0 == 4:
            outs.append(copy_out(a.at[pl.ds(4, 4)], r["send"].at[pl.ds(0, 4)]))
            outs.append(copy_out(kap.at[pl.ds(3, 3)], r["send"].at[pl.ds(4, 3)]))
        ready = i1 - 1
        if ready > done:
            run(a, b, done, ready)
            done = ready
    if kind == "wet":
        for made in outs:
            made.wait()
        outs = []
    run(b, a, 2, planes - 2)
    run(a, b, 3, planes - 3)
    for start in range(4, planes - 4, 4):
        run(b, a, start, start + 4)
        if kind == "wet":
            for i in range(start, start + 4):
                r["out"][i - 4] = a[i, 0:cy, :]
        else:
            x = x0 + start - 4
            outs.append(
                copy_out(a.at[pl.ds(start, 4), pl.ds(0, cy)], r["out"].at[pl.ds(x, 4)])
            )
    for made in outs:
        made.wait()


def fluid_call(kind, x0, x1, phi, kappa, up, down, *more):
    cx, cy, cz = phi.shape
    planes = x1 - x0 + 8
    field = jax.ShapeDtypeStruct((cx, cy, cz), F32)
    whole = hbm_specs(1)[0]
    if kind == "wet":
        specs = vmem_specs(1) + hbm_specs(3)
        out_shape = [
            jax.ShapeDtypeStruct((x1 - x0, cy, cz), F32),
            jax.ShapeDtypeStruct((7, cy + 8, cz), F32),
        ]
        out_specs = vmem_specs(1) + hbm_specs(1)
    elif kind == "middle":
        specs, out_shape, out_specs = vmem_specs(2), field, whole
    else:
        specs, out_shape, out_specs = hbm_specs(2), field, whole
    cells = planes * (cy + 8) * cz
    return pl.pallas_call(
        functools.partial(fluid, x0, x1, cx, cy, cz, kind),
        in_specs=hbm_specs(4) + specs,
        out_specs=out_specs,
        out_shape=out_shape,
        scratch_shapes=[
            pltpu.VMEM((planes, cy + 8, cz), F32),
            pltpu.VMEM((planes, cy + 8, cz), F32),
            pltpu.VMEM((planes - 2, cy + 8, cz), F32),
            pltpu.VMEM((planes, 8, cz), F32),
            pltpu.VMEM((planes, 8, cz), F32),
            pltpu.SemaphoreType.DMA((48,)),
            pltpu.SemaphoreType.DMA((12,)),
        ],
        input_output_aliases={5: 0} if kind == "end" else {},
        compiler_params=params(),
        cost_estimate=pl.CostEstimate(
            flops=48 * cells, bytes_accessed=12 * cells, transcendentals=0
        ),
        name="fluid_" + kind,
    )(phi, kappa, up, down, *more)


def shifted_pairs(n_gx, n_gy, dx, dy):
    pairs = []
    for gx in range(n_gx):
        for gy in range(n_gy):
            tx, ty = gx + dx, gy + dy
            if 0 <= tx < n_gx and 0 <= ty < n_gy:
                pairs.append((gx * n_gy + gy, tx * n_gy + ty))
    return pairs


def local(phi, kappa, stiffness, face_cell, load_dof, displacement, v_hist, w_hist, r_prev, w_prev):
    n_gx, n_gy = lax.axis_size("gx"), lax.axis_size("gy")
    peers, blk = face_cell.shape[2:]
    cx, cy, cz = phi.shape
    sx, sy = displacement.shape
    hist = v_hist.shape[0]
    wet_planes = cx // 8
    fcell = face_cell.reshape(peers, blk)
    ldof = load_dof.reshape(peers, blk)
    axes = ("gx", "gy")

    def shift(value, dx, dy):
        return lax.ppermute(value, axes, shifted_pairs(n_gx, n_gy, dx, dy))

    def exchange(value):
        return lax.all_to_all(value, axes, split_axis=0, concat_axis=0, tiled=True)

    def call(body, out_shape, scratch, name, specs, *args):
        several = isinstance(out_shape, list)
        return pl.pallas_call(
            body,
            in_specs=specs,
            out_specs=vmem_specs(len(out_shape)) if several else vmem_specs(1)[0],
            out_shape=out_shape,
            scratch_shapes=scratch,
            compiler_params=params(),
            name=name,
        )(*args)

    def f32(*shape):
        return jax.ShapeDtypeStruct(shape, F32)

    sent = call(
        functools.partial(gather_disp, n_gy), f32(peers, 1, 3 * blk),
        [pltpu.VMEM((peers, blk), F32)], "gather_disp", vmem_specs(2), displacement, ldof,
    )
    disp = exchange(sent)
    up_send, down_send, low_send, low_up_send, low_down_send, own = packed(
        phi, kappa, disp, displacement, stiffness, fcell, ldof
    )
    extra = own.shape[0]
    low = shift(low_send, 1, 0)
    up = shift(up_send, 0, -1)
    down = shift(down_send, 0, 1)
    low_up = shift(low_up_send, 1, -1)
    low_down = shift(low_down_send, 1, 1)
    near = shift(jnp.concatenate([own, up[cx:], down[cx:]], axis=0), -1, 0)

    chunks = cz // 128
    forced = call(
        functools.partial(scatter_disp, cx, cy, cz), f32(wet_planes, cy + 8, cz),
        [
            pltpu.VMEM((wet_planes * cy * chunks, 256), F32),
            pltpu.VMEM((512, wet_planes * 4 * chunks), F32),
            pltpu.VMEM((2, (extra - 2) // 2 + (extra - 2) % 2, 8, cz), F32),
            pltpu.SemaphoreType.DMA((2,)),
        ],
        "scatter_disp", vmem_specs(2) + hbm_specs(2), disp, fcell, up, down,
    )
    wet, send = fluid_call(
        "wet", 0, wet_planes, phi, kappa, up, down, forced, low, low_up, low_down
    )
    high = shift(send, -1, 0)
    middle = fluid_call("middle", wet_planes, cx - 4, phi, kappa, up, down, forced, wet)
    field = fluid_call("end", cx - 4, cx, phi, kappa, up, down, high, middle)
    size = 8 * hist
    gram = call(
        gram_rows, f32(peers, 128),
        [
            pltpu.VMEM((sx // 8, hist, 8, sy), F32), pltpu.VMEM((size, size), F32),
            pltpu.VMEM((size, size), F32),
            pltpu.VMEM((max(128, peers, 2 * peers if peers < hist else 0), 128), F32),
            pltpu.SemaphoreType.DMA((sx // 8,)),
        ],
        "gram_rows", hbm_specs(1), v_hist,
    )
    press = call(
        functools.partial(gather_press, n_gx, n_gy), f32(peers, 1, (len(NEAR) + 1) * blk),
        [pltpu.VMEM((peers, blk), F32)], "gather_press", vmem_specs(3) + hbm_specs(1),
        wet, fcell, gram, middle,
    )
    loads = exchange(press)
    resp, late = call(
        shell, [f32(sx, sy), f32(peers, 1, 256)],
        [
            pltpu.VMEM((hist, sx, sy), F32),
            pltpu.VMEM((8, extra, 8, cz), F32),
            pltpu.VMEM((sx * (sy // 128), 256), F32),
            pltpu.VMEM((8 * (sy // 128), 256), F32),
            pltpu.VMEM((sx, 16), F32),
            pltpu.VMEM((8, 16), F32),
            pltpu.VMEM((3, sx + 8, sy + 128), F32),
            pltpu.VMEM((128, 128), F32),
            pltpu.SemaphoreType.DMA((7 + extra,)),
            pltpu.SemaphoreType.DMA((1,)),
        ],
        "shell", vmem_specs(5) + hbm_specs(7),
        loads, ldof, displacement, stiffness, r_prev, v_hist, up, down, low, low_up, low_down, near,
    )
    x_next = call(
        solve, f32(sx, sy),
        [pltpu.VMEM((hist, sx, sy), F32), pltpu.SemaphoreType.DMA((1,))],
        "solve", vmem_specs(3) + hbm_specs(1), exchange(late), resp, w_prev, w_hist,
    )
    return (field, x_next)


def solution(mesh):
    in_specs = (
        P("gx", "gy", None),
        P("gx", "gy", None),
        P("gx", "gy"),
        P("gx", "gy", None, None),
        P("gx", "gy", None, None),
        P("gx", "gy"),
        P(None, "gx", "gy"),
        P(None, "gx", "gy"),
        P("gx", "gy"),
        P("gx", "gy"),
    )
    out_specs = (P("gx", "gy", None), P("gx", "gy"))
    return jax.shard_map(local, mesh=mesh, in_specs=in_specs, out_specs=out_specs, check_vma=False)
```

```python
import functools

import jax
import jax.numpy as jnp
from jax import lax
from jax.experimental import pallas as pl
from jax.experimental.pallas import tpu as pltpu
from jax.sharding import PartitionSpec as P

NSUB = 4
SWEEPS = 3
HIST = 40
VMEM_BYTES = 32 * 1024 * 1024
F32 = jnp.float32
BF16 = jnp.bfloat16


def params():
    return pltpu.CompilerParams(vmem_limit_bytes=VMEM_BYTES)


def vmem_specs(count):
    return [pl.BlockSpec(memory_space=pltpu.VMEM)] * count


def any_specs(count):
    return [pl.BlockSpec(memory_space=pl.ANY)] * count


def hbm_specs(count):
    return [pl.BlockSpec(memory_space=pltpu.HBM)] * count


def pieces(value, count):
    parts = []
    for _ in range(count):
        part = value.astype(BF16)
        parts.append(part)
        value = value - part.astype(F32)
    return parts


def as_row(block):
    return jnp.concatenate([block[i : i + 1] for i in range(block.shape[0])], axis=1)


def both_rows(row):
    return jnp.broadcast_to(row, (16, row.shape[1])).astype(BF16)


def matches(keys, rows):
    ids = lax.broadcasted_iota(jnp.int32, (16, keys.shape[1]), 0).astype(F32).astype(BF16)
    found = []
    for base in range(0, rows, 256):
        key = both_rows((keys - base).astype(F32))
        for start in range(0, min(256, rows - base), 16):
            found.append(key == ids + jnp.bfloat16(start))
    return found


def one_hot(keys, rows):
    one, zero = jnp.bfloat16(1), jnp.bfloat16(0)
    return jnp.concatenate([jnp.where(m, one, zero) for m in matches(keys, rows)], axis=0)


def select_sum(table, lane, group, rows, parts):
    total = table[:rows]
    for part in range(1, parts):
        total = total + table[part * rows : (part + 1) * rows]
    ids = lax.broadcasted_iota(jnp.int32, total.shape, 0)
    return jnp.sum(jnp.where(ids == lane, total, 0.0), axis=0, keepdims=True)


def pick(table_t, index_ref, out_rows, rows, lane_bits, chunk_bits, parts, step=8):
    lanes = 1 << lane_bits
    for base in range(0, index_ref.shape[0], step):
        index = as_row(index_ref[base : base + step, :])
        lane = index & (lanes - 1)
        keys = ((index >> lane_bits) & ((1 << chunk_bits) - 1)) * rows + (
            index >> (lane_bits + chunk_bits)
        )
        hot = one_hot(keys, rows << chunk_bits)
        found = lax.dot_general(
            table_t, hot, (((1,), (0,)), ((), ())), preferred_element_type=F32
        )
        out_rows(base, select_sum(found, lane, step, lanes, parts))


def spread_values(values, lane, lanes, parts):
    zero = jnp.bfloat16(0)
    found = matches(lane, lanes)
    spread = []
    for part in pieces(values, parts):
        part = both_rows(part.astype(F32))
        spread += [jnp.where(m, part, zero) for m in found]
    return jnp.concatenate(spread, axis=0)


NEAR = ((0, 0), (1, 0), (-1, 0), (0, 1), (0, -1), (1, 1), (1, -1), (-1, 1), (-1, -1))


def tile_of(ref, plane, number):
    at = (number % 8) * 128
    return ref[plane + number // 8, :, at : at + 128]


def starter(sems):
    used = [0]

    def copy(src, dst):
        made = pltpu.make_async_copy(src, dst, sems.at[used[0]])
        used[0] += 1
        made.start()
        return made

    return copy


def gather_disp(n_gy, disp_ref, index_ref, out_ref, own_ref):
    sx, sy = disp_ref.shape
    peers, blk = index_ref.shape
    chunk_bits = (sy // 128).bit_length() - 1
    columns = []
    for q in range(sy // 128):
        columns.append(jnp.transpose(disp_ref[:, q * 128 : (q + 1) * 128]))
    table_t = jnp.concatenate(pieces(jnp.concatenate(columns, axis=1), 3), axis=0)

    def write(base, row):
        for i in range(8):
            own_ref[base + i : base + i + 1, :] = row[:, i * blk : (i + 1) * blk]

    pick(table_t, index_ref, write, sx, 7, chunk_bits, 3)
    own = own_ref[...]
    beside = lax.broadcasted_iota(jnp.int32, own.shape, 0) % n_gy
    out_ref[:, 0, 0:blk] = own
    out_ref[:, 0, blk : 2 * blk] = jnp.where(
        beside == n_gy - 1, 0.0, pltpu.roll(own, peers - 1, axis=0)
    )
    out_ref[:, 0, 2 * blk : 3 * blk] = jnp.where(beside == 0, 0.0, pltpu.roll(own, 1, axis=0))


def scatter_disp(cx, cy, cz, disp_ref, cells_ref, up_ref, down_ref, out_ref, acc_ref, side_ref):
    planes = out_ref.shape[0]
    peers, blk = cells_ref.shape
    rows = planes * cy
    chunks = cz // 128
    row_bits = cz.bit_length() - 1
    step = 8
    def accumulate(target, first, left, right):
        added = lax.dot_general(
            left, right, (((1,), (1,)), ((), ())), preferred_element_type=F32
        )
        if first:
            target[...] = added
        else:
            target[...] += added

    for base in range(0, peers, step):
        index = as_row(cells_ref[base : base + step, :])
        values = 0.5 * as_row(disp_ref[base : base + step, 0, 0:blk])
        keys = ((index >> 7) & (chunks - 1)) * rows + (index >> row_bits)
        accumulate(
            acc_ref, base == 0, one_hot(keys, rows * chunks),
            spread_values(values, index & 127, 128, 2),
        )
    for base in range(0, peers, step):
        for side in range(2):
            index = as_row(tile_of(up_ref if side == 0 else down_ref, cx, base // step).astype(jnp.int32))
            values = 0.5 * as_row(
                disp_ref[base : base + step, 0, (side + 1) * blk : (side + 2) * blk]
            )
            row = index >> row_bits
            plane = row // cy
            column = row - plane * cy
            inside = column < 4 if side == 0 else column >= cy - 4
            place = column if side == 0 else column - (cy - 8)
            keys = ((index >> 8) & (chunks // 2 - 1)) * (planes * 8) + plane * 8 + place
            keys = jnp.where(inside, keys, -1)
            accumulate(
                side_ref, base == 0 and side == 0, spread_values(values, index & 255, 256, 2),
                one_hot(keys, planes * 4 * chunks),
            )
    for q in range(chunks):
        part = acc_ref[q * rows : (q + 1) * rows, :]
        out_ref[:, 0:cy, q * 128 : (q + 1) * 128] = (part[:, :128] + part[:, 128:]).reshape(
            planes, cy, 128
        )
    both = jnp.transpose(side_ref[0:256, :] + side_ref[256:512, :])
    for q in range(chunks // 2):
        part = both[q * planes * 8 : (q + 1) * planes * 8, :]
        out_ref[:, cy : cy + 8, q * 256 : (q + 1) * 256] = part.reshape(planes, 8, 256)


def gather_press(n_gx, n_gy, wet_ref, index_ref, gram_ref, after_ref, out_ref, own_ref):
    planes, cy, cz = wet_ref.shape
    peers, blk = index_ref.shape
    rows = planes * cy
    chunks = cz // 256
    columns = []
    for q in range(chunks):
        part = wet_ref[:, :, q * 256 : (q + 1) * 256].reshape(rows, 256)
        columns.append(jnp.transpose(part))
    table_t = jnp.concatenate(pieces(jnp.concatenate(columns, axis=1), 2), axis=0)

    def write(base, row):
        for i in range(8):
            own_ref[base + i : base + i + 1, :] = row[:, i * blk : (i + 1) * blk]

    pick(table_t, index_ref, write, rows, 8, chunks.bit_length() - 1, 2)
    own = own_ref[...]
    number = lax.broadcasted_iota(jnp.int32, own.shape, 0)
    at_x, at_y = number // n_gy, number % n_gy
    for k, (dx, dy) in enumerate(NEAR):
        ok = (at_x + dx >= 0) & (at_x + dx < n_gx) & (at_y + dy >= 0) & (at_y + dy < n_gy)
        moved = pltpu.roll(own, (-(dx * n_gy + dy)) % peers, axis=0) if k else own
        out_ref[:, 0, k * blk : (k + 1) * blk] = jnp.where(ok, moved, 0.0)
    out_ref[:, 0, len(NEAR) * blk : (len(NEAR) + 1) * blk] = gram_ref[...]


def gram_rows(v_ref, out_ref, v, same, cross, wide, sems):
    hist, sx, sy = v_ref.shape
    tiles = sx // 8
    copy = starter(sems)
    copies = [
        copy(v_ref.at[:, pl.ds(8 * t, 8), :], v.at[t]) for t in range(tiles)
    ]
    for t in range(tiles):
        copies[t].wait()
        high, low = pieces(v[t].reshape(hist * 8, sy), 2)

        def dot(x, y):
            return lax.dot_general(x, y, (((1,), (1,)), ((), ())), preferred_element_type=F32)

        if t == 0:
            same[...] = dot(high, high) + dot(low, low)
            cross[...] = dot(high, low)
        else:
            same[...] += dot(high, high) + dot(low, low)
            cross[...] += dot(high, low)
    size = hist * 8
    row = lax.broadcasted_iota(jnp.int32, (size, size), 0)
    column = lax.broadcasted_iota(jnp.int32, (size, size), 1)
    match = (row & 7) == (column & 7)
    group = (
        lax.broadcasted_iota(jnp.int32, (size, 128), 0) // 8
        == lax.broadcasted_iota(jnp.int32, (size, 128), 1)
    ).astype(F32)

    def reduced(ref):
        part = jnp.sum(jnp.where(match, ref[...], 0.0).reshape(hist, 8, size), axis=1)
        return jnp.dot(part, group, precision=lax.Precision.HIGHEST, preferred_element_type=F32)

    wide[...] = jnp.zeros_like(wide)
    wide[0:hist, :] = reduced(cross)
    turned = jnp.transpose(wide[0:128, :])
    wide[0:128, :] = wide[0:128, :] + turned
    wide[0:hist, :] = wide[0:hist, :] + reduced(same)
    peers = out_ref.shape[0]
    if peers >= hist:
        out_ref[...] = wide[0:peers, :]
    else:
        out_ref[...] = wide[0:peers, :] + pltpu.roll(wide[peers : 2 * peers, :], 64, axis=1)


def shell(recv_ref, index_ref, disp_ref, stiff_ref, prev_ref, up_ref, down_ref, low_ref,
          low_up_ref, low_down_ref, high_ref, v_ref, after_ref, resp_ref, late_ref, v, acc, rows_acc,
          cols_acc, corner_acc, ext, dots, v_sem):
    sx, sy = disp_ref.shape
    peers, blk = index_ref.shape
    load_tiles = peers // 8
    index_planes = -(-2 * load_tiles // 8)
    corner_planes = -(-(load_tiles + 4) // 8)
    chunks = sy // 128
    hist = v_ref.shape[0]
    v_copy = pltpu.make_async_copy(v_ref, v, v_sem.at[0])
    v_copy.start()
    top = up_ref.shape[0] - (index_planes + 2 + corner_planes)
    low_top = low_ref.shape[0] - (index_planes + 1)
    corner_top = low_up_ref.shape[0] - corner_planes
    near_top = index_planes + 1
    load_at = [
        (high_ref, 0, load_tiles), (low_ref, low_top, load_tiles), (up_ref, top, load_tiles),
        (down_ref, top, load_tiles), (high_ref, near_top, 0),
        (high_ref, near_top + corner_planes, 0), (low_up_ref, corner_top, 0),
        (low_down_ref, corner_top, 0),
    ]

    def accumulate(target, first, keys, height, lane, lanes, values):
        added = lax.dot_general(
            one_hot(keys, height), spread_values(values, lane, lanes, 2),
            (((1,), (1,)), ((), ())), preferred_element_type=F32,
        )
        if first:
            target[...] = added
        else:
            target[...] += added

    def values_of(k, base):
        return as_row(recv_ref[base : base + 8, 0, k * blk : (k + 1) * blk])

    for base in range(0, peers, 8):
        index = as_row(index_ref[base : base + 8, :])
        keys = ((index >> 7) & (chunks - 1)) * sx + index // sy
        accumulate(acc, base == 0, keys, sx * chunks, index & 127, 128, values_of(0, base))
    for k, (dx, dy) in enumerate(NEAR):
        if k == 0:
            continue
        for base in range(0, peers, 8):
            ref, plane, number = load_at[k - 1]
            index = as_row(tile_of(ref, plane, number + base // 8).astype(jnp.int32))
            row = index // sy
            lane = index & (sy - 1)
            if dx == 1:
                row8 = jnp.where(row < 4, row, -1)
            elif dx == -1:
                row8 = jnp.where(row >= sx - 4, row - (sx - 8), -1)
            if dy == 1:
                lane8 = jnp.where(lane < 4, lane, -1)
            elif dy == -1:
                lane8 = jnp.where(lane >= sy - 4, lane - (sy - 8), -1)
            values = values_of(k, base)
            if dy == 0:
                keys = jnp.where(row8 < 0, -1, (lane >> 7) * 8 + row8)
                accumulate(
                    rows_acc, k == 1 and base == 0, keys, 8 * chunks, lane & 127, 128, values
                )
            elif dx == 0:
                accumulate(cols_acc, k == 3 and base == 0, row, sx, lane8, 16, values)
            else:
                accumulate(corner_acc, k == 5 and base == 0, row8, 16, lane8, 16, values)

    ids = lax.broadcasted_iota(jnp.int32, (16, 128), 0)
    lanes = lax.broadcasted_iota(jnp.int32, (16, 128), 1)
    placed = (jnp.where(ids < 4, ids, jnp.where(ids < 8, ids + 120, -1)) == lanes).astype(F32)

    def widened(ref):
        both = ref[:, 0:16] + ref[:, 16:32]
        return jnp.dot(both, placed, precision=lax.Precision.HIGHEST, preferred_element_type=F32)

    force, disp, stiff = ext.at[0], ext.at[1], ext.at[2]
    for q in range(chunks):
        at = slice(q * 128, (q + 1) * 128)
        part = acc[q * sx : (q + 1) * sx, :]
        force[0:sx, at] = part[:, 0:128] + part[:, 128:256]
        part = rows_acc[q * 8 : (q + 1) * 8, :]
        force[sx : sx + 8, at] = part[:, 0:128] + part[:, 128:256]
    side = slice(sy, sy + 128)
    force[0:sx, side] = widened(cols_acc)
    force[sx : sx + 8, side] = widened(corner_acc)[0:8]
    sub = lax.broadcasted_iota(jnp.int32, (8, sy), 0) < 4
    sub1 = lax.broadcasted_iota(jnp.int32, (8, 128), 0) < 4
    lane = lax.broadcasted_iota(jnp.int32, (sx, 128), 1)
    lane1 = lax.broadcasted_iota(jnp.int32, (8, 128), 1)
    for kind, (target, own) in enumerate(((disp, disp_ref), (stiff, stiff_ref))):

        def row_tile(ref, plane):
            return ref[plane, :, kind * sy : (kind + 1) * sy]

        def col_tile(ref):
            plane = top + index_planes + 1
            return jnp.concatenate([tile_of(ref, plane, m) for m in range(sx // 8)], axis=0)

        target[0:sx, 0:sy] = own[...]
        target[sx : sx + 8, 0:sy] = jnp.where(
            sub, row_tile(high_ref, index_planes), row_tile(low_ref, low_top + index_planes)
        )
        ahead, behind = col_tile(up_ref), col_tile(down_ref)
        if kind == 0:
            behind = pltpu.roll(behind, 64, axis=1)
        else:
            ahead = pltpu.roll(ahead, 64, axis=1)
        target[0:sx, side] = jnp.where(lane < 32, ahead, jnp.where(lane >= 96, behind, 0.0))

        def corner_tile(ahead, ahead_plane, behind, behind_plane):
            number = load_tiles + 2 * kind
            return jnp.where(
                lane1 < 32, tile_of(ahead, ahead_plane, number),
                jnp.where(lane1 >= 96, tile_of(behind, behind_plane, number + 1), 0.0),
            )

        target[sx : sx + 8, side] = jnp.where(
            sub1, corner_tile(high_ref, near_top, high_ref, near_top + corner_planes),
            corner_tile(low_up_ref, corner_top, low_down_ref, corner_top),
        )

    load = force[...]
    k = stiff[...]
    diag = 1.0 + 4.0 * k
    scale = 0.8 / diag
    resp = disp[...]
    high, wide = sx + 8, sy + 128
    for sweep in range(SWEEPS):
        beside = (pltpu.roll(resp, 1, axis=0) + pltpu.roll(resp, high - 1, axis=0)) + (
            pltpu.roll(resp, 1, axis=1) + pltpu.roll(resp, wide - 1, axis=1)
        )
        resp = resp + scale * (load - (diag * resp - k * beside))
    own = resp[0:sx, 0:sy]
    resp_ref[...] = own
    resid = own - disp_ref[...]
    newest = resid - prev_ref[...]
    dots[...] = jnp.zeros_like(dots)

    def folded(value):
        total = value[0:8]
        for t in range(1, sx // 8):
            total = total + value[8 * t : 8 * t + 8]
        out = total[:, 0:128]
        for q in range(1, chunks):
            out = out + total[:, q * 128 : (q + 1) * 128]
        return jnp.sum(out, axis=0, keepdims=True)

    dots[0:1, :] = folded(newest * newest)
    dots[64:65, :] = folded(resid * newest)
    v_copy.wait()
    for number in range(1, hist):
        column = v[number]
        dots[number : number + 1, :] = folded(column * newest)
        dots[64 + number : 65 + number, :] = folded(column * resid)
    late = lax.dot_general(
        jnp.ones((8, 128), F32), dots[...], (((1,), (1,)), ((), ())),
        precision=lax.Precision.HIGHEST, preferred_element_type=F32,
    )
    gram_at = len(NEAR) * blk
    gram = jnp.sum(recv_ref[:, 0, gram_at : gram_at + 128], axis=0, keepdims=True)
    late_ref[:, 0, 0:128] = jnp.broadcast_to(late[0:1], (peers, 128))
    late_ref[:, 0, 128:256] = jnp.broadcast_to(gram, (peers, 128))


def solve(recv_ref, resp_ref, prev_ref, w_ref, out_ref, w, sems):
    peers = recv_ref.shape[0]
    hist = w_ref.shape[0]
    sx, sy = resp_ref.shape
    w_copy = pltpu.make_async_copy(w_ref, w, sems.at[0])
    w_copy.start()
    late = jnp.sum(recv_ref[:, 0, 0:128], axis=0, keepdims=True)
    rows = recv_ref[:, 0, 128:256]
    if peers >= hist:
        gram = rows[0:hist]
    else:
        gram = jnp.concatenate(
            [rows, pltpu.roll(rows, 64, axis=1)[0 : hist - peers]], axis=0
        )
    row = lax.broadcasted_iota(jnp.int32, (hist, 128), 0)
    lane = lax.broadcasted_iota(jnp.int32, (hist, 128), 1)
    turned = jnp.transpose(jnp.broadcast_to(late, (128, 128)))
    gram = jnp.where(row == 0, jnp.broadcast_to(late, (hist, 128)), gram)
    gram = jnp.where(lane == 0, turned[0:hist], gram)
    gram = jnp.where(lane < hist, gram, 0.0)
    unit = row == lane
    trace = jnp.sum(jnp.where(unit, gram, 0.0), keepdims=True)
    a = gram + jnp.where(unit, 0.001 * trace / hist, 0.0)
    a = jnp.where(lane == 64, -turned[64 : 64 + hist], a)
    for j in range(hist):
        column = jnp.broadcast_to(a[:, j : j + 1], (hist, 128))
        scaled = a[j : j + 1, :] / column[j : j + 1, :]
        a = jnp.where(row == j, scaled, a - column * scaled)
    coef = jnp.broadcast_to(a[:, 64:65], (hist, 128))
    coef = jnp.concatenate([coef] * (sy // 128), axis=1)
    resp = resp_ref[...]
    total = resp + coef[0:1] * (resp - prev_ref[...])
    w_copy.wait()
    for number in range(1, hist):
        total = total + coef[number : number + 1] * w[number]
    out_ref[...] = total


def pack(phi_ref, kappa_ref, after_ref, gram_ref, disp_ref, stiff_ref, cells_ref, loads_ref,
         up_ref, down_ref, low_ref, low_up_ref, low_down_ref, own_ref, phi_lo, kap_lo, phi_hi,
         kap_hi, in_sems):
    cx, cy, cz = phi_ref.shape
    sx, sy = disp_ref.shape
    peers = cells_ref.shape[0]
    tiles = peers // 8
    index_planes = -(-2 * tiles // 8)
    corner_planes = -(-(tiles + 4) // 8)
    copy_in = starter(in_sems)
    depth = 8
    lows = []
    for n, (ref, x) in enumerate(
        [(phi_ref, x) for x in range(cx - 4, cx)] + [(kappa_ref, x) for x in range(cx - 3, cx)]
    ):
        for t in range(cy // 8):
            lows.append(copy_in(ref.at[x, pl.ds(8 * t, 8)], low_ref.at[n * (cy // 8) + t]))
    groups = []
    for x in range(0, cx, depth):
        at = pl.ds(x, depth)
        groups.append([
            copy_in(phi_ref.at[at, pl.ds(0, 8)], phi_lo.at[at]),
            copy_in(kappa_ref.at[at, pl.ds(0, 8)], kap_lo.at[at]),
            copy_in(phi_ref.at[at, pl.ds(cy - 8, 8)], phi_hi.at[at]),
            copy_in(kappa_ref.at[at, pl.ds(cy - 8, 8)], kap_hi.at[at]),
        ])
    own_ref[...] = jnp.zeros_like(own_ref)

    def put(plane, number, tile):
        own_ref[plane + number // 8, :, (number % 8) * 128 : (number % 8 + 1) * 128] = tile

    corner = index_planes + 2
    for n in range(tiles):
        put(0, n, cells_ref[8 * n : 8 * n + 8, :].astype(F32))
        loads = loads_ref[8 * n : 8 * n + 8, :].astype(F32)
        put(0, tiles + n, loads)
        put(corner, n, loads)
    sub = lax.broadcasted_iota(jnp.int32, (8, sy), 0) < 4
    for kind, ref in enumerate((disp_ref, stiff_ref)):
        edge = jnp.where(sub, ref[0:8, :], ref[sx - 8 : sx, :])
        own_ref[index_planes, :, kind * sy : (kind + 1) * sy] = edge
        put(corner, tiles + 2 * kind, edge[:, 0:128])
        put(corner, tiles + 2 * kind + 1, edge[:, sy - 128 : sy])
    lane = lax.broadcasted_iota(jnp.int32, (sx, 128), 1)
    first, final = slice(0, 128), slice(sy - 128, sy)
    columns = jnp.where(
        lane < 32, disp_ref[:, first],
        jnp.where(
            lane < 64, pltpu.roll(disp_ref[:, final], 64, axis=1),
            jnp.where(lane < 96, pltpu.roll(stiff_ref[:, first], 64, axis=1), stiff_ref[:, final]),
        ),
    )
    for m in range(sx // 8):
        put(index_planes + 1, m, columns[8 * m : 8 * m + 8, :])
    own = own_ref[...]
    up_ref[cx:] = own
    down_ref[cx:] = own
    low_ref[7 * (cy // 8) :] = own[: index_planes + 1]
    low_up_ref[3:] = own[corner:]
    low_down_ref[3:] = own[corner:]
    upper = lax.broadcasted_iota(jnp.int32, (depth, 8, cz), 1) < 4
    for number, copies in enumerate(groups):
        for made in copies:
            made.wait()
        at = slice(number * depth, (number + 1) * depth)
        up = jnp.where(upper, phi_lo[at], pltpu.roll(kap_lo[at], 4, axis=1))
        down = jnp.where(upper, pltpu.roll(kap_hi[at], 4, axis=1), phi_hi[at])
        up_ref[at] = up
        down_ref[at] = down
        if (number + 1) * depth == cx:
            low_up_ref[0:3] = up[depth - 3 :]
            low_down_ref[0:3] = down[depth - 3 :]
    for made in lows:
        made.wait()


def packed(phi, kappa, after, gram, displacement, stiffness, cells, loads):
    cx, cy, cz = phi.shape
    tiles = cells.shape[0] // 8
    index_planes = -(-2 * tiles // 8)
    corner_planes = -(-(tiles + 4) // 8)
    extra = index_planes + 2 + corner_planes
    low_planes = 7 * (cy // 8)

    def shape(planes):
        return jax.ShapeDtypeStruct((planes, 8, cz), F32)

    return pl.pallas_call(
        pack,
        in_specs=hbm_specs(2) + any_specs(2) + vmem_specs(4),
        out_specs=vmem_specs(6),
        out_shape=[
            shape(cx + extra), shape(cx + extra), shape(low_planes + index_planes + 1),
            shape(3 + corner_planes), shape(3 + corner_planes), shape(extra),
        ],
        scratch_shapes=[pltpu.VMEM((cx, 8, cz), F32)] * 4
        + [pltpu.SemaphoreType.DMA((cx // 2 + low_planes,))],
        compiler_params=params(),
        name="pack",
    )(phi, kappa, after, gram, displacement, stiffness, cells, loads)


def substep(src, kap, dst, plane, advect, cy, cz):
    wide = cy + 8
    chunks = cz // 128
    lane = lax.broadcasted_iota(jnp.int32, (wide, 128), 1)
    first, last = lane == 0, lane == 127

    def take(at, q, start=8):
        return src[at, q, pl.ds(start, wide), :]

    for q in range(chunks):
        now = take(plane, q)
        left = take(plane, q - 1) if q else 0.0
        right = take(plane, q + 1) if q + 1 < chunks else 0.0
        total = pltpu.roll(jnp.where(last, left, now), 1, axis=1) + pltpu.roll(
            jnp.where(first, right, now), 127, axis=1
        )
        total = total + (take(plane, q, 7) + take(plane, q, 9))
        before = take(plane - 1, q)
        total = total + (before + take(plane + 1, q))
        new = now + advect * (before - now) + kap[plane - 1, q] * (total - 6.0 * now)
        dst[plane, q, 8 : 8 + wide, :] = new
        dst[plane, q, 7:8, :] = new[wide - 1 :]
        dst[plane, q, 8 + wide : 9 + wide, :] = new[0:1]


def fluid(x0, x1, cx, cy, cz, kind, *refs):
    planes = x1 - x0 + 8
    wide = cy + 8
    chunks = cz // 128
    names = ["phi", "kappa", "up", "down"]
    names += {"wet": ["forced", "low", "low_up", "low_down"],
              "middle": ["forced", "wet", "near"], "end": ["high", "whole"]}[kind]
    names += {"wet": ["out", "send"]}.get(kind, ["out"])
    names += ["a", "b", "kap", "sems", "out_sems"]
    r = dict(zip(names, refs))
    a, b, kap = r["a"], r["b"], r["kap"]
    is_last = lax.axis_index("gx") == lax.axis_size("gx") - 1
    copy, copy_out = starter(r["sems"]), starter(r["out_sems"])

    def chunked(src, s0, count, dst, d0, row):
        return [
            copy(
                src.at[pl.ds(s0, count), :, pl.ds(q * 128, 128)],
                dst.at[pl.ds(d0, count), q, pl.ds(row, cy)],
            )
            for q in range(chunks)
        ]

    def unchunked(src, s0, count, row, rows, dst, d0):
        return [
            copy_out(
                src.at[pl.ds(s0, count), q, pl.ds(row, rows)],
                dst.at[pl.ds(d0, count), :, pl.ds(q * 128, 128)],
            )
            for q in range(chunks)
        ]

    own0, own1 = max(0, x0 - 4), min(cx, x1 + 4)
    groups = []
    start = own0
    while start < own1:
        count = min(8, own1 - start)
        i = start - (x0 - 4)
        k0, k1 = max(start, x0 - 3), min(start + count, x1 + 3)
        groups.append((i, i + count, chunked(r["phi"], start, count, a, i, 8)
                       + chunked(r["kappa"], k0, k1 - k0, kap, k0 - (x0 - 3), 0)))
        start += count
    outs = []
    if kind == "middle":
        outs.append(copy_out(r["wet"], r["out"].at[pl.ds(0, x0)]))

    upper = lax.broadcasted_iota(jnp.int32, (8, cz), 0) < 4

    def assemble(i):
        x = x0 - 4 + i
        inner = 1 <= i < planes - 1
        if x >= cx:
            for q in range(chunks):
                at = slice(q * 128, (q + 1) * 128)
                a[i, q, 8 : 8 + wide, :] = r["high"][x - cx, :, at]
                if inner:
                    kap[i - 1, q] = r["high"][4 + x - cx, :, at]
        else:
            if x >= 0:
                up, down = r["up"][x], r["down"][x]
            elif x > -4:
                up, down = r["low_up"][x + 3], r["low_down"][x + 3]
            else:
                up = down = jnp.zeros((8, cz), F32)
            edge = jnp.where(upper, up, down)
            kedge = pltpu.roll(jnp.where(upper, down, up), 4, axis=0)
            for q in range(chunks):
                at = slice(q * 128, (q + 1) * 128)
                if x < 0:
                    for t in range(cy // 8):
                        a[i, q, 8 + 8 * t : 16 + 8 * t, :] = r["low"][(x + 4) * (cy // 8) + t, :, at]
                        if inner:
                            kap[i - 1, q, 8 * t : 8 * t + 8, :] = r["low"][
                                (x + 7) * (cy // 8) + t, :, at
                            ]
                a[i, q, 8 + cy : 8 + wide, :] = edge[:, at]
                if inner:
                    kap[i - 1, q, cy:wide, :] = kedge[:, at]
                if "forced" in r and 0 <= x < r["forced"].shape[0]:
                    a[i, q, 8 : 8 + wide, :] = a[i, q, 8 : 8 + wide, :] + r["forced"][x, :, at]
        for q in range(chunks):
            a[i, q, 7:8, :] = a[i, q, 7 + wide : 8 + wide, :]
            a[i, q, 8 + wide : 9 + wide, :] = a[i, q, 8:9, :]

    def run(src, dst, lo, hi):
        def body(i, carry):
            advect = 0.25
            if kind == "end":
                outside = jnp.logical_and(is_last, i + (x0 - 4) >= cx)
                advect = jnp.where(outside, 0.0, 0.25)
            substep(src, kap, dst, i, advect, cy, cz)
            return carry

        if hi > lo:
            lax.fori_loop(lo, hi, body, 0)

    if kind == "wet":
        for i in range(4):
            assemble(i)
    done = 1
    for i0, i1, copies in groups:
        for made in copies:
            made.wait()
        for i in range(i0, i1):
            assemble(i)
        if kind == "wet":
            for i in range(4, 8):
                for q in range(chunks):
                    at = slice(q * 128, (q + 1) * 128)
                    r["send"][i - 4, :, at] = a[i, q, 8 : 8 + wide, :]
                    if i < 7:
                        r["send"][i, :, at] = kap[i - 1, q]
        run(a, b, done, i1 - 1)
        done = i1 - 1
    if kind == "end":
        for i in range(planes - 4, planes):
            assemble(i)
        run(a, b, done, planes - 1)
    run(b, a, 2, planes - 2)
    run(a, b, 3, planes - 3)
    for start in range(4, planes - 4, 4):
        run(b, a, start, start + 4)
        if kind == "wet":
            for i in range(start, start + 4):
                for q in range(chunks):
                    r["out"][i - 4, :, q * 128 : (q + 1) * 128] = a[i, q, 8 : 8 + cy, :]
        else:
            outs += unchunked(a, start, 4, 8, cy, r["out"], x0 + start - 4)
    for made in outs:
        made.wait()


def fluid_call(kind, x0, x1, phi, kappa, up, down, *more):
    cx, cy, cz = phi.shape
    planes = x1 - x0 + 8
    field = jax.ShapeDtypeStruct((cx, cy, cz), F32)
    whole = hbm_specs(1)[0]
    if kind == "wet":
        specs = vmem_specs(4)
        out_shape = [
            jax.ShapeDtypeStruct((x1 - x0, cy, cz), F32),
            jax.ShapeDtypeStruct((7, cy + 8, cz), F32),
        ]
        out_specs = vmem_specs(2)
    elif kind == "middle":
        specs, out_shape, out_specs = vmem_specs(2) + any_specs(1), field, whole
    else:
        specs, out_shape, out_specs = vmem_specs(1) + hbm_specs(1), field, whole
    cells = planes * (cy + 8) * cz
    return pl.pallas_call(
        functools.partial(fluid, x0, x1, cx, cy, cz, kind),
        in_specs=hbm_specs(2) + vmem_specs(2) + specs,
        out_specs=out_specs,
        out_shape=out_shape,
        scratch_shapes=[
            pltpu.VMEM((planes, cz // 128, cy + 24, 128), F32),
            pltpu.VMEM((planes, cz // 128, cy + 24, 128), F32),
            pltpu.VMEM((planes - 2, cz // 128, cy + 8, 128), F32),
            pltpu.SemaphoreType.DMA((80,)),
            pltpu.SemaphoreType.DMA((80,)),
        ],
        input_output_aliases={5: 0} if kind == "end" else {},
        compiler_params=params(),
        cost_estimate=pl.CostEstimate(
            flops=48 * cells, bytes_accessed=12 * cells, transcendentals=0
        ),
        name="fluid_" + kind,
    )(phi, kappa, up, down, *more)


def shifted_pairs(n_gx, n_gy, dx, dy):
    pairs = []
    for gx in range(n_gx):
        for gy in range(n_gy):
            tx, ty = gx + dx, gy + dy
            if 0 <= tx < n_gx and 0 <= ty < n_gy:
                pairs.append((gx * n_gy + gy, tx * n_gy + ty))
    return pairs


def local(phi, kappa, stiffness, face_cell, load_dof, displacement, v_hist, w_hist, r_prev, w_prev):
    n_gx, n_gy = lax.axis_size("gx"), lax.axis_size("gy")
    peers, blk = face_cell.shape[2:]
    cx, cy, cz = phi.shape
    sx, sy = displacement.shape
    hist = v_hist.shape[0]
    wet_planes = cx // 8
    fcell = face_cell.reshape(peers, blk)
    ldof = load_dof.reshape(peers, blk)
    axes = ("gx", "gy")

    def shift(value, dx, dy):
        return lax.ppermute(value, axes, shifted_pairs(n_gx, n_gy, dx, dy))

    def exchange(value):
        return lax.all_to_all(value, axes, split_axis=0, concat_axis=0, tiled=True)

    def call(body, out_shape, scratch, name, specs, *args):
        several = isinstance(out_shape, list)
        return pl.pallas_call(
            body,
            in_specs=specs,
            out_specs=vmem_specs(len(out_shape)) if several else vmem_specs(1)[0],
            out_shape=out_shape,
            scratch_shapes=scratch,
            compiler_params=params(),
            name=name,
        )(*args)

    def f32(*shape):
        return jax.ShapeDtypeStruct(shape, F32)

    sent = call(
        functools.partial(gather_disp, n_gy), f32(peers, 1, 3 * blk),
        [pltpu.VMEM((peers, blk), F32)], "gather_disp", vmem_specs(2), displacement, ldof,
    )
    disp = exchange(sent)
    size = 8 * hist
    gram = call(
        gram_rows, f32(peers, 128),
        [
            pltpu.VMEM((sx // 8, hist, 8, sy), F32), pltpu.VMEM((size, size), F32),
            pltpu.VMEM((size, size), F32),
            pltpu.VMEM((max(128, peers, 2 * peers if peers < hist else 0), 128), F32),
            pltpu.SemaphoreType.DMA((sx // 8,)),
        ],
        "gram_rows", hbm_specs(1), v_hist,
    )
    up_send, down_send, low_send, low_up_send, low_down_send, own = packed(
        phi, kappa, disp, gram, displacement, stiffness, fcell, ldof
    )
    index_planes = -(-2 * (peers // 8) // 8)
    low = shift(low_send, 1, 0)
    up = shift(up_send, 0, -1)
    down = shift(down_send, 0, 1)
    low_up = shift(low_up_send, 1, -1)
    low_down = shift(low_down_send, 1, 1)
    corner = cx + index_planes + 2
    near = shift(
        jnp.concatenate([own[: index_planes + 1], up[corner:], down[corner:]], axis=0), -1, 0
    )

    chunks = cz // 128
    forced = call(
        functools.partial(scatter_disp, cx, cy, cz), f32(wet_planes, cy + 8, cz),
        [
            pltpu.VMEM((wet_planes * cy * chunks, 256), F32),
            pltpu.VMEM((512, wet_planes * 4 * chunks), F32),
        ],
        "scatter_disp", vmem_specs(4), disp, fcell, up, down,
    )
    wet, send = fluid_call(
        "wet", 0, wet_planes, phi, kappa, up, down, forced, low, low_up, low_down
    )
    high = shift(send, -1, 0)
    middle = fluid_call("middle", wet_planes, cx - 4, phi, kappa, up, down, forced, wet, near)
    field = fluid_call("end", cx - 4, cx, phi, kappa, up, down, high, middle)
    press = call(
        functools.partial(gather_press, n_gx, n_gy), f32(peers, 1, (len(NEAR) + 1) * blk),
        [pltpu.VMEM((peers, blk), F32)], "gather_press", vmem_specs(3) + hbm_specs(1),
        wet, fcell, gram, middle,
    )
    loads = exchange(press)
    resp, late = call(
        shell, [f32(sx, sy), f32(peers, 1, 256)],
        [
            pltpu.VMEM((hist, sx, sy), F32),
            pltpu.VMEM((sx * (sy // 128), 256), F32),
            pltpu.VMEM((8 * (sy // 128), 256), F32),
            pltpu.VMEM((sx, 32), F32),
            pltpu.VMEM((16, 32), F32),
            pltpu.VMEM((3, sx + 8, sy + 128), F32),
            pltpu.VMEM((128, 128), F32),
            pltpu.SemaphoreType.DMA((1,)),
        ],
        "shell", vmem_specs(11) + hbm_specs(2),
        loads, ldof, displacement, stiffness, r_prev, up, down, low, low_up, low_down, near,
        v_hist, field,
    )
    x_next = call(
        solve, f32(sx, sy),
        [pltpu.VMEM((hist, sx, sy), F32), pltpu.SemaphoreType.DMA((1,))],
        "solve", vmem_specs(3) + hbm_specs(1), exchange(late), resp, w_prev, w_hist,
    )
    return (field, x_next)


def solution(mesh):
    in_specs = (
        P("gx", "gy", None),
        P("gx", "gy", None),
        P("gx", "gy"),
        P("gx", "gy", None, None),
        P("gx", "gy", None, None),
        P("gx", "gy"),
        P(None, "gx", "gy"),
        P(None, "gx", "gy"),
        P("gx", "gy"),
        P("gx", "gy"),
    )
    out_specs = (P("gx", "gy", None), P("gx", "gy"))
    return jax.shard_map(local, mesh=mesh, in_specs=in_specs, out_specs=out_specs, check_vma=False)
```

```python
import functools

import jax
import jax.numpy as jnp
from jax import lax
from jax.experimental import pallas as pl
from jax.experimental.pallas import tpu as pltpu
from jax.sharding import PartitionSpec as P

NSUB = 4
SWEEPS = 3
HIST = 40
VMEM_BYTES = 50 * 1024 * 1024
F32 = jnp.float32
BF16 = jnp.bfloat16


def params():
    return pltpu.CompilerParams(vmem_limit_bytes=VMEM_BYTES)


def vmem_specs(count):
    return [pl.BlockSpec(memory_space=pltpu.VMEM)] * count


def any_specs(count):
    return [pl.BlockSpec(memory_space=pl.ANY)] * count


def hbm_specs(count):
    return [pl.BlockSpec(memory_space=pltpu.HBM)] * count


def pieces(value, count):
    parts = []
    for _ in range(count):
        part = value.astype(BF16)
        parts.append(part)
        value = value - part.astype(F32)
    return parts


def as_row(block):
    return jnp.concatenate([block[i : i + 1] for i in range(block.shape[0])], axis=1)


def both_rows(row):
    return jnp.broadcast_to(row, (16, row.shape[1])).astype(BF16)


def matches(keys, rows):
    ids = lax.broadcasted_iota(jnp.int32, (16, keys.shape[1]), 0).astype(F32).astype(BF16)
    found = []
    for base in range(0, rows, 256):
        key = both_rows((keys - base).astype(F32))
        for start in range(0, min(256, rows - base), 16):
            found.append(key == ids + jnp.bfloat16(start))
    return found


def one_hot(keys, rows):
    one, zero = jnp.bfloat16(1), jnp.bfloat16(0)
    return jnp.concatenate([jnp.where(m, one, zero) for m in matches(keys, rows)], axis=0)


def select_sum(table, lane, group, rows, parts):
    total = table[:rows]
    for part in range(1, parts):
        total = total + table[part * rows : (part + 1) * rows]
    ids = lax.broadcasted_iota(jnp.int32, total.shape, 0)
    return jnp.sum(jnp.where(ids == lane, total, 0.0), axis=0, keepdims=True)


def pick(table_t, index_ref, out_rows, rows, lane_bits, chunk_bits, parts, step=8):
    lanes = 1 << lane_bits
    for base in range(0, index_ref.shape[0], step):
        index = as_row(index_ref[base : base + step, :])
        lane = index & (lanes - 1)
        keys = ((index >> lane_bits) & ((1 << chunk_bits) - 1)) * rows + (
            index >> (lane_bits + chunk_bits)
        )
        hot = one_hot(keys, rows << chunk_bits)
        found = lax.dot_general(
            table_t, hot, (((1,), (0,)), ((), ())), preferred_element_type=F32
        )
        out_rows(base, select_sum(found, lane, step, lanes, parts))


def spread_values(values, lane, lanes, parts):
    zero = jnp.bfloat16(0)
    found = matches(lane, lanes)
    spread = []
    for part in pieces(values, parts):
        part = both_rows(part.astype(F32))
        spread += [jnp.where(m, part, zero) for m in found]
    return jnp.concatenate(spread, axis=0)


NEAR = ((0, 0), (1, 0), (-1, 0), (0, 1), (0, -1), (1, 1), (1, -1), (-1, 1), (-1, -1))


def tile_of(ref, plane, number):
    at = (number % 8) * 128
    return ref[plane + number // 8, :, at : at + 128]


def starter(sems):
    used = [0]

    def copy(src, dst):
        made = pltpu.make_async_copy(src, dst, sems.at[used[0]])
        used[0] += 1
        made.start()
        return made

    return copy


def gather_disp(n_gy, disp_ref, index_ref, out_ref, own_ref):
    sx, sy = disp_ref.shape
    peers, blk = index_ref.shape
    chunk_bits = (sy // 128).bit_length() - 1
    columns = []
    for q in range(sy // 128):
        columns.append(jnp.transpose(disp_ref[:, q * 128 : (q + 1) * 128]))
    table_t = jnp.concatenate(pieces(jnp.concatenate(columns, axis=1), 3), axis=0)

    def write(base, row):
        for i in range(8):
            own_ref[base + i : base + i + 1, :] = row[:, i * blk : (i + 1) * blk]

    pick(table_t, index_ref, write, sx, 7, chunk_bits, 3)
    own = own_ref[...]
    beside = lax.broadcasted_iota(jnp.int32, own.shape, 0) % n_gy
    out_ref[:, 0, 0:blk] = own
    out_ref[:, 0, blk : 2 * blk] = jnp.where(
        beside == n_gy - 1, 0.0, pltpu.roll(own, peers - 1, axis=0)
    )
    out_ref[:, 0, 2 * blk : 3 * blk] = jnp.where(beside == 0, 0.0, pltpu.roll(own, 1, axis=0))


def scatter_disp(cx, cy, cz, disp_ref, cells_ref, up_ref, down_ref, out_ref, acc_ref, side_ref):
    planes = out_ref.shape[0]
    peers, blk = cells_ref.shape
    rows = planes * cy
    chunks = cz // 128
    row_bits = cz.bit_length() - 1
    step = 8
    def accumulate(target, first, left, right):
        added = lax.dot_general(
            left, right, (((1,), (1,)), ((), ())), preferred_element_type=F32
        )
        if first:
            target[...] = added
        else:
            target[...] += added

    for base in range(0, peers, step):
        index = as_row(cells_ref[base : base + step, :])
        values = 0.5 * as_row(disp_ref[base : base + step, 0, 0:blk])
        keys = ((index >> 7) & (chunks - 1)) * rows + (index >> row_bits)
        accumulate(
            acc_ref, base == 0, one_hot(keys, rows * chunks),
            spread_values(values, index & 127, 128, 2),
        )
    for base in range(0, peers, step):
        for side in range(2):
            index = as_row(tile_of(up_ref if side == 0 else down_ref, cx, base // step).astype(jnp.int32))
            values = 0.5 * as_row(
                disp_ref[base : base + step, 0, (side + 1) * blk : (side + 2) * blk]
            )
            row = index >> row_bits
            plane = row // cy
            column = row - plane * cy
            inside = column < 4 if side == 0 else column >= cy - 4
            place = column if side == 0 else column - (cy - 8)
            keys = ((index >> 8) & (chunks // 2 - 1)) * (planes * 8) + plane * 8 + place
            keys = jnp.where(inside, keys, -1)
            accumulate(
                side_ref, base == 0 and side == 0, spread_values(values, index & 255, 256, 2),
                one_hot(keys, planes * 4 * chunks),
            )
    for q in range(chunks):
        part = acc_ref[q * rows : (q + 1) * rows, :]
        out_ref[:, 0:cy, q * 128 : (q + 1) * 128] = (part[:, :128] + part[:, 128:]).reshape(
            planes, cy, 128
        )
    both = jnp.transpose(side_ref[0:256, :] + side_ref[256:512, :])
    for q in range(chunks // 2):
        part = both[q * planes * 8 : (q + 1) * planes * 8, :]
        out_ref[:, cy : cy + 8, q * 256 : (q + 1) * 256] = part.reshape(planes, 8, 256)


def gather_press(n_gx, n_gy, wet_ref, index_ref, gram_ref, after_ref, out_ref, own_ref):
    planes, cy, cz = wet_ref.shape
    peers, blk = index_ref.shape
    rows = planes * cy
    chunks = cz // 256
    columns = []
    for q in range(chunks):
        part = wet_ref[:, :, q * 256 : (q + 1) * 256].reshape(rows, 256)
        columns.append(jnp.transpose(part))
    table_t = jnp.concatenate(pieces(jnp.concatenate(columns, axis=1), 2), axis=0)

    def write(base, row):
        for i in range(8):
            own_ref[base + i : base + i + 1, :] = row[:, i * blk : (i + 1) * blk]

    pick(table_t, index_ref, write, rows, 8, chunks.bit_length() - 1, 2)
    own = own_ref[...]
    number = lax.broadcasted_iota(jnp.int32, own.shape, 0)
    at_x, at_y = number // n_gy, number % n_gy
    for k, (dx, dy) in enumerate(NEAR):
        ok = (at_x + dx >= 0) & (at_x + dx < n_gx) & (at_y + dy >= 0) & (at_y + dy < n_gy)
        moved = pltpu.roll(own, (-(dx * n_gy + dy)) % peers, axis=0) if k else own
        out_ref[:, 0, k * blk : (k + 1) * blk] = jnp.where(ok, moved, 0.0)
    out_ref[:, 0, len(NEAR) * blk : (len(NEAR) + 1) * blk] = gram_ref[...]


def gram_rows(v_ref, out_ref, v, same, cross, wide, sems):
    hist, sx, sy = v_ref.shape
    tiles = sx // 8
    copy = starter(sems)
    copies = [
        copy(v_ref.at[:, pl.ds(8 * t, 8), :], v.at[t]) for t in range(tiles)
    ]
    for t in range(tiles):
        copies[t].wait()
        high, low = pieces(v[t].reshape(hist * 8, sy), 2)

        def dot(x, y):
            return lax.dot_general(x, y, (((1,), (1,)), ((), ())), preferred_element_type=F32)

        if t == 0:
            same[...] = dot(high, high) + dot(low, low)
            cross[...] = dot(high, low)
        else:
            same[...] += dot(high, high) + dot(low, low)
            cross[...] += dot(high, low)
    size = hist * 8
    row = lax.broadcasted_iota(jnp.int32, (size, size), 0)
    column = lax.broadcasted_iota(jnp.int32, (size, size), 1)
    match = (row & 7) == (column & 7)
    group = (
        lax.broadcasted_iota(jnp.int32, (size, 128), 0) // 8
        == lax.broadcasted_iota(jnp.int32, (size, 128), 1)
    ).astype(F32)

    def reduced(ref):
        part = jnp.sum(jnp.where(match, ref[...], 0.0).reshape(hist, 8, size), axis=1)
        return jnp.dot(part, group, precision=lax.Precision.HIGHEST, preferred_element_type=F32)

    wide[...] = jnp.zeros_like(wide)
    wide[0:hist, :] = reduced(cross)
    turned = jnp.transpose(wide[0:128, :])
    wide[0:128, :] = wide[0:128, :] + turned
    wide[0:hist, :] = wide[0:hist, :] + reduced(same)
    peers = out_ref.shape[0]
    if peers >= hist:
        out_ref[...] = wide[0:peers, :]
    else:
        out_ref[...] = wide[0:peers, :] + pltpu.roll(wide[peers : 2 * peers, :], 64, axis=1)


def shell(recv_ref, index_ref, disp_ref, stiff_ref, prev_ref, up_ref, down_ref, low_ref,
          low_up_ref, low_down_ref, high_ref, v_ref, after_ref, resp_ref, late_ref, v, acc, rows_acc,
          cols_acc, corner_acc, ext, dots, v_sem):
    sx, sy = disp_ref.shape
    peers, blk = index_ref.shape
    load_tiles = peers // 8
    index_planes = -(-2 * load_tiles // 8)
    corner_planes = -(-(load_tiles + 4) // 8)
    chunks = sy // 128
    hist = v_ref.shape[0]
    v_copy = pltpu.make_async_copy(v_ref, v, v_sem.at[0])
    v_copy.start()
    top = up_ref.shape[0] - (index_planes + 2 + corner_planes)
    low_top = low_ref.shape[0] - (index_planes + 1)
    corner_top = low_up_ref.shape[0] - corner_planes
    near_top = index_planes + 1
    load_at = [
        (high_ref, 0, load_tiles), (low_ref, low_top, load_tiles), (up_ref, top, load_tiles),
        (down_ref, top, load_tiles), (high_ref, near_top, 0),
        (high_ref, near_top + corner_planes, 0), (low_up_ref, corner_top, 0),
        (low_down_ref, corner_top, 0),
    ]

    def accumulate(target, first, keys, height, lane, lanes, values):
        added = lax.dot_general(
            one_hot(keys, height), spread_values(values, lane, lanes, 2),
            (((1,), (1,)), ((), ())), preferred_element_type=F32,
        )
        if first:
            target[...] = added
        else:
            target[...] += added

    def values_of(k, base):
        return as_row(recv_ref[base : base + 8, 0, k * blk : (k + 1) * blk])

    for base in range(0, peers, 8):
        index = as_row(index_ref[base : base + 8, :])
        keys = ((index >> 7) & (chunks - 1)) * sx + index // sy
        accumulate(acc, base == 0, keys, sx * chunks, index & 127, 128, values_of(0, base))
    for k, (dx, dy) in enumerate(NEAR):
        if k == 0:
            continue
        for base in range(0, peers, 8):
            ref, plane, number = load_at[k - 1]
            index = as_row(tile_of(ref, plane, number + base // 8).astype(jnp.int32))
            row = index // sy
            lane = index & (sy - 1)
            if dx == 1:
                row8 = jnp.where(row < 4, row, -1)
            elif dx == -1:
                row8 = jnp.where(row >= sx - 4, row - (sx - 8), -1)
            if dy == 1:
                lane8 = jnp.where(lane < 4, lane, -1)
            elif dy == -1:
                lane8 = jnp.where(lane >= sy - 4, lane - (sy - 8), -1)
            values = values_of(k, base)
            if dy == 0:
                keys = jnp.where(row8 < 0, -1, (lane >> 7) * 8 + row8)
                accumulate(
                    rows_acc, k == 1 and base == 0, keys, 8 * chunks, lane & 127, 128, values
                )
            elif dx == 0:
                accumulate(cols_acc, k == 3 and base == 0, row, sx, lane8, 16, values)
            else:
                accumulate(corner_acc, k == 5 and base == 0, row8, 16, lane8, 16, values)

    ids = lax.broadcasted_iota(jnp.int32, (16, 128), 0)
    lanes = lax.broadcasted_iota(jnp.int32, (16, 128), 1)
    placed = (jnp.where(ids < 4, ids, jnp.where(ids < 8, ids + 120, -1)) == lanes).astype(F32)

    def widened(ref):
        both = ref[:, 0:16] + ref[:, 16:32]
        return jnp.dot(both, placed, precision=lax.Precision.HIGHEST, preferred_element_type=F32)

    force, disp, stiff = ext.at[0], ext.at[1], ext.at[2]
    for q in range(chunks):
        at = slice(q * 128, (q + 1) * 128)
        part = acc[q * sx : (q + 1) * sx, :]
        force[0:sx, at] = part[:, 0:128] + part[:, 128:256]
        part = rows_acc[q * 8 : (q + 1) * 8, :]
        force[sx : sx + 8, at] = part[:, 0:128] + part[:, 128:256]
    side = slice(sy, sy + 128)
    force[0:sx, side] = widened(cols_acc)
    force[sx : sx + 8, side] = widened(corner_acc)[0:8]
    sub = lax.broadcasted_iota(jnp.int32, (8, sy), 0) < 4
    sub1 = lax.broadcasted_iota(jnp.int32, (8, 128), 0) < 4
    lane = lax.broadcasted_iota(jnp.int32, (sx, 128), 1)
    lane1 = lax.broadcasted_iota(jnp.int32, (8, 128), 1)
    for kind, (target, own) in enumerate(((disp, disp_ref), (stiff, stiff_ref))):

        def row_tile(ref, plane):
            return ref[plane, :, kind * sy : (kind + 1) * sy]

        def col_tile(ref):
            plane = top + index_planes + 1
            return jnp.concatenate([tile_of(ref, plane, m) for m in range(sx // 8)], axis=0)

        target[0:sx, 0:sy] = own[...]
        target[sx : sx + 8, 0:sy] = jnp.where(
            sub, row_tile(high_ref, index_planes), row_tile(low_ref, low_top + index_planes)
        )
        ahead, behind = col_tile(up_ref), col_tile(down_ref)
        if kind == 0:
            behind = pltpu.roll(behind, 64, axis=1)
        else:
            ahead = pltpu.roll(ahead, 64, axis=1)
        target[0:sx, side] = jnp.where(lane < 32, ahead, jnp.where(lane >= 96, behind, 0.0))

        def corner_tile(ahead, ahead_plane, behind, behind_plane):
            number = load_tiles + 2 * kind
            return jnp.where(
                lane1 < 32, tile_of(ahead, ahead_plane, number),
                jnp.where(lane1 >= 96, tile_of(behind, behind_plane, number + 1), 0.0),
            )

        target[sx : sx + 8, side] = jnp.where(
            sub1, corner_tile(high_ref, near_top, high_ref, near_top + corner_planes),
            corner_tile(low_up_ref, corner_top, low_down_ref, corner_top),
        )

    load = force[...]
    k = stiff[...]
    diag = 1.0 + 4.0 * k
    scale = 0.8 / diag
    resp = disp[...]
    high, wide = sx + 8, sy + 128
    for sweep in range(SWEEPS):
        beside = (pltpu.roll(resp, 1, axis=0) + pltpu.roll(resp, high - 1, axis=0)) + (
            pltpu.roll(resp, 1, axis=1) + pltpu.roll(resp, wide - 1, axis=1)
        )
        resp = resp + scale * (load - (diag * resp - k * beside))
    own = resp[0:sx, 0:sy]
    resp_ref[...] = own
    resid = own - disp_ref[...]
    newest = resid - prev_ref[...]
    dots[...] = jnp.zeros_like(dots)

    def folded(value):
        total = value[0:8]
        for t in range(1, sx // 8):
            total = total + value[8 * t : 8 * t + 8]
        out = total[:, 0:128]
        for q in range(1, chunks):
            out = out + total[:, q * 128 : (q + 1) * 128]
        return jnp.sum(out, axis=0, keepdims=True)

    dots[0:1, :] = folded(newest * newest)
    dots[64:65, :] = folded(resid * newest)
    v_copy.wait()
    for number in range(1, hist):
        column = v[number]
        dots[number : number + 1, :] = folded(column * newest)
        dots[64 + number : 65 + number, :] = folded(column * resid)
    late = lax.dot_general(
        jnp.ones((8, 128), F32), dots[...], (((1,), (1,)), ((), ())),
        precision=lax.Precision.HIGHEST, preferred_element_type=F32,
    )
    gram_at = len(NEAR) * blk
    gram = jnp.sum(recv_ref[:, 0, gram_at : gram_at + 128], axis=0, keepdims=True)
    late_ref[:, 0, 0:128] = jnp.broadcast_to(late[0:1], (peers, 128))
    late_ref[:, 0, 128:256] = jnp.broadcast_to(gram, (peers, 128))


def solve(recv_ref, resp_ref, prev_ref, w_ref, out_ref, w, sems):
    peers = recv_ref.shape[0]
    hist = w_ref.shape[0]
    sx, sy = resp_ref.shape
    w_copy = pltpu.make_async_copy(w_ref, w, sems.at[0])
    w_copy.start()
    late = jnp.sum(recv_ref[:, 0, 0:128], axis=0, keepdims=True)
    rows = recv_ref[:, 0, 128:256]
    if peers >= hist:
        gram = rows[0:hist]
    else:
        gram = jnp.concatenate(
            [rows, pltpu.roll(rows, 64, axis=1)[0 : hist - peers]], axis=0
        )
    row = lax.broadcasted_iota(jnp.int32, (hist, 128), 0)
    lane = lax.broadcasted_iota(jnp.int32, (hist, 128), 1)
    turned = jnp.transpose(jnp.broadcast_to(late, (128, 128)))
    gram = jnp.where(row == 0, jnp.broadcast_to(late, (hist, 128)), gram)
    gram = jnp.where(lane == 0, turned[0:hist], gram)
    gram = jnp.where(lane < hist, gram, 0.0)
    unit = row == lane
    trace = jnp.sum(jnp.where(unit, gram, 0.0), keepdims=True)
    a = gram + jnp.where(unit, 0.001 * trace / hist, 0.0)
    a = jnp.where(lane == 64, -turned[64 : 64 + hist], a)
    for j in range(hist):
        column = jnp.broadcast_to(a[:, j : j + 1], (hist, 128))
        scaled = a[j : j + 1, :] / column[j : j + 1, :]
        a = jnp.where(row == j, scaled, a - column * scaled)
    coef = jnp.broadcast_to(a[:, 64:65], (hist, 128))
    coef = jnp.concatenate([coef] * (sy // 128), axis=1)
    resp = resp_ref[...]
    total = resp + coef[0:1] * (resp - prev_ref[...])
    w_copy.wait()
    for number in range(1, hist):
        total = total + coef[number : number + 1] * w[number]
    out_ref[...] = total


def pack(phi_ref, kappa_ref, after_ref, disp_ref, stiff_ref, cells_ref, loads_ref,
         up_ref, down_ref, low_ref, low_up_ref, low_down_ref, own_ref, phi_lo, kap_lo, phi_hi,
         kap_hi, in_sems):
    cx, cy, cz = phi_ref.shape
    sx, sy = disp_ref.shape
    peers = cells_ref.shape[0]
    tiles = peers // 8
    index_planes = -(-2 * tiles // 8)
    corner_planes = -(-(tiles + 4) // 8)
    copy_in = starter(in_sems)
    depth = 8
    lows = []
    for n, (ref, x) in enumerate(
        [(phi_ref, x) for x in range(cx - 4, cx)] + [(kappa_ref, x) for x in range(cx - 3, cx)]
    ):
        for t in range(cy // 8):
            lows.append(copy_in(ref.at[x, pl.ds(8 * t, 8)], low_ref.at[n * (cy // 8) + t]))
    groups = []
    for x in range(0, cx, depth):
        at = pl.ds(x, depth)
        groups.append([
            copy_in(phi_ref.at[at, pl.ds(0, 8)], phi_lo.at[at]),
            copy_in(kappa_ref.at[at, pl.ds(0, 8)], kap_lo.at[at]),
            copy_in(phi_ref.at[at, pl.ds(cy - 8, 8)], phi_hi.at[at]),
            copy_in(kappa_ref.at[at, pl.ds(cy - 8, 8)], kap_hi.at[at]),
        ])
    own_ref[...] = jnp.zeros_like(own_ref)

    def put(plane, number, tile):
        own_ref[plane + number // 8, :, (number % 8) * 128 : (number % 8 + 1) * 128] = tile

    corner = index_planes + 2
    for n in range(tiles):
        put(0, n, cells_ref[8 * n : 8 * n + 8, :].astype(F32))
        loads = loads_ref[8 * n : 8 * n + 8, :].astype(F32)
        put(0, tiles + n, loads)
        put(corner, n, loads)
    sub = lax.broadcasted_iota(jnp.int32, (8, sy), 0) < 4
    for kind, ref in enumerate((disp_ref, stiff_ref)):
        edge = jnp.where(sub, ref[0:8, :], ref[sx - 8 : sx, :])
        own_ref[index_planes, :, kind * sy : (kind + 1) * sy] = edge
        put(corner, tiles + 2 * kind, edge[:, 0:128])
        put(corner, tiles + 2 * kind + 1, edge[:, sy - 128 : sy])
    lane = lax.broadcasted_iota(jnp.int32, (sx, 128), 1)
    first, final = slice(0, 128), slice(sy - 128, sy)
    columns = jnp.where(
        lane < 32, disp_ref[:, first],
        jnp.where(
            lane < 64, pltpu.roll(disp_ref[:, final], 64, axis=1),
            jnp.where(lane < 96, pltpu.roll(stiff_ref[:, first], 64, axis=1), stiff_ref[:, final]),
        ),
    )
    for m in range(sx // 8):
        put(index_planes + 1, m, columns[8 * m : 8 * m + 8, :])
    own = own_ref[...]
    up_ref[cx:] = own
    down_ref[cx:] = own
    low_ref[7 * (cy // 8) :] = own[: index_planes + 1]
    low_up_ref[3:] = own[corner:]
    low_down_ref[3:] = own[corner:]
    upper = lax.broadcasted_iota(jnp.int32, (depth, 8, cz), 1) < 4
    for number, copies in enumerate(groups):
        for made in copies:
            made.wait()
        at = slice(number * depth, (number + 1) * depth)
        up = jnp.where(upper, phi_lo[at], pltpu.roll(kap_lo[at], 4, axis=1))
        down = jnp.where(upper, pltpu.roll(kap_hi[at], 4, axis=1), phi_hi[at])
        up_ref[at] = up
        down_ref[at] = down
        if (number + 1) * depth == cx:
            low_up_ref[0:3] = up[depth - 3 :]
            low_down_ref[0:3] = down[depth - 3 :]
    for made in lows:
        made.wait()


def packed(phi, kappa, after, displacement, stiffness, cells, loads):
    cx, cy, cz = phi.shape
    tiles = cells.shape[0] // 8
    index_planes = -(-2 * tiles // 8)
    corner_planes = -(-(tiles + 4) // 8)
    extra = index_planes + 2 + corner_planes
    low_planes = 7 * (cy // 8)

    def shape(planes):
        return jax.ShapeDtypeStruct((planes, 8, cz), F32)

    return pl.pallas_call(
        pack,
        in_specs=hbm_specs(2) + any_specs(1) + vmem_specs(4),
        out_specs=vmem_specs(6),
        out_shape=[
            shape(cx + extra), shape(cx + extra), shape(low_planes + index_planes + 1),
            shape(3 + corner_planes), shape(3 + corner_planes), shape(extra),
        ],
        scratch_shapes=[pltpu.VMEM((cx, 8, cz), F32)] * 4
        + [pltpu.SemaphoreType.DMA((cx // 2 + low_planes,))],
        compiler_params=params(),
        name="pack",
    )(phi, kappa, after, displacement, stiffness, cells, loads)


def substep(src, kap, dst, plane, advect, cy, cz):
    wide = cy + 8
    chunks = cz // 128
    lane = lax.broadcasted_iota(jnp.int32, (wide, 128), 1)
    first, last = lane == 0, lane == 127

    def take(at, q, start=8):
        return src[at, q, pl.ds(start, wide), :]

    for q in range(chunks):
        now = take(plane, q)
        left = take(plane, q - 1) if q else 0.0
        right = take(plane, q + 1) if q + 1 < chunks else 0.0
        total = pltpu.roll(jnp.where(last, left, now), 1, axis=1) + pltpu.roll(
            jnp.where(first, right, now), 127, axis=1
        )
        total = total + (take(plane, q, 7) + take(plane, q, 9))
        before = take(plane - 1, q)
        total = total + (before + take(plane + 1, q))
        new = now + advect * (before - now) + kap[plane - 1, q] * (total - 6.0 * now)
        dst[plane, q, 8 : 8 + wide, :] = new
        dst[plane, q, 7:8, :] = new[wide - 1 :]
        dst[plane, q, 8 + wide : 9 + wide, :] = new[0:1]


def fluid(x0, x1, cx, cy, cz, kind, *refs):
    planes = x1 - x0 + 8
    wide = cy + 8
    chunks = cz // 128
    names = ["phi", "kappa", "up", "down"]
    names += {"wet": ["forced", "low", "low_up", "low_down", "near", "gram"],
              "middle": ["forced", "wet"], "end": ["high", "whole"]}[kind]
    names += {"wet": ["out", "send"]}.get(kind, ["out"])
    names += ["a", "b", "kap", "sems", "out_sems"]
    r = dict(zip(names, refs))
    a, b, kap = r["a"], r["b"], r["kap"]
    is_last = lax.axis_index("gx") == lax.axis_size("gx") - 1
    copy, copy_out = starter(r["sems"]), starter(r["out_sems"])

    def chunked(src, s0, count, dst, d0, row):
        return [
            copy(
                src.at[pl.ds(s0, count), :, pl.ds(q * 128, 128)],
                dst.at[pl.ds(d0, count), q, pl.ds(row, cy)],
            )
            for q in range(chunks)
        ]

    def unchunked(src, s0, count, row, rows, dst, d0):
        return [
            copy_out(
                src.at[pl.ds(s0, count), q, pl.ds(row, rows)],
                dst.at[pl.ds(d0, count), :, pl.ds(q * 128, 128)],
            )
            for q in range(chunks)
        ]

    own0, own1 = max(0, x0 - 4), min(cx, x1 + 4)
    groups = []
    start = own0
    while start < own1:
        count = min(8, own1 - start)
        i = start - (x0 - 4)
        k0, k1 = max(start, x0 - 3), min(start + count, x1 + 3)
        groups.append((i, i + count, chunked(r["phi"], start, count, a, i, 8)
                       + chunked(r["kappa"], k0, k1 - k0, kap, k0 - (x0 - 3), 0)))
        start += count
    outs = []
    if kind == "middle":
        outs.append(copy_out(r["wet"], r["out"].at[pl.ds(0, x0)]))

    upper = lax.broadcasted_iota(jnp.int32, (8, cz), 0) < 4

    def assemble(i):
        x = x0 - 4 + i
        inner = 1 <= i < planes - 1
        if x >= cx:
            for q in range(chunks):
                at = slice(q * 128, (q + 1) * 128)
                a[i, q, 8 : 8 + wide, :] = r["high"][x - cx, :, at]
                if inner:
                    kap[i - 1, q] = r["high"][4 + x - cx, :, at]
        else:
            if x >= 0:
                up, down = r["up"][x], r["down"][x]
            elif x > -4:
                up, down = r["low_up"][x + 3], r["low_down"][x + 3]
            else:
                up = down = jnp.zeros((8, cz), F32)
            edge = jnp.where(upper, up, down)
            kedge = pltpu.roll(jnp.where(upper, down, up), 4, axis=0)
            for q in range(chunks):
                at = slice(q * 128, (q + 1) * 128)
                if x < 0:
                    for t in range(cy // 8):
                        a[i, q, 8 + 8 * t : 16 + 8 * t, :] = r["low"][(x + 4) * (cy // 8) + t, :, at]
                        if inner:
                            kap[i - 1, q, 8 * t : 8 * t + 8, :] = r["low"][
                                (x + 7) * (cy // 8) + t, :, at
                            ]
                a[i, q, 8 + cy : 8 + wide, :] = edge[:, at]
                if inner:
                    kap[i - 1, q, cy:wide, :] = kedge[:, at]
                if "forced" in r and 0 <= x < r["forced"].shape[0]:
                    a[i, q, 8 : 8 + wide, :] = a[i, q, 8 : 8 + wide, :] + r["forced"][x, :, at]
        for q in range(chunks):
            a[i, q, 7:8, :] = a[i, q, 7 + wide : 8 + wide, :]
            a[i, q, 8 + wide : 9 + wide, :] = a[i, q, 8:9, :]

    def run(src, dst, lo, hi):
        def body(i, carry):
            advect = 0.25
            if kind == "end":
                outside = jnp.logical_and(is_last, i + (x0 - 4) >= cx)
                advect = jnp.where(outside, 0.0, 0.25)
            substep(src, kap, dst, i, advect, cy, cz)
            return carry

        if hi > lo:
            lax.fori_loop(lo, hi, body, 0)

    if kind == "wet":
        for i in range(4):
            assemble(i)
    done = 1
    for i0, i1, copies in groups:
        for made in copies:
            made.wait()
        for i in range(i0, i1):
            assemble(i)
        if kind == "wet":
            for i in range(4, 8):
                for q in range(chunks):
                    at = slice(q * 128, (q + 1) * 128)
                    r["send"][i - 4, :, at] = a[i, q, 8 : 8 + wide, :]
                    if i < 7:
                        r["send"][i, :, at] = kap[i - 1, q]
        run(a, b, done, i1 - 1)
        done = i1 - 1
    if kind == "end":
        for i in range(planes - 4, planes):
            assemble(i)
        run(a, b, done, planes - 1)
    run(b, a, 2, planes - 2)
    run(a, b, 3, planes - 3)
    for start in range(4, planes - 4, 4):
        run(b, a, start, start + 4)
        if kind == "wet":
            for i in range(start, start + 4):
                for q in range(chunks):
                    r["out"][i - 4, :, q * 128 : (q + 1) * 128] = a[i, q, 8 : 8 + cy, :]
        else:
            outs += unchunked(a, start, 4, 8, cy, r["out"], x0 + start - 4)
    for made in outs:
        made.wait()


def fluid_call(kind, x0, x1, phi, kappa, up, down, *more):
    cx, cy, cz = phi.shape
    planes = x1 - x0 + 8
    field = jax.ShapeDtypeStruct((cx, cy, cz), F32)
    whole = hbm_specs(1)[0]
    if kind == "wet":
        specs = vmem_specs(4) + any_specs(2)
        out_shape = [
            jax.ShapeDtypeStruct((x1 - x0, cy, cz), F32),
            jax.ShapeDtypeStruct((7, cy + 8, cz), F32),
        ]
        out_specs = vmem_specs(2)
    elif kind == "middle":
        specs, out_shape, out_specs = vmem_specs(2), field, whole
    else:
        specs, out_shape, out_specs = vmem_specs(1) + hbm_specs(1), field, whole
    cells = planes * (cy + 8) * cz
    return pl.pallas_call(
        functools.partial(fluid, x0, x1, cx, cy, cz, kind),
        in_specs=hbm_specs(2) + vmem_specs(2) + specs,
        out_specs=out_specs,
        out_shape=out_shape,
        scratch_shapes=[
            pltpu.VMEM((planes, cz // 128, cy + 24, 128), F32),
            pltpu.VMEM((planes, cz // 128, cy + 24, 128), F32),
            pltpu.VMEM((planes - 2, cz // 128, cy + 8, 128), F32),
            pltpu.SemaphoreType.DMA((80,)),
            pltpu.SemaphoreType.DMA((80,)),
        ],
        input_output_aliases={5: 0} if kind == "end" else {},
        compiler_params=params(),
        cost_estimate=pl.CostEstimate(
            flops=48 * cells, bytes_accessed=12 * cells, transcendentals=0
        ),
        name="fluid_" + kind,
    )(phi, kappa, up, down, *more)


def shifted_pairs(n_gx, n_gy, dx, dy):
    pairs = []
    for gx in range(n_gx):
        for gy in range(n_gy):
            tx, ty = gx + dx, gy + dy
            if 0 <= tx < n_gx and 0 <= ty < n_gy:
                pairs.append((gx * n_gy + gy, tx * n_gy + ty))
    return pairs


def local(phi, kappa, stiffness, face_cell, load_dof, displacement, v_hist, w_hist, r_prev, w_prev):
    n_gx, n_gy = lax.axis_size("gx"), lax.axis_size("gy")
    peers, blk = face_cell.shape[2:]
    cx, cy, cz = phi.shape
    sx, sy = displacement.shape
    hist = v_hist.shape[0]
    wet_planes = cx // 8
    fcell = face_cell.reshape(peers, blk)
    ldof = load_dof.reshape(peers, blk)
    axes = ("gx", "gy")

    def shift(value, dx, dy):
        return lax.ppermute(value, axes, shifted_pairs(n_gx, n_gy, dx, dy))

    def exchange(value):
        return lax.all_to_all(value, axes, split_axis=0, concat_axis=0, tiled=True)

    def call(body, out_shape, scratch, name, specs, *args):
        several = isinstance(out_shape, list)
        return pl.pallas_call(
            body,
            in_specs=specs,
            out_specs=vmem_specs(len(out_shape)) if several else vmem_specs(1)[0],
            out_shape=out_shape,
            scratch_shapes=scratch,
            compiler_params=params(),
            name=name,
        )(*args)

    def f32(*shape):
        return jax.ShapeDtypeStruct(shape, F32)

    sent = call(
        functools.partial(gather_disp, n_gy), f32(peers, 1, 3 * blk),
        [pltpu.VMEM((peers, blk), F32)], "gather_disp", vmem_specs(2), displacement, ldof,
    )
    disp = exchange(sent)
    size = 8 * hist
    gram = call(
        gram_rows, f32(peers, 128),
        [
            pltpu.VMEM((sx // 8, hist, 8, sy), F32), pltpu.VMEM((size, size), F32),
            pltpu.VMEM((size, size), F32),
            pltpu.VMEM((max(128, peers, 2 * peers if peers < hist else 0), 128), F32),
            pltpu.SemaphoreType.DMA((sx // 8,)),
        ],
        "gram_rows", hbm_specs(1), v_hist,
    )
    up_send, down_send, low_send, low_up_send, low_down_send, own = packed(
        phi, kappa, disp, displacement, stiffness, fcell, ldof
    )
    index_planes = -(-2 * (peers // 8) // 8)
    low = shift(low_send, 1, 0)
    up = shift(up_send, 0, -1)
    down = shift(down_send, 0, 1)
    low_up = shift(low_up_send, 1, -1)
    low_down = shift(low_down_send, 1, 1)
    corner = cx + index_planes + 2
    near = shift(
        jnp.concatenate([own[: index_planes + 1], up[corner:], down[corner:]], axis=0), -1, 0
    )

    chunks = cz // 128
    forced = call(
        functools.partial(scatter_disp, cx, cy, cz), f32(wet_planes, cy + 8, cz),
        [
            pltpu.VMEM((wet_planes * cy * chunks, 256), F32),
            pltpu.VMEM((512, wet_planes * 4 * chunks), F32),
        ],
        "scatter_disp", vmem_specs(4), disp, fcell, up, down,
    )
    wet, send = fluid_call(
        "wet", 0, wet_planes, phi, kappa, up, down, forced, low, low_up, low_down, near, gram
    )
    high = shift(send, -1, 0)
    middle = fluid_call("middle", wet_planes, cx - 4, phi, kappa, up, down, forced, wet)
    field = fluid_call("end", cx - 4, cx, phi, kappa, up, down, high, middle)
    press = call(
        functools.partial(gather_press, n_gx, n_gy), f32(peers, 1, (len(NEAR) + 1) * blk),
        [pltpu.VMEM((peers, blk), F32)], "gather_press", vmem_specs(3) + hbm_specs(1),
        wet, fcell, gram, middle,
    )
    loads = exchange(press)
    resp, late = call(
        shell, [f32(sx, sy), f32(peers, 1, 256)],
        [
            pltpu.VMEM((hist, sx, sy), F32),
            pltpu.VMEM((sx * (sy // 128), 256), F32),
            pltpu.VMEM((8 * (sy // 128), 256), F32),
            pltpu.VMEM((sx, 32), F32),
            pltpu.VMEM((16, 32), F32),
            pltpu.VMEM((3, sx + 8, sy + 128), F32),
            pltpu.VMEM((128, 128), F32),
            pltpu.SemaphoreType.DMA((1,)),
        ],
        "shell", vmem_specs(11) + hbm_specs(2),
        loads, ldof, displacement, stiffness, r_prev, up, down, low, low_up, low_down, near,
        v_hist, field,
    )
    x_next = call(
        solve, f32(sx, sy),
        [pltpu.VMEM((hist, sx, sy), F32), pltpu.SemaphoreType.DMA((1,))],
        "solve", vmem_specs(3) + hbm_specs(1), exchange(late), resp, w_prev, w_hist,
    )
    return (field, x_next)


def solution(mesh):
    in_specs = (
        P("gx", "gy", None),
        P("gx", "gy", None),
        P("gx", "gy"),
        P("gx", "gy", None, None),
        P("gx", "gy", None, None),
        P("gx", "gy"),
        P(None, "gx", "gy"),
        P(None, "gx", "gy"),
        P("gx", "gy"),
        P("gx", "gy"),
    )
    out_specs = (P("gx", "gy", None), P("gx", "gy"))
    return jax.shard_map(local, mesh=mesh, in_specs=in_specs, out_specs=out_specs, check_vma=False)
```

```python
import functools

import jax
import jax.numpy as jnp
from jax import lax
from jax.experimental import pallas as pl
from jax.experimental.pallas import tpu as pltpu
from jax.sharding import PartitionSpec as P

NSUB = 4
SWEEPS = 3
HIST = 40
VMEM_BYTES = 50 * 1024 * 1024
F32 = jnp.float32
BF16 = jnp.bfloat16


def params():
    return pltpu.CompilerParams(vmem_limit_bytes=VMEM_BYTES)


def vmem_specs(count):
    return [pl.BlockSpec(memory_space=pltpu.VMEM)] * count


def any_specs(count):
    return [pl.BlockSpec(memory_space=pl.ANY)] * count


def hbm_specs(count):
    return [pl.BlockSpec(memory_space=pltpu.HBM)] * count


def pieces(value, count):
    parts = []
    for _ in range(count):
        part = value.astype(BF16)
        parts.append(part)
        value = value - part.astype(F32)
    return parts


def as_row(block):
    return jnp.concatenate([block[i : i + 1] for i in range(block.shape[0])], axis=1)


def both_rows(row):
    return jnp.broadcast_to(row, (16, row.shape[1])).astype(BF16)


def matches(keys, rows):
    ids = lax.broadcasted_iota(jnp.int32, (16, keys.shape[1]), 0).astype(F32).astype(BF16)
    found = []
    for base in range(0, rows, 256):
        key = both_rows((keys - base).astype(F32))
        for start in range(0, min(256, rows - base), 16):
            found.append(key == ids + jnp.bfloat16(start))
    return found


def one_hot(keys, rows):
    one, zero = jnp.bfloat16(1), jnp.bfloat16(0)
    return jnp.concatenate([jnp.where(m, one, zero) for m in matches(keys, rows)], axis=0)


def select_sum(table, lane, group, rows, parts):
    total = table[:rows]
    for part in range(1, parts):
        total = total + table[part * rows : (part + 1) * rows]
    ids = lax.broadcasted_iota(jnp.int32, total.shape, 0)
    return jnp.sum(jnp.where(ids == lane, total, 0.0), axis=0, keepdims=True)


def pick(table_t, index_ref, out_rows, rows, lane_bits, chunk_bits, parts, step=8):
    lanes = 1 << lane_bits
    for base in range(0, index_ref.shape[0], step):
        index = as_row(index_ref[base : base + step, :])
        lane = index & (lanes - 1)
        keys = ((index >> lane_bits) & ((1 << chunk_bits) - 1)) * rows + (
            index >> (lane_bits + chunk_bits)
        )
        hot = one_hot(keys, rows << chunk_bits)
        found = lax.dot_general(
            table_t, hot, (((1,), (0,)), ((), ())), preferred_element_type=F32
        )
        out_rows(base, select_sum(found, lane, step, lanes, parts))


def spread_values(values, lane, lanes, parts):
    zero = jnp.bfloat16(0)
    found = matches(lane, lanes)
    spread = []
    for part in pieces(values, parts):
        part = both_rows(part.astype(F32))
        spread += [jnp.where(m, part, zero) for m in found]
    return jnp.concatenate(spread, axis=0)


NEAR = ((0, 0), (1, 0), (-1, 0), (0, 1), (0, -1), (1, 1), (1, -1), (-1, 1), (-1, -1))


def tile_of(ref, plane, number):
    at = (number % 8) * 128
    return ref[plane + number // 8, :, at : at + 128]


def starter(sems):
    used = [0]

    def copy(src, dst):
        made = pltpu.make_async_copy(src, dst, sems.at[used[0]])
        used[0] += 1
        made.start()
        return made

    return copy


def gather_disp(n_gy, small_ref, numbers_ref, out_ref, own_ref):
    disp_ref = small_ref.at[0]
    peers, blk = own_ref.shape
    index_ref = numbers_ref.at[pl.ds(peers, peers)]
    sx, sy = disp_ref.shape
    chunk_bits = (sy // 128).bit_length() - 1
    columns = []
    for q in range(sy // 128):
        columns.append(jnp.transpose(disp_ref[:, q * 128 : (q + 1) * 128]))
    table_t = jnp.concatenate(pieces(jnp.concatenate(columns, axis=1), 3), axis=0)

    def write(base, row):
        for i in range(8):
            own_ref[base + i : base + i + 1, :] = row[:, i * blk : (i + 1) * blk]

    pick(table_t, index_ref, write, sx, 7, chunk_bits, 3)
    own = own_ref[...]
    beside = lax.broadcasted_iota(jnp.int32, own.shape, 0) % n_gy
    out_ref[:, 0, 0:blk] = own
    out_ref[:, 0, blk : 2 * blk] = jnp.where(
        beside == n_gy - 1, 0.0, pltpu.roll(own, peers - 1, axis=0)
    )
    out_ref[:, 0, 2 * blk : 3 * blk] = jnp.where(beside == 0, 0.0, pltpu.roll(own, 1, axis=0))


def scatter_disp(cx, cy, cz, disp_ref, numbers_ref, up_ref, down_ref, out_ref, acc_ref, side_ref):
    planes = out_ref.shape[0]
    peers, blk = disp_ref.shape[0], numbers_ref.shape[1]
    cells_ref = numbers_ref.at[pl.ds(0, peers)]
    rows = planes * cy
    chunks = cz // 128
    row_bits = cz.bit_length() - 1
    step = 8
    def accumulate(target, first, left, right):
        added = lax.dot_general(
            left, right, (((1,), (1,)), ((), ())), preferred_element_type=F32
        )
        if first:
            target[...] = added
        else:
            target[...] += added

    for base in range(0, peers, step):
        index = as_row(cells_ref[base : base + step, :])
        values = 0.5 * as_row(disp_ref[base : base + step, 0, 0:blk])
        keys = ((index >> 7) & (chunks - 1)) * rows + (index >> row_bits)
        accumulate(
            acc_ref, base == 0, one_hot(keys, rows * chunks),
            spread_values(values, index & 127, 128, 2),
        )
    for base in range(0, peers, step):
        for side in range(2):
            index = as_row(tile_of(up_ref if side == 0 else down_ref, cx, base // step).astype(jnp.int32))
            values = 0.5 * as_row(
                disp_ref[base : base + step, 0, (side + 1) * blk : (side + 2) * blk]
            )
            row = index >> row_bits
            plane = row // cy
            column = row - plane * cy
            inside = column < 4 if side == 0 else column >= cy - 4
            place = column if side == 0 else column - (cy - 8)
            keys = ((index >> 8) & (chunks // 2 - 1)) * (planes * 8) + plane * 8 + place
            keys = jnp.where(inside, keys, -1)
            accumulate(
                side_ref, base == 0 and side == 0, spread_values(values, index & 255, 256, 2),
                one_hot(keys, planes * 4 * chunks),
            )
    for q in range(chunks):
        part = acc_ref[q * rows : (q + 1) * rows, :]
        out_ref[:, 0:cy, q * 128 : (q + 1) * 128] = (part[:, :128] + part[:, 128:]).reshape(
            planes, cy, 128
        )
    both = jnp.transpose(side_ref[0:256, :] + side_ref[256:512, :])
    for q in range(chunks // 2):
        part = both[q * planes * 8 : (q + 1) * planes * 8, :]
        out_ref[:, cy : cy + 8, q * 256 : (q + 1) * 256] = part.reshape(planes, 8, 256)


def gather_press(n_gx, n_gy, wet_ref, numbers_ref, gram_ref, after_ref, out_ref, own_ref):
    index_ref = numbers_ref.at[pl.ds(0, own_ref.shape[0])]
    planes, cy, cz = wet_ref.shape
    peers, blk = own_ref.shape
    rows = planes * cy
    chunks = cz // 256
    columns = []
    for q in range(chunks):
        part = wet_ref[:, :, q * 256 : (q + 1) * 256].reshape(rows, 256)
        columns.append(jnp.transpose(part))
    table_t = jnp.concatenate(pieces(jnp.concatenate(columns, axis=1), 2), axis=0)

    def write(base, row):
        for i in range(8):
            own_ref[base + i : base + i + 1, :] = row[:, i * blk : (i + 1) * blk]

    pick(table_t, index_ref, write, rows, 8, chunks.bit_length() - 1, 2)
    own = own_ref[...]
    number = lax.broadcasted_iota(jnp.int32, own.shape, 0)
    at_x, at_y = number // n_gy, number % n_gy
    for k, (dx, dy) in enumerate(NEAR):
        ok = (at_x + dx >= 0) & (at_x + dx < n_gx) & (at_y + dy >= 0) & (at_y + dy < n_gy)
        moved = pltpu.roll(own, (-(dx * n_gy + dy)) % peers, axis=0) if k else own
        out_ref[:, 0, k * blk : (k + 1) * blk] = jnp.where(ok, moved, 0.0)
    out_ref[:, 0, len(NEAR) * blk : (len(NEAR) + 1) * blk] = gram_ref[...]


def gram_rows(v_ref, out_ref, v, same, cross, wide, sems):
    hist, sx, sy = v_ref.shape
    tiles = sx // 8
    copy = starter(sems)
    copies = [
        copy(v_ref.at[:, pl.ds(8 * t, 8), :], v.at[t]) for t in range(tiles)
    ]
    for t in range(tiles):
        copies[t].wait()
        high, low = pieces(v[t].reshape(hist * 8, sy), 2)

        def dot(x, y):
            return lax.dot_general(x, y, (((1,), (1,)), ((), ())), preferred_element_type=F32)

        if t == 0:
            same[...] = dot(high, high) + dot(low, low)
            cross[...] = dot(high, low)
        else:
            same[...] += dot(high, high) + dot(low, low)
            cross[...] += dot(high, low)
    size = hist * 8
    row = lax.broadcasted_iota(jnp.int32, (size, size), 0)
    column = lax.broadcasted_iota(jnp.int32, (size, size), 1)
    match = (row & 7) == (column & 7)
    group = (
        lax.broadcasted_iota(jnp.int32, (size, 128), 0) // 8
        == lax.broadcasted_iota(jnp.int32, (size, 128), 1)
    ).astype(F32)

    def reduced(ref):
        part = jnp.sum(jnp.where(match, ref[...], 0.0).reshape(hist, 8, size), axis=1)
        return jnp.dot(part, group, precision=lax.Precision.HIGHEST, preferred_element_type=F32)

    wide[...] = jnp.zeros_like(wide)
    wide[0:hist, :] = reduced(cross)
    turned = jnp.transpose(wide[0:128, :])
    wide[0:128, :] = wide[0:128, :] + turned
    wide[0:hist, :] = wide[0:hist, :] + reduced(same)
    peers = out_ref.shape[0]
    if peers >= hist:
        out_ref[...] = wide[0:peers, :]
    else:
        out_ref[...] = wide[0:peers, :] + pltpu.roll(wide[peers : 2 * peers, :], 64, axis=1)


def shell(recv_ref, numbers_ref, small_ref, up_ref, down_ref, low_ref,
          low_up_ref, low_down_ref, high_ref, v_ref, after_ref, resp_ref, late_ref, v, acc, rows_acc,
          cols_acc, corner_acc, ext, dots, v_sem):
    disp_ref, stiff_ref, prev_ref = small_ref.at[0], small_ref.at[1], small_ref.at[2]
    sx, sy = disp_ref.shape
    peers, blk = recv_ref.shape[0], numbers_ref.shape[1]
    index_ref = numbers_ref.at[pl.ds(peers, peers)]
    load_tiles = peers // 8
    index_planes = -(-2 * load_tiles // 8)
    corner_planes = -(-(load_tiles + 4) // 8)
    chunks = sy // 128
    hist = v_ref.shape[0]
    v_copy = pltpu.make_async_copy(v_ref, v, v_sem.at[0])
    v_copy.start()
    top = up_ref.shape[0] - (index_planes + 2 + corner_planes)
    low_top = low_ref.shape[0] - (index_planes + 1)
    corner_top = low_up_ref.shape[0] - corner_planes
    near_top = index_planes + 1
    load_at = [
        (high_ref, 0, load_tiles), (low_ref, low_top, load_tiles), (up_ref, top, load_tiles),
        (down_ref, top, load_tiles), (high_ref, near_top, 0),
        (high_ref, near_top + corner_planes, 0), (low_up_ref, corner_top, 0),
        (low_down_ref, corner_top, 0),
    ]

    def accumulate(target, first, keys, height, lane, lanes, values):
        added = lax.dot_general(
            one_hot(keys, height), spread_values(values, lane, lanes, 2),
            (((1,), (1,)), ((), ())), preferred_element_type=F32,
        )
        if first:
            target[...] = added
        else:
            target[...] += added

    def values_of(k, base):
        return as_row(recv_ref[base : base + 8, 0, k * blk : (k + 1) * blk])

    for base in range(0, peers, 8):
        index = as_row(index_ref[base : base + 8, :])
        keys = ((index >> 7) & (chunks - 1)) * sx + index // sy
        accumulate(acc, base == 0, keys, sx * chunks, index & 127, 128, values_of(0, base))
    for k, (dx, dy) in enumerate(NEAR):
        if k == 0:
            continue
        for base in range(0, peers, 8):
            ref, plane, number = load_at[k - 1]
            index = as_row(tile_of(ref, plane, number + base // 8).astype(jnp.int32))
            row = index // sy
            lane = index & (sy - 1)
            if dx == 1:
                row8 = jnp.where(row < 4, row, -1)
            elif dx == -1:
                row8 = jnp.where(row >= sx - 4, row - (sx - 8), -1)
            if dy == 1:
                lane8 = jnp.where(lane < 4, lane, -1)
            elif dy == -1:
                lane8 = jnp.where(lane >= sy - 4, lane - (sy - 8), -1)
            values = values_of(k, base)
            if dy == 0:
                keys = jnp.where(row8 < 0, -1, (lane >> 7) * 8 + row8)
                accumulate(
                    rows_acc, k == 1 and base == 0, keys, 8 * chunks, lane & 127, 128, values
                )
            elif dx == 0:
                accumulate(cols_acc, k == 3 and base == 0, row, sx, lane8, 16, values)
            else:
                accumulate(corner_acc, k == 5 and base == 0, row8, 16, lane8, 16, values)

    ids = lax.broadcasted_iota(jnp.int32, (16, 128), 0)
    lanes = lax.broadcasted_iota(jnp.int32, (16, 128), 1)
    placed = (jnp.where(ids < 4, ids, jnp.where(ids < 8, ids + 120, -1)) == lanes).astype(F32)

    def widened(ref):
        both = ref[:, 0:16] + ref[:, 16:32]
        return jnp.dot(both, placed, precision=lax.Precision.HIGHEST, preferred_element_type=F32)

    force, disp, stiff = ext.at[0], ext.at[1], ext.at[2]
    for q in range(chunks):
        at = slice(q * 128, (q + 1) * 128)
        part = acc[q * sx : (q + 1) * sx, :]
        force[0:sx, at] = part[:, 0:128] + part[:, 128:256]
        part = rows_acc[q * 8 : (q + 1) * 8, :]
        force[sx : sx + 8, at] = part[:, 0:128] + part[:, 128:256]
    side = slice(sy, sy + 128)
    force[0:sx, side] = widened(cols_acc)
    force[sx : sx + 8, side] = widened(corner_acc)[0:8]
    sub = lax.broadcasted_iota(jnp.int32, (8, sy), 0) < 4
    sub1 = lax.broadcasted_iota(jnp.int32, (8, 128), 0) < 4
    lane = lax.broadcasted_iota(jnp.int32, (sx, 128), 1)
    lane1 = lax.broadcasted_iota(jnp.int32, (8, 128), 1)
    for kind, (target, own) in enumerate(((disp, disp_ref), (stiff, stiff_ref))):

        def row_tile(ref, plane):
            return ref[plane, :, kind * sy : (kind + 1) * sy]

        def col_tile(ref):
            plane = top + index_planes + 1
            return jnp.concatenate([tile_of(ref, plane, m) for m in range(sx // 8)], axis=0)

        target[0:sx, 0:sy] = own[...]
        target[sx : sx + 8, 0:sy] = jnp.where(
            sub, row_tile(high_ref, index_planes), row_tile(low_ref, low_top + index_planes)
        )
        ahead, behind = col_tile(up_ref), col_tile(down_ref)
        if kind == 0:
            behind = pltpu.roll(behind, 64, axis=1)
        else:
            ahead = pltpu.roll(ahead, 64, axis=1)
        target[0:sx, side] = jnp.where(lane < 32, ahead, jnp.where(lane >= 96, behind, 0.0))

        def corner_tile(ahead, ahead_plane, behind, behind_plane):
            number = load_tiles + 2 * kind
            return jnp.where(
                lane1 < 32, tile_of(ahead, ahead_plane, number),
                jnp.where(lane1 >= 96, tile_of(behind, behind_plane, number + 1), 0.0),
            )

        target[sx : sx + 8, side] = jnp.where(
            sub1, corner_tile(high_ref, near_top, high_ref, near_top + corner_planes),
            corner_tile(low_up_ref, corner_top, low_down_ref, corner_top),
        )

    load = force[...]
    k = stiff[...]
    diag = 1.0 + 4.0 * k
    scale = 0.8 / diag
    resp = disp[...]
    high, wide = sx + 8, sy + 128
    for sweep in range(SWEEPS):
        beside = (pltpu.roll(resp, 1, axis=0) + pltpu.roll(resp, high - 1, axis=0)) + (
            pltpu.roll(resp, 1, axis=1) + pltpu.roll(resp, wide - 1, axis=1)
        )
        resp = resp + scale * (load - (diag * resp - k * beside))
    own = resp[0:sx, 0:sy]
    resp_ref[...] = own
    resid = own - disp_ref[...]
    newest = resid - prev_ref[...]
    dots[...] = jnp.zeros_like(dots)

    def folded(value):
        total = value[0:8]
        for t in range(1, sx // 8):
            total = total + value[8 * t : 8 * t + 8]
        out = total[:, 0:128]
        for q in range(1, chunks):
            out = out + total[:, q * 128 : (q + 1) * 128]
        return jnp.sum(out, axis=0, keepdims=True)

    dots[0:1, :] = folded(newest * newest)
    dots[64:65, :] = folded(resid * newest)
    v_copy.wait()
    for number in range(1, hist):
        column = v[number]
        dots[number : number + 1, :] = folded(column * newest)
        dots[64 + number : 65 + number, :] = folded(column * resid)
    late = lax.dot_general(
        jnp.ones((8, 128), F32), dots[...], (((1,), (1,)), ((), ())),
        precision=lax.Precision.HIGHEST, preferred_element_type=F32,
    )
    gram_at = len(NEAR) * blk
    gram = jnp.sum(recv_ref[:, 0, gram_at : gram_at + 128], axis=0, keepdims=True)
    late_ref[:, 0, 0:128] = jnp.broadcast_to(late[0:1], (peers, 128))
    late_ref[:, 0, 128:256] = jnp.broadcast_to(gram, (peers, 128))


def solve(recv_ref, resp_ref, small_ref, w_ref, out_ref, w, sems):
    peers = recv_ref.shape[0]
    hist = w_ref.shape[0]
    prev_ref = small_ref.at[3]
    sx, sy = resp_ref.shape
    w_copy = pltpu.make_async_copy(w_ref, w, sems.at[0])
    w_copy.start()
    late = jnp.sum(recv_ref[:, 0, 0:128], axis=0, keepdims=True)
    rows = recv_ref[:, 0, 128:256]
    if peers >= hist:
        gram = rows[0:hist]
    else:
        gram = jnp.concatenate(
            [rows, pltpu.roll(rows, 64, axis=1)[0 : hist - peers]], axis=0
        )
    row = lax.broadcasted_iota(jnp.int32, (hist, 128), 0)
    lane = lax.broadcasted_iota(jnp.int32, (hist, 128), 1)
    turned = jnp.transpose(jnp.broadcast_to(late, (128, 128)))
    gram = jnp.where(row == 0, jnp.broadcast_to(late, (hist, 128)), gram)
    gram = jnp.where(lane == 0, turned[0:hist], gram)
    gram = jnp.where(lane < hist, gram, 0.0)
    unit = row == lane
    trace = jnp.sum(jnp.where(unit, gram, 0.0), keepdims=True)
    a = gram + jnp.where(unit, 0.001 * trace / hist, 0.0)
    a = jnp.where(lane == 64, -turned[64 : 64 + hist], a)
    for j in range(hist):
        column = jnp.broadcast_to(a[:, j : j + 1], (hist, 128))
        scaled = a[j : j + 1, :] / column[j : j + 1, :]
        a = jnp.where(row == j, scaled, a - column * scaled)
    coef = jnp.broadcast_to(a[:, 64:65], (hist, 128))
    coef = jnp.concatenate([coef] * (sy // 128), axis=1)
    resp = resp_ref[...]
    total = resp + coef[0:1] * (resp - prev_ref[...])
    w_copy.wait()
    for number in range(1, hist):
        total = total + coef[number : number + 1] * w[number]
    out_ref[...] = total


def pack(phi_ref, kappa_ref, after_ref, small_ref, numbers_ref, up_ref, down_ref, low_ref, low_up_ref, low_down_ref, own_ref, phi_lo, kap_lo, phi_hi,
         kap_hi, in_sems):
    cx, cy, cz = phi_ref.shape
    disp_ref, stiff_ref = small_ref.at[0], small_ref.at[1]
    sx, sy = disp_ref.shape
    peers = numbers_ref.shape[0] // 2
    cells_ref, loads_ref = numbers_ref.at[pl.ds(0, peers)], numbers_ref.at[pl.ds(peers, peers)]
    tiles = peers // 8
    index_planes = -(-2 * tiles // 8)
    corner_planes = -(-(tiles + 4) // 8)
    copy_in = starter(in_sems)
    depth = 8
    lows = []
    for n, (ref, x) in enumerate(
        [(phi_ref, x) for x in range(cx - 4, cx)] + [(kappa_ref, x) for x in range(cx - 3, cx)]
    ):
        for t in range(cy // 8):
            lows.append(copy_in(ref.at[x, pl.ds(8 * t, 8)], low_ref.at[n * (cy // 8) + t]))
    groups = []
    for x in range(0, cx, depth):
        at = pl.ds(x, depth)
        groups.append([
            copy_in(phi_ref.at[at, pl.ds(0, 8)], phi_lo.at[at]),
            copy_in(kappa_ref.at[at, pl.ds(0, 8)], kap_lo.at[at]),
            copy_in(phi_ref.at[at, pl.ds(cy - 8, 8)], phi_hi.at[at]),
            copy_in(kappa_ref.at[at, pl.ds(cy - 8, 8)], kap_hi.at[at]),
        ])
    own_ref[...] = jnp.zeros_like(own_ref)

    def put(plane, number, tile):
        own_ref[plane + number // 8, :, (number % 8) * 128 : (number % 8 + 1) * 128] = tile

    corner = index_planes + 2
    for n in range(tiles):
        put(0, n, cells_ref[8 * n : 8 * n + 8, :].astype(F32))
        loads = loads_ref[8 * n : 8 * n + 8, :].astype(F32)
        put(0, tiles + n, loads)
        put(corner, n, loads)
    sub = lax.broadcasted_iota(jnp.int32, (8, sy), 0) < 4
    for kind, ref in enumerate((disp_ref, stiff_ref)):
        edge = jnp.where(sub, ref[0:8, :], ref[sx - 8 : sx, :])
        own_ref[index_planes, :, kind * sy : (kind + 1) * sy] = edge
        put(corner, tiles + 2 * kind, edge[:, 0:128])
        put(corner, tiles + 2 * kind + 1, edge[:, sy - 128 : sy])
    lane = lax.broadcasted_iota(jnp.int32, (sx, 128), 1)
    first, final = slice(0, 128), slice(sy - 128, sy)
    columns = jnp.where(
        lane < 32, disp_ref[:, first],
        jnp.where(
            lane < 64, pltpu.roll(disp_ref[:, final], 64, axis=1),
            jnp.where(lane < 96, pltpu.roll(stiff_ref[:, first], 64, axis=1), stiff_ref[:, final]),
        ),
    )
    for m in range(sx // 8):
        put(index_planes + 1, m, columns[8 * m : 8 * m + 8, :])
    own = own_ref[...]
    up_ref[cx:] = own
    down_ref[cx:] = own
    low_ref[7 * (cy // 8) :] = own[: index_planes + 1]
    low_up_ref[3:] = own[corner:]
    low_down_ref[3:] = own[corner:]
    upper = lax.broadcasted_iota(jnp.int32, (depth, 8, cz), 1) < 4
    for number, copies in enumerate(groups):
        for made in copies:
            made.wait()
        at = slice(number * depth, (number + 1) * depth)
        up = jnp.where(upper, phi_lo[at], pltpu.roll(kap_lo[at], 4, axis=1))
        down = jnp.where(upper, pltpu.roll(kap_hi[at], 4, axis=1), phi_hi[at])
        up_ref[at] = up
        down_ref[at] = down
        if (number + 1) * depth == cx:
            low_up_ref[0:3] = up[depth - 3 :]
            low_down_ref[0:3] = down[depth - 3 :]
    for made in lows:
        made.wait()


def packed(phi, kappa, after, small, numbers):
    cx, cy, cz = phi.shape
    tiles = numbers.shape[0] // 16
    index_planes = -(-2 * tiles // 8)
    corner_planes = -(-(tiles + 4) // 8)
    extra = index_planes + 2 + corner_planes
    low_planes = 7 * (cy // 8)

    def shape(planes):
        return jax.ShapeDtypeStruct((planes, 8, cz), F32)

    return pl.pallas_call(
        pack,
        in_specs=hbm_specs(2) + any_specs(1) + vmem_specs(2),
        out_specs=vmem_specs(6),
        out_shape=[
            shape(cx + extra), shape(cx + extra), shape(low_planes + index_planes + 1),
            shape(3 + corner_planes), shape(3 + corner_planes), shape(extra),
        ],
        scratch_shapes=[pltpu.VMEM((cx, 8, cz), F32)] * 4
        + [pltpu.SemaphoreType.DMA((cx // 2 + low_planes,))],
        compiler_params=params(),
        name="pack",
    )(phi, kappa, after, small, numbers)


def band(ref):
    row = lax.broadcasted_iota(jnp.int32, (256, 256), 0)
    column = lax.broadcasted_iota(jnp.int32, (256, 256), 1)
    inner = jnp.where(jnp.abs(row - column) == 1, 1.0, 0.0).astype(BF16)
    row, column = row[0:128], column[0:128]
    target = jnp.where(row == 0, 255, jnp.where(row == 127, 0, -1))
    outer = jnp.where(column == target, 1.0, 0.0).astype(BF16)
    ref[...] = jnp.concatenate([inner, inner, outer, outer], axis=0)


def substeps(src, kap, dst, near, plane, count, advect, cy, cz):
    wide = cy + 8
    chunks = cz // 128
    ahead = lax.broadcasted_iota(jnp.int32, (wide, 128), 1) < 64

    def take(at, q, start=8):
        return src[at, q, pl.ds(start, wide), :]

    own, edge = [], []
    zero = jnp.zeros((wide, 128), F32)
    for p in range(count):
        for q in range(0, chunks, 2):
            own.append(jnp.concatenate([take(plane + p, q), take(plane + p, q + 1)], axis=1))
            before = take(plane + p, q - 1) if q else zero
            after = take(plane + p, q + 2) if q + 2 < chunks else zero
            edge.append(jnp.where(ahead, after, before))
    parts = pieces(jnp.concatenate(own, axis=0), 2) + pieces(jnp.concatenate(edge, axis=0), 2)
    beside = jnp.dot(jnp.concatenate(parts, axis=1), near[...], preferred_element_type=F32)
    for p in range(count):
        at = plane + p
        for q in range(chunks):
            now = take(at, q)
            row = (p * chunks + q) // 2 * wide
            lane = q % 2 * 128
            total = beside[row : row + wide, lane : lane + 128]
            total = total + (take(at, q, 7) + take(at, q, 9))
            before = take(at - 1, q)
            total = total + (before + take(at + 1, q))
            k = kap[at - 1, :, q * 128 : (q + 1) * 128]
            new = now + advect(at) * (before - now) + k * (total - 6.0 * now)
            dst[at, q, 8 : 8 + wide, :] = new
            dst[at, q, 7:8, :] = new[wide - 1 :]
            dst[at, q, 8 + wide : 9 + wide, :] = new[0:1]


def fluid(x0, x1, cx, cy, cz, kind, *refs):
    planes = x1 - x0 + 8
    wide = cy + 8
    chunks = cz // 128
    names = ["phi", "kappa", "up", "down"]
    names += {"wet": ["forced", "low", "low_up", "low_down", "near", "gram"],
              "middle": ["forced", "wet"], "end": ["high", "whole"]}[kind]
    names += {"wet": ["out", "send"]}.get(kind, ["out"])
    names += ["a", "b", "kap", "stage", "near_lanes", "sems", "out_sems"]
    r = dict(zip(names, refs))
    a, b, kap, stage = r["a"], r["b"], r["kap"], r["stage"]
    is_last = lax.axis_index("gx") == lax.axis_size("gx") - 1
    copy, copy_out = starter(r["sems"]), starter(r["out_sems"])

    def unchunked(src, s0, count, row, rows, dst, d0):
        return [
            copy_out(
                src.at[pl.ds(s0, count), q, pl.ds(row, rows)],
                dst.at[pl.ds(d0, count), :, pl.ds(q * 128, 128)],
            )
            for q in range(chunks)
        ]

    own0, own1 = max(0, x0 - 4), min(cx, x1 + 4)
    groups = []
    start = own0
    while start < own1:
        count = min(4, own1 - start)
        i = start - (x0 - 4)
        k0, k1 = max(start, x0 - 3), min(start + count, x1 + 3)
        groups.append((i, i + count, [
            copy(r["phi"].at[pl.ds(start, count)], stage.at[pl.ds(start - own0, count)]),
            copy(r["kappa"].at[pl.ds(k0, k1 - k0)],
                 kap.at[pl.ds(k0 - (x0 - 3), k1 - k0), pl.ds(0, cy)]),
        ]))
        start += count
    outs = []
    if kind == "middle":
        outs.append(copy_out(r["wet"], r["out"].at[pl.ds(0, x0)]))

    upper = lax.broadcasted_iota(jnp.int32, (8, cz), 0) < 4

    def assemble(i):
        x = x0 - 4 + i
        inner = 1 <= i < planes - 1
        if x >= cx:
            for q in range(chunks):
                at = slice(q * 128, (q + 1) * 128)
                a[i, q, 8 : 8 + wide, :] = r["high"][x - cx, :, at]
                if inner:
                    kap[i - 1, :, at] = r["high"][4 + x - cx, :, at]
        else:
            if x >= 0:
                up, down = r["up"][x], r["down"][x]
            elif x > -4:
                up, down = r["low_up"][x + 3], r["low_down"][x + 3]
            else:
                up = down = jnp.zeros((8, cz), F32)
            edge = jnp.where(upper, up, down)
            kedge = pltpu.roll(jnp.where(upper, down, up), 4, axis=0)
            for q in range(chunks):
                at = slice(q * 128, (q + 1) * 128)
                if x < 0:
                    for t in range(cy // 8):
                        a[i, q, 8 + 8 * t : 16 + 8 * t, :] = r["low"][(x + 4) * (cy // 8) + t, :, at]
                        if inner:
                            kap[i - 1, 8 * t : 8 * t + 8, at] = r["low"][
                                (x + 7) * (cy // 8) + t, :, at
                            ]
                else:
                    a[i, q, 8 : 8 + cy, :] = stage[x - own0, :, at]
                a[i, q, 8 + cy : 8 + wide, :] = edge[:, at]
                if inner:
                    kap[i - 1, cy:wide, at] = kedge[:, at]
                if "forced" in r and 0 <= x < r["forced"].shape[0]:
                    a[i, q, 8 : 8 + wide, :] = a[i, q, 8 : 8 + wide, :] + r["forced"][x, :, at]
        for q in range(chunks):
            a[i, q, 7:8, :] = a[i, q, 7 + wide : 8 + wide, :]
            a[i, q, 8 + wide : 9 + wide, :] = a[i, q, 8:9, :]

    band(r["near_lanes"])

    def advect(i):
        if kind != "end":
            return 0.25
        return jnp.where(jnp.logical_and(is_last, i + (x0 - 4) >= cx), 0.0, 0.25)

    def run(src, dst, lo, hi):
        def body(n, carry):
            substeps(src, kap, dst, r["near_lanes"], lo + 2 * n, 2, advect, cy, cz)
            return carry

        if hi > lo:
            lax.fori_loop(0, (hi - lo) // 2, body, 0)

    if kind == "wet":
        for i in range(4):
            assemble(i)
    done = 1
    for i0, i1, copies in groups:
        for made in copies:
            made.wait()
        for i in range(i0, i1):
            assemble(i)
        if kind == "wet":
            for i in range(4, 8):
                for q in range(chunks):
                    at = slice(q * 128, (q + 1) * 128)
                    r["send"][i - 4, :, at] = a[i, q, 8 : 8 + wide, :]
                    if i < 7:
                        r["send"][i, :, at] = kap[i - 1, :, at]
        ready = done + (i1 - 1 - done) // 2 * 2
        run(a, b, done, ready)
        done = ready
    if kind == "end":
        for i in range(planes - 4, planes):
            assemble(i)
        run(a, b, done, planes - 1)
    run(b, a, 2, planes - 2)
    run(a, b, 3, planes - 3)
    for start in range(4, planes - 4, 4):
        run(b, a, start, start + 4)
        if kind == "wet":
            for i in range(start, start + 4):
                for q in range(chunks):
                    r["out"][i - 4, :, q * 128 : (q + 1) * 128] = a[i, q, 8 : 8 + cy, :]
        else:
            outs += unchunked(a, start, 4, 8, cy, r["out"], x0 + start - 4)
    for made in outs:
        made.wait()


def fluid_call(kind, x0, x1, phi, kappa, up, down, *more):
    cx, cy, cz = phi.shape
    planes = x1 - x0 + 8
    field = jax.ShapeDtypeStruct((cx, cy, cz), F32)
    whole = hbm_specs(1)[0]
    if kind == "wet":
        specs = vmem_specs(4) + any_specs(2)
        out_shape = [
            jax.ShapeDtypeStruct((x1 - x0, cy, cz), F32),
            jax.ShapeDtypeStruct((7, cy + 8, cz), F32),
        ]
        out_specs = vmem_specs(2)
    elif kind == "middle":
        specs, out_shape, out_specs = vmem_specs(2), field, whole
    else:
        specs, out_shape, out_specs = vmem_specs(1) + hbm_specs(1), field, whole
    cells = planes * (cy + 8) * cz
    return pl.pallas_call(
        functools.partial(fluid, x0, x1, cx, cy, cz, kind),
        in_specs=hbm_specs(2) + vmem_specs(2) + specs,
        out_specs=out_specs,
        out_shape=out_shape,
        scratch_shapes=[
            pltpu.VMEM((planes, cz // 128, cy + 24, 128), F32),
            pltpu.VMEM((planes, cz // 128, cy + 24, 128), F32),
            pltpu.VMEM((planes - 2, cy + 8, cz), F32),
            pltpu.VMEM((min(cx, x1 + 4) - max(0, x0 - 4), cy, cz), F32),
            pltpu.VMEM((768, 256), BF16),
            pltpu.SemaphoreType.DMA((80,)),
            pltpu.SemaphoreType.DMA((80,)),
        ],
        input_output_aliases={5: 0} if kind == "end" else {},
        compiler_params=params(),
        cost_estimate=pl.CostEstimate(
            flops=48 * cells, bytes_accessed=12 * cells, transcendentals=0
        ),
        name="fluid_" + kind,
    )(phi, kappa, up, down, *more)


def held_for(awaited, *arrays):
    def nothing(*refs):
        pass

    return pl.pallas_call(
        nothing,
        in_specs=any_specs(1 + len(arrays)),
        out_specs=any_specs(len(arrays)),
        out_shape=[jax.ShapeDtypeStruct(a.shape, a.dtype) for a in arrays],
        input_output_aliases={i + 1: i for i in range(len(arrays))},
        name="held",
    )(awaited, *arrays)


def shifted_pairs(n_gx, n_gy, dx, dy):
    pairs = []
    for gx in range(n_gx):
        for gy in range(n_gy):
            tx, ty = gx + dx, gy + dy
            if 0 <= tx < n_gx and 0 <= ty < n_gy:
                pairs.append((gx * n_gy + gy, tx * n_gy + ty))
    return pairs


def local(phi, kappa, stiffness, face_cell, load_dof, displacement, v_hist, w_hist, r_prev, w_prev):
    n_gx, n_gy = lax.axis_size("gx"), lax.axis_size("gy")
    peers, blk = face_cell.shape[2:]
    cx, cy, cz = phi.shape
    sx, sy = displacement.shape
    hist = v_hist.shape[0]
    wet_planes = cx // 8
    fcell = face_cell.reshape(peers, blk)
    ldof = load_dof.reshape(peers, blk)
    axes = ("gx", "gy")

    def shift(value, dx, dy):
        return lax.ppermute(value, axes, shifted_pairs(n_gx, n_gy, dx, dy))

    def exchange(value):
        return lax.all_to_all(value, axes, split_axis=0, concat_axis=0, tiled=True)

    def call(body, out_shape, scratch, name, specs, *args):
        several = isinstance(out_shape, list)
        return pl.pallas_call(
            body,
            in_specs=specs,
            out_specs=vmem_specs(len(out_shape)) if several else vmem_specs(1)[0],
            out_shape=out_shape,
            scratch_shapes=scratch,
            compiler_params=params(),
            name=name,
        )(*args)

    def f32(*shape):
        return jax.ShapeDtypeStruct(shape, F32)

    small = jnp.stack([displacement, stiffness, r_prev, w_prev])
    numbers = jnp.concatenate([fcell, ldof], axis=0)
    sent = call(
        functools.partial(gather_disp, n_gy), f32(peers, 1, 3 * blk),
        [pltpu.VMEM((peers, blk), F32)], "gather_disp", vmem_specs(2), small, numbers,
    )
    disp = exchange(sent)
    size = 8 * hist
    gram = call(
        gram_rows, f32(peers, 128),
        [
            pltpu.VMEM((sx // 8, hist, 8, sy), F32), pltpu.VMEM((size, size), F32),
            pltpu.VMEM((size, size), F32),
            pltpu.VMEM((max(128, peers, 2 * peers if peers < hist else 0), 128), F32),
            pltpu.SemaphoreType.DMA((sx // 8,)),
        ],
        "gram_rows", hbm_specs(1), v_hist,
    )
    up_send, down_send, low_send, low_up_send, low_down_send, own = packed(
        phi, kappa, sent, small, numbers
    )
    index_planes = -(-2 * (peers // 8) // 8)
    up_send, down_send, low_send, low_up_send, low_down_send = held_for(
        disp, up_send, down_send, low_send, low_up_send, low_down_send
    )
    low = shift(low_send, 1, 0)
    up = shift(up_send, 0, -1)
    down = shift(down_send, 0, 1)
    low_up = shift(low_up_send, 1, -1)
    low_down = shift(low_down_send, 1, 1)
    corner = cx + index_planes + 2
    near = shift(
        jnp.concatenate([own[: index_planes + 1], up[corner:], down[corner:]], axis=0), -1, 0
    )

    chunks = cz // 128
    forced = call(
        functools.partial(scatter_disp, cx, cy, cz), f32(wet_planes, cy + 8, cz),
        [
            pltpu.VMEM((wet_planes * cy * chunks, 256), F32),
            pltpu.VMEM((512, wet_planes * 4 * chunks), F32),
        ],
        "scatter_disp", vmem_specs(4), disp, numbers, up, down,
    )
    wet, send = fluid_call(
        "wet", 0, wet_planes, phi, kappa, up, down, forced, low, low_up, low_down, near, gram
    )
    high = shift(send, -1, 0)
    middle = fluid_call("middle", wet_planes, cx - 4, phi, kappa, up, down, forced, wet)
    field = fluid_call("end", cx - 4, cx, phi, kappa, up, down, high, middle)
    press = call(
        functools.partial(gather_press, n_gx, n_gy), f32(peers, 1, (len(NEAR) + 1) * blk),
        [pltpu.VMEM((peers, blk), F32)], "gather_press", vmem_specs(3) + hbm_specs(1),
        wet, numbers, gram, middle,
    )
    loads = exchange(press)
    resp, late = call(
        shell, [f32(sx, sy), f32(peers, 1, 256)],
        [
            pltpu.VMEM((hist, sx, sy), F32),
            pltpu.VMEM((sx * (sy // 128), 256), F32),
            pltpu.VMEM((8 * (sy // 128), 256), F32),
            pltpu.VMEM((sx, 32), F32),
            pltpu.VMEM((16, 32), F32),
            pltpu.VMEM((3, sx + 8, sy + 128), F32),
            pltpu.VMEM((128, 128), F32),
            pltpu.SemaphoreType.DMA((1,)),
        ],
        "shell", vmem_specs(9) + hbm_specs(2),
        loads, numbers, small, up, down, low, low_up, low_down, near,
        v_hist, field,
    )
    x_next = call(
        solve, f32(sx, sy),
        [pltpu.VMEM((hist, sx, sy), F32), pltpu.SemaphoreType.DMA((1,))],
        "solve", vmem_specs(3) + hbm_specs(1), exchange(late), resp, small, w_hist,
    )
    return (field, x_next)


def solution(mesh):
    in_specs = (
        P("gx", "gy", None),
        P("gx", "gy", None),
        P("gx", "gy"),
        P("gx", "gy", None, None),
        P("gx", "gy", None, None),
        P("gx", "gy"),
        P(None, "gx", "gy"),
        P(None, "gx", "gy"),
        P("gx", "gy"),
        P("gx", "gy"),
    )
    out_specs = (P("gx", "gy", None), P("gx", "gy"))
    return jax.shard_map(local, mesh=mesh, in_specs=in_specs, out_specs=out_specs, check_vma=False)
```

```python
import functools

import jax
import jax.numpy as jnp
from jax import lax
from jax.experimental import pallas as pl
from jax.experimental.pallas import tpu as pltpu
from jax.sharding import PartitionSpec as P

NSUB = 4
SWEEPS = 3
HIST = 40
VMEM_BYTES = 50 * 1024 * 1024
F32 = jnp.float32
BF16 = jnp.bfloat16


def params():
    return pltpu.CompilerParams(vmem_limit_bytes=VMEM_BYTES)


def vmem_specs(count):
    return [pl.BlockSpec(memory_space=pltpu.VMEM)] * count


def any_specs(count):
    return [pl.BlockSpec(memory_space=pl.ANY)] * count


def hbm_specs(count):
    return [pl.BlockSpec(memory_space=pltpu.HBM)] * count


def pieces(value, count):
    parts = []
    for _ in range(count):
        part = value.astype(BF16)
        parts.append(part)
        value = value - part.astype(F32)
    return parts


def as_row(block):
    return jnp.concatenate([block[i : i + 1] for i in range(block.shape[0])], axis=1)


def both_rows(row):
    return jnp.broadcast_to(row, (16, row.shape[1])).astype(BF16)


def matches(keys, rows):
    ids = lax.broadcasted_iota(jnp.int32, (16, keys.shape[1]), 0).astype(F32).astype(BF16)
    found = []
    for base in range(0, rows, 256):
        key = both_rows((keys - base).astype(F32))
        for start in range(0, min(256, rows - base), 16):
            found.append(key == ids + jnp.bfloat16(start))
    return found


def one_hot(keys, rows):
    one, zero = jnp.bfloat16(1), jnp.bfloat16(0)
    return jnp.concatenate([jnp.where(m, one, zero) for m in matches(keys, rows)], axis=0)


def select_sum(table, lane, group, rows, parts):
    total = table[:rows]
    for part in range(1, parts):
        total = total + table[part * rows : (part + 1) * rows]
    ids = lax.broadcasted_iota(jnp.int32, total.shape, 0)
    return jnp.sum(jnp.where(ids == lane, total, 0.0), axis=0, keepdims=True)


def pick(table_t, index_ref, out_rows, rows, lane_bits, chunk_bits, parts, step=8):
    lanes = 1 << lane_bits
    for base in range(0, index_ref.shape[0], step):
        index = as_row(index_ref[base : base + step, :])
        lane = index & (lanes - 1)
        keys = ((index >> lane_bits) & ((1 << chunk_bits) - 1)) * rows + (
            index >> (lane_bits + chunk_bits)
        )
        hot = one_hot(keys, rows << chunk_bits)
        found = lax.dot_general(
            table_t, hot, (((1,), (0,)), ((), ())), preferred_element_type=F32
        )
        out_rows(base, select_sum(found, lane, step, lanes, parts))


def spread_values(values, lane, lanes, parts):
    zero = jnp.bfloat16(0)
    found = matches(lane, lanes)
    spread = []
    for part in pieces(values, parts):
        part = both_rows(part.astype(F32))
        spread += [jnp.where(m, part, zero) for m in found]
    return jnp.concatenate(spread, axis=0)


NEAR = ((0, 0), (1, 0), (-1, 0), (0, 1), (0, -1), (1, 1), (1, -1), (-1, 1), (-1, -1))


def tile_of(ref, plane, number):
    at = (number % 8) * 128
    return ref[plane + number // 8, :, at : at + 128]


def starter(sems):
    used = [0]

    def copy(src, dst):
        made = pltpu.make_async_copy(src, dst, sems.at[used[0]])
        used[0] += 1
        made.start()
        return made

    return copy


def gather_disp(n_gy, small_ref, numbers_ref, out_ref, own_ref):
    disp_ref = small_ref.at[0]
    peers, blk = own_ref.shape
    index_ref = numbers_ref.at[pl.ds(peers, peers)]
    sx, sy = disp_ref.shape
    chunk_bits = (sy // 128).bit_length() - 1
    columns = []
    for q in range(sy // 128):
        columns.append(jnp.transpose(disp_ref[:, q * 128 : (q + 1) * 128]))
    table_t = jnp.concatenate(pieces(jnp.concatenate(columns, axis=1), 3), axis=0)

    def write(base, row):
        for i in range(8):
            own_ref[base + i : base + i + 1, :] = row[:, i * blk : (i + 1) * blk]

    pick(table_t, index_ref, write, sx, 7, chunk_bits, 3)
    own = own_ref[...]
    beside = lax.broadcasted_iota(jnp.int32, own.shape, 0) % n_gy
    out_ref[:, 0, 0:blk] = own
    out_ref[:, 0, blk : 2 * blk] = jnp.where(
        beside == n_gy - 1, 0.0, pltpu.roll(own, peers - 1, axis=0)
    )
    out_ref[:, 0, 2 * blk : 3 * blk] = jnp.where(beside == 0, 0.0, pltpu.roll(own, 1, axis=0))


def scatter_disp(cx, cy, cz, disp_ref, numbers_ref, up_ref, down_ref, phi_ref, kappa_ref, out_ref,
                 acc_ref, side_ref, stage, kstage, sems):
    planes = stage.shape[0]
    copy = starter(sems)
    copies = [
        copy(phi_ref.at[pl.ds(0, planes)], stage),
        copy(kappa_ref.at[pl.ds(0, planes - 1)], kstage),
    ]
    peers, blk = disp_ref.shape[0], numbers_ref.shape[1]
    cells_ref = numbers_ref.at[pl.ds(0, peers)]
    rows = planes * cy
    chunks = cz // 128
    row_bits = cz.bit_length() - 1
    step = 8
    def accumulate(target, first, left, right):
        added = lax.dot_general(
            left, right, (((1,), (1,)), ((), ())), preferred_element_type=F32
        )
        if first:
            target[...] = added
        else:
            target[...] += added

    for base in range(0, peers, step):
        index = as_row(cells_ref[base : base + step, :])
        values = 0.5 * as_row(disp_ref[base : base + step, 0, 0:blk])
        keys = ((index >> 7) & (chunks - 1)) * rows + (index >> row_bits)
        accumulate(
            acc_ref, base == 0, one_hot(keys, rows * chunks),
            spread_values(values, index & 127, 128, 2),
        )
    for base in range(0, peers, step):
        for side in range(2):
            index = as_row(tile_of(up_ref if side == 0 else down_ref, cx, base // step).astype(jnp.int32))
            values = 0.5 * as_row(
                disp_ref[base : base + step, 0, (side + 1) * blk : (side + 2) * blk]
            )
            row = index >> row_bits
            plane = row // cy
            column = row - plane * cy
            inside = column < 4 if side == 0 else column >= cy - 4
            place = column if side == 0 else column - (cy - 8)
            keys = ((index >> 8) & (chunks // 2 - 1)) * (planes * 8) + plane * 8 + place
            keys = jnp.where(inside, keys, -1)
            accumulate(
                side_ref, base == 0 and side == 0, spread_values(values, index & 255, 256, 2),
                one_hot(keys, planes * 4 * chunks),
            )
    for made in copies:
        made.wait()
    upper = lax.broadcasted_iota(jnp.int32, (8, cz), 0) < 4
    for x in range(planes):
        up, down = up_ref[x], down_ref[x]
        out_ref[x, cy : cy + 8, :] = jnp.where(upper, up, down)
        if x < planes - 1:
            out_ref[planes + x, 0:cy, :] = kstage[x]
            out_ref[planes + x, cy : cy + 8, :] = pltpu.roll(
                jnp.where(upper, down, up), 4, axis=0
            )
    for q in range(chunks):
        part = acc_ref[q * rows : (q + 1) * rows, :]
        at = slice(q * 128, (q + 1) * 128)
        out_ref[0:planes, 0:cy, at] = stage[:, :, at] + (part[:, :128] + part[:, 128:]).reshape(
            planes, cy, 128
        )
    both = jnp.transpose(side_ref[0:256, :] + side_ref[256:512, :])
    for q in range(chunks // 2):
        part = both[q * planes * 8 : (q + 1) * planes * 8, :]
        at = slice(q * 256, (q + 1) * 256)
        out_ref[0:planes, cy : cy + 8, at] = out_ref[0:planes, cy : cy + 8, at] + part.reshape(
            planes, 8, 256
        )


def gather_press(n_gx, n_gy, wet_ref, numbers_ref, gram_ref, out_ref, own_ref):
    index_ref = numbers_ref.at[pl.ds(0, own_ref.shape[0])]
    planes, cy, cz = wet_ref.shape
    peers, blk = own_ref.shape
    rows = planes * cy
    chunks = cz // 256
    columns = []
    for q in range(chunks):
        part = wet_ref[:, :, q * 256 : (q + 1) * 256].reshape(rows, 256)
        columns.append(jnp.transpose(part))
    table_t = jnp.concatenate(pieces(jnp.concatenate(columns, axis=1), 2), axis=0)

    def write(base, row):
        for i in range(8):
            own_ref[base + i : base + i + 1, :] = row[:, i * blk : (i + 1) * blk]

    pick(table_t, index_ref, write, rows, 8, chunks.bit_length() - 1, 2)
    own = own_ref[...]
    number = lax.broadcasted_iota(jnp.int32, own.shape, 0)
    at_x, at_y = number // n_gy, number % n_gy
    for k, (dx, dy) in enumerate(NEAR):
        ok = (at_x + dx >= 0) & (at_x + dx < n_gx) & (at_y + dy >= 0) & (at_y + dy < n_gy)
        moved = pltpu.roll(own, (-(dx * n_gy + dy)) % peers, axis=0) if k else own
        out_ref[:, 0, k * blk : (k + 1) * blk] = jnp.where(ok, moved, 0.0)
    out_ref[:, 0, len(NEAR) * blk : (len(NEAR) + 1) * blk] = gram_ref[...]


def gram_rows(v_ref, out_ref, v, same, cross, wide, sems):
    hist, sx, sy = v_ref.shape
    tiles = sx // 8
    copy = starter(sems)
    copies = [
        copy(v_ref.at[:, pl.ds(8 * t, 8), :], v.at[t]) for t in range(tiles)
    ]
    for t in range(tiles):
        copies[t].wait()
        high, low = pieces(v[t].reshape(hist * 8, sy), 2)

        def dot(x, y):
            return lax.dot_general(x, y, (((1,), (1,)), ((), ())), preferred_element_type=F32)

        if t == 0:
            same[...] = dot(high, high) + dot(low, low)
            cross[...] = dot(high, low)
        else:
            same[...] += dot(high, high) + dot(low, low)
            cross[...] += dot(high, low)
    size = hist * 8
    row = lax.broadcasted_iota(jnp.int32, (size, size), 0)
    column = lax.broadcasted_iota(jnp.int32, (size, size), 1)
    match = (row & 7) == (column & 7)
    group = (
        lax.broadcasted_iota(jnp.int32, (size, 128), 0) // 8
        == lax.broadcasted_iota(jnp.int32, (size, 128), 1)
    ).astype(F32)

    def reduced(ref):
        part = jnp.sum(jnp.where(match, ref[...], 0.0).reshape(hist, 8, size), axis=1)
        return jnp.dot(part, group, precision=lax.Precision.HIGHEST, preferred_element_type=F32)

    wide[...] = jnp.zeros_like(wide)
    wide[0:hist, :] = reduced(cross)
    turned = jnp.transpose(wide[0:128, :])
    wide[0:128, :] = wide[0:128, :] + turned
    wide[0:hist, :] = wide[0:hist, :] + reduced(same)
    peers = out_ref.shape[0]
    if peers >= hist:
        out_ref[...] = wide[0:peers, :]
    else:
        out_ref[...] = wide[0:peers, :] + pltpu.roll(wide[peers : 2 * peers, :], 64, axis=1)


def shell(recv_ref, numbers_ref, small_ref, up_ref, down_ref, low_ref,
          low_up_ref, low_down_ref, high_ref, v_ref, after_ref, resp_ref, late_ref, v, acc, rows_acc,
          cols_acc, corner_acc, ext, dots, v_sem):
    disp_ref, stiff_ref, prev_ref = small_ref.at[0], small_ref.at[1], small_ref.at[2]
    sx, sy = disp_ref.shape
    peers, blk = recv_ref.shape[0], numbers_ref.shape[1]
    index_ref = numbers_ref.at[pl.ds(peers, peers)]
    load_tiles = peers // 8
    index_planes = -(-2 * load_tiles // 8)
    corner_planes = -(-(load_tiles + 4) // 8)
    chunks = sy // 128
    hist = v_ref.shape[0]
    v_copy = pltpu.make_async_copy(v_ref, v, v_sem.at[0])
    v_copy.start()
    top = up_ref.shape[0] - (index_planes + 2 + corner_planes)
    low_top = low_ref.shape[0] - (index_planes + 1)
    corner_top = low_up_ref.shape[0] - corner_planes
    near_top = index_planes + 1
    load_at = [
        (high_ref, 0, load_tiles), (low_ref, low_top, load_tiles), (up_ref, top, load_tiles),
        (down_ref, top, load_tiles), (high_ref, near_top, 0),
        (high_ref, near_top + corner_planes, 0), (low_up_ref, corner_top, 0),
        (low_down_ref, corner_top, 0),
    ]

    def accumulate(target, first, keys, height, lane, lanes, values):
        added = lax.dot_general(
            one_hot(keys, height), spread_values(values, lane, lanes, 2),
            (((1,), (1,)), ((), ())), preferred_element_type=F32,
        )
        if first:
            target[...] = added
        else:
            target[...] += added

    def values_of(k, base):
        return as_row(recv_ref[base : base + 8, 0, k * blk : (k + 1) * blk])

    for base in range(0, peers, 8):
        index = as_row(index_ref[base : base + 8, :])
        keys = ((index >> 7) & (chunks - 1)) * sx + index // sy
        accumulate(acc, base == 0, keys, sx * chunks, index & 127, 128, values_of(0, base))
    for k, (dx, dy) in enumerate(NEAR):
        if k == 0:
            continue
        for base in range(0, peers, 8):
            ref, plane, number = load_at[k - 1]
            index = as_row(tile_of(ref, plane, number + base // 8).astype(jnp.int32))
            row = index // sy
            lane = index & (sy - 1)
            if dx == 1:
                row8 = jnp.where(row < 4, row, -1)
            elif dx == -1:
                row8 = jnp.where(row >= sx - 4, row - (sx - 8), -1)
            if dy == 1:
                lane8 = jnp.where(lane < 4, lane, -1)
            elif dy == -1:
                lane8 = jnp.where(lane >= sy - 4, lane - (sy - 8), -1)
            values = values_of(k, base)
            if dy == 0:
                keys = jnp.where(row8 < 0, -1, (lane >> 7) * 8 + row8)
                accumulate(
                    rows_acc, k == 1 and base == 0, keys, 8 * chunks, lane & 127, 128, values
                )
            elif dx == 0:
                accumulate(cols_acc, k == 3 and base == 0, row, sx, lane8, 16, values)
            else:
                accumulate(corner_acc, k == 5 and base == 0, row8, 16, lane8, 16, values)

    ids = lax.broadcasted_iota(jnp.int32, (16, 128), 0)
    lanes = lax.broadcasted_iota(jnp.int32, (16, 128), 1)
    placed = (jnp.where(ids < 4, ids, jnp.where(ids < 8, ids + 120, -1)) == lanes).astype(F32)

    def widened(ref):
        both = ref[:, 0:16] + ref[:, 16:32]
        return jnp.dot(both, placed, precision=lax.Precision.HIGHEST, preferred_element_type=F32)

    force, disp, stiff = ext.at[0], ext.at[1], ext.at[2]
    for q in range(chunks):
        at = slice(q * 128, (q + 1) * 128)
        part = acc[q * sx : (q + 1) * sx, :]
        force[0:sx, at] = part[:, 0:128] + part[:, 128:256]
        part = rows_acc[q * 8 : (q + 1) * 8, :]
        force[sx : sx + 8, at] = part[:, 0:128] + part[:, 128:256]
    side = slice(sy, sy + 128)
    force[0:sx, side] = widened(cols_acc)
    force[sx : sx + 8, side] = widened(corner_acc)[0:8]
    sub = lax.broadcasted_iota(jnp.int32, (8, sy), 0) < 4
    sub1 = lax.broadcasted_iota(jnp.int32, (8, 128), 0) < 4
    lane = lax.broadcasted_iota(jnp.int32, (sx, 128), 1)
    lane1 = lax.broadcasted_iota(jnp.int32, (8, 128), 1)
    for kind, (target, own) in enumerate(((disp, disp_ref), (stiff, stiff_ref))):

        def row_tile(ref, plane):
            return ref[plane, :, kind * sy : (kind + 1) * sy]

        def col_tile(ref):
            plane = top + index_planes + 1
            return jnp.concatenate([tile_of(ref, plane, m) for m in range(sx // 8)], axis=0)

        target[0:sx, 0:sy] = own[...]
        target[sx : sx + 8, 0:sy] = jnp.where(
            sub, row_tile(high_ref, index_planes), row_tile(low_ref, low_top + index_planes)
        )
        ahead, behind = col_tile(up_ref), col_tile(down_ref)
        if kind == 0:
            behind = pltpu.roll(behind, 64, axis=1)
        else:
            ahead = pltpu.roll(ahead, 64, axis=1)
        target[0:sx, side] = jnp.where(lane < 32, ahead, jnp.where(lane >= 96, behind, 0.0))

        def corner_tile(ahead, ahead_plane, behind, behind_plane):
            number = load_tiles + 2 * kind
            return jnp.where(
                lane1 < 32, tile_of(ahead, ahead_plane, number),
                jnp.where(lane1 >= 96, tile_of(behind, behind_plane, number + 1), 0.0),
            )

        target[sx : sx + 8, side] = jnp.where(
            sub1, corner_tile(high_ref, near_top, high_ref, near_top + corner_planes),
            corner_tile(low_up_ref, corner_top, low_down_ref, corner_top),
        )

    load = force[...]
    k = stiff[...]
    diag = 1.0 + 4.0 * k
    scale = 0.8 / diag
    resp = disp[...]
    high, wide = sx + 8, sy + 128
    for sweep in range(SWEEPS):
        beside = (pltpu.roll(resp, 1, axis=0) + pltpu.roll(resp, high - 1, axis=0)) + (
            pltpu.roll(resp, 1, axis=1) + pltpu.roll(resp, wide - 1, axis=1)
        )
        resp = resp + scale * (load - (diag * resp - k * beside))
    own = resp[0:sx, 0:sy]
    resp_ref[...] = own
    resid = own - disp_ref[...]
    newest = resid - prev_ref[...]
    dots[...] = jnp.zeros_like(dots)

    def folded(value):
        total = value[0:8]
        for t in range(1, sx // 8):
            total = total + value[8 * t : 8 * t + 8]
        out = total[:, 0:128]
        for q in range(1, chunks):
            out = out + total[:, q * 128 : (q + 1) * 128]
        return jnp.sum(out, axis=0, keepdims=True)

    dots[0:1, :] = folded(newest * newest)
    dots[64:65, :] = folded(resid * newest)
    v_copy.wait()
    for number in range(1, hist):
        column = v[number]
        dots[number : number + 1, :] = folded(column * newest)
        dots[64 + number : 65 + number, :] = folded(column * resid)
    late = lax.dot_general(
        jnp.ones((8, 128), F32), dots[...], (((1,), (1,)), ((), ())),
        precision=lax.Precision.HIGHEST, preferred_element_type=F32,
    )
    gram_at = len(NEAR) * blk
    gram = jnp.sum(recv_ref[:, 0, gram_at : gram_at + 128], axis=0, keepdims=True)
    late_ref[:, 0, 0:128] = jnp.broadcast_to(late[0:1], (peers, 128))
    late_ref[:, 0, 128:256] = jnp.broadcast_to(gram, (peers, 128))


def solve(recv_ref, resp_ref, small_ref, w_ref, after_ref, out_ref, w, sems):
    peers = recv_ref.shape[0]
    hist = w_ref.shape[0]
    prev_ref = small_ref.at[3]
    sx, sy = resp_ref.shape
    w_copy = pltpu.make_async_copy(w_ref, w, sems.at[0])
    w_copy.start()
    late = jnp.sum(recv_ref[:, 0, 0:128], axis=0, keepdims=True)
    rows = recv_ref[:, 0, 128:256]
    if peers >= hist:
        gram = rows[0:hist]
    else:
        gram = jnp.concatenate(
            [rows, pltpu.roll(rows, 64, axis=1)[0 : hist - peers]], axis=0
        )
    row = lax.broadcasted_iota(jnp.int32, (hist, 128), 0)
    lane = lax.broadcasted_iota(jnp.int32, (hist, 128), 1)
    turned = jnp.transpose(jnp.broadcast_to(late, (128, 128)))
    gram = jnp.where(row == 0, jnp.broadcast_to(late, (hist, 128)), gram)
    gram = jnp.where(lane == 0, turned[0:hist], gram)
    gram = jnp.where(lane < hist, gram, 0.0)
    unit = row == lane
    trace = jnp.sum(jnp.where(unit, gram, 0.0), keepdims=True)
    a = gram + jnp.where(unit, 0.001 * trace / hist, 0.0)
    a = jnp.where(lane == 64, -turned[64 : 64 + hist], a)
    for j in range(hist):
        column = jnp.broadcast_to(a[:, j : j + 1], (hist, 128))
        scaled = a[j : j + 1, :] / column[j : j + 1, :]
        a = jnp.where(row == j, scaled, a - column * scaled)
    coef = jnp.broadcast_to(a[:, 64:65], (hist, 128))
    coef = jnp.concatenate([coef] * (sy // 128), axis=1)
    resp = resp_ref[...]
    total = resp + coef[0:1] * (resp - prev_ref[...])
    w_copy.wait()
    for number in range(1, hist):
        total = total + coef[number : number + 1] * w[number]
    out_ref[...] = total


def pack(phi_ref, kappa_ref, after_ref, small_ref, numbers_ref, up_ref, down_ref, low_ref, low_up_ref, low_down_ref, own_ref, phi_lo, kap_lo, phi_hi,
         kap_hi, in_sems):
    cx, cy, cz = phi_ref.shape
    disp_ref, stiff_ref = small_ref.at[0], small_ref.at[1]
    sx, sy = disp_ref.shape
    peers = numbers_ref.shape[0] // 2
    cells_ref, loads_ref = numbers_ref.at[pl.ds(0, peers)], numbers_ref.at[pl.ds(peers, peers)]
    tiles = peers // 8
    index_planes = -(-2 * tiles // 8)
    corner_planes = -(-(tiles + 4) // 8)
    copy_in = starter(in_sems)
    depth = 8
    lows = []
    for n, (ref, x) in enumerate(
        [(phi_ref, x) for x in range(cx - 4, cx)] + [(kappa_ref, x) for x in range(cx - 3, cx)]
    ):
        for t in range(cy // 8):
            lows.append(copy_in(ref.at[x, pl.ds(8 * t, 8)], low_ref.at[n * (cy // 8) + t]))
    groups = []
    for x in range(0, cx, depth):
        at = pl.ds(x, depth)
        groups.append([
            copy_in(phi_ref.at[at, pl.ds(0, 8)], phi_lo.at[at]),
            copy_in(kappa_ref.at[at, pl.ds(0, 8)], kap_lo.at[at]),
            copy_in(phi_ref.at[at, pl.ds(cy - 8, 8)], phi_hi.at[at]),
            copy_in(kappa_ref.at[at, pl.ds(cy - 8, 8)], kap_hi.at[at]),
        ])
    own_ref[...] = jnp.zeros_like(own_ref)

    def put(plane, number, tile):
        own_ref[plane + number // 8, :, (number % 8) * 128 : (number % 8 + 1) * 128] = tile

    corner = index_planes + 2
    for n in range(tiles):
        put(0, n, cells_ref[8 * n : 8 * n + 8, :].astype(F32))
        loads = loads_ref[8 * n : 8 * n + 8, :].astype(F32)
        put(0, tiles + n, loads)
        put(corner, n, loads)
    sub = lax.broadcasted_iota(jnp.int32, (8, sy), 0) < 4
    for kind, ref in enumerate((disp_ref, stiff_ref)):
        edge = jnp.where(sub, ref[0:8, :], ref[sx - 8 : sx, :])
        own_ref[index_planes, :, kind * sy : (kind + 1) * sy] = edge
        put(corner, tiles + 2 * kind, edge[:, 0:128])
        put(corner, tiles + 2 * kind + 1, edge[:, sy - 128 : sy])
    lane = lax.broadcasted_iota(jnp.int32, (sx, 128), 1)
    first, final = slice(0, 128), slice(sy - 128, sy)
    columns = jnp.where(
        lane < 32, disp_ref[:, first],
        jnp.where(
            lane < 64, pltpu.roll(disp_ref[:, final], 64, axis=1),
            jnp.where(lane < 96, pltpu.roll(stiff_ref[:, first], 64, axis=1), stiff_ref[:, final]),
        ),
    )
    for m in range(sx // 8):
        put(index_planes + 1, m, columns[8 * m : 8 * m + 8, :])
    own = own_ref[...]
    up_ref[cx:] = own
    down_ref[cx:] = own
    low_ref[7 * (cy // 8) :] = own[: index_planes + 1]
    low_up_ref[3:] = own[corner:]
    low_down_ref[3:] = own[corner:]
    upper = lax.broadcasted_iota(jnp.int32, (depth, 8, cz), 1) < 4
    for number, copies in enumerate(groups):
        for made in copies:
            made.wait()
        at = slice(number * depth, (number + 1) * depth)
        up = jnp.where(upper, phi_lo[at], pltpu.roll(kap_lo[at], 4, axis=1))
        down = jnp.where(upper, pltpu.roll(kap_hi[at], 4, axis=1), phi_hi[at])
        up_ref[at] = up
        down_ref[at] = down
        if (number + 1) * depth == cx:
            low_up_ref[0:3] = up[depth - 3 :]
            low_down_ref[0:3] = down[depth - 3 :]
    for made in lows:
        made.wait()


def packed(phi, kappa, after, small, numbers):
    cx, cy, cz = phi.shape
    tiles = numbers.shape[0] // 16
    index_planes = -(-2 * tiles // 8)
    corner_planes = -(-(tiles + 4) // 8)
    extra = index_planes + 2 + corner_planes
    low_planes = 7 * (cy // 8)

    def shape(planes):
        return jax.ShapeDtypeStruct((planes, 8, cz), F32)

    return pl.pallas_call(
        pack,
        in_specs=hbm_specs(2) + any_specs(1) + vmem_specs(2),
        out_specs=vmem_specs(6),
        out_shape=[
            shape(cx + extra), shape(cx + extra), shape(low_planes + index_planes + 1),
            shape(3 + corner_planes), shape(3 + corner_planes), shape(extra),
        ],
        scratch_shapes=[pltpu.VMEM((cx, 8, cz), F32)] * 4
        + [pltpu.SemaphoreType.DMA((cx // 2 + low_planes,))],
        compiler_params=params(),
        name="pack",
    )(phi, kappa, after, small, numbers)


def substep(src, kap, dst, plane, advect, cy, cz):
    wide = cy + 8
    chunks = cz // 128
    lane = lax.broadcasted_iota(jnp.int32, (wide, 128), 1)
    first, last = lane == 0, lane == 127

    def take(at, q, start=8):
        return src[at, q, pl.ds(start, wide), :]

    result = []
    for q in range(chunks):
        now = take(plane, q)
        left = take(plane, q - 1) if q else 0.0
        right = take(plane, q + 1) if q + 1 < chunks else 0.0
        total = pltpu.roll(jnp.where(last, left, now), 1, axis=1) + pltpu.roll(
            jnp.where(first, right, now), 127, axis=1
        )
        total = total + (take(plane, q, 7) + take(plane, q, 9))
        before = take(plane - 1, q)
        total = total + (before + take(plane + 1, q))
        k = kap[plane - 1, :, q * 128 : (q + 1) * 128]
        result.append(now + advect * (before - now) + k * (total - 6.0 * now))
    for q, new in enumerate(result):
        dst[plane, q, 8 : 8 + wide, :] = new
        dst[plane, q, 7:8, :] = new[wide - 1 :]
        dst[plane, q, 8 + wide : 9 + wide, :] = new[0:1]


def fluid(x0, x1, cx, cy, cz, kind, *refs):
    planes = x1 - x0 + 8
    wide = cy + 8
    chunks = cz // 128
    names = ["phi", "kappa", "up", "down"]
    names += {"wet": ["forced", "low", "low_up", "low_down", "gram"],
              "middle": ["forced", "wet", "press"], "end": ["high", "whole", "late"]}[kind]
    names += ["out", "a", "b", "kap", "stage", "sems", "out_sems"]
    r = dict(zip(names, refs))
    a, b, kap, stage = r["a"], r["b"], r["kap"], r["stage"]
    is_last = lax.axis_index("gx") == lax.axis_size("gx") - 1
    copy, copy_out = starter(r["sems"]), starter(r["out_sems"])

    def unchunked(src, s0, count, row, rows, dst, d0):
        return [
            copy_out(
                src.at[pl.ds(s0, count), q, pl.ds(row, rows)],
                dst.at[pl.ds(d0, count), :, pl.ds(q * 128, 128)],
            )
            for q in range(chunks)
        ]

    own0, own1 = max(0, x0 - 4), min(cx, x1 + 4)
    groups = []
    start = own0
    while start < own1:
        count = min(4, own1 - start)
        i = start - (x0 - 4)
        k0, k1 = max(start, x0 - 3), min(start + count, x1 + 3)
        copies = [
            copy(r["kappa"].at[pl.ds(k0, k1 - k0)],
                 kap.at[pl.ds(k0 - (x0 - 3), k1 - k0), pl.ds(0, cy)]),
        ]
        if "forced" not in r or start >= 4:
            copies.append(
                copy(r["phi"].at[pl.ds(start, count)], stage.at[pl.ds(start - own0, count)])
            )
        groups.append((i, i + count, copies))
        start += count
    outs = []
    if kind == "middle":
        outs.append(copy_out(r["wet"], r["out"].at[pl.ds(0, x0)]))

    upper = lax.broadcasted_iota(jnp.int32, (8, cz), 0) < 4

    def assemble(i):
        x = x0 - 4 + i
        inner = 1 <= i < planes - 1
        if x >= cx:
            for q in range(chunks):
                at = slice(q * 128, (q + 1) * 128)
                a[i, q, 8 : 8 + wide, :] = r["high"][x - cx, :, at]
                if inner:
                    kap[i - 1, :, at] = r["high"][4 + x - cx, :, at]
        else:
            if x >= 0:
                up, down = r["up"][x], r["down"][x]
            elif x > -4:
                up, down = r["low_up"][x + 3], r["low_down"][x + 3]
            else:
                up = down = jnp.zeros((8, cz), F32)
            edge = jnp.where(upper, up, down)
            kedge = pltpu.roll(jnp.where(upper, down, up), 4, axis=0)
            for q in range(chunks):
                at = slice(q * 128, (q + 1) * 128)
                if x < 0:
                    for t in range(cy // 8):
                        a[i, q, 8 + 8 * t : 16 + 8 * t, :] = r["low"][(x + 4) * (cy // 8) + t, :, at]
                        if inner:
                            kap[i - 1, 8 * t : 8 * t + 8, at] = r["low"][
                                (x + 7) * (cy // 8) + t, :, at
                            ]
                if "forced" in r and 0 <= x < 4:
                    a[i, q, 8 : 8 + wide, :] = r["forced"][x, :, at]
                else:
                    if x >= 0:
                        a[i, q, 8 : 8 + cy, :] = stage[x - own0, :, at]
                    a[i, q, 8 + cy : 8 + wide, :] = edge[:, at]
                if inner:
                    kap[i - 1, cy:wide, at] = kedge[:, at]
        for q in range(chunks):
            a[i, q, 7:8, :] = a[i, q, 7 + wide : 8 + wide, :]
            a[i, q, 8 + wide : 9 + wide, :] = a[i, q, 8:9, :]

    def run(src, dst, lo, hi):
        def body(i, carry):
            advect = 0.25
            if kind == "end":
                outside = jnp.logical_and(is_last, i + (x0 - 4) >= cx)
                advect = jnp.where(outside, 0.0, 0.25)
            substep(src, kap, dst, i, advect, cy, cz)
            return carry

        if hi > lo:
            lax.fori_loop(lo, hi, body, 0)

    if kind == "wet":
        for i in range(4):
            assemble(i)
    done = 1
    for i0, i1, copies in groups:
        for made in copies:
            made.wait()
        for i in range(i0, i1):
            assemble(i)
        run(a, b, done, i1 - 1)
        done = i1 - 1
    if kind == "end":
        for i in range(planes - 4, planes):
            assemble(i)
        run(a, b, done, planes - 1)
    run(b, a, 2, planes - 2)
    run(a, b, 3, planes - 3)
    for start in range(4, planes - 4, 4):
        run(b, a, start, start + 4)
        if kind == "wet":
            for i in range(start, start + 4):
                for q in range(chunks):
                    r["out"][i - 4, :, q * 128 : (q + 1) * 128] = a[i, q, 8 : 8 + cy, :]
        else:
            outs += unchunked(a, start, 4, 8, cy, r["out"], x0 + start - 4)
    for made in outs:
        made.wait()


def fluid_call(kind, x0, x1, phi, kappa, up, down, *more):
    cx, cy, cz = phi.shape
    planes = x1 - x0 + 8
    field = jax.ShapeDtypeStruct((cx, cy, cz), F32)
    whole = hbm_specs(1)[0]
    if kind == "wet":
        specs = vmem_specs(4) + any_specs(1)
        out_shape, out_specs = jax.ShapeDtypeStruct((x1 - x0, cy, cz), F32), vmem_specs(1)[0]
    elif kind == "middle":
        specs, out_shape, out_specs = vmem_specs(2) + any_specs(1), field, whole
    else:
        specs = vmem_specs(1) + hbm_specs(1) + any_specs(1)
        out_shape, out_specs = field, whole
    cells = planes * (cy + 8) * cz
    return pl.pallas_call(
        functools.partial(fluid, x0, x1, cx, cy, cz, kind),
        in_specs=hbm_specs(2) + vmem_specs(2) + specs,
        out_specs=out_specs,
        out_shape=out_shape,
        scratch_shapes=[
            pltpu.VMEM((planes, cz // 128, cy + 24, 128), F32),
            pltpu.VMEM((planes, cz // 128, cy + 24, 128), F32),
            pltpu.VMEM((planes - 2, cy + 8, cz), F32),
            pltpu.VMEM((min(cx, x1 + 4) - max(0, x0 - 4), cy, cz), F32),
            pltpu.SemaphoreType.DMA((80,)),
            pltpu.SemaphoreType.DMA((80,)),
        ],
        input_output_aliases={5: 0} if kind == "end" else {},
        compiler_params=params(),
        cost_estimate=pl.CostEstimate(
            flops=48 * cells, bytes_accessed=12 * cells, transcendentals=0
        ),
        name="fluid_" + kind,
    )(phi, kappa, up, down, *more)


def shifted_pairs(n_gx, n_gy, dx, dy):
    pairs = []
    for gx in range(n_gx):
        for gy in range(n_gy):
            tx, ty = gx + dx, gy + dy
            if 0 <= tx < n_gx and 0 <= ty < n_gy:
                pairs.append((gx * n_gy + gy, tx * n_gy + ty))
    return pairs


def local(phi, kappa, stiffness, face_cell, load_dof, displacement, v_hist, w_hist, r_prev, w_prev):
    n_gx, n_gy = lax.axis_size("gx"), lax.axis_size("gy")
    peers, blk = face_cell.shape[2:]
    cx, cy, cz = phi.shape
    sx, sy = displacement.shape
    hist = v_hist.shape[0]
    wet_planes = cx // 8
    fcell = face_cell.reshape(peers, blk)
    ldof = load_dof.reshape(peers, blk)
    axes = ("gx", "gy")

    def shift(value, dx, dy):
        return lax.ppermute(value, axes, shifted_pairs(n_gx, n_gy, dx, dy))

    def exchange(value):
        return lax.all_to_all(value, axes, split_axis=0, concat_axis=0, tiled=True)

    def call(body, out_shape, scratch, name, specs, *args):
        several = isinstance(out_shape, list)
        return pl.pallas_call(
            body,
            in_specs=specs,
            out_specs=vmem_specs(len(out_shape)) if several else vmem_specs(1)[0],
            out_shape=out_shape,
            scratch_shapes=scratch,
            compiler_params=params(),
            name=name,
        )(*args)

    def f32(*shape):
        return jax.ShapeDtypeStruct(shape, F32)

    small = jnp.stack([displacement, stiffness, r_prev, w_prev])
    numbers = jnp.concatenate([fcell, ldof], axis=0)
    sent = call(
        functools.partial(gather_disp, n_gy), f32(peers, 1, 3 * blk),
        [pltpu.VMEM((peers, blk), F32)], "gather_disp", vmem_specs(2), small, numbers,
    )
    disp = exchange(sent)
    size = 8 * hist
    gram = call(
        gram_rows, f32(peers, 128),
        [
            pltpu.VMEM((sx // 8, hist, 8, sy), F32), pltpu.VMEM((size, size), F32),
            pltpu.VMEM((size, size), F32),
            pltpu.VMEM((max(128, peers, 2 * peers if peers < hist else 0), 128), F32),
            pltpu.SemaphoreType.DMA((sx // 8,)),
        ],
        "gram_rows", hbm_specs(1), v_hist,
    )
    up_send, down_send, low_send, low_up_send, low_down_send, own = packed(
        phi, kappa, sent, small, numbers
    )
    index_planes = -(-2 * (peers // 8) // 8)
    low = shift(low_send, 1, 0)
    up = shift(up_send, 0, -1)
    down = shift(down_send, 0, 1)
    low_up = shift(low_up_send, 1, -1)
    low_down = shift(low_down_send, 1, 1)
    corner = cx + index_planes + 2
    near = shift(
        jnp.concatenate([own[: index_planes + 1], up[corner:], down[corner:]], axis=0), -1, 0
    )

    chunks = cz // 128
    forced = call(
        functools.partial(scatter_disp, cx, cy, cz), f32(2 * wet_planes - 1, cy + 8, cz),
        [
            pltpu.VMEM((wet_planes * cy * chunks, 256), F32),
            pltpu.VMEM((512, wet_planes * 4 * chunks), F32),
            pltpu.VMEM((wet_planes, cy, cz), F32),
            pltpu.VMEM((wet_planes - 1, cy, cz), F32),
            pltpu.SemaphoreType.DMA((2,)),
        ],
        "scatter_disp", vmem_specs(4) + hbm_specs(2), disp, numbers, up, down, phi, kappa,
    )
    high = shift(forced, -1, 0)
    wet = fluid_call(
        "wet", 0, wet_planes, phi, kappa, up, down, forced, low, low_up, low_down, gram
    )
    press = call(
        functools.partial(gather_press, n_gx, n_gy), f32(peers, 1, (len(NEAR) + 1) * blk),
        [pltpu.VMEM((peers, blk), F32)], "gather_press", vmem_specs(3), wet, numbers, gram,
    )
    loads = exchange(press)
    middle = fluid_call("middle", wet_planes, cx - 4, phi, kappa, up, down, forced, wet, press)
    resp, late = call(
        shell, [f32(sx, sy), f32(peers, 1, 256)],
        [
            pltpu.VMEM((hist, sx, sy), F32),
            pltpu.VMEM((sx * (sy // 128), 256), F32),
            pltpu.VMEM((8 * (sy // 128), 256), F32),
            pltpu.VMEM((sx, 32), F32),
            pltpu.VMEM((16, 32), F32),
            pltpu.VMEM((3, sx + 8, sy + 128), F32),
            pltpu.VMEM((128, 128), F32),
            pltpu.SemaphoreType.DMA((1,)),
        ],
        "shell", vmem_specs(9) + hbm_specs(2),
        loads, numbers, small, up, down, low, low_up, low_down, near,
        v_hist, middle,
    )
    field = fluid_call("end", cx - 4, cx, phi, kappa, up, down, high, middle, late)
    x_next = call(
        solve, f32(sx, sy),
        [pltpu.VMEM((hist, sx, sy), F32), pltpu.SemaphoreType.DMA((1,))],
        "solve", vmem_specs(3) + hbm_specs(2), exchange(late), resp, small, w_hist, field,
    )
    return (field, x_next)


def solution(mesh):
    in_specs = (
        P("gx", "gy", None),
        P("gx", "gy", None),
        P("gx", "gy"),
        P("gx", "gy", None, None),
        P("gx", "gy", None, None),
        P("gx", "gy"),
        P(None, "gx", "gy"),
        P(None, "gx", "gy"),
        P("gx", "gy"),
        P("gx", "gy"),
    )
    out_specs = (P("gx", "gy", None), P("gx", "gy"))
    return jax.shard_map(local, mesh=mesh, in_specs=in_specs, out_specs=out_specs, check_vma=False)
```

```python
import functools

import jax
import jax.numpy as jnp
from jax import lax
from jax.experimental import pallas as pl
from jax.experimental.pallas import tpu as pltpu
from jax.sharding import PartitionSpec as P

NSUB = 4
SWEEPS = 3
HIST = 40
VMEM_BYTES = 50 * 1024 * 1024
F32 = jnp.float32
BF16 = jnp.bfloat16


def params():
    return pltpu.CompilerParams(vmem_limit_bytes=VMEM_BYTES)


def vmem_specs(count):
    return [pl.BlockSpec(memory_space=pltpu.VMEM)] * count


def any_specs(count):
    return [pl.BlockSpec(memory_space=pl.ANY)] * count


def hbm_specs(count):
    return [pl.BlockSpec(memory_space=pltpu.HBM)] * count


def pieces(value, count):
    parts = []
    for _ in range(count):
        part = value.astype(BF16)
        parts.append(part)
        value = value - part.astype(F32)
    return parts


def as_row(block):
    return jnp.concatenate([block[i : i + 1] for i in range(block.shape[0])], axis=1)


def both_rows(row):
    return jnp.broadcast_to(row, (16, row.shape[1])).astype(BF16)


def matches(keys, rows):
    ids = lax.broadcasted_iota(jnp.int32, (16, keys.shape[1]), 0).astype(F32).astype(BF16)
    found = []
    for base in range(0, rows, 256):
        key = both_rows((keys - base).astype(F32))
        for start in range(0, min(256, rows - base), 16):
            found.append(key == ids + jnp.bfloat16(start))
    return found


def one_hot(keys, rows):
    one, zero = jnp.bfloat16(1), jnp.bfloat16(0)
    return jnp.concatenate([jnp.where(m, one, zero) for m in matches(keys, rows)], axis=0)


def select_sum(table, lane, group, rows, parts):
    total = table[:rows]
    for part in range(1, parts):
        total = total + table[part * rows : (part + 1) * rows]
    ids = lax.broadcasted_iota(jnp.int32, total.shape, 0)
    return jnp.sum(jnp.where(ids == lane, total, 0.0), axis=0, keepdims=True)


def pick(table_t, index_ref, out_rows, rows, lane_bits, chunk_bits, parts, step=8):
    lanes = 1 << lane_bits
    for base in range(0, index_ref.shape[0], step):
        index = as_row(index_ref[base : base + step, :])
        lane = index & (lanes - 1)
        keys = ((index >> lane_bits) & ((1 << chunk_bits) - 1)) * rows + (
            index >> (lane_bits + chunk_bits)
        )
        hot = one_hot(keys, rows << chunk_bits)
        found = lax.dot_general(
            table_t, hot, (((1,), (0,)), ((), ())), preferred_element_type=F32
        )
        out_rows(base, select_sum(found, lane, step, lanes, parts))


def spread_values(values, lane, lanes, parts):
    zero = jnp.bfloat16(0)
    found = matches(lane, lanes)
    spread = []
    for part in pieces(values, parts):
        part = both_rows(part.astype(F32))
        spread += [jnp.where(m, part, zero) for m in found]
    return jnp.concatenate(spread, axis=0)


NEAR = ((0, 0), (1, 0), (-1, 0), (0, 1), (0, -1), (1, 1), (1, -1), (-1, 1), (-1, -1))


def tile_of(ref, plane, number):
    at = (number % 8) * 128
    return ref[plane + number // 8, :, at : at + 128]


def starter(sems):
    used = [0]

    def copy(src, dst):
        made = pltpu.make_async_copy(src, dst, sems.at[used[0]])
        used[0] += 1
        made.start()
        return made

    return copy


def gather_disp(n_gy, small_ref, numbers_ref, out_ref, own_ref):
    disp_ref = small_ref.at[0]
    peers, blk = own_ref.shape
    index_ref = numbers_ref.at[pl.ds(peers, peers)]
    sx, sy = disp_ref.shape
    chunk_bits = (sy // 128).bit_length() - 1
    columns = []
    for q in range(sy // 128):
        columns.append(jnp.transpose(disp_ref[:, q * 128 : (q + 1) * 128]))
    table_t = jnp.concatenate(pieces(jnp.concatenate(columns, axis=1), 3), axis=0)

    def write(base, row):
        for i in range(8):
            own_ref[base + i : base + i + 1, :] = row[:, i * blk : (i + 1) * blk]

    pick(table_t, index_ref, write, sx, 7, chunk_bits, 3)
    own = own_ref[...]
    beside = lax.broadcasted_iota(jnp.int32, own.shape, 0) % n_gy
    out_ref[:, 0, 0:blk] = own
    out_ref[:, 0, blk : 2 * blk] = jnp.where(
        beside == n_gy - 1, 0.0, pltpu.roll(own, peers - 1, axis=0)
    )
    out_ref[:, 0, 2 * blk : 3 * blk] = jnp.where(beside == 0, 0.0, pltpu.roll(own, 1, axis=0))


def scatter_disp(cx, cy, cz, disp_ref, numbers_ref, up_ref, down_ref, phi_ref, kappa_ref, out_ref,
                 acc_ref, side_ref, stage, kstage, sems):
    planes = stage.shape[0]
    copy = starter(sems)
    copies = [
        copy(phi_ref.at[pl.ds(0, planes)], stage),
        copy(kappa_ref.at[pl.ds(0, planes - 1)], kstage),
    ]
    peers, blk = disp_ref.shape[0], numbers_ref.shape[1]
    cells_ref = numbers_ref.at[pl.ds(0, peers)]
    rows = planes * cy
    chunks = cz // 128
    row_bits = cz.bit_length() - 1
    step = 8
    def accumulate(target, first, left, right):
        added = lax.dot_general(
            left, right, (((1,), (1,)), ((), ())), preferred_element_type=F32
        )
        if first:
            target[...] = added
        else:
            target[...] += added

    for base in range(0, peers, step):
        index = as_row(cells_ref[base : base + step, :])
        values = 0.5 * as_row(disp_ref[base : base + step, 0, 0:blk])
        keys = ((index >> 7) & (chunks - 1)) * rows + (index >> row_bits)
        accumulate(
            acc_ref, base == 0, one_hot(keys, rows * chunks),
            spread_values(values, index & 127, 128, 2),
        )
    for base in range(0, peers, step):
        for side in range(2):
            index = as_row(tile_of(up_ref if side == 0 else down_ref, cx, base // step).astype(jnp.int32))
            values = 0.5 * as_row(
                disp_ref[base : base + step, 0, (side + 1) * blk : (side + 2) * blk]
            )
            row = index >> row_bits
            plane = row // cy
            column = row - plane * cy
            inside = column < 4 if side == 0 else column >= cy - 4
            place = column if side == 0 else column - (cy - 8)
            keys = ((index >> 8) & (chunks // 2 - 1)) * (planes * 8) + plane * 8 + place
            keys = jnp.where(inside, keys, -1)
            accumulate(
                side_ref, base == 0 and side == 0, spread_values(values, index & 255, 256, 2),
                one_hot(keys, planes * 4 * chunks),
            )
    for made in copies:
        made.wait()
    upper = lax.broadcasted_iota(jnp.int32, (8, cz), 0) < 4
    for x in range(planes):
        up, down = up_ref[x], down_ref[x]
        out_ref[x, cy : cy + 8, :] = jnp.where(upper, up, down)
        if x < planes - 1:
            out_ref[planes + x, 0:cy, :] = kstage[x]
            out_ref[planes + x, cy : cy + 8, :] = pltpu.roll(
                jnp.where(upper, down, up), 4, axis=0
            )
    for q in range(chunks):
        part = acc_ref[q * rows : (q + 1) * rows, :]
        at = slice(q * 128, (q + 1) * 128)
        out_ref[0:planes, 0:cy, at] = stage[:, :, at] + (part[:, :128] + part[:, 128:]).reshape(
            planes, cy, 128
        )
    both = jnp.transpose(side_ref[0:256, :] + side_ref[256:512, :])
    for q in range(chunks // 2):
        part = both[q * planes * 8 : (q + 1) * planes * 8, :]
        at = slice(q * 256, (q + 1) * 256)
        out_ref[0:planes, cy : cy + 8, at] = out_ref[0:planes, cy : cy + 8, at] + part.reshape(
            planes, 8, 256
        )


def gather_press(n_gx, n_gy, wet_ref, numbers_ref, gram_ref, after_ref, out_ref, own_ref):
    index_ref = numbers_ref.at[pl.ds(0, own_ref.shape[0])]
    planes, cy, cz = wet_ref.shape
    peers, blk = own_ref.shape
    rows = planes * cy
    chunks = cz // 256
    columns = []
    for q in range(chunks):
        part = wet_ref[:, :, q * 256 : (q + 1) * 256].reshape(rows, 256)
        columns.append(jnp.transpose(part))
    table_t = jnp.concatenate(pieces(jnp.concatenate(columns, axis=1), 2), axis=0)

    def write(base, row):
        for i in range(8):
            own_ref[base + i : base + i + 1, :] = row[:, i * blk : (i + 1) * blk]

    pick(table_t, index_ref, write, rows, 8, chunks.bit_length() - 1, 2)
    own = own_ref[...]
    number = lax.broadcasted_iota(jnp.int32, own.shape, 0)
    at_x, at_y = number // n_gy, number % n_gy
    for k, (dx, dy) in enumerate(NEAR):
        ok = (at_x + dx >= 0) & (at_x + dx < n_gx) & (at_y + dy >= 0) & (at_y + dy < n_gy)
        moved = pltpu.roll(own, (-(dx * n_gy + dy)) % peers, axis=0) if k else own
        out_ref[:, 0, k * blk : (k + 1) * blk] = jnp.where(ok, moved, 0.0)
    out_ref[:, 0, len(NEAR) * blk : (len(NEAR) + 1) * blk] = gram_ref[...]


def gram_rows(v_ref, out_ref, v, same, cross, wide, sems):
    hist, sx, sy = v_ref.shape
    tiles = sx // 8
    copy = starter(sems)
    copies = [
        copy(v_ref.at[:, pl.ds(8 * t, 8), :], v.at[t]) for t in range(tiles)
    ]
    for t in range(tiles):
        copies[t].wait()
        high, low = pieces(v[t].reshape(hist * 8, sy), 2)

        def dot(x, y):
            return lax.dot_general(x, y, (((1,), (1,)), ((), ())), preferred_element_type=F32)

        if t == 0:
            same[...] = dot(high, high) + dot(low, low)
            cross[...] = dot(high, low)
        else:
            same[...] += dot(high, high) + dot(low, low)
            cross[...] += dot(high, low)
    size = hist * 8
    row = lax.broadcasted_iota(jnp.int32, (size, size), 0)
    column = lax.broadcasted_iota(jnp.int32, (size, size), 1)
    match = (row & 7) == (column & 7)
    group = (
        lax.broadcasted_iota(jnp.int32, (size, 128), 0) // 8
        == lax.broadcasted_iota(jnp.int32, (size, 128), 1)
    ).astype(F32)

    def reduced(ref):
        part = jnp.sum(jnp.where(match, ref[...], 0.0).reshape(hist, 8, size), axis=1)
        return jnp.dot(part, group, precision=lax.Precision.HIGHEST, preferred_element_type=F32)

    wide[...] = jnp.zeros_like(wide)
    wide[0:hist, :] = reduced(cross)
    turned = jnp.transpose(wide[0:128, :])
    wide[0:128, :] = wide[0:128, :] + turned
    wide[0:hist, :] = wide[0:hist, :] + reduced(same)
    peers = out_ref.shape[0]
    if peers >= hist:
        out_ref[...] = wide[0:peers, :]
    else:
        out_ref[...] = wide[0:peers, :] + pltpu.roll(wide[peers : 2 * peers, :], 64, axis=1)


def shell(recv_ref, numbers_ref, small_ref, up_ref, down_ref, low_ref,
          low_up_ref, low_down_ref, high_ref, v_ref, after_ref, resp_ref, late_ref, v, acc, rows_acc,
          cols_acc, corner_acc, ext, dots, v_sem):
    disp_ref, stiff_ref, prev_ref = small_ref.at[0], small_ref.at[1], small_ref.at[2]
    sx, sy = disp_ref.shape
    peers, blk = recv_ref.shape[0], numbers_ref.shape[1]
    index_ref = numbers_ref.at[pl.ds(peers, peers)]
    load_tiles = peers // 8
    index_planes = -(-2 * load_tiles // 8)
    corner_planes = -(-(load_tiles + 4) // 8)
    chunks = sy // 128
    hist = v_ref.shape[0]
    v_copy = pltpu.make_async_copy(v_ref, v, v_sem.at[0])
    v_copy.start()
    top = up_ref.shape[0] - (index_planes + 2 + corner_planes)
    low_top = low_ref.shape[0] - (index_planes + 1)
    corner_top = low_up_ref.shape[0] - corner_planes
    near_top = index_planes + 1
    load_at = [
        (high_ref, 0, load_tiles), (low_ref, low_top, load_tiles), (up_ref, top, load_tiles),
        (down_ref, top, load_tiles), (high_ref, near_top, 0),
        (high_ref, near_top + corner_planes, 0), (low_up_ref, corner_top, 0),
        (low_down_ref, corner_top, 0),
    ]

    def accumulate(target, first, keys, height, lane, lanes, values):
        added = lax.dot_general(
            one_hot(keys, height), spread_values(values, lane, lanes, 2),
            (((1,), (1,)), ((), ())), preferred_element_type=F32,
        )
        if first:
            target[...] = added
        else:
            target[...] += added

    def values_of(k, base):
        return as_row(recv_ref[base : base + 8, 0, k * blk : (k + 1) * blk])

    for base in range(0, peers, 8):
        index = as_row(index_ref[base : base + 8, :])
        keys = ((index >> 7) & (chunks - 1)) * sx + index // sy
        accumulate(acc, base == 0, keys, sx * chunks, index & 127, 128, values_of(0, base))
    for k, (dx, dy) in enumerate(NEAR):
        if k == 0:
            continue
        for base in range(0, peers, 8):
            ref, plane, number = load_at[k - 1]
            index = as_row(tile_of(ref, plane, number + base // 8).astype(jnp.int32))
            row = index // sy
            lane = index & (sy - 1)
            if dx == 1:
                row8 = jnp.where(row < 4, row, -1)
            elif dx == -1:
                row8 = jnp.where(row >= sx - 4, row - (sx - 8), -1)
            if dy == 1:
                lane8 = jnp.where(lane < 4, lane, -1)
            elif dy == -1:
                lane8 = jnp.where(lane >= sy - 4, lane - (sy - 8), -1)
            values = values_of(k, base)
            if dy == 0:
                keys = jnp.where(row8 < 0, -1, (lane >> 7) * 8 + row8)
                accumulate(
                    rows_acc, k == 1 and base == 0, keys, 8 * chunks, lane & 127, 128, values
                )
            elif dx == 0:
                accumulate(cols_acc, k == 3 and base == 0, row, sx, lane8, 16, values)
            else:
                accumulate(corner_acc, k == 5 and base == 0, row8, 16, lane8, 16, values)

    ids = lax.broadcasted_iota(jnp.int32, (16, 128), 0)
    lanes = lax.broadcasted_iota(jnp.int32, (16, 128), 1)
    placed = (jnp.where(ids < 4, ids, jnp.where(ids < 8, ids + 120, -1)) == lanes).astype(F32)

    def widened(ref):
        both = ref[:, 0:16] + ref[:, 16:32]
        return jnp.dot(both, placed, precision=lax.Precision.HIGHEST, preferred_element_type=F32)

    force, disp, stiff = ext.at[0], ext.at[1], ext.at[2]
    for q in range(chunks):
        at = slice(q * 128, (q + 1) * 128)
        part = acc[q * sx : (q + 1) * sx, :]
        force[0:sx, at] = part[:, 0:128] + part[:, 128:256]
        part = rows_acc[q * 8 : (q + 1) * 8, :]
        force[sx : sx + 8, at] = part[:, 0:128] + part[:, 128:256]
    side = slice(sy, sy + 128)
    force[0:sx, side] = widened(cols_acc)
    force[sx : sx + 8, side] = widened(corner_acc)[0:8]
    sub = lax.broadcasted_iota(jnp.int32, (8, sy), 0) < 4
    sub1 = lax.broadcasted_iota(jnp.int32, (8, 128), 0) < 4
    lane = lax.broadcasted_iota(jnp.int32, (sx, 128), 1)
    lane1 = lax.broadcasted_iota(jnp.int32, (8, 128), 1)
    for kind, (target, own) in enumerate(((disp, disp_ref), (stiff, stiff_ref))):

        def row_tile(ref, plane):
            return ref[plane, :, kind * sy : (kind + 1) * sy]

        def col_tile(ref):
            plane = top + index_planes + 1
            return jnp.concatenate([tile_of(ref, plane, m) for m in range(sx // 8)], axis=0)

        target[0:sx, 0:sy] = own[...]
        target[sx : sx + 8, 0:sy] = jnp.where(
            sub, row_tile(high_ref, index_planes), row_tile(low_ref, low_top + index_planes)
        )
        ahead, behind = col_tile(up_ref), col_tile(down_ref)
        if kind == 0:
            behind = pltpu.roll(behind, 64, axis=1)
        else:
            ahead = pltpu.roll(ahead, 64, axis=1)
        target[0:sx, side] = jnp.where(lane < 32, ahead, jnp.where(lane >= 96, behind, 0.0))

        def corner_tile(ahead, ahead_plane, behind, behind_plane):
            number = load_tiles + 2 * kind
            return jnp.where(
                lane1 < 32, tile_of(ahead, ahead_plane, number),
                jnp.where(lane1 >= 96, tile_of(behind, behind_plane, number + 1), 0.0),
            )

        target[sx : sx + 8, side] = jnp.where(
            sub1, corner_tile(high_ref, near_top, high_ref, near_top + corner_planes),
            corner_tile(low_up_ref, corner_top, low_down_ref, corner_top),
        )

    load = force[...]
    k = stiff[...]
    diag = 1.0 + 4.0 * k
    scale = 0.8 / diag
    resp = disp[...]
    high, wide = sx + 8, sy + 128
    for sweep in range(SWEEPS):
        beside = (pltpu.roll(resp, 1, axis=0) + pltpu.roll(resp, high - 1, axis=0)) + (
            pltpu.roll(resp, 1, axis=1) + pltpu.roll(resp, wide - 1, axis=1)
        )
        resp = resp + scale * (load - (diag * resp - k * beside))
    own = resp[0:sx, 0:sy]
    resp_ref[...] = own
    resid = own - disp_ref[...]
    newest = resid - prev_ref[...]
    dots[...] = jnp.zeros_like(dots)

    def folded(value):
        total = value[0:8]
        for t in range(1, sx // 8):
            total = total + value[8 * t : 8 * t + 8]
        out = total[:, 0:128]
        for q in range(1, chunks):
            out = out + total[:, q * 128 : (q + 1) * 128]
        return jnp.sum(out, axis=0, keepdims=True)

    dots[0:1, :] = folded(newest * newest)
    dots[64:65, :] = folded(resid * newest)
    v_copy.wait()
    for number in range(1, hist):
        column = v[number]
        dots[number : number + 1, :] = folded(column * newest)
        dots[64 + number : 65 + number, :] = folded(column * resid)
    late = lax.dot_general(
        jnp.ones((8, 128), F32), dots[...], (((1,), (1,)), ((), ())),
        precision=lax.Precision.HIGHEST, preferred_element_type=F32,
    )
    gram_at = len(NEAR) * blk
    gram = jnp.sum(recv_ref[:, 0, gram_at : gram_at + 128], axis=0, keepdims=True)
    late_ref[:, 0, 0:128] = jnp.broadcast_to(late[0:1], (peers, 128))
    late_ref[:, 0, 128:256] = jnp.broadcast_to(gram, (peers, 128))


def solve(recv_ref, resp_ref, small_ref, w_ref, out_ref, w, sems):
    peers = recv_ref.shape[0]
    hist = w_ref.shape[0]
    prev_ref = small_ref.at[3]
    sx, sy = resp_ref.shape
    w_copy = pltpu.make_async_copy(w_ref, w, sems.at[0])
    w_copy.start()
    late = jnp.sum(recv_ref[:, 0, 0:128], axis=0, keepdims=True)
    rows = recv_ref[:, 0, 128:256]
    if peers >= hist:
        gram = rows[0:hist]
    else:
        gram = jnp.concatenate(
            [rows, pltpu.roll(rows, 64, axis=1)[0 : hist - peers]], axis=0
        )
    row = lax.broadcasted_iota(jnp.int32, (hist, 128), 0)
    lane = lax.broadcasted_iota(jnp.int32, (hist, 128), 1)
    turned = jnp.transpose(jnp.broadcast_to(late, (128, 128)))
    gram = jnp.where(row == 0, jnp.broadcast_to(late, (hist, 128)), gram)
    gram = jnp.where(lane == 0, turned[0:hist], gram)
    gram = jnp.where(lane < hist, gram, 0.0)
    unit = row == lane
    trace = jnp.sum(jnp.where(unit, gram, 0.0), keepdims=True)
    a = gram + jnp.where(unit, 0.001 * trace / hist, 0.0)
    a = jnp.where(lane == 64, -turned[64 : 64 + hist], a)
    for j in range(hist):
        column = jnp.broadcast_to(a[:, j : j + 1], (hist, 128))
        scaled = a[j : j + 1, :] / column[j : j + 1, :]
        a = jnp.where(row == j, scaled, a - column * scaled)
    coef = jnp.broadcast_to(a[:, 64:65], (hist, 128))
    coef = jnp.concatenate([coef] * (sy // 128), axis=1)
    resp = resp_ref[...]
    total = resp + coef[0:1] * (resp - prev_ref[...])
    w_copy.wait()
    for number in range(1, hist):
        total = total + coef[number : number + 1] * w[number]
    out_ref[...] = total


def pack(phi_ref, kappa_ref, after_ref, small_ref, numbers_ref, up_ref, down_ref, low_ref, low_up_ref, low_down_ref, own_ref, phi_lo, kap_lo, phi_hi,
         kap_hi, in_sems):
    cx, cy, cz = phi_ref.shape
    disp_ref, stiff_ref = small_ref.at[0], small_ref.at[1]
    sx, sy = disp_ref.shape
    peers = numbers_ref.shape[0] // 2
    cells_ref, loads_ref = numbers_ref.at[pl.ds(0, peers)], numbers_ref.at[pl.ds(peers, peers)]
    tiles = peers // 8
    index_planes = -(-2 * tiles // 8)
    corner_planes = -(-(tiles + 4) // 8)
    copy_in = starter(in_sems)
    depth = 8
    lows = []
    for n, (ref, x) in enumerate(
        [(phi_ref, x) for x in range(cx - 4, cx)] + [(kappa_ref, x) for x in range(cx - 3, cx)]
    ):
        for t in range(cy // 8):
            lows.append(copy_in(ref.at[x, pl.ds(8 * t, 8)], low_ref.at[n * (cy // 8) + t]))
    groups = []
    for x in range(0, cx, depth):
        at = pl.ds(x, depth)
        groups.append([
            copy_in(phi_ref.at[at, pl.ds(0, 8)], phi_lo.at[at]),
            copy_in(kappa_ref.at[at, pl.ds(0, 8)], kap_lo.at[at]),
            copy_in(phi_ref.at[at, pl.ds(cy - 8, 8)], phi_hi.at[at]),
            copy_in(kappa_ref.at[at, pl.ds(cy - 8, 8)], kap_hi.at[at]),
        ])
    own_ref[...] = jnp.zeros_like(own_ref)

    def put(plane, number, tile):
        own_ref[plane + number // 8, :, (number % 8) * 128 : (number % 8 + 1) * 128] = tile

    corner = index_planes + 2
    for n in range(tiles):
        put(0, n, cells_ref[8 * n : 8 * n + 8, :].astype(F32))
        loads = loads_ref[8 * n : 8 * n + 8, :].astype(F32)
        put(0, tiles + n, loads)
        put(corner, n, loads)
    sub = lax.broadcasted_iota(jnp.int32, (8, sy), 0) < 4
    for kind, ref in enumerate((disp_ref, stiff_ref)):
        edge = jnp.where(sub, ref[0:8, :], ref[sx - 8 : sx, :])
        own_ref[index_planes, :, kind * sy : (kind + 1) * sy] = edge
        put(corner, tiles + 2 * kind, edge[:, 0:128])
        put(corner, tiles + 2 * kind + 1, edge[:, sy - 128 : sy])
    lane = lax.broadcasted_iota(jnp.int32, (sx, 128), 1)
    first, final = slice(0, 128), slice(sy - 128, sy)
    columns = jnp.where(
        lane < 32, disp_ref[:, first],
        jnp.where(
            lane < 64, pltpu.roll(disp_ref[:, final], 64, axis=1),
            jnp.where(lane < 96, pltpu.roll(stiff_ref[:, first], 64, axis=1), stiff_ref[:, final]),
        ),
    )
    for m in range(sx // 8):
        put(index_planes + 1, m, columns[8 * m : 8 * m + 8, :])
    own = own_ref[...]
    up_ref[cx:] = own
    down_ref[cx:] = own
    low_ref[7 * (cy // 8) :] = own[: index_planes + 1]
    low_up_ref[3:] = own[corner:]
    low_down_ref[3:] = own[corner:]
    upper = lax.broadcasted_iota(jnp.int32, (depth, 8, cz), 1) < 4
    for number, copies in enumerate(groups):
        for made in copies:
            made.wait()
        at = slice(number * depth, (number + 1) * depth)
        up = jnp.where(upper, phi_lo[at], pltpu.roll(kap_lo[at], 4, axis=1))
        down = jnp.where(upper, pltpu.roll(kap_hi[at], 4, axis=1), phi_hi[at])
        up_ref[at] = up
        down_ref[at] = down
        if (number + 1) * depth == cx:
            low_up_ref[0:3] = up[depth - 3 :]
            low_down_ref[0:3] = down[depth - 3 :]
    for made in lows:
        made.wait()


def packed(phi, kappa, after, small, numbers):
    cx, cy, cz = phi.shape
    tiles = numbers.shape[0] // 16
    index_planes = -(-2 * tiles // 8)
    corner_planes = -(-(tiles + 4) // 8)
    extra = index_planes + 2 + corner_planes
    low_planes = 7 * (cy // 8)

    def shape(planes):
        return jax.ShapeDtypeStruct((planes, 8, cz), F32)

    return pl.pallas_call(
        pack,
        in_specs=hbm_specs(2) + any_specs(1) + vmem_specs(2),
        out_specs=vmem_specs(6),
        out_shape=[
            shape(cx + extra), shape(cx + extra), shape(low_planes + index_planes + 1),
            shape(3 + corner_planes), shape(3 + corner_planes), shape(extra),
        ],
        scratch_shapes=[pltpu.VMEM((cx, 8, cz), F32)] * 4
        + [pltpu.SemaphoreType.DMA((cx // 2 + low_planes,))],
        compiler_params=params(),
        name="pack",
    )(phi, kappa, after, small, numbers)


def substep(src, kap, coef, dst, plane, advect, rows, cz):
    chunks = cz // 128
    wide = kap.shape[1]
    lane = lax.broadcasted_iota(jnp.int32, (rows, 128), 1)
    first, last = lane == 0, lane == 127

    def take(at, q, start=8):
        return src[at, q, pl.ds(start, rows), :]

    for q in range(chunks):
        now = take(plane, q)
        left = take(plane, q - 1) if q else 0.0
        right = take(plane, q + 1) if q + 1 < chunks else 0.0
        total = pltpu.roll(jnp.where(last, left, now), 1, axis=1) + pltpu.roll(
            jnp.where(first, right, now), 127, axis=1
        )
        total = total + (take(plane, q, 7) + take(plane, q, 9))
        before = take(plane - 1, q)
        total = total + (before + take(plane + 1, q))
        at = slice(q * 128, (q + 1) * 128)
        new = (coef[plane - 1, 0:rows, at] * now + advect * before) + kap[
            plane - 1, 0:rows, at
        ] * total
        dst[plane, q, 8 : 8 + rows, :] = new
        if rows == wide:
            dst[plane, q, 7:8, :] = new[wide - 1 :]
            dst[plane, q, 8 + wide : 9 + wide, :] = new[0:1]


def fluid(x0, x1, cx, cy, cz, kind, *refs):
    planes = x1 - x0 + 8
    wide = cy + 8
    chunks = cz // 128
    names = ["phi", "kappa", "up", "down"]
    names += {"wet": ["forced", "low", "low_up", "low_down", "near", "gram"],
              "middle": ["state_a", "state_b", "wet"],
              "end": ["state_a", "state_b", "high", "whole"]}[kind]
    names += {"wet": ["out", "next_a", "next_b", "send"], "middle": ["out", "next_a", "next_b"],
              "end": ["out"]}[kind]
    names += ["a", "b", "kap", "coef", "stage", "sems", "out_sems"]
    r = dict(zip(names, refs))
    a, b, kap, coef, stage = r["a"], r["b"], r["kap"], r["coef"], r["stage"]
    carried = kind != "wet"
    is_last = lax.axis_index("gx") == lax.axis_size("gx") - 1
    copy, copy_out = starter(r["sems"]), starter(r["out_sems"])

    def unchunked(src, s0, count, row, rows, dst, d0):
        return [
            copy_out(
                src.at[pl.ds(s0, count), q, pl.ds(row, rows)],
                dst.at[pl.ds(d0, count), :, pl.ds(q * 128, 128)],
            )
            for q in range(chunks)
        ]

    own0, own1 = x0 + 4 if carried else x0, min(cx, x1 + 4)
    kap0 = x0 if carried else x0 - 3
    groups = []
    if carried:
        kappa_first = copy(r["kappa"].at[pl.ds(x0, 4)], kap.at[pl.ds(3, 4), pl.ds(0, cy)])
    start = own0
    while start < own1:
        count = min(4, own1 - start)
        i = start - (x0 - 4)
        k0, k1 = start, min(start + count, x1 + 3)
        copies = [] if k1 <= k0 else [
            copy(r["kappa"].at[pl.ds(k0, k1 - k0)],
                 kap.at[pl.ds(k0 - (x0 - 3), k1 - k0), pl.ds(0, cy)]),
        ]
        if carried or start >= 4:
            copies.append(
                copy(r["phi"].at[pl.ds(start, count)], stage.at[pl.ds(start - own0, count)])
            )
        groups.append((i, i + count, copies))
        start += count
    outs = []
    if kind == "middle":
        outs.append(copy_out(r["wet"], r["out"].at[pl.ds(0, x0)]))

    upper = lax.broadcasted_iota(jnp.int32, (8, cz), 0) < 4

    def assemble(i, only_kappa=False):
        x = x0 - 4 + i
        inner = 1 <= i < planes - 1
        whole = slice(8, 8 + wide)
        if x >= cx:
            if inner:
                kap[i - 1] = r["high"][4 + x - cx]
        else:
            if x >= 0:
                up, down = r["up"][x], r["down"][x]
            elif x > -4:
                up, down = r["low_up"][x + 3], r["low_down"][x + 3]
            else:
                up = down = jnp.zeros((8, cz), F32)
            edge = jnp.where(upper, up, down)
            if inner:
                if x < 0:
                    for t in range(cy // 8):
                        kap[i - 1, 8 * t : 8 * t + 8, :] = r["low"][(x + 7) * (cy // 8) + t]
                kap[i - 1, cy:wide, :] = pltpu.roll(jnp.where(upper, down, up), 4, axis=0)
        if inner:
            coef[i - 1] = 0.75 - 6.0 * kap[i - 1]
        if only_kappa:
            return
        for q in range(chunks):
            at = slice(q * 128, (q + 1) * 128)
            if x >= cx:
                a[i, q, whole, :] = r["high"][x - cx, :, at]
            elif kind == "wet" and 0 <= x < 4:
                a[i, q, whole, :] = r["forced"][x, :, at]
            else:
                if x < 0:
                    for t in range(cy // 8):
                        a[i, q, 8 + 8 * t : 16 + 8 * t, :] = r["low"][(x + 4) * (cy // 8) + t, :, at]
                else:
                    a[i, q, 8 : 8 + cy, :] = stage[x - own0, :, at]
                a[i, q, 8 + cy : 8 + wide, :] = edge[:, at]
            a[i, q, 7:8, :] = a[i, q, 7 + wide : 8 + wide, :]
            a[i, q, 8 + wide : 9 + wide, :] = a[i, q, 8:9, :]

    def run(src, dst, lo, hi, rows=wide):
        def body(i, carry):
            advect = 0.25
            if kind == "end":
                outside = jnp.logical_and(is_last, i + (x0 - 4) >= cx)
                advect = jnp.where(outside, 0.0, 0.25)
            substep(src, kap, coef, dst, i, advect, rows, cz)
            return carry

        if hi > lo:
            lax.fori_loop(lo, hi, body, 0)

    if kind == "wet":
        for i in range(4):
            assemble(i)
        done = 1
    else:
        a[4:8] = r["state_a"][...]
        b[3:7] = r["state_b"][...]
        kappa_first.wait()
        for i in range(4, 8):
            assemble(i, True)
        done = 7
    for i0, i1, copies in groups:
        for made in copies:
            made.wait()
        for i in range(i0, i1):
            assemble(i)
        run(a, b, done, i1 - 1)
        done = i1 - 1
    if kind == "end":
        for i in range(planes - 4, planes):
            assemble(i)
        run(a, b, done, planes - 1)
    run(b, a, 6 if carried else 2, planes - 2)
    run(a, b, 5 if carried else 3, planes - 3)
    if kind == "wet":
        r["send"][...] = r["forced"][...]
    for start in range(4, planes - 4, 4):
        run(b, a, start, start + 4, cy)
        if kind == "wet":
            for i in range(start, start + 4):
                for q in range(chunks):
                    r["out"][i - 4, :, q * 128 : (q + 1) * 128] = a[i, q, 8 : 8 + cy, :]
        else:
            outs += unchunked(a, start, 4, 8, cy, r["out"], x0 + start - 4)
    if kind != "end":
        r["next_a"][...] = a[planes - 4 : planes]
        r["next_b"][...] = b[planes - 5 : planes - 1]
    for made in outs:
        made.wait()


def fluid_call(kind, x0, x1, phi, kappa, up, down, *more):
    cx, cy, cz = phi.shape
    planes = x1 - x0 + 8
    field = jax.ShapeDtypeStruct((cx, cy, cz), F32)
    state = [jax.ShapeDtypeStruct((4, cz // 128, cy + 24, 128), F32)] * 2
    if kind == "wet":
        specs = vmem_specs(4) + any_specs(2)
        out_shape = [
            jax.ShapeDtypeStruct((x1 - x0, cy, cz), F32), *state,
            jax.ShapeDtypeStruct((7, cy + 8, cz), F32),
        ]
        out_specs = vmem_specs(4)
    elif kind == "middle":
        specs = vmem_specs(3)
        out_shape, out_specs = [field, *state], hbm_specs(1) + vmem_specs(2)
    else:
        specs = vmem_specs(3) + hbm_specs(1)
        out_shape, out_specs = field, hbm_specs(1)[0]
    cells = planes * (cy + 8) * cz
    return pl.pallas_call(
        functools.partial(fluid, x0, x1, cx, cy, cz, kind),
        in_specs=hbm_specs(2) + vmem_specs(2) + specs,
        out_specs=out_specs,
        out_shape=out_shape,
        scratch_shapes=[
            pltpu.VMEM((planes, cz // 128, cy + 24, 128), F32),
            pltpu.VMEM((planes, cz // 128, cy + 24, 128), F32),
            pltpu.VMEM((planes - 2, cy + 8, cz), F32),
            pltpu.VMEM((planes - 2, cy + 8, cz), F32),
            pltpu.VMEM((max(min(cx, x1 + 4) - (x0 if kind == "wet" else x0 + 4), 1), cy, cz), F32),
            pltpu.SemaphoreType.DMA((80,)),
            pltpu.SemaphoreType.DMA((80,)),
        ],
        input_output_aliases={7: 0} if kind == "end" else {},
        compiler_params=params(),
        cost_estimate=pl.CostEstimate(
            flops=48 * cells, bytes_accessed=12 * cells, transcendentals=0
        ),
        name="fluid_" + kind,
    )(phi, kappa, up, down, *more)


def shifted_pairs(n_gx, n_gy, dx, dy):
    pairs = []
    for gx in range(n_gx):
        for gy in range(n_gy):
            tx, ty = gx + dx, gy + dy
            if 0 <= tx < n_gx and 0 <= ty < n_gy:
                pairs.append((gx * n_gy + gy, tx * n_gy + ty))
    return pairs


def local(phi, kappa, stiffness, face_cell, load_dof, displacement, v_hist, w_hist, r_prev, w_prev):
    n_gx, n_gy = lax.axis_size("gx"), lax.axis_size("gy")
    peers, blk = face_cell.shape[2:]
    cx, cy, cz = phi.shape
    sx, sy = displacement.shape
    hist = v_hist.shape[0]
    wet_planes = cx // 8
    fcell = face_cell.reshape(peers, blk)
    ldof = load_dof.reshape(peers, blk)
    axes = ("gx", "gy")

    def shift(value, dx, dy):
        return lax.ppermute(value, axes, shifted_pairs(n_gx, n_gy, dx, dy))

    def exchange(value):
        return lax.all_to_all(value, axes, split_axis=0, concat_axis=0, tiled=True)

    def call(body, out_shape, scratch, name, specs, *args):
        several = isinstance(out_shape, list)
        return pl.pallas_call(
            body,
            in_specs=specs,
            out_specs=vmem_specs(len(out_shape)) if several else vmem_specs(1)[0],
            out_shape=out_shape,
            scratch_shapes=scratch,
            compiler_params=params(),
            name=name,
        )(*args)

    def f32(*shape):
        return jax.ShapeDtypeStruct(shape, F32)

    small = jnp.stack([displacement, stiffness, r_prev, w_prev])
    numbers = jnp.concatenate([fcell, ldof], axis=0)
    sent = call(
        functools.partial(gather_disp, n_gy), f32(peers, 1, 3 * blk),
        [pltpu.VMEM((peers, blk), F32)], "gather_disp", vmem_specs(2), small, numbers,
    )
    disp = exchange(sent)
    size = 8 * hist
    gram = call(
        gram_rows, f32(peers, 128),
        [
            pltpu.VMEM((sx // 8, hist, 8, sy), F32), pltpu.VMEM((size, size), F32),
            pltpu.VMEM((size, size), F32),
            pltpu.VMEM((max(128, peers, 2 * peers if peers < hist else 0), 128), F32),
            pltpu.SemaphoreType.DMA((sx // 8,)),
        ],
        "gram_rows", hbm_specs(1), v_hist,
    )
    up_send, down_send, low_send, low_up_send, low_down_send, own = packed(
        phi, kappa, disp, small, numbers
    )
    index_planes = -(-2 * (peers // 8) // 8)
    low = shift(low_send, 1, 0)
    up = shift(up_send, 0, -1)
    down = shift(down_send, 0, 1)
    low_up = shift(low_up_send, 1, -1)
    low_down = shift(low_down_send, 1, 1)
    corner = cx + index_planes + 2
    near = shift(
        jnp.concatenate([own[: index_planes + 1], up[corner:], down[corner:]], axis=0), -1, 0
    )

    chunks = cz // 128
    forced = call(
        functools.partial(scatter_disp, cx, cy, cz), f32(2 * wet_planes - 1, cy + 8, cz),
        [
            pltpu.VMEM((wet_planes * cy * chunks, 256), F32),
            pltpu.VMEM((512, wet_planes * 4 * chunks), F32),
            pltpu.VMEM((wet_planes, cy, cz), F32),
            pltpu.VMEM((wet_planes - 1, cy, cz), F32),
            pltpu.SemaphoreType.DMA((2,)),
        ],
        "scatter_disp", vmem_specs(4) + hbm_specs(2), disp, numbers, up, down, phi, kappa,
    )
    wet, state_a, state_b, send = fluid_call(
        "wet", 0, wet_planes, phi, kappa, up, down, forced, low, low_up, low_down, near, gram
    )
    high = shift(send, -1, 0)
    middle, state_a, state_b = fluid_call(
        "middle", wet_planes, cx - 4, phi, kappa, up, down, state_a, state_b, wet
    )
    field = fluid_call(
        "end", cx - 4, cx, phi, kappa, up, down, state_a, state_b, high, middle
    )
    press = call(
        functools.partial(gather_press, n_gx, n_gy), f32(peers, 1, (len(NEAR) + 1) * blk),
        [pltpu.VMEM((peers, blk), F32)], "gather_press", vmem_specs(3) + any_specs(1),
        wet, numbers, gram, middle,
    )
    loads = exchange(press)
    resp, late = call(
        shell, [f32(sx, sy), f32(peers, 1, 256)],
        [
            pltpu.VMEM((hist, sx, sy), F32),
            pltpu.VMEM((sx * (sy // 128), 256), F32),
            pltpu.VMEM((8 * (sy // 128), 256), F32),
            pltpu.VMEM((sx, 32), F32),
            pltpu.VMEM((16, 32), F32),
            pltpu.VMEM((3, sx + 8, sy + 128), F32),
            pltpu.VMEM((128, 128), F32),
            pltpu.SemaphoreType.DMA((1,)),
        ],
        "shell", vmem_specs(9) + hbm_specs(2),
        loads, numbers, small, up, down, low, low_up, low_down, near,
        v_hist, field,
    )
    x_next = call(
        solve, f32(sx, sy),
        [pltpu.VMEM((hist, sx, sy), F32), pltpu.SemaphoreType.DMA((1,))],
        "solve", vmem_specs(3) + hbm_specs(1), exchange(late), resp, small, w_hist,
    )
    return (field, x_next)


def solution(mesh):
    in_specs = (
        P("gx", "gy", None),
        P("gx", "gy", None),
        P("gx", "gy"),
        P("gx", "gy", None, None),
        P("gx", "gy", None, None),
        P("gx", "gy"),
        P(None, "gx", "gy"),
        P(None, "gx", "gy"),
        P("gx", "gy"),
        P("gx", "gy"),
    )
    out_specs = (P("gx", "gy", None), P("gx", "gy"))
    return jax.shard_map(local, mesh=mesh, in_specs=in_specs, out_specs=out_specs, check_vma=False)
```

```python
import functools

import jax
import jax.numpy as jnp
from jax import lax
from jax.experimental import pallas as pl
from jax.experimental.pallas import tpu as pltpu
from jax.sharding import PartitionSpec as P

NSUB = 4
SWEEPS = 3
HIST = 40
VMEM_BYTES = 50 * 1024 * 1024
F32 = jnp.float32
BF16 = jnp.bfloat16


def params():
    return pltpu.CompilerParams(vmem_limit_bytes=VMEM_BYTES)


def vmem_specs(count):
    return [pl.BlockSpec(memory_space=pltpu.VMEM)] * count


def any_specs(count):
    return [pl.BlockSpec(memory_space=pl.ANY)] * count


def hbm_specs(count):
    return [pl.BlockSpec(memory_space=pltpu.HBM)] * count


def pieces(value, count):
    parts = []
    for _ in range(count):
        part = value.astype(BF16)
        parts.append(part)
        value = value - part.astype(F32)
    return parts


def as_row(block):
    return jnp.concatenate([block[i : i + 1] for i in range(block.shape[0])], axis=1)


def both_rows(row):
    return jnp.broadcast_to(row, (16, row.shape[1])).astype(BF16)


def matches(keys, rows):
    ids = lax.broadcasted_iota(jnp.int32, (16, keys.shape[1]), 0).astype(F32).astype(BF16)
    found = []
    for base in range(0, rows, 256):
        key = both_rows((keys - base).astype(F32))
        for start in range(0, min(256, rows - base), 16):
            found.append(key == ids + jnp.bfloat16(start))
    return found


def one_hot(keys, rows):
    one, zero = jnp.bfloat16(1), jnp.bfloat16(0)
    return jnp.concatenate([jnp.where(m, one, zero) for m in matches(keys, rows)], axis=0)


def select_sum(table, lane, group, rows, parts):
    total = table[:rows]
    for part in range(1, parts):
        total = total + table[part * rows : (part + 1) * rows]
    ids = lax.broadcasted_iota(jnp.int32, total.shape, 0)
    return jnp.sum(jnp.where(ids == lane, total, 0.0), axis=0, keepdims=True)


def pick(table_t, index_ref, out_rows, rows, lane_bits, chunk_bits, parts, step=8):
    lanes = 1 << lane_bits
    for base in range(0, index_ref.shape[0], step):
        index = as_row(index_ref[base : base + step, :])
        lane = index & (lanes - 1)
        keys = ((index >> lane_bits) & ((1 << chunk_bits) - 1)) * rows + (
            index >> (lane_bits + chunk_bits)
        )
        hot = one_hot(keys, rows << chunk_bits)
        found = lax.dot_general(
            table_t, hot, (((1,), (0,)), ((), ())), preferred_element_type=F32
        )
        out_rows(base, select_sum(found, lane, step, lanes, parts))


def spread_values(values, lane, lanes, parts):
    zero = jnp.bfloat16(0)
    found = matches(lane, lanes)
    spread = []
    for part in pieces(values, parts):
        part = both_rows(part.astype(F32))
        spread += [jnp.where(m, part, zero) for m in found]
    return jnp.concatenate(spread, axis=0)


NEAR = ((0, 0), (1, 0), (-1, 0), (0, 1), (0, -1), (1, 1), (1, -1), (-1, 1), (-1, -1))


def tile_of(ref, plane, number):
    at = (number % 8) * 128
    return ref[plane + number // 8, :, at : at + 128]


def starter(sems):
    used = [0]

    def copy(src, dst):
        made = pltpu.make_async_copy(src, dst, sems.at[used[0]])
        used[0] += 1
        made.start()
        return made

    return copy


def gather_disp(n_gy, small_ref, numbers_ref, out_ref, own_ref):
    disp_ref = small_ref.at[0]
    peers, blk = own_ref.shape
    index_ref = numbers_ref.at[pl.ds(peers, peers)]
    sx, sy = disp_ref.shape
    chunk_bits = (sy // 128).bit_length() - 1
    columns = []
    for q in range(sy // 128):
        columns.append(jnp.transpose(disp_ref[:, q * 128 : (q + 1) * 128]))
    table_t = jnp.concatenate(pieces(jnp.concatenate(columns, axis=1), 3), axis=0)

    def write(base, row):
        for i in range(8):
            own_ref[base + i : base + i + 1, :] = row[:, i * blk : (i + 1) * blk]

    pick(table_t, index_ref, write, sx, 7, chunk_bits, 3)
    own = own_ref[...]
    beside = lax.broadcasted_iota(jnp.int32, own.shape, 0) % n_gy
    out_ref[:, 0, 0:blk] = own
    out_ref[:, 0, blk : 2 * blk] = jnp.where(
        beside == n_gy - 1, 0.0, pltpu.roll(own, peers - 1, axis=0)
    )
    out_ref[:, 0, 2 * blk : 3 * blk] = jnp.where(beside == 0, 0.0, pltpu.roll(own, 1, axis=0))


def scatter_disp(cx, cy, cz, disp_ref, numbers_ref, up_ref, down_ref, phi_ref, kappa_ref, out_ref,
                 acc_ref, side_ref, stage, kstage, sems):
    planes = stage.shape[0]
    copy = starter(sems)
    copies = [
        copy(phi_ref.at[pl.ds(0, planes)], stage),
        copy(kappa_ref.at[pl.ds(0, planes - 1)], kstage),
    ]
    peers, blk = disp_ref.shape[0], numbers_ref.shape[1]
    cells_ref = numbers_ref.at[pl.ds(0, peers)]
    rows = planes * cy
    chunks = cz // 128
    row_bits = cz.bit_length() - 1
    step = 8
    def accumulate(target, first, left, right):
        added = lax.dot_general(
            left, right, (((1,), (1,)), ((), ())), preferred_element_type=F32
        )
        if first:
            target[...] = added
        else:
            target[...] += added

    for base in range(0, peers, step):
        index = as_row(cells_ref[base : base + step, :])
        values = 0.5 * as_row(disp_ref[base : base + step, 0, 0:blk])
        keys = ((index >> 7) & (chunks - 1)) * rows + (index >> row_bits)
        accumulate(
            acc_ref, base == 0, one_hot(keys, rows * chunks),
            spread_values(values, index & 127, 128, 2),
        )
    for base in range(0, peers, step):
        for side in range(2):
            index = as_row(tile_of(up_ref if side == 0 else down_ref, cx, base // step).astype(jnp.int32))
            values = 0.5 * as_row(
                disp_ref[base : base + step, 0, (side + 1) * blk : (side + 2) * blk]
            )
            row = index >> row_bits
            plane = row // cy
            column = row - plane * cy
            inside = column < 4 if side == 0 else column >= cy - 4
            place = column if side == 0 else column - (cy - 8)
            keys = ((index >> 8) & (chunks // 2 - 1)) * (planes * 8) + plane * 8 + place
            keys = jnp.where(inside, keys, -1)
            accumulate(
                side_ref, base == 0 and side == 0, spread_values(values, index & 255, 256, 2),
                one_hot(keys, planes * 4 * chunks),
            )
    for made in copies:
        made.wait()
    upper = lax.broadcasted_iota(jnp.int32, (8, cz), 0) < 4
    for x in range(planes):
        up, down = up_ref[x], down_ref[x]
        out_ref[x, cy : cy + 8, :] = jnp.where(upper, up, down)
        if x < planes - 1:
            out_ref[planes + x, 0:cy, :] = kstage[x]
            out_ref[planes + x, cy : cy + 8, :] = pltpu.roll(
                jnp.where(upper, down, up), 4, axis=0
            )
    for q in range(chunks):
        part = acc_ref[q * rows : (q + 1) * rows, :]
        at = slice(q * 128, (q + 1) * 128)
        out_ref[0:planes, 0:cy, at] = stage[:, :, at] + (part[:, :128] + part[:, 128:]).reshape(
            planes, cy, 128
        )
    both = jnp.transpose(side_ref[0:256, :] + side_ref[256:512, :])
    for q in range(chunks // 2):
        part = both[q * planes * 8 : (q + 1) * planes * 8, :]
        at = slice(q * 256, (q + 1) * 256)
        out_ref[0:planes, cy : cy + 8, at] = out_ref[0:planes, cy : cy + 8, at] + part.reshape(
            planes, 8, 256
        )


def gather_press(n_gx, n_gy, wet_ref, numbers_ref, gram_ref, after_ref, out_ref, own_ref):
    index_ref = numbers_ref.at[pl.ds(0, own_ref.shape[0])]
    planes, cy, cz = wet_ref.shape
    peers, blk = own_ref.shape
    rows = planes * cy
    chunks = cz // 256
    columns = []
    for q in range(chunks):
        part = wet_ref[:, :, q * 256 : (q + 1) * 256].reshape(rows, 256)
        columns.append(jnp.transpose(part))
    table_t = jnp.concatenate(pieces(jnp.concatenate(columns, axis=1), 2), axis=0)

    def write(base, row):
        for i in range(8):
            own_ref[base + i : base + i + 1, :] = row[:, i * blk : (i + 1) * blk]

    pick(table_t, index_ref, write, rows, 8, chunks.bit_length() - 1, 2)
    own = own_ref[...]
    number = lax.broadcasted_iota(jnp.int32, own.shape, 0)
    at_x, at_y = number // n_gy, number % n_gy
    for k, (dx, dy) in enumerate(NEAR):
        ok = (at_x + dx >= 0) & (at_x + dx < n_gx) & (at_y + dy >= 0) & (at_y + dy < n_gy)
        moved = pltpu.roll(own, (-(dx * n_gy + dy)) % peers, axis=0) if k else own
        out_ref[:, 0, k * blk : (k + 1) * blk] = jnp.where(ok, moved, 0.0)
    out_ref[:, 0, len(NEAR) * blk : (len(NEAR) + 1) * blk] = gram_ref[...]


def gram_rows(v_ref, out_ref, v, same, cross, wide, sems):
    hist, sx, sy = v_ref.shape
    tiles = sx // 8
    copy = starter(sems)
    copies = [
        copy(v_ref.at[:, pl.ds(8 * t, 8), :], v.at[t]) for t in range(tiles)
    ]
    for t in range(tiles):
        copies[t].wait()
        high, low = pieces(v[t].reshape(hist * 8, sy), 2)

        def dot(x, y):
            return lax.dot_general(x, y, (((1,), (1,)), ((), ())), preferred_element_type=F32)

        if t == 0:
            same[...] = dot(high, high) + dot(low, low)
            cross[...] = dot(high, low)
        else:
            same[...] += dot(high, high) + dot(low, low)
            cross[...] += dot(high, low)
    size = hist * 8
    row = lax.broadcasted_iota(jnp.int32, (size, size), 0)
    column = lax.broadcasted_iota(jnp.int32, (size, size), 1)
    match = (row & 7) == (column & 7)
    group = (
        lax.broadcasted_iota(jnp.int32, (size, 128), 0) // 8
        == lax.broadcasted_iota(jnp.int32, (size, 128), 1)
    ).astype(F32)

    def reduced(ref):
        part = jnp.sum(jnp.where(match, ref[...], 0.0).reshape(hist, 8, size), axis=1)
        return jnp.dot(part, group, precision=lax.Precision.HIGHEST, preferred_element_type=F32)

    wide[...] = jnp.zeros_like(wide)
    wide[0:hist, :] = reduced(cross)
    turned = jnp.transpose(wide[0:128, :])
    wide[0:128, :] = wide[0:128, :] + turned
    wide[0:hist, :] = wide[0:hist, :] + reduced(same)
    peers = out_ref.shape[0]
    if peers >= hist:
        out_ref[...] = wide[0:peers, :]
    else:
        out_ref[...] = wide[0:peers, :] + pltpu.roll(wide[peers : 2 * peers, :], 64, axis=1)


def shell(recv_ref, numbers_ref, small_ref, up_ref, down_ref, low_ref,
          low_up_ref, low_down_ref, high_ref, v_ref, after_ref, resp_ref, late_ref, v, acc, rows_acc,
          cols_acc, corner_acc, ext, dots, v_sem):
    disp_ref, stiff_ref, prev_ref = small_ref.at[0], small_ref.at[1], small_ref.at[2]
    sx, sy = disp_ref.shape
    peers, blk = recv_ref.shape[0], numbers_ref.shape[1]
    index_ref = numbers_ref.at[pl.ds(peers, peers)]
    load_tiles = peers // 8
    index_planes = -(-2 * load_tiles // 8)
    corner_planes = -(-(load_tiles + 4) // 8)
    chunks = sy // 128
    hist = v_ref.shape[0]
    v_copy = pltpu.make_async_copy(v_ref, v, v_sem.at[0])
    v_copy.start()
    top = up_ref.shape[0] - (index_planes + 2 + corner_planes)
    low_top = low_ref.shape[0] - (index_planes + 1)
    corner_top = low_up_ref.shape[0] - corner_planes
    near_top = index_planes + 1
    load_at = [
        (high_ref, 0, load_tiles), (low_ref, low_top, load_tiles), (up_ref, top, load_tiles),
        (down_ref, top, load_tiles), (high_ref, near_top, 0),
        (high_ref, near_top + corner_planes, 0), (low_up_ref, corner_top, 0),
        (low_down_ref, corner_top, 0),
    ]

    def accumulate(target, first, keys, height, lane, lanes, values):
        added = lax.dot_general(
            one_hot(keys, height), spread_values(values, lane, lanes, 2),
            (((1,), (1,)), ((), ())), preferred_element_type=F32,
        )
        if first:
            target[...] = added
        else:
            target[...] += added

    def values_of(k, base):
        return as_row(recv_ref[base : base + 8, 0, k * blk : (k + 1) * blk])

    for base in range(0, peers, 8):
        index = as_row(index_ref[base : base + 8, :])
        keys = ((index >> 7) & (chunks - 1)) * sx + index // sy
        accumulate(acc, base == 0, keys, sx * chunks, index & 127, 128, values_of(0, base))
    for k, (dx, dy) in enumerate(NEAR):
        if k == 0:
            continue
        for base in range(0, peers, 8):
            ref, plane, number = load_at[k - 1]
            index = as_row(tile_of(ref, plane, number + base // 8).astype(jnp.int32))
            row = index // sy
            lane = index & (sy - 1)
            if dx == 1:
                row8 = jnp.where(row < 4, row, -1)
            elif dx == -1:
                row8 = jnp.where(row >= sx - 4, row - (sx - 8), -1)
            if dy == 1:
                lane8 = jnp.where(lane < 4, lane, -1)
            elif dy == -1:
                lane8 = jnp.where(lane >= sy - 4, lane - (sy - 8), -1)
            values = values_of(k, base)
            if dy == 0:
                keys = jnp.where(row8 < 0, -1, (lane >> 7) * 8 + row8)
                accumulate(
                    rows_acc, k == 1 and base == 0, keys, 8 * chunks, lane & 127, 128, values
                )
            elif dx == 0:
                accumulate(cols_acc, k == 3 and base == 0, row, sx, lane8, 16, values)
            else:
                accumulate(corner_acc, k == 5 and base == 0, row8, 16, lane8, 16, values)

    ids = lax.broadcasted_iota(jnp.int32, (16, 128), 0)
    lanes = lax.broadcasted_iota(jnp.int32, (16, 128), 1)
    placed = (jnp.where(ids < 4, ids, jnp.where(ids < 8, ids + 120, -1)) == lanes).astype(F32)

    def widened(ref):
        both = ref[:, 0:16] + ref[:, 16:32]
        return jnp.dot(both, placed, precision=lax.Precision.HIGHEST, preferred_element_type=F32)

    force, disp, stiff = ext.at[0], ext.at[1], ext.at[2]
    for q in range(chunks):
        at = slice(q * 128, (q + 1) * 128)
        part = acc[q * sx : (q + 1) * sx, :]
        force[0:sx, at] = part[:, 0:128] + part[:, 128:256]
        part = rows_acc[q * 8 : (q + 1) * 8, :]
        force[sx : sx + 8, at] = part[:, 0:128] + part[:, 128:256]
    side = slice(sy, sy + 128)
    force[0:sx, side] = widened(cols_acc)
    force[sx : sx + 8, side] = widened(corner_acc)[0:8]
    sub = lax.broadcasted_iota(jnp.int32, (8, sy), 0) < 4
    sub1 = lax.broadcasted_iota(jnp.int32, (8, 128), 0) < 4
    lane = lax.broadcasted_iota(jnp.int32, (sx, 128), 1)
    lane1 = lax.broadcasted_iota(jnp.int32, (8, 128), 1)
    for kind, (target, own) in enumerate(((disp, disp_ref), (stiff, stiff_ref))):

        def row_tile(ref, plane):
            return ref[plane, :, kind * sy : (kind + 1) * sy]

        def col_tile(ref):
            plane = top + index_planes + 1
            return jnp.concatenate([tile_of(ref, plane, m) for m in range(sx // 8)], axis=0)

        target[0:sx, 0:sy] = own[...]
        target[sx : sx + 8, 0:sy] = jnp.where(
            sub, row_tile(high_ref, index_planes), row_tile(low_ref, low_top + index_planes)
        )
        ahead, behind = col_tile(up_ref), col_tile(down_ref)
        if kind == 0:
            behind = pltpu.roll(behind, 64, axis=1)
        else:
            ahead = pltpu.roll(ahead, 64, axis=1)
        target[0:sx, side] = jnp.where(lane < 32, ahead, jnp.where(lane >= 96, behind, 0.0))

        def corner_tile(ahead, ahead_plane, behind, behind_plane):
            number = load_tiles + 2 * kind
            return jnp.where(
                lane1 < 32, tile_of(ahead, ahead_plane, number),
                jnp.where(lane1 >= 96, tile_of(behind, behind_plane, number + 1), 0.0),
            )

        target[sx : sx + 8, side] = jnp.where(
            sub1, corner_tile(high_ref, near_top, high_ref, near_top + corner_planes),
            corner_tile(low_up_ref, corner_top, low_down_ref, corner_top),
        )

    load = force[...]
    k = stiff[...]
    diag = 1.0 + 4.0 * k
    scale = 0.8 / diag
    resp = disp[...]
    high, wide = sx + 8, sy + 128
    for sweep in range(SWEEPS):
        beside = (pltpu.roll(resp, 1, axis=0) + pltpu.roll(resp, high - 1, axis=0)) + (
            pltpu.roll(resp, 1, axis=1) + pltpu.roll(resp, wide - 1, axis=1)
        )
        resp = resp + scale * (load - (diag * resp - k * beside))
    own = resp[0:sx, 0:sy]
    resp_ref[...] = own
    resid = own - disp_ref[...]
    newest = resid - prev_ref[...]
    dots[...] = jnp.zeros_like(dots)

    def folded(value):
        total = value[0:8]
        for t in range(1, sx // 8):
            total = total + value[8 * t : 8 * t + 8]
        out = total[:, 0:128]
        for q in range(1, chunks):
            out = out + total[:, q * 128 : (q + 1) * 128]
        return jnp.sum(out, axis=0, keepdims=True)

    dots[0:1, :] = folded(newest * newest)
    dots[64:65, :] = folded(resid * newest)
    v_copy.wait()
    for number in range(1, hist):
        column = v[number]
        dots[number : number + 1, :] = folded(column * newest)
        dots[64 + number : 65 + number, :] = folded(column * resid)
    late = lax.dot_general(
        jnp.ones((8, 128), F32), dots[...], (((1,), (1,)), ((), ())),
        precision=lax.Precision.HIGHEST, preferred_element_type=F32,
    )
    gram_at = len(NEAR) * blk
    gram = jnp.sum(recv_ref[:, 0, gram_at : gram_at + 128], axis=0, keepdims=True)
    late_ref[:, 0, 0:128] = jnp.broadcast_to(late[0:1], (peers, 128))
    late_ref[:, 0, 128:256] = jnp.broadcast_to(gram, (peers, 128))


def solve(recv_ref, resp_ref, small_ref, w_ref, out_ref, w, sems):
    peers = recv_ref.shape[0]
    hist = w_ref.shape[0]
    prev_ref = small_ref.at[3]
    sx, sy = resp_ref.shape
    w_copy = pltpu.make_async_copy(w_ref, w, sems.at[0])
    w_copy.start()
    late = jnp.sum(recv_ref[:, 0, 0:128], axis=0, keepdims=True)
    rows = recv_ref[:, 0, 128:256]
    if peers >= hist:
        gram = rows[0:hist]
    else:
        gram = jnp.concatenate(
            [rows, pltpu.roll(rows, 64, axis=1)[0 : hist - peers]], axis=0
        )
    row = lax.broadcasted_iota(jnp.int32, (hist, 128), 0)
    lane = lax.broadcasted_iota(jnp.int32, (hist, 128), 1)
    turned = jnp.transpose(jnp.broadcast_to(late, (128, 128)))
    gram = jnp.where(row == 0, jnp.broadcast_to(late, (hist, 128)), gram)
    gram = jnp.where(lane == 0, turned[0:hist], gram)
    gram = jnp.where(lane < hist, gram, 0.0)
    unit = row == lane
    trace = jnp.sum(jnp.where(unit, gram, 0.0), keepdims=True)
    a = gram + jnp.where(unit, 0.001 * trace / hist, 0.0)
    a = jnp.where(lane == 64, -turned[64 : 64 + hist], a)
    for j in range(hist):
        column = jnp.broadcast_to(a[:, j : j + 1], (hist, 128))
        scaled = a[j : j + 1, :] / column[j : j + 1, :]
        a = jnp.where(row == j, scaled, a - column * scaled)
    coef = jnp.broadcast_to(a[:, 64:65], (hist, 128))
    coef = jnp.concatenate([coef] * (sy // 128), axis=1)
    resp = resp_ref[...]
    total = resp + coef[0:1] * (resp - prev_ref[...])
    w_copy.wait()
    for number in range(1, hist):
        total = total + coef[number : number + 1] * w[number]
    out_ref[...] = total


def pack(phi_ref, kappa_ref, after_ref, small_ref, numbers_ref, up_ref, down_ref, low_ref, low_up_ref, low_down_ref, own_ref, phi_lo, kap_lo, phi_hi,
         kap_hi, in_sems):
    cx, cy, cz = phi_ref.shape
    disp_ref, stiff_ref = small_ref.at[0], small_ref.at[1]
    sx, sy = disp_ref.shape
    peers = numbers_ref.shape[0] // 2
    cells_ref, loads_ref = numbers_ref.at[pl.ds(0, peers)], numbers_ref.at[pl.ds(peers, peers)]
    tiles = peers // 8
    index_planes = -(-2 * tiles // 8)
    corner_planes = -(-(tiles + 4) // 8)
    copy_in = starter(in_sems)
    depth = 8
    lows = []
    for n, (ref, x) in enumerate(
        [(phi_ref, x) for x in range(cx - 4, cx)] + [(kappa_ref, x) for x in range(cx - 3, cx)]
    ):
        for t in range(cy // 8):
            lows.append(copy_in(ref.at[x, pl.ds(8 * t, 8)], low_ref.at[n * (cy // 8) + t]))
    groups = []
    for x in range(0, cx, depth):
        at = pl.ds(x, depth)
        groups.append([
            copy_in(phi_ref.at[at, pl.ds(0, 8)], phi_lo.at[at]),
            copy_in(kappa_ref.at[at, pl.ds(0, 8)], kap_lo.at[at]),
            copy_in(phi_ref.at[at, pl.ds(cy - 8, 8)], phi_hi.at[at]),
            copy_in(kappa_ref.at[at, pl.ds(cy - 8, 8)], kap_hi.at[at]),
        ])
    own_ref[...] = jnp.zeros_like(own_ref)

    def put(plane, number, tile):
        own_ref[plane + number // 8, :, (number % 8) * 128 : (number % 8 + 1) * 128] = tile

    corner = index_planes + 2
    for n in range(tiles):
        put(0, n, cells_ref[8 * n : 8 * n + 8, :].astype(F32))
        loads = loads_ref[8 * n : 8 * n + 8, :].astype(F32)
        put(0, tiles + n, loads)
        put(corner, n, loads)
    sub = lax.broadcasted_iota(jnp.int32, (8, sy), 0) < 4
    for kind, ref in enumerate((disp_ref, stiff_ref)):
        edge = jnp.where(sub, ref[0:8, :], ref[sx - 8 : sx, :])
        own_ref[index_planes, :, kind * sy : (kind + 1) * sy] = edge
        put(corner, tiles + 2 * kind, edge[:, 0:128])
        put(corner, tiles + 2 * kind + 1, edge[:, sy - 128 : sy])
    lane = lax.broadcasted_iota(jnp.int32, (sx, 128), 1)
    first, final = slice(0, 128), slice(sy - 128, sy)
    columns = jnp.where(
        lane < 32, disp_ref[:, first],
        jnp.where(
            lane < 64, pltpu.roll(disp_ref[:, final], 64, axis=1),
            jnp.where(lane < 96, pltpu.roll(stiff_ref[:, first], 64, axis=1), stiff_ref[:, final]),
        ),
    )
    for m in range(sx // 8):
        put(index_planes + 1, m, columns[8 * m : 8 * m + 8, :])
    own = own_ref[...]
    up_ref[cx:] = own
    down_ref[cx:] = own
    low_ref[7 * (cy // 8) :] = own[: index_planes + 1]
    low_up_ref[3:] = own[corner:]
    low_down_ref[3:] = own[corner:]
    upper = lax.broadcasted_iota(jnp.int32, (depth, 8, cz), 1) < 4
    for number, copies in enumerate(groups):
        for made in copies:
            made.wait()
        at = slice(number * depth, (number + 1) * depth)
        up = jnp.where(upper, phi_lo[at], pltpu.roll(kap_lo[at], 4, axis=1))
        down = jnp.where(upper, pltpu.roll(kap_hi[at], 4, axis=1), phi_hi[at])
        up_ref[at] = up
        down_ref[at] = down
        if (number + 1) * depth == cx:
            low_up_ref[0:3] = up[depth - 3 :]
            low_down_ref[0:3] = down[depth - 3 :]
    for made in lows:
        made.wait()


def packed(phi, kappa, after, small, numbers):
    cx, cy, cz = phi.shape
    tiles = numbers.shape[0] // 16
    index_planes = -(-2 * tiles // 8)
    corner_planes = -(-(tiles + 4) // 8)
    extra = index_planes + 2 + corner_planes
    low_planes = 7 * (cy // 8)

    def shape(planes):
        return jax.ShapeDtypeStruct((planes, 8, cz), F32)

    return pl.pallas_call(
        pack,
        in_specs=hbm_specs(2) + any_specs(1) + vmem_specs(2),
        out_specs=vmem_specs(6),
        out_shape=[
            shape(cx + extra), shape(cx + extra), shape(low_planes + index_planes + 1),
            shape(3 + corner_planes), shape(3 + corner_planes), shape(extra),
        ],
        scratch_shapes=[pltpu.VMEM((cx, 8, cz), F32)] * 4
        + [pltpu.SemaphoreType.DMA((cx // 2 + low_planes,))],
        compiler_params=params(),
        name="pack",
    )(phi, kappa, after, small, numbers)


def substep(src, kap, coef, write, plane, advect, rows):
    chunks = src.shape[1]
    lane = lax.broadcasted_iota(jnp.int32, (rows, 128), 1)
    first, last = lane == 0, lane == 127

    def take(at, q, start=8):
        return src[at, q, pl.ds(start, rows), :]

    for q in range(chunks):
        now = take(plane, q)
        left = take(plane, q - 1) if q else 0.0
        right = take(plane, q + 1) if q + 1 < chunks else 0.0
        total = pltpu.roll(jnp.where(last, left, now), 1, axis=1) + pltpu.roll(
            jnp.where(first, right, now), 127, axis=1
        )
        total = total + (take(plane, q, 7) + take(plane, q, 9))
        before = take(plane - 1, q)
        total = total + (before + take(plane + 1, q))
        at = slice(q * 128, (q + 1) * 128)
        write(q, (coef[plane, 0:rows, at] * now + advect * before) + kap[
            plane, 0:rows, at
        ] * total)


def fluid(x0, x1, cx, cy, cz, kind, *refs):
    planes = x1 - x0 + 8
    wide = cy + 8
    chunks = cz // 128
    tiles = cy // 8
    names = ["phi", "kappa", "up", "down"]
    names += {"wet": ["forced", "low", "low_up", "low_down", "near", "gram"],
              "middle": ["state_a", "state_b", "wet"],
              "end": ["state_a", "state_b", "high", "whole"]}[kind]
    names += {"wet": ["out", "next_a", "next_b", "send"], "middle": ["out", "next_a", "next_b"],
              "end": ["out"]}[kind]
    names += ["a", "b", "kap", "coef", "stage", "done", "sems", "kap_sems", "out_sems", "more_sems"]
    r = dict(zip(names, refs))
    a, b, kap, coef, stage = r["a"], r["b"], r["kap"], r["coef"], r["stage"]
    carried = kind != "wet"
    is_last = lax.axis_index("gx") == lax.axis_size("gx") - 1
    copy = starter(r["more_sems"])
    phi0, own1 = x0 + 4, min(cx, x1 + 4)

    def loop(lo, hi, body):
        def run(i, carry):
            body(i)
            return carry

        if hi > lo:
            lax.fori_loop(lo, hi, run, 0)

    def phi_copy(x):
        return pltpu.make_async_copy(r["phi"].at[x], stage.at[x - phi0], r["sems"].at[x - phi0])

    def kappa_copy(x):
        return pltpu.make_async_copy(
            r["kappa"].at[x], kap.at[x - (x0 - 4), pl.ds(0, cy)], r["kap_sems"].at[x - x0]
        )

    states = []
    if carried:
        states = [copy(r["state_a"], a.at[pl.ds(4, 4)]), copy(r["state_b"], b.at[pl.ds(3, 4)])]
    loop(x0, min(x0 + 4, own1), lambda x: kappa_copy(x).start())

    def start_own(x):
        phi_copy(x).start()
        kappa_copy(x).start()

    loop(phi0, own1, start_own)
    outs = []
    if kind == "middle":
        outs.append(copy(r["wet"], r["out"].at[pl.ds(0, x0)]))
    upper = lax.broadcasted_iota(jnp.int32, (8, cz), 0) < 4

    def set_kappa_edge(i, up, down):
        kap[i, cy:wide, :] = pltpu.roll(jnp.where(upper, down, up), 4, axis=0)

    def set_coef(i):
        coef[i] = 0.75 - 6.0 * kap[i]

    def repeat_rows(i, q):
        a[i, q, 7:8, :] = a[i, q, 7 + wide : 8 + wide, :]
        a[i, q, 8 + wide : 9 + wide, :] = a[i, q, 8:9, :]

    def lanes(q):
        return slice(q * 128, (q + 1) * 128)

    def set_low(i):
        from_tiles = jnp.maximum(i - 1, 0)
        up, down = r["low_up"][from_tiles], r["low_down"][from_tiles]
        edge = jnp.where(upper, up, down)
        for t in range(tiles):
            rows = r["low"][i * tiles + t]
            kap[i, 8 * t : 8 * t + 8, :] = r["low"][(i + 3) * tiles + t]
            for q in range(chunks):
                a[i, q, 8 + 8 * t : 16 + 8 * t, :] = rows[:, lanes(q)]
        set_kappa_edge(i, up, down)
        set_coef(i)
        for q in range(chunks):
            a[i, q, 8 + cy : 8 + wide, :] = edge[:, lanes(q)]
            repeat_rows(i, q)

    def set_first(i):
        x = i + (x0 - 4)
        kappa_copy(x).wait()
        set_kappa_edge(i, r["up"][x], r["down"][x])
        set_coef(i)
        if kind == "wet":
            for q in range(chunks):
                a[i, q, 8 : 8 + wide, :] = r["forced"][x, :, lanes(q)]
                repeat_rows(i, q)

    def set_own(i):
        x = i + (x0 - 4)
        phi_copy(x).wait()
        kappa_copy(x).wait()
        up, down = r["up"][x], r["down"][x]
        edge = jnp.where(upper, up, down)
        set_kappa_edge(i, up, down)
        set_coef(i)
        for q in range(chunks):
            a[i, q, 8 : 8 + cy, :] = stage[x - phi0, :, lanes(q)]
            a[i, q, 8 + cy : 8 + wide, :] = edge[:, lanes(q)]
            repeat_rows(i, q)

    def set_high(i):
        x = i + (x0 - 4) - cx
        kap[i] = r["high"][jnp.minimum(x + 4, 6)]
        set_coef(i)
        for q in range(chunks):
            a[i, q, 8 : 8 + wide, :] = r["high"][x, :, lanes(q)]
            repeat_rows(i, q)

    def step(src, dst, i):
        advect = 0.25
        if kind == "end":
            advect = jnp.where(jnp.logical_and(is_last, i + (x0 - 4) >= cx), 0.0, 0.25)

        def write(q, new):
            dst[i, q, 8 : 8 + wide, :] = new
            dst[i, q, 7:8, :] = new[wide - 1 :]
            dst[i, q, 8 + wide : 9 + wide, :] = new[0:1]

        substep(src, kap, coef, write, i, advect, wide)

    def out_copy(i):
        return pltpu.make_async_copy(
            r["done"].at[i - 4], r["out"].at[x0 + i - 4], r["out_sems"].at[i - 4]
        )

    def final(i):
        target = r["out"] if kind == "wet" else r["done"]

        def write(q, new):
            target[i - 4, :, lanes(q)] = new

        substep(b, kap, coef, write, i, 0.25, cy)
        if kind != "wet":
            out_copy(i).start()

    if kind == "wet":
        loop(0, 4, set_low)
    loop(4, 8, set_first)
    for made in states:
        made.wait()
    if kind == "wet":
        loop(8, planes, set_own)
        loop(1, planes - 1, lambda i: step(a, b, i))
    elif kind == "middle":

        def first_level(i):
            set_own(i + 1)
            step(a, b, i)

        loop(7, planes - 1, first_level)
    else:
        loop(8, planes, set_high)
        loop(7, planes - 1, lambda i: step(a, b, i))
    loop(6 if carried else 2, planes - 2, lambda i: step(b, a, i))
    loop(5 if carried else 3, planes - 3, lambda i: step(a, b, i))
    if kind != "end":
        outs.append(copy(a.at[pl.ds(planes - 4, 4)], r["next_a"]))
        outs.append(copy(b.at[pl.ds(planes - 5, 4)], r["next_b"]))
    if kind == "wet":
        outs.append(copy(r["forced"], r["send"]))
    loop(4, planes - 4, final)
    for made in outs:
        made.wait()
    if kind != "wet":
        loop(4, planes - 4, lambda i: out_copy(i).wait())


def fluid_call(kind, x0, x1, phi, kappa, up, down, *more):
    cx, cy, cz = phi.shape
    planes = x1 - x0 + 8
    field = jax.ShapeDtypeStruct((cx, cy, cz), F32)
    state = [jax.ShapeDtypeStruct((4, cz // 128, cy + 24, 128), F32)] * 2
    if kind == "wet":
        specs = vmem_specs(4) + any_specs(2)
        out_shape = [
            jax.ShapeDtypeStruct((x1 - x0, cy, cz), F32), *state,
            jax.ShapeDtypeStruct((7, cy + 8, cz), F32),
        ]
        out_specs = vmem_specs(1) + any_specs(3)
    elif kind == "middle":
        specs = any_specs(2) + vmem_specs(1)
        out_shape, out_specs = [field, *state], hbm_specs(1) + any_specs(2)
    else:
        specs = any_specs(2) + vmem_specs(1) + hbm_specs(1)
        out_shape, out_specs = field, hbm_specs(1)[0]
    cells = planes * (cy + 8) * cz
    stepped = pltpu.VMEM((planes, cz // 128, cy + 24, 128), F32)
    wide = pltpu.VMEM((planes, cy + 8, cz), F32)
    sems = pltpu.SemaphoreType.DMA((planes,))
    return pl.pallas_call(
        functools.partial(fluid, x0, x1, cx, cy, cz, kind),
        in_specs=hbm_specs(2) + vmem_specs(2) + specs,
        out_specs=out_specs,
        out_shape=out_shape,
        scratch_shapes=[
            stepped, stepped, wide, wide,
            pltpu.VMEM((max(min(cx, x1 + 4) - x0 - 4, 1), cy, cz), F32),
            pltpu.VMEM((1 if kind == "wet" else x1 - x0, cy, cz), F32),
            sems, sems, sems, pltpu.SemaphoreType.DMA((8,)),
        ],
        input_output_aliases={7: 0} if kind == "end" else {},
        compiler_params=params(),
        cost_estimate=pl.CostEstimate(
            flops=48 * cells, bytes_accessed=12 * cells, transcendentals=0
        ),
        name="fluid_" + kind,
    )(phi, kappa, up, down, *more)


def shifted_pairs(n_gx, n_gy, dx, dy):
    pairs = []
    for gx in range(n_gx):
        for gy in range(n_gy):
            tx, ty = gx + dx, gy + dy
            if 0 <= tx < n_gx and 0 <= ty < n_gy:
                pairs.append((gx * n_gy + gy, tx * n_gy + ty))
    return pairs


def local(phi, kappa, stiffness, face_cell, load_dof, displacement, v_hist, w_hist, r_prev, w_prev):
    n_gx, n_gy = lax.axis_size("gx"), lax.axis_size("gy")
    peers, blk = face_cell.shape[2:]
    cx, cy, cz = phi.shape
    sx, sy = displacement.shape
    hist = v_hist.shape[0]
    wet_planes = cx // 8
    fcell = face_cell.reshape(peers, blk)
    ldof = load_dof.reshape(peers, blk)
    axes = ("gx", "gy")

    def shift(value, dx, dy):
        return lax.ppermute(value, axes, shifted_pairs(n_gx, n_gy, dx, dy))

    def exchange(value):
        return lax.all_to_all(value, axes, split_axis=0, concat_axis=0, tiled=True)

    def call(body, out_shape, scratch, name, specs, *args):
        several = isinstance(out_shape, list)
        return pl.pallas_call(
            body,
            in_specs=specs,
            out_specs=vmem_specs(len(out_shape)) if several else vmem_specs(1)[0],
            out_shape=out_shape,
            scratch_shapes=scratch,
            compiler_params=params(),
            name=name,
        )(*args)

    def f32(*shape):
        return jax.ShapeDtypeStruct(shape, F32)

    small = jnp.stack([displacement, stiffness, r_prev, w_prev])
    numbers = jnp.concatenate([fcell, ldof], axis=0)
    sent = call(
        functools.partial(gather_disp, n_gy), f32(peers, 1, 3 * blk),
        [pltpu.VMEM((peers, blk), F32)], "gather_disp", vmem_specs(2), small, numbers,
    )
    disp = exchange(sent)
    size = 8 * hist
    gram = call(
        gram_rows, f32(peers, 128),
        [
            pltpu.VMEM((sx // 8, hist, 8, sy), F32), pltpu.VMEM((size, size), F32),
            pltpu.VMEM((size, size), F32),
            pltpu.VMEM((max(128, peers, 2 * peers if peers < hist else 0), 128), F32),
            pltpu.SemaphoreType.DMA((sx // 8,)),
        ],
        "gram_rows", hbm_specs(1), v_hist,
    )
    up_send, down_send, low_send, low_up_send, low_down_send, own = packed(
        phi, kappa, disp, small, numbers
    )
    index_planes = -(-2 * (peers // 8) // 8)
    low = shift(low_send, 1, 0)
    up = shift(up_send, 0, -1)
    down = shift(down_send, 0, 1)
    low_up = shift(low_up_send, 1, -1)
    low_down = shift(low_down_send, 1, 1)
    corner = cx + index_planes + 2
    near = shift(
        jnp.concatenate([own[: index_planes + 1], up[corner:], down[corner:]], axis=0), -1, 0
    )

    chunks = cz // 128
    forced = call(
        functools.partial(scatter_disp, cx, cy, cz), f32(2 * wet_planes - 1, cy + 8, cz),
        [
            pltpu.VMEM((wet_planes * cy * chunks, 256), F32),
            pltpu.VMEM((512, wet_planes * 4 * chunks), F32),
            pltpu.VMEM((wet_planes, cy, cz), F32),
            pltpu.VMEM((wet_planes - 1, cy, cz), F32),
            pltpu.SemaphoreType.DMA((2,)),
        ],
        "scatter_disp", vmem_specs(4) + hbm_specs(2), disp, numbers, up, down, phi, kappa,
    )
    wet, state_a, state_b, send = fluid_call(
        "wet", 0, wet_planes, phi, kappa, up, down, forced, low, low_up, low_down, near, gram
    )
    high = shift(send, -1, 0)
    middle, state_a, state_b = fluid_call(
        "middle", wet_planes, cx - 4, phi, kappa, up, down, state_a, state_b, wet
    )
    field = fluid_call(
        "end", cx - 4, cx, phi, kappa, up, down, state_a, state_b, high, middle
    )
    press = call(
        functools.partial(gather_press, n_gx, n_gy), f32(peers, 1, (len(NEAR) + 1) * blk),
        [pltpu.VMEM((peers, blk), F32)], "gather_press", vmem_specs(3) + any_specs(1),
        wet, numbers, gram, middle,
    )
    loads = exchange(press)
    resp, late = call(
        shell, [f32(sx, sy), f32(peers, 1, 256)],
        [
            pltpu.VMEM((hist, sx, sy), F32),
            pltpu.VMEM((sx * (sy // 128), 256), F32),
            pltpu.VMEM((8 * (sy // 128), 256), F32),
            pltpu.VMEM((sx, 32), F32),
            pltpu.VMEM((16, 32), F32),
            pltpu.VMEM((3, sx + 8, sy + 128), F32),
            pltpu.VMEM((128, 128), F32),
            pltpu.SemaphoreType.DMA((1,)),
        ],
        "shell", vmem_specs(9) + hbm_specs(2),
        loads, numbers, small, up, down, low, low_up, low_down, near,
        v_hist, field,
    )
    x_next = call(
        solve, f32(sx, sy),
        [pltpu.VMEM((hist, sx, sy), F32), pltpu.SemaphoreType.DMA((1,))],
        "solve", vmem_specs(3) + hbm_specs(1), exchange(late), resp, small, w_hist,
    )
    return (field, x_next)


def solution(mesh):
    in_specs = (
        P("gx", "gy", None),
        P("gx", "gy", None),
        P("gx", "gy"),
        P("gx", "gy", None, None),
        P("gx", "gy", None, None),
        P("gx", "gy"),
        P(None, "gx", "gy"),
        P(None, "gx", "gy"),
        P("gx", "gy"),
        P("gx", "gy"),
    )
    out_specs = (P("gx", "gy", None), P("gx", "gy"))
    return jax.shard_map(local, mesh=mesh, in_specs=in_specs, out_specs=out_specs, check_vma=False)
```

```python
import functools

import jax
import jax.numpy as jnp
from jax import lax
from jax.experimental import pallas as pl
from jax.experimental.pallas import tpu as pltpu
from jax.sharding import PartitionSpec as P

NSUB = 4
SWEEPS = 3
HIST = 40
VMEM_BYTES = 46 * 1024 * 1024
F32 = jnp.float32
BF16 = jnp.bfloat16


def params():
    return pltpu.CompilerParams(vmem_limit_bytes=VMEM_BYTES)


def vmem_specs(count):
    return [pl.BlockSpec(memory_space=pltpu.VMEM)] * count


def any_specs(count):
    return [pl.BlockSpec(memory_space=pl.ANY)] * count


def hbm_specs(count):
    return [pl.BlockSpec(memory_space=pltpu.HBM)] * count


def pieces(value, count):
    parts = []
    for _ in range(count):
        part = value.astype(BF16)
        parts.append(part)
        value = value - part.astype(F32)
    return parts


def as_row(block):
    return jnp.concatenate([block[i : i + 1] for i in range(block.shape[0])], axis=1)


def both_rows(row):
    return jnp.broadcast_to(row, (16, row.shape[1])).astype(BF16)


def matches(keys, rows):
    ids = lax.broadcasted_iota(jnp.int32, (16, keys.shape[1]), 0).astype(F32).astype(BF16)
    found = []
    for base in range(0, rows, 256):
        key = both_rows((keys - base).astype(F32))
        for start in range(0, min(256, rows - base), 16):
            found.append(key == ids + jnp.bfloat16(start))
    return found


def one_hot(keys, rows):
    one, zero = jnp.bfloat16(1), jnp.bfloat16(0)
    return jnp.concatenate([jnp.where(m, one, zero) for m in matches(keys, rows)], axis=0)


def select_sum(table, lane, group, rows, parts):
    total = table[:rows]
    for part in range(1, parts):
        total = total + table[part * rows : (part + 1) * rows]
    ids = lax.broadcasted_iota(jnp.int32, total.shape, 0)
    return jnp.sum(jnp.where(ids == lane, total, 0.0), axis=0, keepdims=True)


def pick(table_t, index_ref, out_rows, rows, lane_bits, chunk_bits, parts, step=8):
    lanes = 1 << lane_bits
    for base in range(0, index_ref.shape[0], step):
        index = as_row(index_ref[base : base + step, :])
        lane = index & (lanes - 1)
        keys = ((index >> lane_bits) & ((1 << chunk_bits) - 1)) * rows + (
            index >> (lane_bits + chunk_bits)
        )
        hot = one_hot(keys, rows << chunk_bits)
        found = lax.dot_general(
            table_t, hot, (((1,), (0,)), ((), ())), preferred_element_type=F32
        )
        out_rows(base, select_sum(found, lane, step, lanes, parts))


def spread_values(values, lane, lanes, parts):
    zero = jnp.bfloat16(0)
    found = matches(lane, lanes)
    spread = []
    for part in pieces(values, parts):
        part = both_rows(part.astype(F32))
        spread += [jnp.where(m, part, zero) for m in found]
    return jnp.concatenate(spread, axis=0)


NEAR = ((0, 0), (1, 0), (-1, 0), (0, 1), (0, -1), (1, 1), (1, -1), (-1, 1), (-1, -1))


def tile_of(ref, plane, number):
    at = (number % 8) * 128
    return ref[plane + number // 8, :, at : at + 128]


def starter(sems):
    used = [0]

    def copy(src, dst):
        made = pltpu.make_async_copy(src, dst, sems.at[used[0]])
        used[0] += 1
        made.start()
        return made

    return copy


def gather_disp(n_gy, small_ref, numbers_ref, out_ref, own_ref):
    disp_ref = small_ref.at[0]
    peers, blk = own_ref.shape
    index_ref = numbers_ref.at[pl.ds(peers, peers)]
    sx, sy = disp_ref.shape
    chunk_bits = (sy // 128).bit_length() - 1
    columns = []
    for q in range(sy // 128):
        columns.append(jnp.transpose(disp_ref[:, q * 128 : (q + 1) * 128]))
    table_t = jnp.concatenate(pieces(jnp.concatenate(columns, axis=1), 3), axis=0)

    def write(base, row):
        for i in range(8):
            own_ref[base + i : base + i + 1, :] = row[:, i * blk : (i + 1) * blk]

    pick(table_t, index_ref, write, sx, 7, chunk_bits, 3)
    own = own_ref[...]
    beside = lax.broadcasted_iota(jnp.int32, own.shape, 0) % n_gy
    out_ref[:, 0, 0:blk] = own
    out_ref[:, 0, blk : 2 * blk] = jnp.where(
        beside == n_gy - 1, 0.0, pltpu.roll(own, peers - 1, axis=0)
    )
    out_ref[:, 0, 2 * blk : 3 * blk] = jnp.where(beside == 0, 0.0, pltpu.roll(own, 1, axis=0))


def scatter_disp(cx, cy, cz, disp_ref, numbers_ref, up_ref, down_ref, phi_ref, kappa_ref, out_ref,
                 acc_ref, side_ref, stage, kstage, sems):
    planes = stage.shape[0]
    copy = starter(sems)
    copies = [
        copy(phi_ref.at[pl.ds(0, planes)], stage),
        copy(kappa_ref.at[pl.ds(0, planes - 1)], kstage),
    ]
    peers, blk = disp_ref.shape[0], numbers_ref.shape[1]
    cells_ref = numbers_ref.at[pl.ds(0, peers)]
    rows = planes * cy
    chunks = cz // 128
    row_bits = cz.bit_length() - 1
    step = 8
    def accumulate(target, first, left, right):
        added = lax.dot_general(
            left, right, (((1,), (1,)), ((), ())), preferred_element_type=F32
        )
        if first:
            target[...] = added
        else:
            target[...] += added

    for base in range(0, peers, step):
        index = as_row(cells_ref[base : base + step, :])
        values = 0.5 * as_row(disp_ref[base : base + step, 0, 0:blk])
        keys = ((index >> 7) & (chunks - 1)) * rows + (index >> row_bits)
        accumulate(
            acc_ref, base == 0, one_hot(keys, rows * chunks),
            spread_values(values, index & 127, 128, 2),
        )
    for base in range(0, peers, step):
        for side in range(2):
            index = as_row(tile_of(up_ref if side == 0 else down_ref, cx, base // step).astype(jnp.int32))
            values = 0.5 * as_row(
                disp_ref[base : base + step, 0, (side + 1) * blk : (side + 2) * blk]
            )
            row = index >> row_bits
            plane = row // cy
            column = row - plane * cy
            inside = column < 4 if side == 0 else column >= cy - 4
            place = column if side == 0 else column - (cy - 8)
            keys = ((index >> 8) & (chunks // 2 - 1)) * (planes * 8) + plane * 8 + place
            keys = jnp.where(inside, keys, -1)
            accumulate(
                side_ref, base == 0 and side == 0, spread_values(values, index & 255, 256, 2),
                one_hot(keys, planes * 4 * chunks),
            )
    for made in copies:
        made.wait()
    upper = lax.broadcasted_iota(jnp.int32, (8, cz), 0) < 4
    for x in range(planes):
        up, down = up_ref[x], down_ref[x]
        out_ref[x, cy : cy + 8, :] = jnp.where(upper, up, down)
        if x < planes - 1:
            out_ref[planes + x, 0:cy, :] = kstage[x]
            out_ref[planes + x, cy : cy + 8, :] = pltpu.roll(
                jnp.where(upper, down, up), 4, axis=0
            )
    for q in range(chunks):
        part = acc_ref[q * rows : (q + 1) * rows, :]
        at = slice(q * 128, (q + 1) * 128)
        out_ref[0:planes, 0:cy, at] = stage[:, :, at] + (part[:, :128] + part[:, 128:]).reshape(
            planes, cy, 128
        )
    both = jnp.transpose(side_ref[0:256, :] + side_ref[256:512, :])
    for q in range(chunks // 2):
        part = both[q * planes * 8 : (q + 1) * planes * 8, :]
        at = slice(q * 256, (q + 1) * 256)
        out_ref[0:planes, cy : cy + 8, at] = out_ref[0:planes, cy : cy + 8, at] + part.reshape(
            planes, 8, 256
        )


def gather_press(n_gx, n_gy, wet_ref, numbers_ref, gram_ref, forced_ref, out_ref, send_ref,
                 own_ref):
    send_ref[...] = forced_ref[...]
    index_ref = numbers_ref.at[pl.ds(0, own_ref.shape[0])]
    planes, cy, cz = wet_ref.shape
    peers, blk = own_ref.shape
    rows = planes * cy
    chunks = cz // 256
    columns = []
    for q in range(chunks):
        part = wet_ref[:, :, q * 256 : (q + 1) * 256].reshape(rows, 256)
        columns.append(jnp.transpose(part))
    table_t = jnp.concatenate(pieces(jnp.concatenate(columns, axis=1), 2), axis=0)

    def write(base, row):
        for i in range(8):
            own_ref[base + i : base + i + 1, :] = row[:, i * blk : (i + 1) * blk]

    pick(table_t, index_ref, write, rows, 8, chunks.bit_length() - 1, 2)
    own = own_ref[...]
    number = lax.broadcasted_iota(jnp.int32, own.shape, 0)
    at_x, at_y = number // n_gy, number % n_gy
    for k, (dx, dy) in enumerate(NEAR):
        ok = (at_x + dx >= 0) & (at_x + dx < n_gx) & (at_y + dy >= 0) & (at_y + dy < n_gy)
        moved = pltpu.roll(own, (-(dx * n_gy + dy)) % peers, axis=0) if k else own
        out_ref[:, 0, k * blk : (k + 1) * blk] = jnp.where(ok, moved, 0.0)
    out_ref[:, 0, len(NEAR) * blk : (len(NEAR) + 1) * blk] = gram_ref[...]


def gram_rows(v_ref, out_ref, v, same, cross, wide, sems):
    hist, sx, sy = v_ref.shape
    tiles = sx // 8
    copy = starter(sems)
    copies = [
        copy(v_ref.at[:, pl.ds(8 * t, 8), :], v.at[t]) for t in range(tiles)
    ]
    for t in range(tiles):
        copies[t].wait()
        high, low = pieces(v[t].reshape(hist * 8, sy), 2)

        def dot(x, y):
            return lax.dot_general(x, y, (((1,), (1,)), ((), ())), preferred_element_type=F32)

        if t == 0:
            same[...] = dot(high, high) + dot(low, low)
            cross[...] = dot(high, low)
        else:
            same[...] += dot(high, high) + dot(low, low)
            cross[...] += dot(high, low)
    size = hist * 8
    row = lax.broadcasted_iota(jnp.int32, (size, size), 0)
    column = lax.broadcasted_iota(jnp.int32, (size, size), 1)
    match = (row & 7) == (column & 7)
    group = (
        lax.broadcasted_iota(jnp.int32, (size, 128), 0) // 8
        == lax.broadcasted_iota(jnp.int32, (size, 128), 1)
    ).astype(F32)

    def reduced(ref):
        part = jnp.sum(jnp.where(match, ref[...], 0.0).reshape(hist, 8, size), axis=1)
        return jnp.dot(part, group, precision=lax.Precision.HIGHEST, preferred_element_type=F32)

    wide[...] = jnp.zeros_like(wide)
    wide[0:hist, :] = reduced(cross)
    turned = jnp.transpose(wide[0:128, :])
    wide[0:128, :] = wide[0:128, :] + turned
    wide[0:hist, :] = wide[0:hist, :] + reduced(same)
    peers = out_ref.shape[0]
    if peers >= hist:
        out_ref[...] = wide[0:peers, :]
    else:
        out_ref[...] = wide[0:peers, :] + pltpu.roll(wide[peers : 2 * peers, :], 64, axis=1)


def shell(recv_ref, numbers_ref, small_ref, up_ref, down_ref, low_ref,
          low_up_ref, low_down_ref, high_ref, v_ref, after_ref, resp_ref, late_ref, v, acc, rows_acc,
          cols_acc, corner_acc, ext, dots, v_sem):
    disp_ref, stiff_ref, prev_ref = small_ref.at[0], small_ref.at[1], small_ref.at[2]
    sx, sy = disp_ref.shape
    peers, blk = recv_ref.shape[0], numbers_ref.shape[1]
    index_ref = numbers_ref.at[pl.ds(peers, peers)]
    load_tiles = peers // 8
    index_planes = -(-2 * load_tiles // 8)
    corner_planes = -(-(load_tiles + 4) // 8)
    chunks = sy // 128
    hist = v_ref.shape[0]
    v_copy = pltpu.make_async_copy(v_ref, v, v_sem.at[0])
    v_copy.start()
    top = up_ref.shape[0] - (index_planes + 2 + corner_planes)
    low_top = low_ref.shape[0] - (index_planes + 1)
    corner_top = low_up_ref.shape[0] - corner_planes
    near_top = index_planes + 1
    load_at = [
        (high_ref, 0, load_tiles), (low_ref, low_top, load_tiles), (up_ref, top, load_tiles),
        (down_ref, top, load_tiles), (high_ref, near_top, 0),
        (high_ref, near_top + corner_planes, 0), (low_up_ref, corner_top, 0),
        (low_down_ref, corner_top, 0),
    ]

    def accumulate(target, first, keys, height, lane, lanes, values):
        added = lax.dot_general(
            one_hot(keys, height), spread_values(values, lane, lanes, 2),
            (((1,), (1,)), ((), ())), preferred_element_type=F32,
        )
        if first:
            target[...] = added
        else:
            target[...] += added

    def values_of(k, base):
        return as_row(recv_ref[base : base + 8, 0, k * blk : (k + 1) * blk])

    for base in range(0, peers, 8):
        index = as_row(index_ref[base : base + 8, :])
        keys = ((index >> 7) & (chunks - 1)) * sx + index // sy
        accumulate(acc, base == 0, keys, sx * chunks, index & 127, 128, values_of(0, base))
    for k, (dx, dy) in enumerate(NEAR):
        if k == 0:
            continue
        for base in range(0, peers, 8):
            ref, plane, number = load_at[k - 1]
            index = as_row(tile_of(ref, plane, number + base // 8).astype(jnp.int32))
            row = index // sy
            lane = index & (sy - 1)
            if dx == 1:
                row8 = jnp.where(row < 4, row, -1)
            elif dx == -1:
                row8 = jnp.where(row >= sx - 4, row - (sx - 8), -1)
            if dy == 1:
                lane8 = jnp.where(lane < 4, lane, -1)
            elif dy == -1:
                lane8 = jnp.where(lane >= sy - 4, lane - (sy - 8), -1)
            values = values_of(k, base)
            if dy == 0:
                keys = jnp.where(row8 < 0, -1, (lane >> 7) * 8 + row8)
                accumulate(
                    rows_acc, k == 1 and base == 0, keys, 8 * chunks, lane & 127, 128, values
                )
            elif dx == 0:
                accumulate(cols_acc, k == 3 and base == 0, row, sx, lane8, 16, values)
            else:
                accumulate(corner_acc, k == 5 and base == 0, row8, 16, lane8, 16, values)

    ids = lax.broadcasted_iota(jnp.int32, (16, 128), 0)
    lanes = lax.broadcasted_iota(jnp.int32, (16, 128), 1)
    placed = (jnp.where(ids < 4, ids, jnp.where(ids < 8, ids + 120, -1)) == lanes).astype(F32)

    def widened(ref):
        both = ref[:, 0:16] + ref[:, 16:32]
        return jnp.dot(both, placed, precision=lax.Precision.HIGHEST, preferred_element_type=F32)

    force, disp, stiff = ext.at[0], ext.at[1], ext.at[2]
    for q in range(chunks):
        at = slice(q * 128, (q + 1) * 128)
        part = acc[q * sx : (q + 1) * sx, :]
        force[0:sx, at] = part[:, 0:128] + part[:, 128:256]
        part = rows_acc[q * 8 : (q + 1) * 8, :]
        force[sx : sx + 8, at] = part[:, 0:128] + part[:, 128:256]
    side = slice(sy, sy + 128)
    force[0:sx, side] = widened(cols_acc)
    force[sx : sx + 8, side] = widened(corner_acc)[0:8]
    sub = lax.broadcasted_iota(jnp.int32, (8, sy), 0) < 4
    sub1 = lax.broadcasted_iota(jnp.int32, (8, 128), 0) < 4
    lane = lax.broadcasted_iota(jnp.int32, (sx, 128), 1)
    lane1 = lax.broadcasted_iota(jnp.int32, (8, 128), 1)
    for kind, (target, own) in enumerate(((disp, disp_ref), (stiff, stiff_ref))):

        def row_tile(ref, plane):
            return ref[plane, :, kind * sy : (kind + 1) * sy]

        def col_tile(ref):
            plane = top + index_planes + 1
            return jnp.concatenate([tile_of(ref, plane, m) for m in range(sx // 8)], axis=0)

        target[0:sx, 0:sy] = own[...]
        target[sx : sx + 8, 0:sy] = jnp.where(
            sub, row_tile(high_ref, index_planes), row_tile(low_ref, low_top + index_planes)
        )
        ahead, behind = col_tile(up_ref), col_tile(down_ref)
        if kind == 0:
            behind = pltpu.roll(behind, 64, axis=1)
        else:
            ahead = pltpu.roll(ahead, 64, axis=1)
        target[0:sx, side] = jnp.where(lane < 32, ahead, jnp.where(lane >= 96, behind, 0.0))

        def corner_tile(ahead, ahead_plane, behind, behind_plane):
            number = load_tiles + 2 * kind
            return jnp.where(
                lane1 < 32, tile_of(ahead, ahead_plane, number),
                jnp.where(lane1 >= 96, tile_of(behind, behind_plane, number + 1), 0.0),
            )

        target[sx : sx + 8, side] = jnp.where(
            sub1, corner_tile(high_ref, near_top, high_ref, near_top + corner_planes),
            corner_tile(low_up_ref, corner_top, low_down_ref, corner_top),
        )

    load = force[...]
    k = stiff[...]
    diag = 1.0 + 4.0 * k
    scale = 0.8 / diag
    resp = disp[...]
    high, wide = sx + 8, sy + 128
    for sweep in range(SWEEPS):
        beside = (pltpu.roll(resp, 1, axis=0) + pltpu.roll(resp, high - 1, axis=0)) + (
            pltpu.roll(resp, 1, axis=1) + pltpu.roll(resp, wide - 1, axis=1)
        )
        resp = resp + scale * (load - (diag * resp - k * beside))
    own = resp[0:sx, 0:sy]
    resp_ref[...] = own
    resid = own - disp_ref[...]
    newest = resid - prev_ref[...]
    dots[...] = jnp.zeros_like(dots)

    def folded(value):
        total = value[0:8]
        for t in range(1, sx // 8):
            total = total + value[8 * t : 8 * t + 8]
        out = total[:, 0:128]
        for q in range(1, chunks):
            out = out + total[:, q * 128 : (q + 1) * 128]
        return jnp.sum(out, axis=0, keepdims=True)

    dots[0:1, :] = folded(newest * newest)
    dots[64:65, :] = folded(resid * newest)
    v_copy.wait()
    for number in range(1, hist):
        column = v[number]
        dots[number : number + 1, :] = folded(column * newest)
        dots[64 + number : 65 + number, :] = folded(column * resid)
    late = lax.dot_general(
        jnp.ones((8, 128), F32), dots[...], (((1,), (1,)), ((), ())),
        precision=lax.Precision.HIGHEST, preferred_element_type=F32,
    )
    gram_at = len(NEAR) * blk
    gram = jnp.sum(recv_ref[:, 0, gram_at : gram_at + 128], axis=0, keepdims=True)
    late_ref[:, 0, 0:128] = jnp.broadcast_to(late[0:1], (peers, 128))
    late_ref[:, 0, 128:256] = jnp.broadcast_to(gram, (peers, 128))


def solve(recv_ref, resp_ref, small_ref, w_ref, after_ref, out_ref, w, sems):
    peers = recv_ref.shape[0]
    hist = w_ref.shape[0]
    prev_ref = small_ref.at[3]
    sx, sy = resp_ref.shape
    w_copy = pltpu.make_async_copy(w_ref, w, sems.at[0])
    w_copy.start()
    late = jnp.sum(recv_ref[:, 0, 0:128], axis=0, keepdims=True)
    rows = recv_ref[:, 0, 128:256]
    if peers >= hist:
        gram = rows[0:hist]
    else:
        gram = jnp.concatenate(
            [rows, pltpu.roll(rows, 64, axis=1)[0 : hist - peers]], axis=0
        )
    row = lax.broadcasted_iota(jnp.int32, (hist, 128), 0)
    lane = lax.broadcasted_iota(jnp.int32, (hist, 128), 1)
    turned = jnp.transpose(jnp.broadcast_to(late, (128, 128)))
    gram = jnp.where(row == 0, jnp.broadcast_to(late, (hist, 128)), gram)
    gram = jnp.where(lane == 0, turned[0:hist], gram)
    gram = jnp.where(lane < hist, gram, 0.0)
    unit = row == lane
    trace = jnp.sum(jnp.where(unit, gram, 0.0), keepdims=True)
    a = gram + jnp.where(unit, 0.001 * trace / hist, 0.0)
    a = jnp.where(lane == 64, -turned[64 : 64 + hist], a)
    for j in range(hist):
        column = jnp.broadcast_to(a[:, j : j + 1], (hist, 128))
        scaled = a[j : j + 1, :] / column[j : j + 1, :]
        a = jnp.where(row == j, scaled, a - column * scaled)
    coef = jnp.broadcast_to(a[:, 64:65], (hist, 128))
    coef = jnp.concatenate([coef] * (sy // 128), axis=1)
    resp = resp_ref[...]
    total = resp + coef[0:1] * (resp - prev_ref[...])
    w_copy.wait()
    for number in range(1, hist):
        total = total + coef[number : number + 1] * w[number]
    out_ref[...] = total


def pack(phi_ref, kappa_ref, after_ref, small_ref, numbers_ref, up_ref, down_ref, low_ref, low_up_ref, low_down_ref, own_ref, phi_lo, kap_lo, phi_hi,
         kap_hi, in_sems):
    cx, cy, cz = phi_ref.shape
    disp_ref, stiff_ref = small_ref.at[0], small_ref.at[1]
    sx, sy = disp_ref.shape
    peers = numbers_ref.shape[0] // 2
    cells_ref, loads_ref = numbers_ref.at[pl.ds(0, peers)], numbers_ref.at[pl.ds(peers, peers)]
    tiles = peers // 8
    index_planes = -(-2 * tiles // 8)
    corner_planes = -(-(tiles + 4) // 8)
    copy_in = starter(in_sems)
    depth = 8
    lows = []
    for n, (ref, x) in enumerate(
        [(phi_ref, x) for x in range(cx - 4, cx)] + [(kappa_ref, x) for x in range(cx - 3, cx)]
    ):
        for t in range(cy // 8):
            lows.append(copy_in(ref.at[x, pl.ds(8 * t, 8)], low_ref.at[n * (cy // 8) + t]))
    groups = []
    for x in range(0, cx, depth):
        at = pl.ds(x, depth)
        groups.append([
            copy_in(phi_ref.at[at, pl.ds(0, 8)], phi_lo.at[at]),
            copy_in(kappa_ref.at[at, pl.ds(0, 8)], kap_lo.at[at]),
            copy_in(phi_ref.at[at, pl.ds(cy - 8, 8)], phi_hi.at[at]),
            copy_in(kappa_ref.at[at, pl.ds(cy - 8, 8)], kap_hi.at[at]),
        ])
    own_ref[...] = jnp.zeros_like(own_ref)

    def put(plane, number, tile):
        own_ref[plane + number // 8, :, (number % 8) * 128 : (number % 8 + 1) * 128] = tile

    corner = index_planes + 2
    for n in range(tiles):
        put(0, n, cells_ref[8 * n : 8 * n + 8, :].astype(F32))
        loads = loads_ref[8 * n : 8 * n + 8, :].astype(F32)
        put(0, tiles + n, loads)
        put(corner, n, loads)
    sub = lax.broadcasted_iota(jnp.int32, (8, sy), 0) < 4
    for kind, ref in enumerate((disp_ref, stiff_ref)):
        edge = jnp.where(sub, ref[0:8, :], ref[sx - 8 : sx, :])
        own_ref[index_planes, :, kind * sy : (kind + 1) * sy] = edge
        put(corner, tiles + 2 * kind, edge[:, 0:128])
        put(corner, tiles + 2 * kind + 1, edge[:, sy - 128 : sy])
    lane = lax.broadcasted_iota(jnp.int32, (sx, 128), 1)
    first, final = slice(0, 128), slice(sy - 128, sy)
    columns = jnp.where(
        lane < 32, disp_ref[:, first],
        jnp.where(
            lane < 64, pltpu.roll(disp_ref[:, final], 64, axis=1),
            jnp.where(lane < 96, pltpu.roll(stiff_ref[:, first], 64, axis=1), stiff_ref[:, final]),
        ),
    )
    for m in range(sx // 8):
        put(index_planes + 1, m, columns[8 * m : 8 * m + 8, :])
    own = own_ref[...]
    up_ref[cx:] = own
    down_ref[cx:] = own
    low_ref[7 * (cy // 8) :] = own[: index_planes + 1]
    low_up_ref[3:] = own[corner:]
    low_down_ref[3:] = own[corner:]
    upper = lax.broadcasted_iota(jnp.int32, (depth, 8, cz), 1) < 4
    for number, copies in enumerate(groups):
        for made in copies:
            made.wait()
        at = slice(number * depth, (number + 1) * depth)
        up = jnp.where(upper, phi_lo[at], pltpu.roll(kap_lo[at], 4, axis=1))
        down = jnp.where(upper, pltpu.roll(kap_hi[at], 4, axis=1), phi_hi[at])
        up_ref[at] = up
        down_ref[at] = down
        if (number + 1) * depth == cx:
            low_up_ref[0:3] = up[depth - 3 :]
            low_down_ref[0:3] = down[depth - 3 :]
    for made in lows:
        made.wait()


def packed(phi, kappa, after, small, numbers):
    cx, cy, cz = phi.shape
    tiles = numbers.shape[0] // 16
    index_planes = -(-2 * tiles // 8)
    corner_planes = -(-(tiles + 4) // 8)
    extra = index_planes + 2 + corner_planes
    low_planes = 7 * (cy // 8)

    def shape(planes):
        return jax.ShapeDtypeStruct((planes, 8, cz), F32)

    return pl.pallas_call(
        pack,
        in_specs=hbm_specs(2) + any_specs(1) + vmem_specs(2),
        out_specs=vmem_specs(6),
        out_shape=[
            shape(cx + extra), shape(cx + extra), shape(low_planes + index_planes + 1),
            shape(3 + corner_planes), shape(3 + corner_planes), shape(extra),
        ],
        scratch_shapes=[pltpu.VMEM((cx, 8, cz), F32)] * 4
        + [pltpu.SemaphoreType.DMA((cx // 2 + low_planes,))],
        compiler_params=params(),
        name="pack",
    )(phi, kappa, after, small, numbers)


def substep(src, kap, coef, write, plane, advect, rows):
    chunks = src.shape[1]
    lane = lax.broadcasted_iota(jnp.int32, (rows, 128), 1)
    first, last = lane == 0, lane == 127

    def take(at, q, start=8):
        return src[at, q, pl.ds(start, rows), :]

    for q in range(chunks):
        now = take(plane, q)
        left = take(plane, q - 1) if q else 0.0
        right = take(plane, q + 1) if q + 1 < chunks else 0.0
        total = pltpu.roll(jnp.where(last, left, now), 1, axis=1) + pltpu.roll(
            jnp.where(first, right, now), 127, axis=1
        )
        total = total + (take(plane, q, 7) + take(plane, q, 9))
        before = take(plane - 1, q)
        total = total + (before + take(plane + 1, q))
        at = slice(q * 128, (q + 1) * 128)
        write(q, (coef[plane, 0:rows, at] * now + advect * before) + kap[
            plane, 0:rows, at
        ] * total)


def fluid(x0, x1, cx, cy, cz, kind, *refs):
    planes = x1 - x0 + 8
    wide = cy + 8
    chunks = cz // 128
    tiles = cy // 8
    names = ["phi", "kappa", "up", "down"]
    names += {"wet": ["forced", "low", "low_up", "low_down", "near", "gram"],
              "middle": ["state_a", "state_b", "wet", "press"],
              "end": ["state_a", "state_b", "high", "whole", "late"]}[kind]
    names += {"wet": ["out", "next_a", "next_b"], "middle": ["out", "next_a", "next_b"],
              "end": ["out", "token"]}[kind]
    names += ["a", "b", "kap", "coef", "stage", "done", "sems", "kap_sems", "out_sems", "more_sems"]
    r = dict(zip(names, refs))
    a, b, kap, coef, stage = r["a"], r["b"], r["kap"], r["coef"], r["stage"]
    carried = kind != "wet"
    is_last = lax.axis_index("gx") == lax.axis_size("gx") - 1
    copy = starter(r["more_sems"])
    phi0, own1 = x0 + 4, min(cx, x1 + 4)

    def loop(lo, hi, body):
        def run(i, carry):
            body(i)
            return carry

        if hi > lo:
            lax.fori_loop(lo, hi, run, 0)

    def phi_copy(x):
        return pltpu.make_async_copy(r["phi"].at[x], stage.at[x - phi0], r["sems"].at[x - phi0])

    def kappa_copy(x):
        return pltpu.make_async_copy(
            r["kappa"].at[x], kap.at[x - (x0 - 4), pl.ds(0, cy)], r["kap_sems"].at[x - x0]
        )

    states = []
    if carried:
        states = [copy(r["state_a"], a.at[pl.ds(4, 4)]), copy(r["state_b"], b.at[pl.ds(3, 4)])]
    loop(x0, min(x0 + 4, own1), lambda x: kappa_copy(x).start())

    def start_own(x):
        phi_copy(x).start()
        kappa_copy(x).start()

    loop(phi0, own1, start_own)
    outs = []
    if kind == "middle":
        outs.append(copy(r["wet"], r["out"].at[pl.ds(0, x0)]))
    upper = lax.broadcasted_iota(jnp.int32, (8, cz), 0) < 4

    def set_kappa_edge(i, up, down):
        kap[i, cy:wide, :] = pltpu.roll(jnp.where(upper, down, up), 4, axis=0)

    def set_coef(i):
        coef[i] = 0.75 - 6.0 * kap[i]

    def repeat_rows(i, q):
        a[i, q, 7:8, :] = a[i, q, 7 + wide : 8 + wide, :]
        a[i, q, 8 + wide : 9 + wide, :] = a[i, q, 8:9, :]

    def lanes(q):
        return slice(q * 128, (q + 1) * 128)

    def set_low(i):
        from_tiles = jnp.maximum(i - 1, 0)
        up, down = r["low_up"][from_tiles], r["low_down"][from_tiles]
        edge = jnp.where(upper, up, down)
        for t in range(tiles):
            rows = r["low"][i * tiles + t]
            kap[i, 8 * t : 8 * t + 8, :] = r["low"][(i + 3) * tiles + t]
            for q in range(chunks):
                a[i, q, 8 + 8 * t : 16 + 8 * t, :] = rows[:, lanes(q)]
        set_kappa_edge(i, up, down)
        set_coef(i)
        for q in range(chunks):
            a[i, q, 8 + cy : 8 + wide, :] = edge[:, lanes(q)]
            repeat_rows(i, q)

    def set_first(i):
        x = i + (x0 - 4)
        kappa_copy(x).wait()
        set_kappa_edge(i, r["up"][x], r["down"][x])
        set_coef(i)
        if kind == "wet":
            for q in range(chunks):
                a[i, q, 8 : 8 + wide, :] = r["forced"][x, :, lanes(q)]
                repeat_rows(i, q)

    def set_own(i):
        x = i + (x0 - 4)
        phi_copy(x).wait()
        kappa_copy(x).wait()
        up, down = r["up"][x], r["down"][x]
        edge = jnp.where(upper, up, down)
        set_kappa_edge(i, up, down)
        set_coef(i)
        for q in range(chunks):
            a[i, q, 8 : 8 + cy, :] = stage[x - phi0, :, lanes(q)]
            a[i, q, 8 + cy : 8 + wide, :] = edge[:, lanes(q)]
            repeat_rows(i, q)

    def set_high(i):
        x = i + (x0 - 4) - cx
        kap[i] = r["high"][jnp.minimum(x + 4, 6)]
        set_coef(i)
        for q in range(chunks):
            a[i, q, 8 : 8 + wide, :] = r["high"][x, :, lanes(q)]
            repeat_rows(i, q)

    def step(src, dst, i):
        advect = 0.25
        if kind == "end":
            advect = jnp.where(jnp.logical_and(is_last, i + (x0 - 4) >= cx), 0.0, 0.25)

        def write(q, new):
            dst[i, q, 8 : 8 + wide, :] = new
            dst[i, q, 7:8, :] = new[wide - 1 :]
            dst[i, q, 8 + wide : 9 + wide, :] = new[0:1]

        substep(src, kap, coef, write, i, advect, wide)

    def out_copy(i):
        return pltpu.make_async_copy(
            r["done"].at[i - 4], r["out"].at[x0 + i - 4], r["out_sems"].at[i - 4]
        )

    def final(i):
        target = r["out"] if kind == "wet" else r["done"]

        def write(q, new):
            target[i - 4, :, lanes(q)] = new

        substep(b, kap, coef, write, i, 0.25, cy)
        if kind != "wet":
            out_copy(i).start()

    if kind == "wet":
        loop(0, 4, set_low)
    loop(4, 8, set_first)
    for made in states:
        made.wait()
    if kind == "wet":
        loop(8, planes, set_own)
        loop(1, planes - 1, lambda i: step(a, b, i))
    elif kind == "middle":

        def first_level(i):
            set_own(i + 1)
            step(a, b, i)

        loop(7, planes - 1, first_level)
    else:
        loop(8, planes, set_high)
        loop(7, planes - 1, lambda i: step(a, b, i))
    loop(6 if carried else 2, planes - 2, lambda i: step(b, a, i))
    loop(5 if carried else 3, planes - 3, lambda i: step(a, b, i))
    if kind != "end":
        outs.append(copy(a.at[pl.ds(planes - 4, 4)], r["next_a"]))
        outs.append(copy(b.at[pl.ds(planes - 5, 4)], r["next_b"]))
    if kind == "end":
        r["token"][...] = jnp.zeros((8, 128), F32)
    loop(4, planes - 4, final)
    for made in outs:
        made.wait()
    if kind != "wet":
        loop(4, planes - 4, lambda i: out_copy(i).wait())


def fluid_call(kind, x0, x1, phi, kappa, up, down, *more):
    cx, cy, cz = phi.shape
    planes = x1 - x0 + 8
    field = jax.ShapeDtypeStruct((cx, cy, cz), F32)
    state = [jax.ShapeDtypeStruct((4, cz // 128, cy + 24, 128), F32)] * 2
    if kind == "wet":
        specs = vmem_specs(4) + any_specs(2)
        out_shape = [
            jax.ShapeDtypeStruct((x1 - x0, cy, cz), F32), *state,
        ]
        out_specs = vmem_specs(1) + any_specs(2)
    elif kind == "middle":
        specs = any_specs(2) + vmem_specs(1) + any_specs(1)
        out_shape, out_specs = [field, *state], hbm_specs(1) + any_specs(2)
    else:
        specs = any_specs(2) + vmem_specs(1) + hbm_specs(1) + any_specs(1)
        out_shape = [field, jax.ShapeDtypeStruct((8, 128), F32)]
        out_specs = hbm_specs(1) + vmem_specs(1)
    cells = planes * (cy + 8) * cz
    stepped = pltpu.VMEM((planes, cz // 128, cy + 24, 128), F32)
    wide = pltpu.VMEM((planes, cy + 8, cz), F32)
    sems = pltpu.SemaphoreType.DMA((planes,))
    return pl.pallas_call(
        functools.partial(fluid, x0, x1, cx, cy, cz, kind),
        in_specs=hbm_specs(2) + vmem_specs(2) + specs,
        out_specs=out_specs,
        out_shape=out_shape,
        scratch_shapes=[
            stepped, stepped, wide, wide,
            pltpu.VMEM((max(min(cx, x1 + 4) - x0 - 4, 1), cy, cz), F32),
            pltpu.VMEM((1 if kind == "wet" else x1 - x0, cy, cz), F32),
            sems, sems, sems, pltpu.SemaphoreType.DMA((8,)),
        ],
        input_output_aliases={7: 0} if kind == "end" else {},
        compiler_params=params(),
        cost_estimate=pl.CostEstimate(
            flops=48 * cells, bytes_accessed=12 * cells, transcendentals=0
        ),
        name="fluid_" + kind,
    )(phi, kappa, up, down, *more)


def shifted_pairs(n_gx, n_gy, dx, dy):
    pairs = []
    for gx in range(n_gx):
        for gy in range(n_gy):
            tx, ty = gx + dx, gy + dy
            if 0 <= tx < n_gx and 0 <= ty < n_gy:
                pairs.append((gx * n_gy + gy, tx * n_gy + ty))
    return pairs


def local(phi, kappa, stiffness, face_cell, load_dof, displacement, v_hist, w_hist, r_prev, w_prev):
    n_gx, n_gy = lax.axis_size("gx"), lax.axis_size("gy")
    peers, blk = face_cell.shape[2:]
    cx, cy, cz = phi.shape
    sx, sy = displacement.shape
    hist = v_hist.shape[0]
    wet_planes = cx // 8
    fcell = face_cell.reshape(peers, blk)
    ldof = load_dof.reshape(peers, blk)
    axes = ("gx", "gy")

    def shift(value, dx, dy):
        return lax.ppermute(value, axes, shifted_pairs(n_gx, n_gy, dx, dy))

    def exchange(value):
        return lax.all_to_all(value, axes, split_axis=0, concat_axis=0, tiled=True)

    def call(body, out_shape, scratch, name, specs, *args):
        several = isinstance(out_shape, list)
        return pl.pallas_call(
            body,
            in_specs=specs,
            out_specs=vmem_specs(len(out_shape)) if several else vmem_specs(1)[0],
            out_shape=out_shape,
            scratch_shapes=scratch,
            compiler_params=params(),
            name=name,
        )(*args)

    def f32(*shape):
        return jax.ShapeDtypeStruct(shape, F32)

    small = jnp.stack([displacement, stiffness, r_prev, w_prev])
    numbers = jnp.concatenate([fcell, ldof], axis=0)
    sent = call(
        functools.partial(gather_disp, n_gy), f32(peers, 1, 3 * blk),
        [pltpu.VMEM((peers, blk), F32)], "gather_disp", vmem_specs(2), small, numbers,
    )
    disp = exchange(sent)
    size = 8 * hist
    gram = call(
        gram_rows, f32(peers, 128),
        [
            pltpu.VMEM((sx // 8, hist, 8, sy), F32), pltpu.VMEM((size, size), F32),
            pltpu.VMEM((size, size), F32),
            pltpu.VMEM((max(128, peers, 2 * peers if peers < hist else 0), 128), F32),
            pltpu.SemaphoreType.DMA((sx // 8,)),
        ],
        "gram_rows", hbm_specs(1), v_hist,
    )
    up_send, down_send, low_send, low_up_send, low_down_send, own = packed(
        phi, kappa, disp, small, numbers
    )
    index_planes = -(-2 * (peers // 8) // 8)
    low = shift(low_send, 1, 0)
    up = shift(up_send, 0, -1)
    down = shift(down_send, 0, 1)
    low_up = shift(low_up_send, 1, -1)
    low_down = shift(low_down_send, 1, 1)
    corner = cx + index_planes + 2
    near = shift(
        jnp.concatenate([own[: index_planes + 1], up[corner:], down[corner:]], axis=0), -1, 0
    )

    chunks = cz // 128
    forced = call(
        functools.partial(scatter_disp, cx, cy, cz), f32(2 * wet_planes - 1, cy + 8, cz),
        [
            pltpu.VMEM((wet_planes * cy * chunks, 256), F32),
            pltpu.VMEM((512, wet_planes * 4 * chunks), F32),
            pltpu.VMEM((wet_planes, cy, cz), F32),
            pltpu.VMEM((wet_planes - 1, cy, cz), F32),
            pltpu.SemaphoreType.DMA((2,)),
        ],
        "scatter_disp", vmem_specs(4) + hbm_specs(2), disp, numbers, up, down, phi, kappa,
    )
    wet, state_a, state_b = fluid_call(
        "wet", 0, wet_planes, phi, kappa, up, down, forced, low, low_up, low_down, near, gram
    )
    press, send = call(
        functools.partial(gather_press, n_gx, n_gy), [f32(peers, 1, (len(NEAR) + 1) * blk), f32(7, cy + 8, cz)],
        [pltpu.VMEM((peers, blk), F32)], "gather_press", vmem_specs(4), wet, numbers, gram, forced,
    )
    loads = exchange(press)
    high = shift(send, -1, 0)
    middle, state_a, state_b = fluid_call(
        "middle", wet_planes, cx - 4, phi, kappa, up, down, state_a, state_b, wet, press
    )
    resp, late = call(
        shell, [f32(sx, sy), f32(peers, 1, 256)],
        [
            pltpu.VMEM((hist, sx, sy), F32),
            pltpu.VMEM((sx * (sy // 128), 256), F32),
            pltpu.VMEM((8 * (sy // 128), 256), F32),
            pltpu.VMEM((sx, 32), F32),
            pltpu.VMEM((16, 32), F32),
            pltpu.VMEM((3, sx + 8, sy + 128), F32),
            pltpu.VMEM((128, 128), F32),
            pltpu.SemaphoreType.DMA((1,)),
        ],
        "shell", vmem_specs(9) + hbm_specs(1) + any_specs(1),
        loads, numbers, small, up, down, low, low_up, low_down, near,
        v_hist, state_a,
    )
    field, token = fluid_call(
        "end", cx - 4, cx, phi, kappa, up, down, state_a, state_b, high, middle, late
    )
    x_next = call(
        solve, f32(sx, sy),
        [pltpu.VMEM((hist, sx, sy), F32), pltpu.SemaphoreType.DMA((1,))],
        "solve", vmem_specs(3) + hbm_specs(1) + any_specs(1), exchange(late), resp, small, w_hist, token,
    )
    return (field, x_next)


def solution(mesh):
    in_specs = (
        P("gx", "gy", None),
        P("gx", "gy", None),
        P("gx", "gy"),
        P("gx", "gy", None, None),
        P("gx", "gy", None, None),
        P("gx", "gy"),
        P(None, "gx", "gy"),
        P(None, "gx", "gy"),
        P("gx", "gy"),
        P("gx", "gy"),
    )
    out_specs = (P("gx", "gy", None), P("gx", "gy"))
    return jax.shard_map(local, mesh=mesh, in_specs=in_specs, out_specs=out_specs, check_vma=False)
```

```python
import functools

import jax
import jax.numpy as jnp
from jax import lax
from jax.experimental import pallas as pl
from jax.experimental.pallas import tpu as pltpu
from jax.sharding import PartitionSpec as P

NSUB = 4
SWEEPS = 3
HIST = 40
VMEM_BYTES = 46 * 1024 * 1024
ALONE_BYTES = 60 * 1024 * 1024
F32 = jnp.float32
BF16 = jnp.bfloat16


def params(alone=False):
    return pltpu.CompilerParams(vmem_limit_bytes=ALONE_BYTES if alone else VMEM_BYTES)


def vmem_specs(count):
    return [pl.BlockSpec(memory_space=pltpu.VMEM)] * count


def any_specs(count):
    return [pl.BlockSpec(memory_space=pl.ANY)] * count


def hbm_specs(count):
    return [pl.BlockSpec(memory_space=pltpu.HBM)] * count


def pieces(value, count):
    parts = []
    for _ in range(count):
        part = value.astype(BF16)
        parts.append(part)
        value = value - part.astype(F32)
    return parts


def as_row(block):
    return jnp.concatenate([block[i : i + 1] for i in range(block.shape[0])], axis=1)


def both_rows(row):
    return jnp.broadcast_to(row, (16, row.shape[1])).astype(BF16)


def matches(keys, rows):
    ids = lax.broadcasted_iota(jnp.int32, (16, keys.shape[1]), 0).astype(F32).astype(BF16)
    found = []
    for base in range(0, rows, 256):
        key = both_rows((keys - base).astype(F32))
        for start in range(0, min(256, rows - base), 16):
            found.append(key == ids + jnp.bfloat16(start))
    return found


def one_hot(keys, rows):
    one, zero = jnp.bfloat16(1), jnp.bfloat16(0)
    return jnp.concatenate([jnp.where(m, one, zero) for m in matches(keys, rows)], axis=0)


def select_sum(table, lane, group, rows, parts):
    total = table[:rows]
    for part in range(1, parts):
        total = total + table[part * rows : (part + 1) * rows]
    ids = lax.broadcasted_iota(jnp.int32, total.shape, 0)
    return jnp.sum(jnp.where(ids == lane, total, 0.0), axis=0, keepdims=True)


def pick(table_t, index_ref, out_rows, rows, lane_bits, chunk_bits, parts, step=8):
    lanes = 1 << lane_bits
    for base in range(0, index_ref.shape[0], step):
        index = as_row(index_ref[base : base + step, :])
        lane = index & (lanes - 1)
        keys = ((index >> lane_bits) & ((1 << chunk_bits) - 1)) * rows + (
            index >> (lane_bits + chunk_bits)
        )
        hot = one_hot(keys, rows << chunk_bits)
        found = lax.dot_general(
            table_t, hot, (((1,), (0,)), ((), ())), preferred_element_type=F32
        )
        out_rows(base, select_sum(found, lane, step, lanes, parts))


def spread_values(values, lane, lanes, parts):
    zero = jnp.bfloat16(0)
    found = matches(lane, lanes)
    spread = []
    for part in pieces(values, parts):
        part = both_rows(part.astype(F32))
        spread += [jnp.where(m, part, zero) for m in found]
    return jnp.concatenate(spread, axis=0)


NEAR = ((0, 0), (1, 0), (-1, 0), (0, 1), (0, -1), (1, 1), (1, -1), (-1, 1), (-1, -1))


def tile_of(ref, plane, number):
    at = (number % 8) * 128
    return ref[plane + number // 8, :, at : at + 128]


def starter(sems):
    used = [0]

    def copy(src, dst):
        made = pltpu.make_async_copy(src, dst, sems.at[used[0]])
        used[0] += 1
        made.start()
        return made

    return copy


def gather_disp(n_gy, small_ref, numbers_ref, out_ref, own_ref):
    disp_ref = small_ref.at[0]
    peers, blk = own_ref.shape
    index_ref = numbers_ref.at[pl.ds(peers, peers)]
    sx, sy = disp_ref.shape
    chunk_bits = (sy // 128).bit_length() - 1
    columns = []
    for q in range(sy // 128):
        columns.append(jnp.transpose(disp_ref[:, q * 128 : (q + 1) * 128]))
    table_t = jnp.concatenate(pieces(jnp.concatenate(columns, axis=1), 3), axis=0)

    def write(base, row):
        for i in range(8):
            own_ref[base + i : base + i + 1, :] = row[:, i * blk : (i + 1) * blk]

    pick(table_t, index_ref, write, sx, 7, chunk_bits, 3)
    own = own_ref[...]
    beside = lax.broadcasted_iota(jnp.int32, own.shape, 0) % n_gy
    out_ref[:, 0, 0:blk] = own
    out_ref[:, 0, blk : 2 * blk] = jnp.where(
        beside == n_gy - 1, 0.0, pltpu.roll(own, peers - 1, axis=0)
    )
    out_ref[:, 0, 2 * blk : 3 * blk] = jnp.where(beside == 0, 0.0, pltpu.roll(own, 1, axis=0))


def scatter_disp(cx, cy, cz, disp_ref, numbers_ref, up_ref, down_ref, phi_ref, kappa_ref, out_ref,
                 acc_ref, side_ref, stage, kstage, sems):
    planes = stage.shape[0]
    copy = starter(sems)
    copies = [
        copy(phi_ref.at[pl.ds(0, planes)], stage),
        copy(kappa_ref.at[pl.ds(0, planes - 1)], kstage),
    ]
    peers, blk = disp_ref.shape[0], numbers_ref.shape[1]
    cells_ref = numbers_ref.at[pl.ds(0, peers)]
    rows = planes * cy
    chunks = cz // 128
    row_bits = cz.bit_length() - 1
    step = 8
    def accumulate(target, first, left, right):
        added = lax.dot_general(
            left, right, (((1,), (1,)), ((), ())), preferred_element_type=F32
        )
        if first:
            target[...] = added
        else:
            target[...] += added

    for base in range(0, peers, step):
        index = as_row(cells_ref[base : base + step, :])
        values = 0.5 * as_row(disp_ref[base : base + step, 0, 0:blk])
        keys = ((index >> 7) & (chunks - 1)) * rows + (index >> row_bits)
        accumulate(
            acc_ref, base == 0, one_hot(keys, rows * chunks),
            spread_values(values, index & 127, 128, 2),
        )
    for base in range(0, peers, step):
        for side in range(2):
            index = as_row(tile_of(up_ref if side == 0 else down_ref, cx, base // step).astype(jnp.int32))
            values = 0.5 * as_row(
                disp_ref[base : base + step, 0, (side + 1) * blk : (side + 2) * blk]
            )
            row = index >> row_bits
            plane = row // cy
            column = row - plane * cy
            inside = column < 4 if side == 0 else column >= cy - 4
            place = column if side == 0 else column - (cy - 8)
            keys = ((index >> 8) & (chunks // 2 - 1)) * (planes * 8) + plane * 8 + place
            keys = jnp.where(inside, keys, -1)
            accumulate(
                side_ref, base == 0 and side == 0, spread_values(values, index & 255, 256, 2),
                one_hot(keys, planes * 4 * chunks),
            )
    for made in copies:
        made.wait()
    upper = lax.broadcasted_iota(jnp.int32, (8, cz), 0) < 4
    for x in range(planes):
        up, down = up_ref[x], down_ref[x]
        out_ref[x, cy : cy + 8, :] = jnp.where(upper, up, down)
        if x < planes - 1:
            out_ref[planes + x, 0:cy, :] = kstage[x]
            out_ref[planes + x, cy : cy + 8, :] = pltpu.roll(
                jnp.where(upper, down, up), 4, axis=0
            )
    for q in range(chunks):
        part = acc_ref[q * rows : (q + 1) * rows, :]
        at = slice(q * 128, (q + 1) * 128)
        out_ref[0:planes, 0:cy, at] = stage[:, :, at] + (part[:, :128] + part[:, 128:]).reshape(
            planes, cy, 128
        )
    both = jnp.transpose(side_ref[0:256, :] + side_ref[256:512, :])
    for q in range(chunks // 2):
        part = both[q * planes * 8 : (q + 1) * planes * 8, :]
        at = slice(q * 256, (q + 1) * 256)
        out_ref[0:planes, cy : cy + 8, at] = out_ref[0:planes, cy : cy + 8, at] + part.reshape(
            planes, 8, 256
        )


def gather_press(n_gx, n_gy, wet_ref, numbers_ref, gram_ref, forced_ref, out_ref, send_ref,
                 token_ref, own_ref):
    send_ref[...] = forced_ref[...]
    token_ref[...] = jnp.zeros((8, 128), F32)
    index_ref = numbers_ref.at[pl.ds(0, own_ref.shape[0])]
    planes, cy, cz = wet_ref.shape
    peers, blk = own_ref.shape
    rows = planes * cy
    chunks = cz // 256
    columns = []
    for q in range(chunks):
        part = wet_ref[:, :, q * 256 : (q + 1) * 256].reshape(rows, 256)
        columns.append(jnp.transpose(part))
    table_t = jnp.concatenate(pieces(jnp.concatenate(columns, axis=1), 2), axis=0)

    def write(base, row):
        for i in range(8):
            own_ref[base + i : base + i + 1, :] = row[:, i * blk : (i + 1) * blk]

    pick(table_t, index_ref, write, rows, 8, chunks.bit_length() - 1, 2)
    own = own_ref[...]
    number = lax.broadcasted_iota(jnp.int32, own.shape, 0)
    at_x, at_y = number // n_gy, number % n_gy
    for k, (dx, dy) in enumerate(NEAR):
        ok = (at_x + dx >= 0) & (at_x + dx < n_gx) & (at_y + dy >= 0) & (at_y + dy < n_gy)
        moved = pltpu.roll(own, (-(dx * n_gy + dy)) % peers, axis=0) if k else own
        out_ref[:, 0, k * blk : (k + 1) * blk] = jnp.where(ok, moved, 0.0)
    out_ref[:, 0, len(NEAR) * blk : (len(NEAR) + 1) * blk] = gram_ref[...]


def gram_rows(v_ref, out_ref, v, same, cross, wide, sems):
    hist, sx, sy = v_ref.shape
    tiles = sx // 8
    copy = starter(sems)
    copies = [
        copy(v_ref.at[:, pl.ds(8 * t, 8), :], v.at[t]) for t in range(tiles)
    ]
    for t in range(tiles):
        copies[t].wait()
        high, low = pieces(v[t].reshape(hist * 8, sy), 2)

        def dot(x, y):
            return lax.dot_general(x, y, (((1,), (1,)), ((), ())), preferred_element_type=F32)

        if t == 0:
            same[...] = dot(high, high) + dot(low, low)
            cross[...] = dot(high, low)
        else:
            same[...] += dot(high, high) + dot(low, low)
            cross[...] += dot(high, low)
    size = hist * 8
    row = lax.broadcasted_iota(jnp.int32, (size, size), 0)
    column = lax.broadcasted_iota(jnp.int32, (size, size), 1)
    match = (row & 7) == (column & 7)
    group = (
        lax.broadcasted_iota(jnp.int32, (size, 128), 0) // 8
        == lax.broadcasted_iota(jnp.int32, (size, 128), 1)
    ).astype(F32)

    def reduced(ref):
        part = jnp.sum(jnp.where(match, ref[...], 0.0).reshape(hist, 8, size), axis=1)
        return jnp.dot(part, group, precision=lax.Precision.HIGHEST, preferred_element_type=F32)

    wide[...] = jnp.zeros_like(wide)
    wide[0:hist, :] = reduced(cross)
    turned = jnp.transpose(wide[0:128, :])
    wide[0:128, :] = wide[0:128, :] + turned
    wide[0:hist, :] = wide[0:hist, :] + reduced(same)
    peers = out_ref.shape[0]
    if peers >= hist:
        out_ref[...] = wide[0:peers, :]
    else:
        out_ref[...] = wide[0:peers, :] + pltpu.roll(wide[peers : 2 * peers, :], 64, axis=1)


def shell(recv_ref, numbers_ref, small_ref, up_ref, down_ref, low_ref,
          low_up_ref, low_down_ref, high_ref, v_ref, after_ref, resp_ref, late_ref, v, acc, rows_acc,
          cols_acc, corner_acc, ext, dots, v_sem):
    disp_ref, stiff_ref, prev_ref = small_ref.at[0], small_ref.at[1], small_ref.at[2]
    sx, sy = disp_ref.shape
    peers, blk = recv_ref.shape[0], numbers_ref.shape[1]
    index_ref = numbers_ref.at[pl.ds(peers, peers)]
    load_tiles = peers // 8
    index_planes = -(-2 * load_tiles // 8)
    corner_planes = -(-(load_tiles + 4) // 8)
    chunks = sy // 128
    hist = v_ref.shape[0]
    v_copy = pltpu.make_async_copy(v_ref, v, v_sem.at[0])
    v_copy.start()
    top = up_ref.shape[0] - (index_planes + 2 + corner_planes)
    low_top = low_ref.shape[0] - (index_planes + 1)
    corner_top = low_up_ref.shape[0] - corner_planes
    near_top = index_planes + 1
    load_at = [
        (high_ref, 0, load_tiles), (low_ref, low_top, load_tiles), (up_ref, top, load_tiles),
        (down_ref, top, load_tiles), (high_ref, near_top, 0),
        (high_ref, near_top + corner_planes, 0), (low_up_ref, corner_top, 0),
        (low_down_ref, corner_top, 0),
    ]

    def accumulate(target, first, keys, height, lane, lanes, values):
        added = lax.dot_general(
            one_hot(keys, height), spread_values(values, lane, lanes, 2),
            (((1,), (1,)), ((), ())), preferred_element_type=F32,
        )
        if first:
            target[...] = added
        else:
            target[...] += added

    def values_of(k, base):
        return as_row(recv_ref[base : base + 8, 0, k * blk : (k + 1) * blk])

    for base in range(0, peers, 8):
        index = as_row(index_ref[base : base + 8, :])
        keys = ((index >> 7) & (chunks - 1)) * sx + index // sy
        accumulate(acc, base == 0, keys, sx * chunks, index & 127, 128, values_of(0, base))
    for k, (dx, dy) in enumerate(NEAR):
        if k == 0:
            continue
        for base in range(0, peers, 8):
            ref, plane, number = load_at[k - 1]
            index = as_row(tile_of(ref, plane, number + base // 8).astype(jnp.int32))
            row = index // sy
            lane = index & (sy - 1)
            if dx == 1:
                row8 = jnp.where(row < 4, row, -1)
            elif dx == -1:
                row8 = jnp.where(row >= sx - 4, row - (sx - 8), -1)
            if dy == 1:
                lane8 = jnp.where(lane < 4, lane, -1)
            elif dy == -1:
                lane8 = jnp.where(lane >= sy - 4, lane - (sy - 8), -1)
            values = values_of(k, base)
            if dy == 0:
                keys = jnp.where(row8 < 0, -1, (lane >> 7) * 8 + row8)
                accumulate(
                    rows_acc, k == 1 and base == 0, keys, 8 * chunks, lane & 127, 128, values
                )
            elif dx == 0:
                accumulate(cols_acc, k == 3 and base == 0, row, sx, lane8, 16, values)
            else:
                accumulate(corner_acc, k == 5 and base == 0, row8, 16, lane8, 16, values)

    ids = lax.broadcasted_iota(jnp.int32, (16, 128), 0)
    lanes = lax.broadcasted_iota(jnp.int32, (16, 128), 1)
    placed = (jnp.where(ids < 4, ids, jnp.where(ids < 8, ids + 120, -1)) == lanes).astype(F32)

    def widened(ref):
        both = ref[:, 0:16] + ref[:, 16:32]
        return jnp.dot(both, placed, precision=lax.Precision.HIGHEST, preferred_element_type=F32)

    force, disp, stiff = ext.at[0], ext.at[1], ext.at[2]
    for q in range(chunks):
        at = slice(q * 128, (q + 1) * 128)
        part = acc[q * sx : (q + 1) * sx, :]
        force[0:sx, at] = part[:, 0:128] + part[:, 128:256]
        part = rows_acc[q * 8 : (q + 1) * 8, :]
        force[sx : sx + 8, at] = part[:, 0:128] + part[:, 128:256]
    side = slice(sy, sy + 128)
    force[0:sx, side] = widened(cols_acc)
    force[sx : sx + 8, side] = widened(corner_acc)[0:8]
    sub = lax.broadcasted_iota(jnp.int32, (8, sy), 0) < 4
    sub1 = lax.broadcasted_iota(jnp.int32, (8, 128), 0) < 4
    lane = lax.broadcasted_iota(jnp.int32, (sx, 128), 1)
    lane1 = lax.broadcasted_iota(jnp.int32, (8, 128), 1)
    for kind, (target, own) in enumerate(((disp, disp_ref), (stiff, stiff_ref))):

        def row_tile(ref, plane):
            return ref[plane, :, kind * sy : (kind + 1) * sy]

        def col_tile(ref):
            plane = top + index_planes + 1
            return jnp.concatenate([tile_of(ref, plane, m) for m in range(sx // 8)], axis=0)

        target[0:sx, 0:sy] = own[...]
        target[sx : sx + 8, 0:sy] = jnp.where(
            sub, row_tile(high_ref, index_planes), row_tile(low_ref, low_top + index_planes)
        )
        ahead, behind = col_tile(up_ref), col_tile(down_ref)
        if kind == 0:
            behind = pltpu.roll(behind, 64, axis=1)
        else:
            ahead = pltpu.roll(ahead, 64, axis=1)
        target[0:sx, side] = jnp.where(lane < 32, ahead, jnp.where(lane >= 96, behind, 0.0))

        def corner_tile(ahead, ahead_plane, behind, behind_plane):
            number = load_tiles + 2 * kind
            return jnp.where(
                lane1 < 32, tile_of(ahead, ahead_plane, number),
                jnp.where(lane1 >= 96, tile_of(behind, behind_plane, number + 1), 0.0),
            )

        target[sx : sx + 8, side] = jnp.where(
            sub1, corner_tile(high_ref, near_top, high_ref, near_top + corner_planes),
            corner_tile(low_up_ref, corner_top, low_down_ref, corner_top),
        )

    load = force[...]
    k = stiff[...]
    diag = 1.0 + 4.0 * k
    scale = 0.8 / diag
    resp = disp[...]
    high, wide = sx + 8, sy + 128
    for sweep in range(SWEEPS):
        beside = (pltpu.roll(resp, 1, axis=0) + pltpu.roll(resp, high - 1, axis=0)) + (
            pltpu.roll(resp, 1, axis=1) + pltpu.roll(resp, wide - 1, axis=1)
        )
        resp = resp + scale * (load - (diag * resp - k * beside))
    own = resp[0:sx, 0:sy]
    resp_ref[...] = own
    resid = own - disp_ref[...]
    newest = resid - prev_ref[...]
    dots[...] = jnp.zeros_like(dots)

    def folded(value):
        total = value[0:8]
        for t in range(1, sx // 8):
            total = total + value[8 * t : 8 * t + 8]
        out = total[:, 0:128]
        for q in range(1, chunks):
            out = out + total[:, q * 128 : (q + 1) * 128]
        return jnp.sum(out, axis=0, keepdims=True)

    dots[0:1, :] = folded(newest * newest)
    dots[64:65, :] = folded(resid * newest)
    v_copy.wait()
    for number in range(1, hist):
        column = v[number]
        dots[number : number + 1, :] = folded(column * newest)
        dots[64 + number : 65 + number, :] = folded(column * resid)
    late = lax.dot_general(
        jnp.ones((8, 128), F32), dots[...], (((1,), (1,)), ((), ())),
        precision=lax.Precision.HIGHEST, preferred_element_type=F32,
    )
    gram_at = len(NEAR) * blk
    gram = jnp.sum(recv_ref[:, 0, gram_at : gram_at + 128], axis=0, keepdims=True)
    late_ref[:, 0, 0:128] = jnp.broadcast_to(late[0:1], (peers, 128))
    late_ref[:, 0, 128:256] = jnp.broadcast_to(gram, (peers, 128))


def solve(recv_ref, resp_ref, small_ref, w_ref, after_ref, out_ref, w, sems):
    peers = recv_ref.shape[0]
    hist = w_ref.shape[0]
    prev_ref = small_ref.at[3]
    sx, sy = resp_ref.shape
    w_copy = pltpu.make_async_copy(w_ref, w, sems.at[0])
    w_copy.start()
    late = jnp.sum(recv_ref[:, 0, 0:128], axis=0, keepdims=True)
    rows = recv_ref[:, 0, 128:256]
    if peers >= hist:
        gram = rows[0:hist]
    else:
        gram = jnp.concatenate(
            [rows, pltpu.roll(rows, 64, axis=1)[0 : hist - peers]], axis=0
        )
    row = lax.broadcasted_iota(jnp.int32, (hist, 128), 0)
    lane = lax.broadcasted_iota(jnp.int32, (hist, 128), 1)
    turned = jnp.transpose(jnp.broadcast_to(late, (128, 128)))
    gram = jnp.where(row == 0, jnp.broadcast_to(late, (hist, 128)), gram)
    gram = jnp.where(lane == 0, turned[0:hist], gram)
    gram = jnp.where(lane < hist, gram, 0.0)
    unit = row == lane
    trace = jnp.sum(jnp.where(unit, gram, 0.0), keepdims=True)
    a = gram + jnp.where(unit, 0.001 * trace / hist, 0.0)
    a = jnp.where(lane == 64, -turned[64 : 64 + hist], a)
    for j in range(hist):
        column = jnp.broadcast_to(a[:, j : j + 1], (hist, 128))
        scaled = a[j : j + 1, :] / column[j : j + 1, :]
        a = jnp.where(row == j, scaled, a - column * scaled)
    coef = jnp.broadcast_to(a[:, 64:65], (hist, 128))
    coef = jnp.concatenate([coef] * (sy // 128), axis=1)
    resp = resp_ref[...]
    total = resp + coef[0:1] * (resp - prev_ref[...])
    w_copy.wait()
    for number in range(1, hist):
        total = total + coef[number : number + 1] * w[number]
    out_ref[...] = total


def pack(phi_ref, kappa_ref, after_ref, small_ref, numbers_ref, up_ref, down_ref, low_ref, low_up_ref, low_down_ref, own_ref, phi_lo, kap_lo, phi_hi,
         kap_hi, in_sems):
    cx, cy, cz = phi_ref.shape
    disp_ref, stiff_ref = small_ref.at[0], small_ref.at[1]
    sx, sy = disp_ref.shape
    peers = numbers_ref.shape[0] // 2
    cells_ref, loads_ref = numbers_ref.at[pl.ds(0, peers)], numbers_ref.at[pl.ds(peers, peers)]
    tiles = peers // 8
    index_planes = -(-2 * tiles // 8)
    corner_planes = -(-(tiles + 4) // 8)
    copy_in = starter(in_sems)
    depth = 8
    lows = []
    for n, (ref, x) in enumerate(
        [(phi_ref, x) for x in range(cx - 4, cx)] + [(kappa_ref, x) for x in range(cx - 3, cx)]
    ):
        for t in range(cy // 8):
            lows.append(copy_in(ref.at[x, pl.ds(8 * t, 8)], low_ref.at[n * (cy // 8) + t]))
    groups = []
    for x in range(0, cx, depth):
        at = pl.ds(x, depth)
        groups.append([
            copy_in(phi_ref.at[at, pl.ds(0, 8)], phi_lo.at[at]),
            copy_in(kappa_ref.at[at, pl.ds(0, 8)], kap_lo.at[at]),
            copy_in(phi_ref.at[at, pl.ds(cy - 8, 8)], phi_hi.at[at]),
            copy_in(kappa_ref.at[at, pl.ds(cy - 8, 8)], kap_hi.at[at]),
        ])
    own_ref[...] = jnp.zeros_like(own_ref)

    def put(plane, number, tile):
        own_ref[plane + number // 8, :, (number % 8) * 128 : (number % 8 + 1) * 128] = tile

    corner = index_planes + 2
    for n in range(tiles):
        put(0, n, cells_ref[8 * n : 8 * n + 8, :].astype(F32))
        loads = loads_ref[8 * n : 8 * n + 8, :].astype(F32)
        put(0, tiles + n, loads)
        put(corner, n, loads)
    sub = lax.broadcasted_iota(jnp.int32, (8, sy), 0) < 4
    for kind, ref in enumerate((disp_ref, stiff_ref)):
        edge = jnp.where(sub, ref[0:8, :], ref[sx - 8 : sx, :])
        own_ref[index_planes, :, kind * sy : (kind + 1) * sy] = edge
        put(corner, tiles + 2 * kind, edge[:, 0:128])
        put(corner, tiles + 2 * kind + 1, edge[:, sy - 128 : sy])
    lane = lax.broadcasted_iota(jnp.int32, (sx, 128), 1)
    first, final = slice(0, 128), slice(sy - 128, sy)
    columns = jnp.where(
        lane < 32, disp_ref[:, first],
        jnp.where(
            lane < 64, pltpu.roll(disp_ref[:, final], 64, axis=1),
            jnp.where(lane < 96, pltpu.roll(stiff_ref[:, first], 64, axis=1), stiff_ref[:, final]),
        ),
    )
    for m in range(sx // 8):
        put(index_planes + 1, m, columns[8 * m : 8 * m + 8, :])
    own = own_ref[...]
    up_ref[cx:] = own
    down_ref[cx:] = own
    low_ref[7 * (cy // 8) :] = own[: index_planes + 1]
    low_up_ref[3:] = own[corner:]
    low_down_ref[3:] = own[corner:]
    upper = lax.broadcasted_iota(jnp.int32, (depth, 8, cz), 1) < 4
    for number, copies in enumerate(groups):
        for made in copies:
            made.wait()
        at = slice(number * depth, (number + 1) * depth)
        up = jnp.where(upper, phi_lo[at], pltpu.roll(kap_lo[at], 4, axis=1))
        down = jnp.where(upper, pltpu.roll(kap_hi[at], 4, axis=1), phi_hi[at])
        up_ref[at] = up
        down_ref[at] = down
        if (number + 1) * depth == cx:
            low_up_ref[0:3] = up[depth - 3 :]
            low_down_ref[0:3] = down[depth - 3 :]
    for made in lows:
        made.wait()


def packed(phi, kappa, after, small, numbers):
    cx, cy, cz = phi.shape
    tiles = numbers.shape[0] // 16
    index_planes = -(-2 * tiles // 8)
    corner_planes = -(-(tiles + 4) // 8)
    extra = index_planes + 2 + corner_planes
    low_planes = 7 * (cy // 8)

    def shape(planes):
        return jax.ShapeDtypeStruct((planes, 8, cz), F32)

    return pl.pallas_call(
        pack,
        in_specs=hbm_specs(2) + any_specs(1) + vmem_specs(2),
        out_specs=vmem_specs(6),
        out_shape=[
            shape(cx + extra), shape(cx + extra), shape(low_planes + index_planes + 1),
            shape(3 + corner_planes), shape(3 + corner_planes), shape(extra),
        ],
        scratch_shapes=[pltpu.VMEM((cx, 8, cz), F32)] * 4
        + [pltpu.SemaphoreType.DMA((cx // 2 + low_planes,))],
        compiler_params=params(),
        name="pack",
    )(phi, kappa, after, small, numbers)


def substep(src, kap, coef, write, plane, advect, rows):
    chunks = src.shape[1]
    lane = lax.broadcasted_iota(jnp.int32, (rows, 128), 1)
    first, last = lane == 0, lane == 127

    def take(at, q, start=8):
        return src[at, q, pl.ds(start, rows), :]

    for q in range(chunks):
        now = take(plane, q)
        left = take(plane, q - 1) if q else 0.0
        right = take(plane, q + 1) if q + 1 < chunks else 0.0
        total = pltpu.roll(jnp.where(last, left, now), 1, axis=1) + pltpu.roll(
            jnp.where(first, right, now), 127, axis=1
        )
        total = total + (take(plane, q, 7) + take(plane, q, 9))
        before = take(plane - 1, q)
        total = total + (before + take(plane + 1, q))
        at = slice(q * 128, (q + 1) * 128)
        write(q, (coef[plane, 0:rows, at] * now + advect * before) + kap[
            plane, 0:rows, at
        ] * total)


def fluid(x0, x1, cx, cy, cz, kind, *refs):
    planes = x1 - x0 + 8
    wide = cy + 8
    chunks = cz // 128
    tiles = cy // 8
    names = ["phi", "kappa", "up", "down"]
    names += {"wet": ["forced", "low", "low_up", "low_down", "near", "gram"],
              "middle": ["state_a", "state_b", "wet", "press"],
              "end": ["state_a", "state_b", "high", "whole", "late"]}[kind]
    names += {"wet": ["out", "next_a", "next_b"], "middle": ["out", "next_a", "next_b", "token"],
              "end": ["out", "token"]}[kind]
    names += ["a", "b", "kap", "coef", "stage", "done", "sems", "kap_sems", "out_sems", "more_sems"]
    r = dict(zip(names, refs))
    a, b, kap, coef, stage = r["a"], r["b"], r["kap"], r["coef"], r["stage"]
    carried = kind != "wet"
    is_last = lax.axis_index("gx") == lax.axis_size("gx") - 1
    copy = starter(r["more_sems"])
    phi0, own1 = x0 + 4, min(cx, x1 + 4)

    def loop(lo, hi, body):
        def run(i, carry):
            body(i)
            return carry

        if hi > lo:
            lax.fori_loop(lo, hi, run, 0)

    def phi_copy(x):
        return pltpu.make_async_copy(r["phi"].at[x], stage.at[x - phi0], r["sems"].at[x - phi0])

    def kappa_copy(x):
        return pltpu.make_async_copy(
            r["kappa"].at[x], kap.at[x - (x0 - 4), pl.ds(0, cy)], r["kap_sems"].at[x - x0]
        )

    states = []
    if carried:
        states = [copy(r["state_a"], a.at[pl.ds(4, 4)]), copy(r["state_b"], b.at[pl.ds(3, 4)])]
    loop(x0, min(x0 + 4, own1), lambda x: kappa_copy(x).start())

    def start_own(x):
        phi_copy(x).start()
        kappa_copy(x).start()

    loop(phi0, own1, start_own)
    outs = []
    if kind == "middle":
        outs.append(copy(r["wet"], r["out"].at[pl.ds(0, x0)]))
    upper = lax.broadcasted_iota(jnp.int32, (8, cz), 0) < 4

    def set_kappa_edge(i, up, down):
        kap[i, cy:wide, :] = pltpu.roll(jnp.where(upper, down, up), 4, axis=0)

    def set_coef(i):
        coef[i] = 0.75 - 6.0 * kap[i]

    def repeat_rows(i, q):
        a[i, q, 7:8, :] = a[i, q, 7 + wide : 8 + wide, :]
        a[i, q, 8 + wide : 9 + wide, :] = a[i, q, 8:9, :]

    def lanes(q):
        return slice(q * 128, (q + 1) * 128)

    def set_low(i):
        from_tiles = jnp.maximum(i - 1, 0)
        up, down = r["low_up"][from_tiles], r["low_down"][from_tiles]
        edge = jnp.where(upper, up, down)
        for t in range(tiles):
            rows = r["low"][i * tiles + t]
            kap[i, 8 * t : 8 * t + 8, :] = r["low"][(i + 3) * tiles + t]
            for q in range(chunks):
                a[i, q, 8 + 8 * t : 16 + 8 * t, :] = rows[:, lanes(q)]
        set_kappa_edge(i, up, down)
        set_coef(i)
        for q in range(chunks):
            a[i, q, 8 + cy : 8 + wide, :] = edge[:, lanes(q)]
            repeat_rows(i, q)

    def set_first(i):
        x = i + (x0 - 4)
        kappa_copy(x).wait()
        set_kappa_edge(i, r["up"][x], r["down"][x])
        set_coef(i)
        if kind == "wet":
            for q in range(chunks):
                a[i, q, 8 : 8 + wide, :] = r["forced"][x, :, lanes(q)]
                repeat_rows(i, q)

    def set_own(i):
        x = i + (x0 - 4)
        phi_copy(x).wait()
        kappa_copy(x).wait()
        up, down = r["up"][x], r["down"][x]
        edge = jnp.where(upper, up, down)
        set_kappa_edge(i, up, down)
        set_coef(i)
        for q in range(chunks):
            a[i, q, 8 : 8 + cy, :] = stage[x - phi0, :, lanes(q)]
            a[i, q, 8 + cy : 8 + wide, :] = edge[:, lanes(q)]
            repeat_rows(i, q)

    def set_high(i):
        x = i + (x0 - 4) - cx
        kap[i] = r["high"][jnp.minimum(x + 4, 6)]
        set_coef(i)
        for q in range(chunks):
            a[i, q, 8 : 8 + wide, :] = r["high"][x, :, lanes(q)]
            repeat_rows(i, q)

    def step(src, dst, i):
        advect = 0.25
        if kind == "end":
            advect = jnp.where(jnp.logical_and(is_last, i + (x0 - 4) >= cx), 0.0, 0.25)

        def write(q, new):
            dst[i, q, 8 : 8 + wide, :] = new
            dst[i, q, 7:8, :] = new[wide - 1 :]
            dst[i, q, 8 + wide : 9 + wide, :] = new[0:1]

        substep(src, kap, coef, write, i, advect, wide)

    def out_copy(i):
        return pltpu.make_async_copy(
            r["done"].at[i - 4], r["out"].at[x0 + i - 4], r["out_sems"].at[i - 4]
        )

    def final(i):
        target = r["out"] if kind == "wet" else r["done"]

        def write(q, new):
            target[i - 4, :, lanes(q)] = new

        substep(b, kap, coef, write, i, 0.25, cy)
        if kind != "wet":
            out_copy(i).start()

    if kind == "wet":
        loop(0, 4, set_low)
    loop(4, 8, set_first)
    for made in states:
        made.wait()
    if kind == "wet":
        loop(8, planes, set_own)
        loop(1, planes - 1, lambda i: step(a, b, i))
    elif kind == "middle":

        def first_level(i):
            set_own(i + 1)
            step(a, b, i)

        loop(7, planes - 1, first_level)
    else:
        loop(8, planes, set_high)
        loop(7, planes - 1, lambda i: step(a, b, i))
    loop(6 if carried else 2, planes - 2, lambda i: step(b, a, i))
    loop(5 if carried else 3, planes - 3, lambda i: step(a, b, i))
    if kind != "end":
        outs.append(copy(a.at[pl.ds(planes - 4, 4)], r["next_a"]))
        outs.append(copy(b.at[pl.ds(planes - 5, 4)], r["next_b"]))
    if kind != "wet":
        r["token"][...] = jnp.zeros((8, 128), F32)
    loop(4, planes - 4, final)
    for made in outs:
        made.wait()
    if kind != "wet":
        loop(4, planes - 4, lambda i: out_copy(i).wait())


def fluid_call(kind, x0, x1, phi, kappa, up, down, *more):
    cx, cy, cz = phi.shape
    planes = x1 - x0 + 8
    field = jax.ShapeDtypeStruct((cx, cy, cz), F32)
    state = [jax.ShapeDtypeStruct((4, cz // 128, cy + 24, 128), F32)] * 2
    if kind == "wet":
        specs = vmem_specs(4) + any_specs(2)
        out_shape = [
            jax.ShapeDtypeStruct((x1 - x0, cy, cz), F32), *state,
        ]
        out_specs = vmem_specs(1) + hbm_specs(2)
    elif kind == "middle":
        specs = hbm_specs(2) + vmem_specs(1) + any_specs(1)
        out_shape = [field, *state, jax.ShapeDtypeStruct((8, 128), F32)]
        out_specs = hbm_specs(3) + vmem_specs(1)
    else:
        specs = hbm_specs(2) + vmem_specs(1) + hbm_specs(1) + any_specs(1)
        out_shape = [field, jax.ShapeDtypeStruct((8, 128), F32)]
        out_specs = hbm_specs(1) + vmem_specs(1)
    cells = planes * (cy + 8) * cz
    stepped = pltpu.VMEM((planes, cz // 128, cy + 24, 128), F32)
    wide = pltpu.VMEM((planes, cy + 8, cz), F32)
    sems = pltpu.SemaphoreType.DMA((planes,))
    return pl.pallas_call(
        functools.partial(fluid, x0, x1, cx, cy, cz, kind),
        in_specs=hbm_specs(2) + vmem_specs(2) + specs,
        out_specs=out_specs,
        out_shape=out_shape,
        scratch_shapes=[
            stepped, stepped, wide, wide,
            pltpu.VMEM((max(min(cx, x1 + 4) - x0 - 4, 1), cy, cz), F32),
            pltpu.VMEM((1 if kind == "wet" else x1 - x0, cy, cz), F32),
            sems, sems, sems, pltpu.SemaphoreType.DMA((8,)),
        ],
        input_output_aliases={7: 0} if kind == "end" else {},
        compiler_params=params(kind != "wet"),
        cost_estimate=pl.CostEstimate(
            flops=48 * cells, bytes_accessed=12 * cells, transcendentals=0
        ),
        name="fluid_" + kind,
    )(phi, kappa, up, down, *more)


def shifted_pairs(n_gx, n_gy, dx, dy):
    pairs = []
    for gx in range(n_gx):
        for gy in range(n_gy):
            tx, ty = gx + dx, gy + dy
            if 0 <= tx < n_gx and 0 <= ty < n_gy:
                pairs.append((gx * n_gy + gy, tx * n_gy + ty))
    return pairs


def local(phi, kappa, stiffness, face_cell, load_dof, displacement, v_hist, w_hist, r_prev, w_prev):
    n_gx, n_gy = lax.axis_size("gx"), lax.axis_size("gy")
    peers, blk = face_cell.shape[2:]
    cx, cy, cz = phi.shape
    sx, sy = displacement.shape
    hist = v_hist.shape[0]
    wet_planes = cx // 8
    fcell = face_cell.reshape(peers, blk)
    ldof = load_dof.reshape(peers, blk)
    axes = ("gx", "gy")

    def shift(value, dx, dy):
        return lax.ppermute(value, axes, shifted_pairs(n_gx, n_gy, dx, dy))

    def exchange(value):
        return lax.all_to_all(value, axes, split_axis=0, concat_axis=0, tiled=True)

    def call(body, out_shape, scratch, name, specs, *args):
        several = isinstance(out_shape, list)
        return pl.pallas_call(
            body,
            in_specs=specs,
            out_specs=vmem_specs(len(out_shape)) if several else vmem_specs(1)[0],
            out_shape=out_shape,
            scratch_shapes=scratch,
            compiler_params=params(name in ("shell", "solve")),
            name=name,
        )(*args)

    def f32(*shape):
        return jax.ShapeDtypeStruct(shape, F32)

    small = jnp.stack([displacement, stiffness, r_prev, w_prev])
    numbers = jnp.concatenate([fcell, ldof], axis=0)
    sent = call(
        functools.partial(gather_disp, n_gy), f32(peers, 1, 3 * blk),
        [pltpu.VMEM((peers, blk), F32)], "gather_disp", vmem_specs(2), small, numbers,
    )
    disp = exchange(sent)
    size = 8 * hist
    gram = call(
        gram_rows, f32(peers, 128),
        [
            pltpu.VMEM((sx // 8, hist, 8, sy), F32), pltpu.VMEM((size, size), F32),
            pltpu.VMEM((size, size), F32),
            pltpu.VMEM((max(128, peers, 2 * peers if peers < hist else 0), 128), F32),
            pltpu.SemaphoreType.DMA((sx // 8,)),
        ],
        "gram_rows", hbm_specs(1), v_hist,
    )
    up_send, down_send, low_send, low_up_send, low_down_send, own = packed(
        phi, kappa, disp, small, numbers
    )
    index_planes = -(-2 * (peers // 8) // 8)
    low = shift(low_send, 1, 0)
    up = shift(up_send, 0, -1)
    down = shift(down_send, 0, 1)
    low_up = shift(low_up_send, 1, -1)
    low_down = shift(low_down_send, 1, 1)
    corner = cx + index_planes + 2
    near = shift(
        jnp.concatenate([own[: index_planes + 1], up[corner:], down[corner:]], axis=0), -1, 0
    )

    chunks = cz // 128
    forced = call(
        functools.partial(scatter_disp, cx, cy, cz), f32(2 * wet_planes - 1, cy + 8, cz),
        [
            pltpu.VMEM((wet_planes * cy * chunks, 256), F32),
            pltpu.VMEM((512, wet_planes * 4 * chunks), F32),
            pltpu.VMEM((wet_planes, cy, cz), F32),
            pltpu.VMEM((wet_planes - 1, cy, cz), F32),
            pltpu.SemaphoreType.DMA((2,)),
        ],
        "scatter_disp", vmem_specs(4) + hbm_specs(2), disp, numbers, up, down, phi, kappa,
    )
    wet, state_a, state_b = fluid_call(
        "wet", 0, wet_planes, phi, kappa, up, down, forced, low, low_up, low_down, near, gram
    )
    press, send, token = call(
        functools.partial(gather_press, n_gx, n_gy), [f32(peers, 1, (len(NEAR) + 1) * blk), f32(7, cy + 8, cz), f32(8, 128)],
        [pltpu.VMEM((peers, blk), F32)], "gather_press", vmem_specs(4), wet, numbers, gram, forced,
    )
    loads = exchange(press)
    high = shift(send, -1, 0)
    middle, state_a, state_b, token = fluid_call(
        "middle", wet_planes, cx - 4, phi, kappa, up, down, state_a, state_b, wet, token
    )
    resp, late = call(
        shell, [f32(sx, sy), f32(peers, 1, 256)],
        [
            pltpu.VMEM((hist, sx, sy), F32),
            pltpu.VMEM((sx * (sy // 128), 256), F32),
            pltpu.VMEM((8 * (sy // 128), 256), F32),
            pltpu.VMEM((sx, 32), F32),
            pltpu.VMEM((16, 32), F32),
            pltpu.VMEM((3, sx + 8, sy + 128), F32),
            pltpu.VMEM((128, 128), F32),
            pltpu.SemaphoreType.DMA((1,)),
        ],
        "shell", vmem_specs(9) + hbm_specs(1) + any_specs(1),
        loads, numbers, small, up, down, low, low_up, low_down, near,
        v_hist, token,
    )
    field, token = fluid_call(
        "end", cx - 4, cx, phi, kappa, up, down, state_a, state_b, high, middle, late
    )
    x_next = call(
        solve, f32(sx, sy),
        [pltpu.VMEM((hist, sx, sy), F32), pltpu.SemaphoreType.DMA((1,))],
        "solve", vmem_specs(3) + hbm_specs(1) + any_specs(1), exchange(late), resp, small, w_hist, token,
    )
    return (field, x_next)


def solution(mesh):
    in_specs = (
        P("gx", "gy", None),
        P("gx", "gy", None),
        P("gx", "gy"),
        P("gx", "gy", None, None),
        P("gx", "gy", None, None),
        P("gx", "gy"),
        P(None, "gx", "gy"),
        P(None, "gx", "gy"),
        P("gx", "gy"),
        P("gx", "gy"),
    )
    out_specs = (P("gx", "gy", None), P("gx", "gy"))
    return jax.shard_map(local, mesh=mesh, in_specs=in_specs, out_specs=out_specs, check_vma=False)
```

```python
import functools

import jax
import jax.numpy as jnp
from jax import lax
from jax.experimental import pallas as pl
from jax.experimental.pallas import tpu as pltpu
from jax.sharding import PartitionSpec as P

NSUB = 4
SWEEPS = 3
HIST = 40
VMEM_BYTES = 46 * 1024 * 1024
ALONE_BYTES = 60 * 1024 * 1024
F32 = jnp.float32
BF16 = jnp.bfloat16


def params(alone=False):
    return pltpu.CompilerParams(vmem_limit_bytes=ALONE_BYTES if alone else VMEM_BYTES)


def vmem_specs(count):
    return [pl.BlockSpec(memory_space=pltpu.VMEM)] * count


def any_specs(count):
    return [pl.BlockSpec(memory_space=pl.ANY)] * count


def hbm_specs(count):
    return [pl.BlockSpec(memory_space=pltpu.HBM)] * count


def pieces(value, count):
    parts = []
    for _ in range(count):
        part = value.astype(BF16)
        parts.append(part)
        value = value - part.astype(F32)
    return parts


def as_row(block):
    return jnp.concatenate([block[i : i + 1] for i in range(block.shape[0])], axis=1)


def both_rows(row):
    return jnp.broadcast_to(row, (16, row.shape[1])).astype(BF16)


def matches(keys, rows):
    ids = lax.broadcasted_iota(jnp.int32, (16, keys.shape[1]), 0).astype(F32).astype(BF16)
    found = []
    for base in range(0, rows, 256):
        key = both_rows((keys - base).astype(F32))
        for start in range(0, min(256, rows - base), 16):
            found.append(key == ids + jnp.bfloat16(start))
    return found


def one_hot(keys, rows):
    one, zero = jnp.bfloat16(1), jnp.bfloat16(0)
    return jnp.concatenate([jnp.where(m, one, zero) for m in matches(keys, rows)], axis=0)


def select_sum(table, lane, group, rows, parts):
    total = table[:rows]
    for part in range(1, parts):
        total = total + table[part * rows : (part + 1) * rows]
    ids = lax.broadcasted_iota(jnp.int32, total.shape, 0)
    return jnp.sum(jnp.where(ids == lane, total, 0.0), axis=0, keepdims=True)


def pick(table_t, index_ref, out_rows, rows, lane_bits, chunk_bits, parts, step=8):
    lanes = 1 << lane_bits
    for base in range(0, index_ref.shape[0], step):
        index = as_row(index_ref[base : base + step, :])
        lane = index & (lanes - 1)
        keys = ((index >> lane_bits) & ((1 << chunk_bits) - 1)) * rows + (
            index >> (lane_bits + chunk_bits)
        )
        hot = one_hot(keys, rows << chunk_bits)
        found = lax.dot_general(
            table_t, hot, (((1,), (0,)), ((), ())), preferred_element_type=F32
        )
        out_rows(base, select_sum(found, lane, step, lanes, parts))


def spread_values(values, lane, lanes, parts):
    zero = jnp.bfloat16(0)
    found = matches(lane, lanes)
    spread = []
    for part in pieces(values, parts):
        part = both_rows(part.astype(F32))
        spread += [jnp.where(m, part, zero) for m in found]
    return jnp.concatenate(spread, axis=0)


NEAR = ((0, 0), (1, 0), (-1, 0), (0, 1), (0, -1), (1, 1), (1, -1), (-1, 1), (-1, -1))


def tile_of(ref, plane, number):
    at = (number % 8) * 128
    return ref[plane + number // 8, :, at : at + 128]


def starter(sems):
    used = [0]

    def copy(src, dst):
        made = pltpu.make_async_copy(src, dst, sems.at[used[0]])
        used[0] += 1
        made.start()
        return made

    return copy


def gather_disp(n_gy, small_ref, numbers_ref, out_ref, own_ref):
    disp_ref = small_ref.at[0]
    peers, blk = own_ref.shape
    index_ref = numbers_ref.at[pl.ds(peers, peers)]
    sx, sy = disp_ref.shape
    chunk_bits = (sy // 128).bit_length() - 1
    columns = []
    for q in range(sy // 128):
        columns.append(jnp.transpose(disp_ref[:, q * 128 : (q + 1) * 128]))
    table_t = jnp.concatenate(pieces(jnp.concatenate(columns, axis=1), 3), axis=0)

    def write(base, row):
        for i in range(8):
            own_ref[base + i : base + i + 1, :] = row[:, i * blk : (i + 1) * blk]

    pick(table_t, index_ref, write, sx, 7, chunk_bits, 3)
    own = own_ref[...]
    beside = lax.broadcasted_iota(jnp.int32, own.shape, 0) % n_gy
    out_ref[:, 0, 0:blk] = own
    out_ref[:, 0, blk : 2 * blk] = jnp.where(
        beside == n_gy - 1, 0.0, pltpu.roll(own, peers - 1, axis=0)
    )
    out_ref[:, 0, 2 * blk : 3 * blk] = jnp.where(beside == 0, 0.0, pltpu.roll(own, 1, axis=0))


def scatter_disp(cx, cy, cz, disp_ref, numbers_ref, up_ref, down_ref, phi_ref, kappa_ref, out_ref,
                 acc_ref, side_ref, stage, kstage, sems):
    planes = stage.shape[0]
    copy = starter(sems)
    copies = [
        copy(phi_ref.at[pl.ds(0, planes)], stage),
        copy(kappa_ref.at[pl.ds(0, planes - 1)], kstage),
    ]
    peers, blk = disp_ref.shape[0], numbers_ref.shape[1]
    cells_ref = numbers_ref.at[pl.ds(0, peers)]
    rows = planes * cy
    chunks = cz // 128
    row_bits = cz.bit_length() - 1
    step = 8
    def accumulate(target, first, left, right):
        added = lax.dot_general(
            left, right, (((1,), (1,)), ((), ())), preferred_element_type=F32
        )
        if first:
            target[...] = added
        else:
            target[...] += added

    for base in range(0, peers, step):
        index = as_row(cells_ref[base : base + step, :])
        values = 0.5 * as_row(disp_ref[base : base + step, 0, 0:blk])
        keys = ((index >> 7) & (chunks - 1)) * rows + (index >> row_bits)
        accumulate(
            acc_ref, base == 0, one_hot(keys, rows * chunks),
            spread_values(values, index & 127, 128, 2),
        )
    for base in range(0, peers, step):
        for side in range(2):
            index = as_row(tile_of(up_ref if side == 0 else down_ref, cx, base // step).astype(jnp.int32))
            values = 0.5 * as_row(
                disp_ref[base : base + step, 0, (side + 1) * blk : (side + 2) * blk]
            )
            row = index >> row_bits
            plane = row // cy
            column = row - plane * cy
            inside = column < 4 if side == 0 else column >= cy - 4
            place = column if side == 0 else column - (cy - 8)
            keys = ((index >> 8) & (chunks // 2 - 1)) * (planes * 8) + plane * 8 + place
            keys = jnp.where(inside, keys, -1)
            accumulate(
                side_ref, base == 0 and side == 0, spread_values(values, index & 255, 256, 2),
                one_hot(keys, planes * 4 * chunks),
            )
    for made in copies:
        made.wait()
    upper = lax.broadcasted_iota(jnp.int32, (8, cz), 0) < 4
    for x in range(planes):
        up, down = up_ref[x], down_ref[x]
        out_ref[x, cy : cy + 8, :] = jnp.where(upper, up, down)
        if x < planes - 1:
            out_ref[planes + x, 0:cy, :] = kstage[x]
            out_ref[planes + x, cy : cy + 8, :] = pltpu.roll(
                jnp.where(upper, down, up), 4, axis=0
            )
    for q in range(chunks):
        part = acc_ref[q * rows : (q + 1) * rows, :]
        at = slice(q * 128, (q + 1) * 128)
        out_ref[0:planes, 0:cy, at] = stage[:, :, at] + (part[:, :128] + part[:, 128:]).reshape(
            planes, cy, 128
        )
    both = jnp.transpose(side_ref[0:256, :] + side_ref[256:512, :])
    for q in range(chunks // 2):
        part = both[q * planes * 8 : (q + 1) * planes * 8, :]
        at = slice(q * 256, (q + 1) * 256)
        out_ref[0:planes, cy : cy + 8, at] = out_ref[0:planes, cy : cy + 8, at] + part.reshape(
            planes, 8, 256
        )


def gather_press(n_gx, n_gy, wet_ref, numbers_ref, gram_ref, out_ref, token_ref, own_ref):
    token_ref[...] = jnp.zeros((8, 128), F32)
    index_ref = numbers_ref.at[pl.ds(0, own_ref.shape[0])]
    planes, cy, cz = wet_ref.shape
    peers, blk = own_ref.shape
    rows = planes * cy
    chunks = cz // 256
    columns = []
    for q in range(chunks):
        part = wet_ref[:, :, q * 256 : (q + 1) * 256].reshape(rows, 256)
        columns.append(jnp.transpose(part))
    table_t = jnp.concatenate(pieces(jnp.concatenate(columns, axis=1), 2), axis=0)

    def write(base, row):
        for i in range(8):
            own_ref[base + i : base + i + 1, :] = row[:, i * blk : (i + 1) * blk]

    pick(table_t, index_ref, write, rows, 8, chunks.bit_length() - 1, 2)
    own = own_ref[...]
    number = lax.broadcasted_iota(jnp.int32, own.shape, 0)
    at_x, at_y = number // n_gy, number % n_gy
    for k, (dx, dy) in enumerate(NEAR):
        ok = (at_x + dx >= 0) & (at_x + dx < n_gx) & (at_y + dy >= 0) & (at_y + dy < n_gy)
        moved = pltpu.roll(own, (-(dx * n_gy + dy)) % peers, axis=0) if k else own
        out_ref[:, 0, k * blk : (k + 1) * blk] = jnp.where(ok, moved, 0.0)
    out_ref[:, 0, len(NEAR) * blk : (len(NEAR) + 1) * blk] = gram_ref[...]


def gram_rows(v_ref, out_ref, v, same, cross, wide, sems):
    hist, sx, sy = v_ref.shape
    tiles = sx // 8
    copy = starter(sems)
    copies = [
        copy(v_ref.at[:, pl.ds(8 * t, 8), :], v.at[t]) for t in range(tiles)
    ]
    for t in range(tiles):
        copies[t].wait()
        high, low = pieces(v[t].reshape(hist * 8, sy), 2)

        def dot(x, y):
            return lax.dot_general(x, y, (((1,), (1,)), ((), ())), preferred_element_type=F32)

        if t == 0:
            same[...] = dot(high, high) + dot(low, low)
            cross[...] = dot(high, low)
        else:
            same[...] += dot(high, high) + dot(low, low)
            cross[...] += dot(high, low)
    size = hist * 8
    row = lax.broadcasted_iota(jnp.int32, (size, size), 0)
    column = lax.broadcasted_iota(jnp.int32, (size, size), 1)
    match = (row & 7) == (column & 7)
    group = (
        lax.broadcasted_iota(jnp.int32, (size, 128), 0) // 8
        == lax.broadcasted_iota(jnp.int32, (size, 128), 1)
    ).astype(F32)

    def reduced(ref):
        part = jnp.sum(jnp.where(match, ref[...], 0.0).reshape(hist, 8, size), axis=1)
        return jnp.dot(part, group, precision=lax.Precision.HIGHEST, preferred_element_type=F32)

    wide[...] = jnp.zeros_like(wide)
    wide[0:hist, :] = reduced(cross)
    turned = jnp.transpose(wide[0:128, :])
    wide[0:128, :] = wide[0:128, :] + turned
    wide[0:hist, :] = wide[0:hist, :] + reduced(same)
    peers = out_ref.shape[0]
    if peers >= hist:
        out_ref[...] = wide[0:peers, :]
    else:
        out_ref[...] = wide[0:peers, :] + pltpu.roll(wide[peers : 2 * peers, :], 64, axis=1)


def shell(recv_ref, numbers_ref, small_ref, up_ref, down_ref, low_ref,
          low_up_ref, low_down_ref, high_ref, v_ref, after_ref, resp_ref, late_ref, v, acc, rows_acc,
          cols_acc, corner_acc, ext, dots, v_sem):
    disp_ref, stiff_ref, prev_ref = small_ref.at[0], small_ref.at[1], small_ref.at[2]
    sx, sy = disp_ref.shape
    peers, blk = recv_ref.shape[0], numbers_ref.shape[1]
    index_ref = numbers_ref.at[pl.ds(peers, peers)]
    load_tiles = peers // 8
    index_planes = -(-2 * load_tiles // 8)
    corner_planes = -(-(load_tiles + 4) // 8)
    chunks = sy // 128
    hist = v_ref.shape[0]
    v_copy = pltpu.make_async_copy(v_ref, v, v_sem.at[0])
    v_copy.start()
    top = up_ref.shape[0] - (index_planes + 2 + corner_planes)
    low_top = low_ref.shape[0] - (index_planes + 1)
    corner_top = low_up_ref.shape[0] - corner_planes
    near_top = index_planes + 1
    load_at = [
        (high_ref, 0, load_tiles), (low_ref, low_top, load_tiles), (up_ref, top, load_tiles),
        (down_ref, top, load_tiles), (high_ref, near_top, 0),
        (high_ref, near_top + corner_planes, 0), (low_up_ref, corner_top, 0),
        (low_down_ref, corner_top, 0),
    ]

    def accumulate(target, first, keys, height, lane, lanes, values):
        added = lax.dot_general(
            one_hot(keys, height), spread_values(values, lane, lanes, 2),
            (((1,), (1,)), ((), ())), preferred_element_type=F32,
        )
        if first:
            target[...] = added
        else:
            target[...] += added

    def values_of(k, base):
        return as_row(recv_ref[base : base + 8, 0, k * blk : (k + 1) * blk])

    for base in range(0, peers, 8):
        index = as_row(index_ref[base : base + 8, :])
        keys = ((index >> 7) & (chunks - 1)) * sx + index // sy
        accumulate(acc, base == 0, keys, sx * chunks, index & 127, 128, values_of(0, base))
    for k, (dx, dy) in enumerate(NEAR):
        if k == 0:
            continue
        for base in range(0, peers, 8):
            ref, plane, number = load_at[k - 1]
            index = as_row(tile_of(ref, plane, number + base // 8).astype(jnp.int32))
            row = index // sy
            lane = index & (sy - 1)
            if dx == 1:
                row8 = jnp.where(row < 4, row, -1)
            elif dx == -1:
                row8 = jnp.where(row >= sx - 4, row - (sx - 8), -1)
            if dy == 1:
                lane8 = jnp.where(lane < 4, lane, -1)
            elif dy == -1:
                lane8 = jnp.where(lane >= sy - 4, lane - (sy - 8), -1)
            values = values_of(k, base)
            if dy == 0:
                keys = jnp.where(row8 < 0, -1, (lane >> 7) * 8 + row8)
                accumulate(
                    rows_acc, k == 1 and base == 0, keys, 8 * chunks, lane & 127, 128, values
                )
            elif dx == 0:
                accumulate(cols_acc, k == 3 and base == 0, row, sx, lane8, 16, values)
            else:
                accumulate(corner_acc, k == 5 and base == 0, row8, 16, lane8, 16, values)

    ids = lax.broadcasted_iota(jnp.int32, (16, 128), 0)
    lanes = lax.broadcasted_iota(jnp.int32, (16, 128), 1)
    placed = (jnp.where(ids < 4, ids, jnp.where(ids < 8, ids + 120, -1)) == lanes).astype(F32)

    def widened(ref):
        both = ref[:, 0:16] + ref[:, 16:32]
        return jnp.dot(both, placed, precision=lax.Precision.HIGHEST, preferred_element_type=F32)

    force, disp, stiff = ext.at[0], ext.at[1], ext.at[2]
    for q in range(chunks):
        at = slice(q * 128, (q + 1) * 128)
        part = acc[q * sx : (q + 1) * sx, :]
        force[0:sx, at] = part[:, 0:128] + part[:, 128:256]
        part = rows_acc[q * 8 : (q + 1) * 8, :]
        force[sx : sx + 8, at] = part[:, 0:128] + part[:, 128:256]
    side = slice(sy, sy + 128)
    force[0:sx, side] = widened(cols_acc)
    force[sx : sx + 8, side] = widened(corner_acc)[0:8]
    sub = lax.broadcasted_iota(jnp.int32, (8, sy), 0) < 4
    sub1 = lax.broadcasted_iota(jnp.int32, (8, 128), 0) < 4
    lane = lax.broadcasted_iota(jnp.int32, (sx, 128), 1)
    lane1 = lax.broadcasted_iota(jnp.int32, (8, 128), 1)
    for kind, (target, own) in enumerate(((disp, disp_ref), (stiff, stiff_ref))):

        def row_tile(ref, plane):
            return ref[plane, :, kind * sy : (kind + 1) * sy]

        def col_tile(ref):
            plane = top + index_planes + 1
            return jnp.concatenate([tile_of(ref, plane, m) for m in range(sx // 8)], axis=0)

        target[0:sx, 0:sy] = own[...]
        target[sx : sx + 8, 0:sy] = jnp.where(
            sub, row_tile(high_ref, index_planes), row_tile(low_ref, low_top + index_planes)
        )
        ahead, behind = col_tile(up_ref), col_tile(down_ref)
        if kind == 0:
            behind = pltpu.roll(behind, 64, axis=1)
        else:
            ahead = pltpu.roll(ahead, 64, axis=1)
        target[0:sx, side] = jnp.where(lane < 32, ahead, jnp.where(lane >= 96, behind, 0.0))

        def corner_tile(ahead, ahead_plane, behind, behind_plane):
            number = load_tiles + 2 * kind
            return jnp.where(
                lane1 < 32, tile_of(ahead, ahead_plane, number),
                jnp.where(lane1 >= 96, tile_of(behind, behind_plane, number + 1), 0.0),
            )

        target[sx : sx + 8, side] = jnp.where(
            sub1, corner_tile(high_ref, near_top, high_ref, near_top + corner_planes),
            corner_tile(low_up_ref, corner_top, low_down_ref, corner_top),
        )

    load = force[...]
    k = stiff[...]
    diag = 1.0 + 4.0 * k
    scale = 0.8 / diag
    resp = disp[...]
    high, wide = sx + 8, sy + 128
    for sweep in range(SWEEPS):
        beside = (pltpu.roll(resp, 1, axis=0) + pltpu.roll(resp, high - 1, axis=0)) + (
            pltpu.roll(resp, 1, axis=1) + pltpu.roll(resp, wide - 1, axis=1)
        )
        resp = resp + scale * (load - (diag * resp - k * beside))
    own = resp[0:sx, 0:sy]
    resp_ref[...] = own
    resid = own - disp_ref[...]
    newest = resid - prev_ref[...]
    dots[...] = jnp.zeros_like(dots)

    def folded(value):
        total = value[0:8]
        for t in range(1, sx // 8):
            total = total + value[8 * t : 8 * t + 8]
        out = total[:, 0:128]
        for q in range(1, chunks):
            out = out + total[:, q * 128 : (q + 1) * 128]
        return jnp.sum(out, axis=0, keepdims=True)

    dots[0:1, :] = folded(newest * newest)
    dots[64:65, :] = folded(resid * newest)
    v_copy.wait()
    for number in range(1, hist):
        column = v[number]
        dots[number : number + 1, :] = folded(column * newest)
        dots[64 + number : 65 + number, :] = folded(column * resid)
    late = lax.dot_general(
        jnp.ones((8, 128), F32), dots[...], (((1,), (1,)), ((), ())),
        precision=lax.Precision.HIGHEST, preferred_element_type=F32,
    )
    gram_at = len(NEAR) * blk
    gram = jnp.sum(recv_ref[:, 0, gram_at : gram_at + 128], axis=0, keepdims=True)
    late_ref[:, 0, 0:128] = jnp.broadcast_to(late[0:1], (peers, 128))
    late_ref[:, 0, 128:256] = jnp.broadcast_to(gram, (peers, 128))


def solve(recv_ref, resp_ref, small_ref, w_ref, after_ref, out_ref, w, sems):
    peers = recv_ref.shape[0]
    hist = w_ref.shape[0]
    prev_ref = small_ref.at[3]
    sx, sy = resp_ref.shape
    w_copy = pltpu.make_async_copy(w_ref, w, sems.at[0])
    w_copy.start()
    late = jnp.sum(recv_ref[:, 0, 0:128], axis=0, keepdims=True)
    rows = recv_ref[:, 0, 128:256]
    if peers >= hist:
        gram = rows[0:hist]
    else:
        gram = jnp.concatenate(
            [rows, pltpu.roll(rows, 64, axis=1)[0 : hist - peers]], axis=0
        )
    row = lax.broadcasted_iota(jnp.int32, (hist, 128), 0)
    lane = lax.broadcasted_iota(jnp.int32, (hist, 128), 1)
    turned = jnp.transpose(jnp.broadcast_to(late, (128, 128)))
    gram = jnp.where(row == 0, jnp.broadcast_to(late, (hist, 128)), gram)
    gram = jnp.where(lane == 0, turned[0:hist], gram)
    gram = jnp.where(lane < hist, gram, 0.0)
    unit = row == lane
    trace = jnp.sum(jnp.where(unit, gram, 0.0), keepdims=True)
    a = gram + jnp.where(unit, 0.001 * trace / hist, 0.0)
    a = jnp.where(lane == 64, -turned[64 : 64 + hist], a)
    for j in range(hist):
        column = jnp.broadcast_to(a[:, j : j + 1], (hist, 128))
        scaled = a[j : j + 1, :] / column[j : j + 1, :]
        a = jnp.where(row == j, scaled, a - column * scaled)
    coef = jnp.broadcast_to(a[:, 64:65], (hist, 128))
    coef = jnp.concatenate([coef] * (sy // 128), axis=1)
    resp = resp_ref[...]
    total = resp + coef[0:1] * (resp - prev_ref[...])
    w_copy.wait()
    for number in range(1, hist):
        total = total + coef[number : number + 1] * w[number]
    out_ref[...] = total


def pack(phi_ref, kappa_ref, after_ref, small_ref, numbers_ref, up_ref, down_ref, low_ref, low_up_ref, low_down_ref, own_ref, phi_lo, kap_lo, phi_hi,
         kap_hi, in_sems):
    cx, cy, cz = phi_ref.shape
    disp_ref, stiff_ref = small_ref.at[0], small_ref.at[1]
    sx, sy = disp_ref.shape
    peers = numbers_ref.shape[0] // 2
    cells_ref, loads_ref = numbers_ref.at[pl.ds(0, peers)], numbers_ref.at[pl.ds(peers, peers)]
    tiles = peers // 8
    index_planes = -(-2 * tiles // 8)
    corner_planes = -(-(tiles + 4) // 8)
    copy_in = starter(in_sems)
    depth = 8
    lows = []
    for n, (ref, x) in enumerate(
        [(phi_ref, x) for x in range(cx - 4, cx)] + [(kappa_ref, x) for x in range(cx - 3, cx)]
    ):
        for t in range(cy // 8):
            lows.append(copy_in(ref.at[x, pl.ds(8 * t, 8)], low_ref.at[n * (cy // 8) + t]))
    groups = []
    for x in range(0, cx, depth):
        at = pl.ds(x, depth)
        groups.append([
            copy_in(phi_ref.at[at, pl.ds(0, 8)], phi_lo.at[at]),
            copy_in(kappa_ref.at[at, pl.ds(0, 8)], kap_lo.at[at]),
            copy_in(phi_ref.at[at, pl.ds(cy - 8, 8)], phi_hi.at[at]),
            copy_in(kappa_ref.at[at, pl.ds(cy - 8, 8)], kap_hi.at[at]),
        ])
    own_ref[...] = jnp.zeros_like(own_ref)

    def put(plane, number, tile):
        own_ref[plane + number // 8, :, (number % 8) * 128 : (number % 8 + 1) * 128] = tile

    corner = index_planes + 2
    for n in range(tiles):
        put(0, n, cells_ref[8 * n : 8 * n + 8, :].astype(F32))
        loads = loads_ref[8 * n : 8 * n + 8, :].astype(F32)
        put(0, tiles + n, loads)
        put(corner, n, loads)
    sub = lax.broadcasted_iota(jnp.int32, (8, sy), 0) < 4
    for kind, ref in enumerate((disp_ref, stiff_ref)):
        edge = jnp.where(sub, ref[0:8, :], ref[sx - 8 : sx, :])
        own_ref[index_planes, :, kind * sy : (kind + 1) * sy] = edge
        put(corner, tiles + 2 * kind, edge[:, 0:128])
        put(corner, tiles + 2 * kind + 1, edge[:, sy - 128 : sy])
    lane = lax.broadcasted_iota(jnp.int32, (sx, 128), 1)
    first, final = slice(0, 128), slice(sy - 128, sy)
    columns = jnp.where(
        lane < 32, disp_ref[:, first],
        jnp.where(
            lane < 64, pltpu.roll(disp_ref[:, final], 64, axis=1),
            jnp.where(lane < 96, pltpu.roll(stiff_ref[:, first], 64, axis=1), stiff_ref[:, final]),
        ),
    )
    for m in range(sx // 8):
        put(index_planes + 1, m, columns[8 * m : 8 * m + 8, :])
    own = own_ref[...]
    up_ref[cx:] = own
    down_ref[cx:] = own
    low_ref[7 * (cy // 8) :] = own[: index_planes + 1]
    low_up_ref[3:] = own[corner:]
    low_down_ref[3:] = own[corner:]
    upper = lax.broadcasted_iota(jnp.int32, (depth, 8, cz), 1) < 4
    for number, copies in enumerate(groups):
        for made in copies:
            made.wait()
        at = slice(number * depth, (number + 1) * depth)
        up = jnp.where(upper, phi_lo[at], pltpu.roll(kap_lo[at], 4, axis=1))
        down = jnp.where(upper, pltpu.roll(kap_hi[at], 4, axis=1), phi_hi[at])
        up_ref[at] = up
        down_ref[at] = down
        if (number + 1) * depth == cx:
            low_up_ref[0:3] = up[depth - 3 :]
            low_down_ref[0:3] = down[depth - 3 :]
    for made in lows:
        made.wait()


def packed(phi, kappa, after, small, numbers):
    cx, cy, cz = phi.shape
    tiles = numbers.shape[0] // 16
    index_planes = -(-2 * tiles // 8)
    corner_planes = -(-(tiles + 4) // 8)
    extra = index_planes + 2 + corner_planes
    low_planes = 7 * (cy // 8)

    def shape(planes):
        return jax.ShapeDtypeStruct((planes, 8, cz), F32)

    return pl.pallas_call(
        pack,
        in_specs=hbm_specs(2) + any_specs(1) + vmem_specs(2),
        out_specs=vmem_specs(6),
        out_shape=[
            shape(cx + extra), shape(cx + extra), shape(low_planes + index_planes + 1),
            shape(3 + corner_planes), shape(3 + corner_planes), shape(extra),
        ],
        scratch_shapes=[pltpu.VMEM((cx, 8, cz), F32)] * 4
        + [pltpu.SemaphoreType.DMA((cx // 2 + low_planes,))],
        compiler_params=params(),
        name="pack",
    )(phi, kappa, after, small, numbers)


def substep(src, kap, coef, write, plane, advect, rows):
    chunks = src.shape[1]
    lane = lax.broadcasted_iota(jnp.int32, (rows, 128), 1)
    first, last = lane == 0, lane == 127

    def take(at, q, start=8):
        return src[at, q, pl.ds(start, rows), :]

    for q in range(chunks):
        now = take(plane, q)
        left = take(plane, q - 1) if q else 0.0
        right = take(plane, q + 1) if q + 1 < chunks else 0.0
        total = pltpu.roll(jnp.where(last, left, now), 1, axis=1) + pltpu.roll(
            jnp.where(first, right, now), 127, axis=1
        )
        total = total + (take(plane, q, 7) + take(plane, q, 9))
        before = take(plane - 1, q)
        total = total + (before + take(plane + 1, q))
        at = slice(q * 128, (q + 1) * 128)
        write(q, (coef[plane, 0:rows, at] * now + advect * before) + kap[
            plane, 0:rows, at
        ] * total)


def fluid(x0, x1, cx, cy, cz, kind, *refs):
    planes = x1 - x0 + 8
    wide = cy + 8
    chunks = cz // 128
    tiles = cy // 8
    names = ["phi", "kappa", "up", "down"]
    names += {"wet": ["forced", "low", "low_up", "low_down", "near", "gram"],
              "middle": ["state_a", "state_b", "wet", "press"],
              "end": ["state_a", "state_b", "high", "whole", "late"]}[kind]
    names += {"wet": ["out", "next_a", "next_b", "send"], "middle": ["out", "next_a", "next_b", "token"],
              "end": ["out", "token"]}[kind]
    names += ["a", "b", "kap", "coef", "stage", "done", "sems", "kap_sems", "out_sems", "more_sems"]
    r = dict(zip(names, refs))
    a, b, kap, coef, stage = r["a"], r["b"], r["kap"], r["coef"], r["stage"]
    carried = kind != "wet"
    is_last = lax.axis_index("gx") == lax.axis_size("gx") - 1
    copy = starter(r["more_sems"])
    phi0, own1 = x0 + 4, min(cx, x1 + 4)

    def loop(lo, hi, body):
        def run(i, carry):
            body(i)
            return carry

        if hi > lo:
            lax.fori_loop(lo, hi, run, 0)

    def phi_copy(x):
        return pltpu.make_async_copy(r["phi"].at[x], stage.at[x - phi0], r["sems"].at[x - phi0])

    def kappa_copy(x):
        return pltpu.make_async_copy(
            r["kappa"].at[x], kap.at[x - (x0 - 4), pl.ds(0, cy)], r["kap_sems"].at[x - x0]
        )

    states = []
    if carried:
        states = [copy(r["state_a"], a.at[pl.ds(4, 4)]), copy(r["state_b"], b.at[pl.ds(3, 4)])]
    loop(x0, min(x0 + 4, own1), lambda x: kappa_copy(x).start())

    def start_own(x):
        phi_copy(x).start()
        kappa_copy(x).start()

    loop(phi0, own1, start_own)
    outs = []
    if kind == "middle":
        outs.append(copy(r["wet"], r["out"].at[pl.ds(0, x0)]))
    upper = lax.broadcasted_iota(jnp.int32, (8, cz), 0) < 4

    def set_kappa_edge(i, up, down):
        kap[i, cy:wide, :] = pltpu.roll(jnp.where(upper, down, up), 4, axis=0)

    def set_coef(i):
        coef[i] = 0.75 - 6.0 * kap[i]

    def repeat_rows(i, q):
        a[i, q, 7:8, :] = a[i, q, 7 + wide : 8 + wide, :]
        a[i, q, 8 + wide : 9 + wide, :] = a[i, q, 8:9, :]

    def lanes(q):
        return slice(q * 128, (q + 1) * 128)

    def set_low(i):
        from_tiles = jnp.maximum(i - 1, 0)
        up, down = r["low_up"][from_tiles], r["low_down"][from_tiles]
        edge = jnp.where(upper, up, down)
        for t in range(tiles):
            rows = r["low"][i * tiles + t]
            kap[i, 8 * t : 8 * t + 8, :] = r["low"][(i + 3) * tiles + t]
            for q in range(chunks):
                a[i, q, 8 + 8 * t : 16 + 8 * t, :] = rows[:, lanes(q)]
        set_kappa_edge(i, up, down)
        set_coef(i)
        for q in range(chunks):
            a[i, q, 8 + cy : 8 + wide, :] = edge[:, lanes(q)]
            repeat_rows(i, q)

    def set_first(i):
        x = i + (x0 - 4)
        kappa_copy(x).wait()
        set_kappa_edge(i, r["up"][x], r["down"][x])
        set_coef(i)
        if kind == "wet":
            for q in range(chunks):
                a[i, q, 8 : 8 + wide, :] = r["forced"][x, :, lanes(q)]
                repeat_rows(i, q)

    def set_own(i):
        x = i + (x0 - 4)
        phi_copy(x).wait()
        kappa_copy(x).wait()
        up, down = r["up"][x], r["down"][x]
        edge = jnp.where(upper, up, down)
        set_kappa_edge(i, up, down)
        set_coef(i)
        for q in range(chunks):
            a[i, q, 8 : 8 + cy, :] = stage[x - phi0, :, lanes(q)]
            a[i, q, 8 + cy : 8 + wide, :] = edge[:, lanes(q)]
            repeat_rows(i, q)

    def set_high(i):
        x = i + (x0 - 4) - cx
        kap[i] = r["high"][jnp.minimum(x + 4, 6)]
        set_coef(i)
        for q in range(chunks):
            a[i, q, 8 : 8 + wide, :] = r["high"][x, :, lanes(q)]
            repeat_rows(i, q)

    def step(src, dst, i):
        advect = 0.25
        if kind == "end":
            advect = jnp.where(jnp.logical_and(is_last, i + (x0 - 4) >= cx), 0.0, 0.25)

        def write(q, new):
            dst[i, q, 8 : 8 + wide, :] = new
            dst[i, q, 7:8, :] = new[wide - 1 :]
            dst[i, q, 8 + wide : 9 + wide, :] = new[0:1]

        substep(src, kap, coef, write, i, advect, wide)

    def out_copy(i):
        return pltpu.make_async_copy(
            r["done"].at[i - 4], r["out"].at[x0 + i - 4], r["out_sems"].at[i - 4]
        )

    def final(i):
        target = r["out"] if kind == "wet" else r["done"]

        def write(q, new):
            target[i - 4, :, lanes(q)] = new

        substep(b, kap, coef, write, i, 0.25, cy)
        if kind != "wet":
            out_copy(i).start()

    if kind == "wet":
        loop(0, 4, set_low)
    loop(4, 8, set_first)
    for made in states:
        made.wait()
    if kind == "wet":
        loop(8, planes, set_own)
        loop(1, planes - 1, lambda i: step(a, b, i))
    elif kind == "middle":

        def first_level(i):
            set_own(i + 1)
            step(a, b, i)

        loop(7, planes - 1, first_level)
    else:
        loop(8, planes, set_high)
        loop(7, planes - 1, lambda i: step(a, b, i))
    loop(6 if carried else 2, planes - 2, lambda i: step(b, a, i))
    loop(5 if carried else 3, planes - 3, lambda i: step(a, b, i))
    if kind != "end":
        outs.append(copy(a.at[pl.ds(planes - 4, 4)], r["next_a"]))
        outs.append(copy(b.at[pl.ds(planes - 5, 4)], r["next_b"]))
    if kind == "wet":
        outs.append(copy(r["forced"], r["send"]))
    else:
        r["token"][...] = jnp.zeros((8, 128), F32)
    loop(4, planes - 4, final)
    for made in outs:
        made.wait()
    if kind != "wet":
        loop(4, planes - 4, lambda i: out_copy(i).wait())


def fluid_call(kind, x0, x1, phi, kappa, up, down, *more):
    cx, cy, cz = phi.shape
    planes = x1 - x0 + 8
    field = jax.ShapeDtypeStruct((cx, cy, cz), F32)
    state = [jax.ShapeDtypeStruct((4, cz // 128, cy + 24, 128), F32)] * 2
    if kind == "wet":
        specs = vmem_specs(4) + any_specs(2)
        out_shape = [
            jax.ShapeDtypeStruct((x1 - x0, cy, cz), F32), *state,
            jax.ShapeDtypeStruct((7, cy + 8, cz), F32),
        ]
        out_specs = vmem_specs(1) + hbm_specs(2) + any_specs(1)
    elif kind == "middle":
        specs = hbm_specs(2) + vmem_specs(1) + any_specs(1)
        out_shape = [field, *state, jax.ShapeDtypeStruct((8, 128), F32)]
        out_specs = hbm_specs(3) + vmem_specs(1)
    else:
        specs = hbm_specs(2) + vmem_specs(1) + hbm_specs(1) + any_specs(1)
        out_shape = [field, jax.ShapeDtypeStruct((8, 128), F32)]
        out_specs = hbm_specs(1) + vmem_specs(1)
    cells = planes * (cy + 8) * cz
    stepped = pltpu.VMEM((planes, cz // 128, cy + 24, 128), F32)
    wide = pltpu.VMEM((planes, cy + 8, cz), F32)
    sems = pltpu.SemaphoreType.DMA((planes,))
    return pl.pallas_call(
        functools.partial(fluid, x0, x1, cx, cy, cz, kind),
        in_specs=hbm_specs(2) + vmem_specs(2) + specs,
        out_specs=out_specs,
        out_shape=out_shape,
        scratch_shapes=[
            stepped, stepped, wide, wide,
            pltpu.VMEM((max(min(cx, x1 + 4) - x0 - 4, 1), cy, cz), F32),
            pltpu.VMEM((1 if kind == "wet" else x1 - x0, cy, cz), F32),
            sems, sems, sems, pltpu.SemaphoreType.DMA((8,)),
        ],
        input_output_aliases={7: 0} if kind == "end" else {},
        compiler_params=params(kind != "wet"),
        cost_estimate=pl.CostEstimate(
            flops=48 * cells, bytes_accessed=12 * cells, transcendentals=0
        ),
        name="fluid_" + kind,
    )(phi, kappa, up, down, *more)


def shifted_pairs(n_gx, n_gy, dx, dy):
    pairs = []
    for gx in range(n_gx):
        for gy in range(n_gy):
            tx, ty = gx + dx, gy + dy
            if 0 <= tx < n_gx and 0 <= ty < n_gy:
                pairs.append((gx * n_gy + gy, tx * n_gy + ty))
    return pairs


def local(phi, kappa, stiffness, face_cell, load_dof, displacement, v_hist, w_hist, r_prev, w_prev):
    n_gx, n_gy = lax.axis_size("gx"), lax.axis_size("gy")
    peers, blk = face_cell.shape[2:]
    cx, cy, cz = phi.shape
    sx, sy = displacement.shape
    hist = v_hist.shape[0]
    wet_planes = cx // 8
    fcell = face_cell.reshape(peers, blk)
    ldof = load_dof.reshape(peers, blk)
    axes = ("gx", "gy")

    def shift(value, dx, dy):
        return lax.ppermute(value, axes, shifted_pairs(n_gx, n_gy, dx, dy))

    def exchange(value):
        return lax.all_to_all(value, axes, split_axis=0, concat_axis=0, tiled=True)

    def call(body, out_shape, scratch, name, specs, *args):
        several = isinstance(out_shape, list)
        return pl.pallas_call(
            body,
            in_specs=specs,
            out_specs=vmem_specs(len(out_shape)) if several else vmem_specs(1)[0],
            out_shape=out_shape,
            scratch_shapes=scratch,
            compiler_params=params(name in ("shell", "solve")),
            name=name,
        )(*args)

    def f32(*shape):
        return jax.ShapeDtypeStruct(shape, F32)

    small = jnp.stack([displacement, stiffness, r_prev, w_prev])
    numbers = jnp.concatenate([fcell, ldof], axis=0)
    sent = call(
        functools.partial(gather_disp, n_gy), f32(peers, 1, 3 * blk),
        [pltpu.VMEM((peers, blk), F32)], "gather_disp", vmem_specs(2), small, numbers,
    )
    disp = exchange(sent)
    size = 8 * hist
    gram = call(
        gram_rows, f32(peers, 128),
        [
            pltpu.VMEM((sx // 8, hist, 8, sy), F32), pltpu.VMEM((size, size), F32),
            pltpu.VMEM((size, size), F32),
            pltpu.VMEM((max(128, peers, 2 * peers if peers < hist else 0), 128), F32),
            pltpu.SemaphoreType.DMA((sx // 8,)),
        ],
        "gram_rows", hbm_specs(1), v_hist,
    )
    up_send, down_send, low_send, low_up_send, low_down_send, own = packed(
        phi, kappa, disp, small, numbers
    )
    index_planes = -(-2 * (peers // 8) // 8)
    low = shift(low_send, 1, 0)
    up = shift(up_send, 0, -1)
    down = shift(down_send, 0, 1)
    low_up = shift(low_up_send, 1, -1)
    low_down = shift(low_down_send, 1, 1)
    corner = cx + index_planes + 2
    near = shift(
        jnp.concatenate([own[: index_planes + 1], up[corner:], down[corner:]], axis=0), -1, 0
    )

    chunks = cz // 128
    forced = call(
        functools.partial(scatter_disp, cx, cy, cz), f32(2 * wet_planes - 1, cy + 8, cz),
        [
            pltpu.VMEM((wet_planes * cy * chunks, 256), F32),
            pltpu.VMEM((512, wet_planes * 4 * chunks), F32),
            pltpu.VMEM((wet_planes, cy, cz), F32),
            pltpu.VMEM((wet_planes - 1, cy, cz), F32),
            pltpu.SemaphoreType.DMA((2,)),
        ],
        "scatter_disp", vmem_specs(4) + hbm_specs(2), disp, numbers, up, down, phi, kappa,
    )
    wet, state_a, state_b, send = fluid_call(
        "wet", 0, wet_planes, phi, kappa, up, down, forced, low, low_up, low_down, near, gram
    )
    press, token = call(
        functools.partial(gather_press, n_gx, n_gy), [f32(peers, 1, (len(NEAR) + 1) * blk), f32(8, 128)],
        [pltpu.VMEM((peers, blk), F32)], "gather_press", vmem_specs(3), wet, numbers, gram,
    )
    loads = exchange(press)
    high = shift(send, -1, 0)
    middle, state_a, state_b, token = fluid_call(
        "middle", wet_planes, cx - 4, phi, kappa, up, down, state_a, state_b, wet, token
    )
    resp, late = call(
        shell, [f32(sx, sy), f32(peers, 1, 256)],
        [
            pltpu.VMEM((hist, sx, sy), F32),
            pltpu.VMEM((sx * (sy // 128), 256), F32),
            pltpu.VMEM((8 * (sy // 128), 256), F32),
            pltpu.VMEM((sx, 32), F32),
            pltpu.VMEM((16, 32), F32),
            pltpu.VMEM((3, sx + 8, sy + 128), F32),
            pltpu.VMEM((128, 128), F32),
            pltpu.SemaphoreType.DMA((1,)),
        ],
        "shell", vmem_specs(9) + hbm_specs(1) + any_specs(1),
        loads, numbers, small, up, down, low, low_up, low_down, near,
        v_hist, token,
    )
    field, token = fluid_call(
        "end", cx - 4, cx, phi, kappa, up, down, state_a, state_b, high, middle, late
    )
    x_next = call(
        solve, f32(sx, sy),
        [pltpu.VMEM((hist, sx, sy), F32), pltpu.SemaphoreType.DMA((1,))],
        "solve", vmem_specs(3) + hbm_specs(1) + any_specs(1), exchange(late), resp, small, w_hist, token,
    )
    return (field, x_next)


def solution(mesh):
    in_specs = (
        P("gx", "gy", None),
        P("gx", "gy", None),
        P("gx", "gy"),
        P("gx", "gy", None, None),
        P("gx", "gy", None, None),
        P("gx", "gy"),
        P(None, "gx", "gy"),
        P(None, "gx", "gy"),
        P("gx", "gy"),
        P("gx", "gy"),
    )
    out_specs = (P("gx", "gy", None), P("gx", "gy"))
    return jax.shard_map(local, mesh=mesh, in_specs=in_specs, out_specs=out_specs, check_vma=False)
```

```python
import functools

import jax
import jax.numpy as jnp
from jax import lax
from jax.experimental import pallas as pl
from jax.experimental.pallas import tpu as pltpu
from jax.sharding import PartitionSpec as P

NSUB = 4
SWEEPS = 3
HIST = 40
VMEM_BYTES = 46 * 1024 * 1024
ALONE_BYTES = 60 * 1024 * 1024
F32 = jnp.float32
BF16 = jnp.bfloat16


def params(alone=False):
    return pltpu.CompilerParams(vmem_limit_bytes=ALONE_BYTES if alone else VMEM_BYTES)


def vmem_specs(count):
    return [pl.BlockSpec(memory_space=pltpu.VMEM)] * count


def any_specs(count):
    return [pl.BlockSpec(memory_space=pl.ANY)] * count


def hbm_specs(count):
    return [pl.BlockSpec(memory_space=pltpu.HBM)] * count


def pieces(value, count):
    parts = []
    for _ in range(count):
        part = value.astype(BF16)
        parts.append(part)
        value = value - part.astype(F32)
    return parts


def as_row(block):
    return jnp.concatenate([block[i : i + 1] for i in range(block.shape[0])], axis=1)


def both_rows(row):
    return jnp.broadcast_to(row, (16, row.shape[1])).astype(BF16)


def matches(keys, rows):
    ids = lax.broadcasted_iota(jnp.int32, (16, keys.shape[1]), 0).astype(F32).astype(BF16)
    found = []
    for base in range(0, rows, 256):
        key = both_rows((keys - base).astype(F32))
        for start in range(0, min(256, rows - base), 16):
            found.append(key == ids + jnp.bfloat16(start))
    return found


def one_hot(keys, rows):
    one, zero = jnp.bfloat16(1), jnp.bfloat16(0)
    return jnp.concatenate([jnp.where(m, one, zero) for m in matches(keys, rows)], axis=0)


def select_sum(table, lane, group, rows, parts):
    total = table[:rows]
    for part in range(1, parts):
        total = total + table[part * rows : (part + 1) * rows]
    ids = lax.broadcasted_iota(jnp.int32, total.shape, 0)
    return jnp.sum(jnp.where(ids == lane, total, 0.0), axis=0, keepdims=True)


def pick(table_t, index_ref, out_rows, rows, lane_bits, chunk_bits, parts, step=8):
    lanes = 1 << lane_bits
    for base in range(0, index_ref.shape[0], step):
        index = as_row(index_ref[base : base + step, :])
        lane = index & (lanes - 1)
        keys = ((index >> lane_bits) & ((1 << chunk_bits) - 1)) * rows + (
            index >> (lane_bits + chunk_bits)
        )
        hot = one_hot(keys, rows << chunk_bits)
        found = lax.dot_general(
            table_t, hot, (((1,), (0,)), ((), ())), preferred_element_type=F32
        )
        out_rows(base, select_sum(found, lane, step, lanes, parts))


def spread_values(values, lane, lanes, parts):
    zero = jnp.bfloat16(0)
    found = matches(lane, lanes)
    spread = []
    for part in pieces(values, parts):
        part = both_rows(part.astype(F32))
        spread += [jnp.where(m, part, zero) for m in found]
    return jnp.concatenate(spread, axis=0)


NEAR = ((0, 0), (1, 0), (-1, 0), (0, 1), (0, -1), (1, 1), (1, -1), (-1, 1), (-1, -1))


def tile_of(ref, plane, number):
    at = (number % 8) * 128
    return ref[plane + number // 8, :, at : at + 128]


def starter(sems):
    used = [0]

    def copy(src, dst):
        made = pltpu.make_async_copy(src, dst, sems.at[used[0]])
        used[0] += 1
        made.start()
        return made

    return copy


def gather_disp(n_gy, small_ref, numbers_ref, out_ref, own_ref):
    disp_ref = small_ref.at[0]
    peers, blk = own_ref.shape
    index_ref = numbers_ref.at[pl.ds(peers, peers)]
    sx, sy = disp_ref.shape
    chunk_bits = (sy // 128).bit_length() - 1
    columns = []
    for q in range(sy // 128):
        columns.append(jnp.transpose(disp_ref[:, q * 128 : (q + 1) * 128]))
    table_t = jnp.concatenate(pieces(jnp.concatenate(columns, axis=1), 3), axis=0)

    def write(base, row):
        for i in range(8):
            own_ref[base + i : base + i + 1, :] = row[:, i * blk : (i + 1) * blk]

    pick(table_t, index_ref, write, sx, 7, chunk_bits, 3)
    own = own_ref[...]
    beside = lax.broadcasted_iota(jnp.int32, own.shape, 0) % n_gy
    out_ref[:, 0, 0:blk] = own
    out_ref[:, 0, blk : 2 * blk] = jnp.where(
        beside == n_gy - 1, 0.0, pltpu.roll(own, peers - 1, axis=0)
    )
    out_ref[:, 0, 2 * blk : 3 * blk] = jnp.where(beside == 0, 0.0, pltpu.roll(own, 1, axis=0))


def scatter_disp(cx, cy, cz, disp_ref, numbers_ref, up_ref, down_ref, phi_ref, kappa_ref, out_ref,
                 acc_ref, side_ref, stage, kstage, sems):
    planes = stage.shape[0]
    copy = starter(sems)
    copies = [
        copy(phi_ref.at[pl.ds(0, planes)], stage),
        copy(kappa_ref.at[pl.ds(0, planes - 1)], kstage),
    ]
    peers, blk = disp_ref.shape[0], numbers_ref.shape[1]
    cells_ref = numbers_ref.at[pl.ds(0, peers)]
    rows = planes * cy
    chunks = cz // 128
    row_bits = cz.bit_length() - 1
    step = 8
    def accumulate(target, first, left, right):
        added = lax.dot_general(
            left, right, (((1,), (1,)), ((), ())), preferred_element_type=F32
        )
        if first:
            target[...] = added
        else:
            target[...] += added

    for base in range(0, peers, step):
        index = as_row(cells_ref[base : base + step, :])
        values = 0.5 * as_row(disp_ref[base : base + step, 0, 0:blk])
        keys = ((index >> 7) & (chunks - 1)) * rows + (index >> row_bits)
        accumulate(
            acc_ref, base == 0, one_hot(keys, rows * chunks),
            spread_values(values, index & 127, 128, 2),
        )
    for base in range(0, peers, step):
        for side in range(2):
            index = as_row(tile_of(up_ref if side == 0 else down_ref, cx, base // step).astype(jnp.int32))
            values = 0.5 * as_row(
                disp_ref[base : base + step, 0, (side + 1) * blk : (side + 2) * blk]
            )
            row = index >> row_bits
            plane = row // cy
            column = row - plane * cy
            inside = column < 4 if side == 0 else column >= cy - 4
            place = column if side == 0 else column - (cy - 8)
            keys = ((index >> 8) & (chunks // 2 - 1)) * (planes * 8) + plane * 8 + place
            keys = jnp.where(inside, keys, -1)
            accumulate(
                side_ref, base == 0 and side == 0, spread_values(values, index & 255, 256, 2),
                one_hot(keys, planes * 4 * chunks),
            )
    for made in copies:
        made.wait()
    upper = lax.broadcasted_iota(jnp.int32, (8, cz), 0) < 4
    for x in range(planes):
        up, down = up_ref[x], down_ref[x]
        out_ref[x, cy : cy + 8, :] = jnp.where(upper, up, down)
        if x < planes - 1:
            out_ref[planes + x, 0:cy, :] = kstage[x]
            out_ref[planes + x, cy : cy + 8, :] = pltpu.roll(
                jnp.where(upper, down, up), 4, axis=0
            )
    for q in range(chunks):
        part = acc_ref[q * rows : (q + 1) * rows, :]
        at = slice(q * 128, (q + 1) * 128)
        out_ref[0:planes, 0:cy, at] = stage[:, :, at] + (part[:, :128] + part[:, 128:]).reshape(
            planes, cy, 128
        )
    both = jnp.transpose(side_ref[0:256, :] + side_ref[256:512, :])
    for q in range(chunks // 2):
        part = both[q * planes * 8 : (q + 1) * planes * 8, :]
        at = slice(q * 256, (q + 1) * 256)
        out_ref[0:planes, cy : cy + 8, at] = out_ref[0:planes, cy : cy + 8, at] + part.reshape(
            planes, 8, 256
        )


def gather_press(n_gx, n_gy, wet_ref, numbers_ref, gram_ref, out_ref, token_ref, own_ref):
    token_ref[...] = jnp.zeros((8, 128), F32)
    index_ref = numbers_ref.at[pl.ds(0, own_ref.shape[0])]
    planes, cy, cz = wet_ref.shape
    peers, blk = own_ref.shape
    rows = planes * cy
    chunks = cz // 256
    columns = []
    for q in range(chunks):
        part = wet_ref[:, :, q * 256 : (q + 1) * 256].reshape(rows, 256)
        columns.append(jnp.transpose(part))
    table_t = jnp.concatenate(pieces(jnp.concatenate(columns, axis=1), 2), axis=0)

    def write(base, row):
        for i in range(8):
            own_ref[base + i : base + i + 1, :] = row[:, i * blk : (i + 1) * blk]

    pick(table_t, index_ref, write, rows, 8, chunks.bit_length() - 1, 2)
    own = own_ref[...]
    number = lax.broadcasted_iota(jnp.int32, own.shape, 0)
    at_x, at_y = number // n_gy, number % n_gy
    for k, (dx, dy) in enumerate(NEAR):
        ok = (at_x + dx >= 0) & (at_x + dx < n_gx) & (at_y + dy >= 0) & (at_y + dy < n_gy)
        moved = pltpu.roll(own, (-(dx * n_gy + dy)) % peers, axis=0) if k else own
        out_ref[:, 0, k * blk : (k + 1) * blk] = jnp.where(ok, moved, 0.0)
    out_ref[:, 0, len(NEAR) * blk : (len(NEAR) + 1) * blk] = gram_ref[...]


def gram_rows(v_ref, out_ref, v, same, cross, wide, sems):
    hist, sx, sy = v_ref.shape
    tiles = sx // 8
    copy = starter(sems)
    copies = [
        copy(v_ref.at[:, pl.ds(8 * t, 8), :], v.at[t]) for t in range(tiles)
    ]
    for t in range(tiles):
        copies[t].wait()
        high, low = pieces(v[t].reshape(hist * 8, sy), 2)

        def dot(x, y):
            return lax.dot_general(x, y, (((1,), (1,)), ((), ())), preferred_element_type=F32)

        if t == 0:
            same[...] = dot(high, high) + dot(low, low)
            cross[...] = dot(high, low)
        else:
            same[...] += dot(high, high) + dot(low, low)
            cross[...] += dot(high, low)
    size = hist * 8
    row = lax.broadcasted_iota(jnp.int32, (size, size), 0)
    column = lax.broadcasted_iota(jnp.int32, (size, size), 1)
    match = (row & 7) == (column & 7)
    group = (
        lax.broadcasted_iota(jnp.int32, (size, 128), 0) // 8
        == lax.broadcasted_iota(jnp.int32, (size, 128), 1)
    ).astype(F32)

    def reduced(ref):
        part = jnp.sum(jnp.where(match, ref[...], 0.0).reshape(hist, 8, size), axis=1)
        return jnp.dot(part, group, precision=lax.Precision.HIGHEST, preferred_element_type=F32)

    wide[...] = jnp.zeros_like(wide)
    wide[0:hist, :] = reduced(cross)
    turned = jnp.transpose(wide[0:128, :])
    wide[0:128, :] = wide[0:128, :] + turned
    wide[0:hist, :] = wide[0:hist, :] + reduced(same)
    peers = out_ref.shape[0]
    if peers >= hist:
        out_ref[...] = wide[0:peers, :]
    else:
        out_ref[...] = wide[0:peers, :] + pltpu.roll(wide[peers : 2 * peers, :], 64, axis=1)


def shell(recv_ref, numbers_ref, small_ref, up_ref, down_ref, low_ref,
          low_up_ref, low_down_ref, high_ref, v_ref, after_ref, resp_ref, late_ref, v, acc, rows_acc,
          cols_acc, corner_acc, ext, dots, v_sem):
    disp_ref, stiff_ref, prev_ref = small_ref.at[0], small_ref.at[1], small_ref.at[2]
    sx, sy = disp_ref.shape
    peers, blk = recv_ref.shape[0], numbers_ref.shape[1]
    index_ref = numbers_ref.at[pl.ds(peers, peers)]
    load_tiles = peers // 8
    index_planes = -(-2 * load_tiles // 8)
    corner_planes = -(-(load_tiles + 4) // 8)
    chunks = sy // 128
    hist = v_ref.shape[0]
    v_copy = pltpu.make_async_copy(v_ref, v, v_sem.at[0])
    v_copy.start()
    top = up_ref.shape[0] - (index_planes + 2 + corner_planes)
    low_top = low_ref.shape[0] - (index_planes + 1)
    corner_top = low_up_ref.shape[0] - corner_planes
    near_top = index_planes + 1
    load_at = [
        (high_ref, 0, load_tiles), (low_ref, low_top, load_tiles), (up_ref, top, load_tiles),
        (down_ref, top, load_tiles), (high_ref, near_top, 0),
        (high_ref, near_top + corner_planes, 0), (low_up_ref, corner_top, 0),
        (low_down_ref, corner_top, 0),
    ]

    def accumulate(target, first, keys, height, lane, lanes, values):
        added = lax.dot_general(
            one_hot(keys, height), spread_values(values, lane, lanes, 2),
            (((1,), (1,)), ((), ())), preferred_element_type=F32,
        )
        if first:
            target[...] = added
        else:
            target[...] += added

    def values_of(k, base):
        return as_row(recv_ref[base : base + 8, 0, k * blk : (k + 1) * blk])

    for base in range(0, peers, 8):
        index = as_row(index_ref[base : base + 8, :])
        keys = ((index >> 7) & (chunks - 1)) * sx + index // sy
        accumulate(acc, base == 0, keys, sx * chunks, index & 127, 128, values_of(0, base))
    for k, (dx, dy) in enumerate(NEAR):
        if k == 0:
            continue
        for base in range(0, peers, 8):
            ref, plane, number = load_at[k - 1]
            index = as_row(tile_of(ref, plane, number + base // 8).astype(jnp.int32))
            row = index // sy
            lane = index & (sy - 1)
            if dx == 1:
                row8 = jnp.where(row < 4, row, -1)
            elif dx == -1:
                row8 = jnp.where(row >= sx - 4, row - (sx - 8), -1)
            if dy == 1:
                lane8 = jnp.where(lane < 4, lane, -1)
            elif dy == -1:
                lane8 = jnp.where(lane >= sy - 4, lane - (sy - 8), -1)
            values = values_of(k, base)
            if dy == 0:
                keys = jnp.where(row8 < 0, -1, (lane >> 7) * 8 + row8)
                accumulate(
                    rows_acc, k == 1 and base == 0, keys, 8 * chunks, lane & 127, 128, values
                )
            elif dx == 0:
                accumulate(cols_acc, k == 3 and base == 0, row, sx, lane8, 16, values)
            else:
                accumulate(corner_acc, k == 5 and base == 0, row8, 16, lane8, 16, values)

    ids = lax.broadcasted_iota(jnp.int32, (16, 128), 0)
    lanes = lax.broadcasted_iota(jnp.int32, (16, 128), 1)
    placed = (jnp.where(ids < 4, ids, jnp.where(ids < 8, ids + 120, -1)) == lanes).astype(F32)

    def widened(ref):
        both = ref[:, 0:16] + ref[:, 16:32]
        return jnp.dot(both, placed, precision=lax.Precision.HIGHEST, preferred_element_type=F32)

    force, disp, stiff = ext.at[0], ext.at[1], ext.at[2]
    for q in range(chunks):
        at = slice(q * 128, (q + 1) * 128)
        part = acc[q * sx : (q + 1) * sx, :]
        force[0:sx, at] = part[:, 0:128] + part[:, 128:256]
        part = rows_acc[q * 8 : (q + 1) * 8, :]
        force[sx : sx + 8, at] = part[:, 0:128] + part[:, 128:256]
    side = slice(sy, sy + 128)
    force[0:sx, side] = widened(cols_acc)
    force[sx : sx + 8, side] = widened(corner_acc)[0:8]
    sub = lax.broadcasted_iota(jnp.int32, (8, sy), 0) < 4
    sub1 = lax.broadcasted_iota(jnp.int32, (8, 128), 0) < 4
    lane = lax.broadcasted_iota(jnp.int32, (sx, 128), 1)
    lane1 = lax.broadcasted_iota(jnp.int32, (8, 128), 1)
    for kind, (target, own) in enumerate(((disp, disp_ref), (stiff, stiff_ref))):

        def row_tile(ref, plane):
            return ref[plane, :, kind * sy : (kind + 1) * sy]

        def col_tile(ref):
            plane = top + index_planes + 1
            return jnp.concatenate([tile_of(ref, plane, m) for m in range(sx // 8)], axis=0)

        target[0:sx, 0:sy] = own[...]
        target[sx : sx + 8, 0:sy] = jnp.where(
            sub, row_tile(high_ref, index_planes), row_tile(low_ref, low_top + index_planes)
        )
        ahead, behind = col_tile(up_ref), col_tile(down_ref)
        if kind == 0:
            behind = pltpu.roll(behind, 64, axis=1)
        else:
            ahead = pltpu.roll(ahead, 64, axis=1)
        target[0:sx, side] = jnp.where(lane < 32, ahead, jnp.where(lane >= 96, behind, 0.0))

        def corner_tile(ahead, ahead_plane, behind, behind_plane):
            number = load_tiles + 2 * kind
            return jnp.where(
                lane1 < 32, tile_of(ahead, ahead_plane, number),
                jnp.where(lane1 >= 96, tile_of(behind, behind_plane, number + 1), 0.0),
            )

        target[sx : sx + 8, side] = jnp.where(
            sub1, corner_tile(high_ref, near_top, high_ref, near_top + corner_planes),
            corner_tile(low_up_ref, corner_top, low_down_ref, corner_top),
        )

    load = force[...]
    k = stiff[...]
    diag = 1.0 + 4.0 * k
    scale = 0.8 / diag
    resp = disp[...]
    high, wide = sx + 8, sy + 128
    for sweep in range(SWEEPS):
        beside = (pltpu.roll(resp, 1, axis=0) + pltpu.roll(resp, high - 1, axis=0)) + (
            pltpu.roll(resp, 1, axis=1) + pltpu.roll(resp, wide - 1, axis=1)
        )
        resp = resp + scale * (load - (diag * resp - k * beside))
    own = resp[0:sx, 0:sy]
    resp_ref[...] = own
    resid = own - disp_ref[...]
    newest = resid - prev_ref[...]
    dots[...] = jnp.zeros_like(dots)

    def folded(value):
        total = value[0:8]
        for t in range(1, sx // 8):
            total = total + value[8 * t : 8 * t + 8]
        out = total[:, 0:128]
        for q in range(1, chunks):
            out = out + total[:, q * 128 : (q + 1) * 128]
        return jnp.sum(out, axis=0, keepdims=True)

    dots[0:1, :] = folded(newest * newest)
    dots[64:65, :] = folded(resid * newest)
    v_copy.wait()
    for number in range(1, hist):
        column = v[number]
        dots[number : number + 1, :] = folded(column * newest)
        dots[64 + number : 65 + number, :] = folded(column * resid)
    late = lax.dot_general(
        jnp.ones((8, 128), F32), dots[...], (((1,), (1,)), ((), ())),
        precision=lax.Precision.HIGHEST, preferred_element_type=F32,
    )
    gram_at = len(NEAR) * blk
    gram = jnp.sum(recv_ref[:, 0, gram_at : gram_at + 128], axis=0, keepdims=True)
    late_ref[:, 0, 0:128] = jnp.broadcast_to(late[0:1], (peers, 128))
    late_ref[:, 0, 128:256] = jnp.broadcast_to(gram, (peers, 128))


def solve(recv_ref, resp_ref, small_ref, w_ref, after_ref, out_ref, w, sems):
    peers = recv_ref.shape[0]
    hist = w_ref.shape[0]
    prev_ref = small_ref.at[3]
    sx, sy = resp_ref.shape
    w_copy = pltpu.make_async_copy(w_ref, w, sems.at[0])
    w_copy.start()
    late = jnp.sum(recv_ref[:, 0, 0:128], axis=0, keepdims=True)
    rows = recv_ref[:, 0, 128:256]
    if peers >= hist:
        gram = rows[0:hist]
    else:
        gram = jnp.concatenate(
            [rows, pltpu.roll(rows, 64, axis=1)[0 : hist - peers]], axis=0
        )
    row = lax.broadcasted_iota(jnp.int32, (hist, 128), 0)
    lane = lax.broadcasted_iota(jnp.int32, (hist, 128), 1)
    turned = jnp.transpose(jnp.broadcast_to(late, (128, 128)))
    gram = jnp.where(row == 0, jnp.broadcast_to(late, (hist, 128)), gram)
    gram = jnp.where(lane == 0, turned[0:hist], gram)
    gram = jnp.where(lane < hist, gram, 0.0)
    unit = row == lane
    trace = jnp.sum(jnp.where(unit, gram, 0.0), keepdims=True)
    a = gram + jnp.where(unit, 0.001 * trace / hist, 0.0)
    a = jnp.where(lane == 64, -turned[64 : 64 + hist], a)
    for j in range(hist):
        column = jnp.broadcast_to(a[:, j : j + 1], (hist, 128))
        scaled = a[j : j + 1, :] / column[j : j + 1, :]
        a = jnp.where(row == j, scaled, a - column * scaled)
    coef = jnp.broadcast_to(a[:, 64:65], (hist, 128))
    coef = jnp.concatenate([coef] * (sy // 128), axis=1)
    resp = resp_ref[...]
    total = resp + coef[0:1] * (resp - prev_ref[...])
    w_copy.wait()
    for number in range(1, hist):
        total = total + coef[number : number + 1] * w[number]
    out_ref[...] = total


def pack(phi_ref, kappa_ref, after_ref, small_ref, numbers_ref, up_ref, down_ref, low_ref, low_up_ref, low_down_ref, own_ref, phi_lo, kap_lo, phi_hi,
         kap_hi, in_sems):
    cx, cy, cz = phi_ref.shape
    disp_ref, stiff_ref = small_ref.at[0], small_ref.at[1]
    sx, sy = disp_ref.shape
    peers = numbers_ref.shape[0] // 2
    cells_ref, loads_ref = numbers_ref.at[pl.ds(0, peers)], numbers_ref.at[pl.ds(peers, peers)]
    tiles = peers // 8
    index_planes = -(-2 * tiles // 8)
    corner_planes = -(-(tiles + 4) // 8)
    copy_in = starter(in_sems)
    depth = 8
    lows = []
    for n, (ref, x) in enumerate(
        [(phi_ref, x) for x in range(cx - 4, cx)] + [(kappa_ref, x) for x in range(cx - 3, cx)]
    ):
        for t in range(cy // 8):
            lows.append(copy_in(ref.at[x, pl.ds(8 * t, 8)], low_ref.at[n * (cy // 8) + t]))
    groups = []
    for x in range(0, cx, depth):
        at = pl.ds(x, depth)
        groups.append([
            copy_in(phi_ref.at[at, pl.ds(0, 8)], phi_lo.at[at]),
            copy_in(kappa_ref.at[at, pl.ds(0, 8)], kap_lo.at[at]),
            copy_in(phi_ref.at[at, pl.ds(cy - 8, 8)], phi_hi.at[at]),
            copy_in(kappa_ref.at[at, pl.ds(cy - 8, 8)], kap_hi.at[at]),
        ])
    own_ref[...] = jnp.zeros_like(own_ref)

    def put(plane, number, tile):
        own_ref[plane + number // 8, :, (number % 8) * 128 : (number % 8 + 1) * 128] = tile

    corner = index_planes + 2
    for n in range(tiles):
        put(0, n, cells_ref[8 * n : 8 * n + 8, :].astype(F32))
        loads = loads_ref[8 * n : 8 * n + 8, :].astype(F32)
        put(0, tiles + n, loads)
        put(corner, n, loads)
    sub = lax.broadcasted_iota(jnp.int32, (8, sy), 0) < 4
    for kind, ref in enumerate((disp_ref, stiff_ref)):
        edge = jnp.where(sub, ref[0:8, :], ref[sx - 8 : sx, :])
        own_ref[index_planes, :, kind * sy : (kind + 1) * sy] = edge
        put(corner, tiles + 2 * kind, edge[:, 0:128])
        put(corner, tiles + 2 * kind + 1, edge[:, sy - 128 : sy])
    lane = lax.broadcasted_iota(jnp.int32, (sx, 128), 1)
    first, final = slice(0, 128), slice(sy - 128, sy)
    columns = jnp.where(
        lane < 32, disp_ref[:, first],
        jnp.where(
            lane < 64, pltpu.roll(disp_ref[:, final], 64, axis=1),
            jnp.where(lane < 96, pltpu.roll(stiff_ref[:, first], 64, axis=1), stiff_ref[:, final]),
        ),
    )
    for m in range(sx // 8):
        put(index_planes + 1, m, columns[8 * m : 8 * m + 8, :])
    own = own_ref[...]
    up_ref[cx:] = own
    down_ref[cx:] = own
    low_ref[7 * (cy // 8) :] = own[: index_planes + 1]
    low_up_ref[3:] = own[corner:]
    low_down_ref[3:] = own[corner:]
    upper = lax.broadcasted_iota(jnp.int32, (depth, 8, cz), 1) < 4
    for number, copies in enumerate(groups):
        for made in copies:
            made.wait()
        at = slice(number * depth, (number + 1) * depth)
        up = jnp.where(upper, phi_lo[at], pltpu.roll(kap_lo[at], 4, axis=1))
        down = jnp.where(upper, pltpu.roll(kap_hi[at], 4, axis=1), phi_hi[at])
        up_ref[at] = up
        down_ref[at] = down
        if (number + 1) * depth == cx:
            low_up_ref[0:3] = up[depth - 3 :]
            low_down_ref[0:3] = down[depth - 3 :]
    for made in lows:
        made.wait()


def packed(phi, kappa, after, small, numbers):
    cx, cy, cz = phi.shape
    tiles = numbers.shape[0] // 16
    index_planes = -(-2 * tiles // 8)
    corner_planes = -(-(tiles + 4) // 8)
    extra = index_planes + 2 + corner_planes
    low_planes = 7 * (cy // 8)

    def shape(planes):
        return jax.ShapeDtypeStruct((planes, 8, cz), F32)

    return pl.pallas_call(
        pack,
        in_specs=hbm_specs(2) + any_specs(1) + vmem_specs(2),
        out_specs=vmem_specs(6),
        out_shape=[
            shape(cx + extra), shape(cx + extra), shape(low_planes + index_planes + 1),
            shape(3 + corner_planes), shape(3 + corner_planes), shape(extra),
        ],
        scratch_shapes=[pltpu.VMEM((cx, 8, cz), F32)] * 4
        + [pltpu.SemaphoreType.DMA((cx // 2 + low_planes,))],
        compiler_params=params(),
        name="pack",
    )(phi, kappa, after, small, numbers)


def substep(src, kap, coef, write, plane, advect, rows):
    chunks = src.shape[1]
    lane = lax.broadcasted_iota(jnp.int32, (rows, 128), 1)
    first, last = lane == 0, lane == 127

    def take(at, q, start=8):
        return src[at, q, pl.ds(start, rows), :]

    for q in range(chunks):
        now = take(plane, q)
        left = take(plane, q - 1) if q else 0.0
        right = take(plane, q + 1) if q + 1 < chunks else 0.0
        total = pltpu.roll(jnp.where(last, left, now), 1, axis=1) + pltpu.roll(
            jnp.where(first, right, now), 127, axis=1
        )
        total = total + (take(plane, q, 7) + take(plane, q, 9))
        before = take(plane - 1, q)
        total = total + (before + take(plane + 1, q))
        at = slice(q * 128, (q + 1) * 128)
        write(q, (coef[plane, 0:rows, at] * now + advect * before) + kap[
            plane, 0:rows, at
        ] * total)


def fluid(x0, x1, cx, cy, cz, kind, *refs):
    planes = x1 - x0 + 8
    wide = cy + 8
    chunks = cz // 128
    tiles = cy // 8
    names = ["phi", "kappa", "up", "down"]
    names += {"wet": ["forced", "low", "low_up", "low_down", "near", "gram"],
              "middle": ["state_a", "state_b", "wet", "press"],
              "end": ["state_a", "state_b", "high", "whole", "late"]}[kind]
    names += {"wet": ["out", "next_a", "next_b", "send"], "middle": ["out", "next_a", "next_b", "token"],
              "end": ["out", "token"]}[kind]
    names += ["a", "b", "kap", "coef", "stage", "done", "sems", "kap_sems", "out_sems", "more_sems"]
    r = dict(zip(names, refs))
    a, b, kap, coef, stage = r["a"], r["b"], r["kap"], r["coef"], r["stage"]
    carried = kind != "wet"
    is_last = lax.axis_index("gx") == lax.axis_size("gx") - 1
    copy = starter(r["more_sems"])
    phi0, own1 = x0 + 4, min(cx, x1 + 4)

    def loop(lo, hi, body):
        def run(i, carry):
            body(i)
            return carry

        if hi > lo:
            lax.fori_loop(lo, hi, run, 0)

    def phi_copy(x):
        return pltpu.make_async_copy(r["phi"].at[x], stage.at[x - phi0], r["sems"].at[x - phi0])

    def kappa_copy(x):
        return pltpu.make_async_copy(
            r["kappa"].at[x], kap.at[x - (x0 - 4), pl.ds(0, cy)], r["kap_sems"].at[x - x0]
        )

    states = []
    if carried:
        states = [copy(r["state_a"], a.at[pl.ds(4, 4)]), copy(r["state_b"], b.at[pl.ds(3, 4)])]
    loop(x0, min(x0 + 4, own1), lambda x: kappa_copy(x).start())

    def start_own(x):
        phi_copy(x).start()
        kappa_copy(x).start()

    loop(phi0, own1, start_own)
    outs = []
    if kind == "middle":
        outs.append(copy(r["wet"], r["out"].at[pl.ds(0, x0)]))
    if kind == "wet":
        outs.append(copy(r["forced"], r["send"]))
    upper = lax.broadcasted_iota(jnp.int32, (8, cz), 0) < 4

    def set_kappa_edge(i, up, down):
        kap[i, cy:wide, :] = pltpu.roll(jnp.where(upper, down, up), 4, axis=0)

    def set_coef(i):
        coef[i] = 0.75 - 6.0 * kap[i]

    def repeat_rows(i, q):
        a[i, q, 7:8, :] = a[i, q, 7 + wide : 8 + wide, :]
        a[i, q, 8 + wide : 9 + wide, :] = a[i, q, 8:9, :]

    def lanes(q):
        return slice(q * 128, (q + 1) * 128)

    def set_low(i):
        from_tiles = jnp.maximum(i - 1, 0)
        up, down = r["low_up"][from_tiles], r["low_down"][from_tiles]
        edge = jnp.where(upper, up, down)
        for t in range(tiles):
            rows = r["low"][i * tiles + t]
            kap[i, 8 * t : 8 * t + 8, :] = r["low"][(i + 3) * tiles + t]
            for q in range(chunks):
                a[i, q, 8 + 8 * t : 16 + 8 * t, :] = rows[:, lanes(q)]
        set_kappa_edge(i, up, down)
        set_coef(i)
        for q in range(chunks):
            a[i, q, 8 + cy : 8 + wide, :] = edge[:, lanes(q)]
            repeat_rows(i, q)

    def set_first(i):
        x = i + (x0 - 4)
        kappa_copy(x).wait()
        set_kappa_edge(i, r["up"][x], r["down"][x])
        set_coef(i)
        if kind == "wet":
            for q in range(chunks):
                a[i, q, 8 : 8 + wide, :] = r["forced"][x, :, lanes(q)]
                repeat_rows(i, q)

    def set_own(i):
        x = i + (x0 - 4)
        phi_copy(x).wait()
        kappa_copy(x).wait()
        up, down = r["up"][x], r["down"][x]
        edge = jnp.where(upper, up, down)
        set_kappa_edge(i, up, down)
        set_coef(i)
        for q in range(chunks):
            a[i, q, 8 : 8 + cy, :] = stage[x - phi0, :, lanes(q)]
            a[i, q, 8 + cy : 8 + wide, :] = edge[:, lanes(q)]
            repeat_rows(i, q)

    def set_high(i):
        x = i + (x0 - 4) - cx
        kap[i] = r["high"][jnp.minimum(x + 4, 6)]
        set_coef(i)
        for q in range(chunks):
            a[i, q, 8 : 8 + wide, :] = r["high"][x, :, lanes(q)]
            repeat_rows(i, q)

    def step(src, dst, i):
        advect = 0.25
        if kind == "end":
            advect = jnp.where(jnp.logical_and(is_last, i + (x0 - 4) >= cx), 0.0, 0.25)

        def write(q, new):
            dst[i, q, 8 : 8 + wide, :] = new
            dst[i, q, 7:8, :] = new[wide - 1 :]
            dst[i, q, 8 + wide : 9 + wide, :] = new[0:1]

        substep(src, kap, coef, write, i, advect, wide)

    def out_copy(i):
        return pltpu.make_async_copy(
            r["done"].at[i - 4], r["out"].at[x0 + i - 4], r["out_sems"].at[i - 4]
        )

    def final(i):
        target = r["out"] if kind == "wet" else r["done"]

        def write(q, new):
            target[i - 4, :, lanes(q)] = new

        substep(b, kap, coef, write, i, 0.25, cy)
        if kind != "wet":
            out_copy(i).start()

    if kind == "wet":
        loop(0, 4, set_low)
    loop(4, 8, set_first)
    for made in states:
        made.wait()
    if kind == "wet":
        loop(8, planes, set_own)
        loop(1, planes - 1, lambda i: step(a, b, i))
    elif kind == "middle":

        def first_level(i):
            set_own(i + 1)
            step(a, b, i)

        loop(7, planes - 1, first_level)
    else:
        loop(8, planes, set_high)
        loop(7, planes - 1, lambda i: step(a, b, i))
    loop(6 if carried else 2, planes - 2, lambda i: step(b, a, i))
    loop(5 if carried else 3, planes - 3, lambda i: step(a, b, i))
    if kind != "end":
        outs.append(copy(a.at[pl.ds(planes - 4, 4)], r["next_a"]))
        outs.append(copy(b.at[pl.ds(planes - 5, 4)], r["next_b"]))
    if kind != "wet":
        r["token"][...] = jnp.zeros((8, 128), F32)
    loop(4, planes - 4, final)
    for made in outs:
        made.wait()
    if kind != "wet":
        loop(4, planes - 4, lambda i: out_copy(i).wait())


def fluid_call(kind, x0, x1, phi, kappa, up, down, *more):
    cx, cy, cz = phi.shape
    planes = x1 - x0 + 8
    field = jax.ShapeDtypeStruct((cx, cy, cz), F32)
    state = [jax.ShapeDtypeStruct((4, cz // 128, cy + 24, 128), F32)] * 2
    if kind == "wet":
        specs = vmem_specs(4) + any_specs(2)
        out_shape = [
            jax.ShapeDtypeStruct((x1 - x0, cy, cz), F32), *state,
            jax.ShapeDtypeStruct((7, cy + 8, cz), F32),
        ]
        out_specs = vmem_specs(1) + hbm_specs(2) + any_specs(1)
    elif kind == "middle":
        specs = hbm_specs(2) + vmem_specs(1) + any_specs(1)
        out_shape = [field, *state, jax.ShapeDtypeStruct((8, 128), F32)]
        out_specs = hbm_specs(3) + vmem_specs(1)
    else:
        specs = hbm_specs(2) + vmem_specs(1) + hbm_specs(1) + any_specs(1)
        out_shape = [field, jax.ShapeDtypeStruct((8, 128), F32)]
        out_specs = hbm_specs(1) + vmem_specs(1)
    cells = planes * (cy + 8) * cz
    stepped = pltpu.VMEM((planes, cz // 128, cy + 24, 128), F32)
    wide = pltpu.VMEM((planes, cy + 8, cz), F32)
    sems = pltpu.SemaphoreType.DMA((planes,))
    return pl.pallas_call(
        functools.partial(fluid, x0, x1, cx, cy, cz, kind),
        in_specs=hbm_specs(2) + vmem_specs(2) + specs,
        out_specs=out_specs,
        out_shape=out_shape,
        scratch_shapes=[
            stepped, stepped, wide, wide,
            pltpu.VMEM((max(min(cx, x1 + 4) - x0 - 4, 1), cy, cz), F32),
            pltpu.VMEM((1 if kind == "wet" else x1 - x0, cy, cz), F32),
            sems, sems, sems, pltpu.SemaphoreType.DMA((8,)),
        ],
        input_output_aliases={7: 0} if kind == "end" else {},
        compiler_params=params(kind != "wet"),
        cost_estimate=pl.CostEstimate(
            flops=48 * cells, bytes_accessed=12 * cells, transcendentals=0
        ),
        name="fluid_" + kind,
    )(phi, kappa, up, down, *more)


def shifted_pairs(n_gx, n_gy, dx, dy):
    pairs = []
    for gx in range(n_gx):
        for gy in range(n_gy):
            tx, ty = gx + dx, gy + dy
            if 0 <= tx < n_gx and 0 <= ty < n_gy:
                pairs.append((gx * n_gy + gy, tx * n_gy + ty))
    return pairs


def local(phi, kappa, stiffness, face_cell, load_dof, displacement, v_hist, w_hist, r_prev, w_prev):
    n_gx, n_gy = lax.axis_size("gx"), lax.axis_size("gy")
    peers, blk = face_cell.shape[2:]
    cx, cy, cz = phi.shape
    sx, sy = displacement.shape
    hist = v_hist.shape[0]
    wet_planes = cx // 8
    fcell = face_cell.reshape(peers, blk)
    ldof = load_dof.reshape(peers, blk)
    axes = ("gx", "gy")

    def shift(value, dx, dy):
        return lax.ppermute(value, axes, shifted_pairs(n_gx, n_gy, dx, dy))

    def exchange(value):
        return lax.all_to_all(value, axes, split_axis=0, concat_axis=0, tiled=True)

    def call(body, out_shape, scratch, name, specs, *args):
        several = isinstance(out_shape, list)
        return pl.pallas_call(
            body,
            in_specs=specs,
            out_specs=vmem_specs(len(out_shape)) if several else vmem_specs(1)[0],
            out_shape=out_shape,
            scratch_shapes=scratch,
            compiler_params=params(name in ("shell", "solve")),
            name=name,
        )(*args)

    def f32(*shape):
        return jax.ShapeDtypeStruct(shape, F32)

    small = jnp.stack([displacement, stiffness, r_prev, w_prev])
    numbers = jnp.concatenate([fcell, ldof], axis=0)
    sent = call(
        functools.partial(gather_disp, n_gy), f32(peers, 1, 3 * blk),
        [pltpu.VMEM((peers, blk), F32)], "gather_disp", vmem_specs(2), small, numbers,
    )
    disp = exchange(sent)
    size = 8 * hist
    gram = call(
        gram_rows, f32(peers, 128),
        [
            pltpu.VMEM((sx // 8, hist, 8, sy), F32), pltpu.VMEM((size, size), F32),
            pltpu.VMEM((size, size), F32),
            pltpu.VMEM((max(128, peers, 2 * peers if peers < hist else 0), 128), F32),
            pltpu.SemaphoreType.DMA((sx // 8,)),
        ],
        "gram_rows", hbm_specs(1), v_hist,
    )
    up_send, down_send, low_send, low_up_send, low_down_send, own = packed(
        phi, kappa, disp, small, numbers
    )
    index_planes = -(-2 * (peers // 8) // 8)
    low = shift(low_send, 1, 0)
    up = shift(up_send, 0, -1)
    down = shift(down_send, 0, 1)
    low_up = shift(low_up_send, 1, -1)
    low_down = shift(low_down_send, 1, 1)
    corner = cx + index_planes + 2
    near = shift(
        jnp.concatenate([own[: index_planes + 1], up[corner:], down[corner:]], axis=0), -1, 0
    )

    chunks = cz // 128
    forced = call(
        functools.partial(scatter_disp, cx, cy, cz), f32(2 * wet_planes - 1, cy + 8, cz),
        [
            pltpu.VMEM((wet_planes * cy * chunks, 256), F32),
            pltpu.VMEM((512, wet_planes * 4 * chunks), F32),
            pltpu.VMEM((wet_planes, cy, cz), F32),
            pltpu.VMEM((wet_planes - 1, cy, cz), F32),
            pltpu.SemaphoreType.DMA((2,)),
        ],
        "scatter_disp", vmem_specs(4) + hbm_specs(2), disp, numbers, up, down, phi, kappa,
    )
    wet, state_a, state_b, send = fluid_call(
        "wet", 0, wet_planes, phi, kappa, up, down, forced, low, low_up, low_down, near, gram
    )
    press, token = call(
        functools.partial(gather_press, n_gx, n_gy), [f32(peers, 1, (len(NEAR) + 1) * blk), f32(8, 128)],
        [pltpu.VMEM((peers, blk), F32)], "gather_press", vmem_specs(3), wet, numbers, gram,
    )
    loads = exchange(press)
    high = shift(send, -1, 0)
    middle, state_a, state_b, token = fluid_call(
        "middle", wet_planes, cx - 4, phi, kappa, up, down, state_a, state_b, wet, token
    )
    resp, late = call(
        shell, [f32(sx, sy), f32(peers, 1, 256)],
        [
            pltpu.VMEM((hist, sx, sy), F32),
            pltpu.VMEM((sx * (sy // 128), 256), F32),
            pltpu.VMEM((8 * (sy // 128), 256), F32),
            pltpu.VMEM((sx, 32), F32),
            pltpu.VMEM((16, 32), F32),
            pltpu.VMEM((3, sx + 8, sy + 128), F32),
            pltpu.VMEM((128, 128), F32),
            pltpu.SemaphoreType.DMA((1,)),
        ],
        "shell", vmem_specs(9) + hbm_specs(1) + any_specs(1),
        loads, numbers, small, up, down, low, low_up, low_down, near,
        v_hist, token,
    )
    field, token = fluid_call(
        "end", cx - 4, cx, phi, kappa, up, down, state_a, state_b, high, middle, late
    )
    x_next = call(
        solve, f32(sx, sy),
        [pltpu.VMEM((hist, sx, sy), F32), pltpu.SemaphoreType.DMA((1,))],
        "solve", vmem_specs(3) + hbm_specs(1) + any_specs(1), exchange(late), resp, small, w_hist, token,
    )
    return (field, x_next)


def solution(mesh):
    in_specs = (
        P("gx", "gy", None),
        P("gx", "gy", None),
        P("gx", "gy"),
        P("gx", "gy", None, None),
        P("gx", "gy", None, None),
        P("gx", "gy"),
        P(None, "gx", "gy"),
        P(None, "gx", "gy"),
        P("gx", "gy"),
        P("gx", "gy"),
    )
    out_specs = (P("gx", "gy", None), P("gx", "gy"))
    return jax.shard_map(local, mesh=mesh, in_specs=in_specs, out_specs=out_specs, check_vma=False)
```
